32 devices in a mesh: section: 2 (over core), dp: 2 (over x), ctx: 2 (over y), tp: 4 (over z).
Axes of the slice: x: 2, y: 2, z: 4, core: 2. Of those that a mesh axis runs over, the one named last changes fastest.
Arguments:
- section_in: bfloat16 [2, 4, 1024, 1536], P(None, 'dp', 'ctx'), may hold values from -6 to 6
- segments: int32 [2, 4, 1024], P(None, 'dp', 'ctx'), may hold values from 0 to 5, as said below
- positions: int32 [2, 4, 1024], P(None, 'dp', 'ctx'), may hold values from 0 to 3070, as said below
- query_weight: bfloat16 [2, 1536, 1536], P('section', ('dp', 'ctx'), 'tp'), may hold values from -0.15625 to 0.15625
- kv_weight: bfloat16 [2, 2, 1536, 256], P('section', None, ('dp', 'ctx')), may hold values from -0.15625 to 0.15625
- output_weight: bfloat16 [2, 1536, 1536], P('section', 'tp', ('dp', 'ctx')), may hold values from -0.625 to 0.625
- gate_up: bfloat16 [2, 2, 1536, 8960], P('section', None, ('dp', 'ctx'), 'tp'), may hold values from -0.15625 to 0.15625
- down_weight: bfloat16 [2, 8960, 1536], P('section', 'tp', ('dp', 'ctx')), may hold values from -0.125 to 0.125
- norm_gains: bfloat16 [2, 2, 1536], P('section', None, ('dp', 'ctx')), may hold values from 0.099609375 to 1.8984375
- query_bias: bfloat16 [2, 12, 128], P('section', 'tp', ('dp', 'ctx')), may hold values from -3 to 3
- kv_bias: bfloat16 [2, 2, 2, 128], P('section', None, None, ('dp', 'ctx')), may hold values from -3 to 3
- out_grad: bfloat16 [2, 4, 1024, 1536], P(None, 'dp', 'ctx'), may hold values from -6 to 6
Outputs:
- section_out: bfloat16 [2, 2, 4, 1024, 1536], P('section', None, 'dp', 'ctx')
- input_grad: bfloat16 [2, 2, 4, 1024, 1536], P('section', None, 'dp', 'ctx')
- query_weight_grad: float32 [2, 1536, 1536], P('section', ('dp', 'ctx'), 'tp')
- kv_weight_grad: float32 [2, 2, 1536, 256], P('section', None, ('dp', 'ctx'))
- output_weight_grad: float32 [2, 1536, 1536], P('section', 'tp', ('dp', 'ctx'))
- gate_up_grad: float32 [2, 2, 1536, 8960], P('section', None, ('dp', 'ctx'), 'tp')
- down_weight_grad: float32 [2, 8960, 1536], P('section', 'tp', ('dp', 'ctx'))
- norm_gains_grad: float32 [2, 2, 1536], P('section', None, ('dp', 'ctx'))
- query_bias_grad: float32 [2, 12, 128], P('section', 'tp', ('dp', 'ctx'))
- kv_bias_grad: float32 [2, 2, 2, 128], P('section', None, None, ('dp', 'ctx'))
The draws below stay inside these ranges and needn't reach their ends.
Inputs may be any that keep to these rules, and one draw needn't show every extreme that they name: `segments`: in each sequence the numbers start at 0 and rise by one where a document begins; documents hold 200 to 900 tokens, except the last one, which the sequence's end cuts. In each micro-batch, on each index of dp, one of the 2 sequences is a single document, and another is packed with as many documents as fit, so that its last number is the promised most. `positions`: A token's position is its place within its document plus an offset below 2048 drawn for each document.
All inputs are finite; a program needn't handle non-finite values.
Results may differ from the reference program's by a relative error of at most 0.03.
Values may be sent and summed in bfloat16 or wider, within the bound.
A program may use at most 448 MiB of HBM per device.

```python
import jax
import jax.numpy as jnp
from jax import lax

D = 1536
HEADS = 12
KV_HEADS = 2
HEAD = 128
FF = 8960
SEQ_LEN = 1024
DOC_MIN = 200
DOC_MAX = 900
POS_SHIFT = 2048
MICRO = 2
SEQS = 2
SEQS_ALL = 4
N_DP = 2


def doc_layout(key):
    count = SEQ_LEN // DOC_MIN + 1
    most_docs = (SEQ_LEN - 1) // DOC_MIN
    extra = (SEQ_LEN - 1 - most_docs * DOC_MIN) // most_docs
    pick = jax.random.randint(jax.random.fold_in(key, 13), (MICRO, N_DP, 1), 0, SEQS)
    whole = (jnp.arange(SEQS)[None, None, :] == pick).reshape(MICRO, SEQS_ALL, 1)
    dense = (jnp.arange(SEQS)[None, None, :] == (pick + 1) % SEQS).reshape(MICRO, SEQS_ALL, 1)
    lengths = jax.random.randint(jax.random.fold_in(key, 11), (MICRO, SEQS_ALL, count), DOC_MIN, DOC_MAX + 1)
    packed = DOC_MIN + jax.random.randint(jax.random.fold_in(key, 14), (MICRO, SEQS_ALL, count), 0, extra + 1)
    lengths = jnp.where(dense, packed, lengths)
    ends = jnp.cumsum(lengths, axis=-1)
    starts = ends - lengths
    place = jnp.arange(SEQ_LEN)
    seg_ids = jnp.sum((ends[..., None, :] <= place[:, None]).astype(jnp.int32), axis=-1)
    shifts = jax.random.randint(jax.random.fold_in(key, 12), (MICRO, SEQS_ALL, count), 0, POS_SHIFT)
    begin = jnp.take_along_axis(starts, seg_ids, axis=-1)
    offset = jnp.take_along_axis(shifts, seg_ids, axis=-1)
    places = place - begin + offset
    seg_ids = jnp.where(whole, 0, seg_ids)
    places = jnp.where(whole, place + shifts[..., :1], places)
    return (seg_ids.astype(jnp.int32), places.astype(jnp.int32))


def draw_segments(key, part):
    seg_ids, places = doc_layout(key)
    return seg_ids


def draw_positions(key, part):
    seg_ids, places = doc_layout(key)
    return places


def levels(own_key, dims, cuts, low, top_value):
    level = 1.0
    for dim, shards_of in cuts:
        heights = jax.random.uniform(jax.random.fold_in(jax.random.fold_in(own_key, 6), dim), (shards_of,), jnp.float32, low / len(cuts), top_value / len(cuts))
        level = level * jnp.repeat(jnp.exp(heights), dims[dim] // shards_of).reshape((-1,) + (1,) * (len(dims) - 1 - dim))
    return level


def bell_draw(own_key, extent, deviation, limit, cuts=(), kind=jnp.bfloat16):
    entries = deviation * jax.random.normal(own_key, extent, jnp.float32)
    if cuts:
        entries = entries * levels(own_key, extent, cuts, -0.22, 0.18)
    return jnp.clip(entries, -limit, limit).astype(kind)


def setup_inputs(seed: int = 0) -> dict:
    key_of = jax.random.split(jax.random.key(seed), 13)
    section_in = bell_draw(key_of[0], (MICRO, SEQS_ALL, SEQ_LEN, D), 1.0, 6.0, ((1, 2), (2, 2)))
    segments = draw_segments(jax.random.fold_in(key_of[12], 71), 0)
    positions = draw_positions(jax.random.fold_in(key_of[12], 71), 0)
    query_weight = bell_draw(key_of[3], (2, D, HEADS * HEAD), D ** -0.5, 0.15625, ((0, 2), (1, 4), (2, 4)))
    kv_weight = bell_draw(key_of[4], (2, 2, D, KV_HEADS * HEAD), D ** -0.5, 0.15625, ((0, 2), (2, 4)))
    output_weight = bell_draw(key_of[5], (2, HEADS * HEAD, D), (HEADS * HEAD // 16) ** -0.5, 0.625, ((0, 2), (1, 4), (2, 4)))
    gate_up = bell_draw(key_of[6], (2, 2, D, FF), D ** -0.5, 0.15625, ((0, 2), (2, 4), (3, 4)))
    down_weight = bell_draw(key_of[7], (2, FF, D), (FF // 4) ** -0.5, 0.125, ((0, 2), (1, 4), (2, 4)))
    norm_gains = jnp.clip(1.0 + 0.18 * jax.random.normal(key_of[8], (2, 2, D), jnp.float32), 0.099609375, 1.8984375).astype(jnp.bfloat16)
    query_bias = bell_draw(key_of[9], (2, HEADS, HEAD), 0.5, 3.0, ((0, 2), (1, 4), (2, 4)))
    kv_bias = bell_draw(key_of[10], (2, 2, KV_HEADS, HEAD), 0.5, 3.0, ((0, 2), (3, 4)))
    out_grad = bell_draw(key_of[11], (MICRO, SEQS_ALL, SEQ_LEN, D), 1.0, 6.0, ((1, 2), (2, 2)))
    return dict(section_in=section_in, segments=segments, positions=positions, query_weight=query_weight, kv_weight=kv_weight, output_weight=output_weight, gate_up=gate_up, down_weight=down_weight, norm_gains=norm_gains, query_bias=query_bias, kv_bias=kv_bias, out_grad=out_grad)


EPS = 1e-06
ROPE_BASE = 1000000.0
NEG = -1e+30

@jax.custom_vjp
def lower_section(v):
    return lax.optimization_barrier(v.astype(jnp.bfloat16)).astype(jnp.float32)

@jax.custom_vjp
def lower_section_backward(v):
    return v

def low_keep(v):
    return (lower_section(v), None)

def low_pass(kept, grad):
    return (grad,)

def back_keep(v):
    return (v, None)

def back_low(kept, grad):
    return (lower_section(grad),)
lower_section.defvjp(low_keep, low_pass)
lower_section_backward.defvjp(back_keep, back_low)

def highest_precision(form, left, right):
    return jnp.einsum(form, left, right, precision=lax.Precision.HIGHEST)

def rotate(values, cosine, sine):
    half = values.shape[-1] // 2
    turned = jnp.concatenate([-values[..., half:], values[..., :half]], axis=-1)
    return values * cosine + turned * sine

def rope_tables(places):
    steps = jnp.arange(HEAD // 2, dtype=jnp.float32) * (2.0 / HEAD)
    inverse = ROPE_BASE ** (-steps)
    angles = places.astype(jnp.float32)[..., None] * inverse
    angles = jnp.concatenate([angles, angles], axis=-1)
    return (jnp.cos(angles), jnp.sin(angles))

def normalize(rows_in, gain):
    return rows_in * lax.rsqrt(lax.optimization_barrier(jnp.mean(rows_in * rows_in, axis=-1, keepdims=True)) + EPS) * gain

def attend(pieces):
    query, keys, values, seg_ids = pieces
    group = HEADS // KV_HEADS
    keys = jnp.repeat(keys, group, axis=1)
    values = jnp.repeat(values, group, axis=1)
    scores = lower_section_backward(highest_precision('ihd,jhd->hij', query, keys) * HEAD ** (-0.5))
    place = jnp.arange(seg_ids.shape[0])
    mask = (place[None, :] <= place[:, None]) & (seg_ids[:, None] == seg_ids[None, :])
    scores = jnp.where(mask[None], scores, NEG)
    probs = lower_section(jax.nn.softmax(scores, axis=-1))
    return highest_precision('hij,jhd->ihd', probs, values)

def layer(layer_input, params, seg_ids, places):
    query_projection_weight, key_value_weight, output_projection_weight, gate_projection_weight, down_projection_weight, gains, query_projection_bias, key_value_bias = params
    seqs, length, width = layer_input.shape
    first_normalized = lower_section(normalize(layer_input, gains[0]))
    query_linear = lower_section_backward(highest_precision('kah,hm->kam', first_normalized, query_projection_weight) + query_projection_bias.reshape(-1))
    key_linear = lower_section_backward(highest_precision('kah,hm->kam', first_normalized, key_value_weight[0]) + key_value_bias[0].reshape(-1))
    value_rows = lower_section_backward(lower_section(highest_precision('kah,hm->kam', first_normalized, key_value_weight[1]) + key_value_bias[1].reshape(-1)))
    cosine, sine = rope_tables(places)
    query_rot = lower_section(rotate(query_linear.reshape(seqs, length, HEADS, HEAD), cosine[:, :, None], sine[:, :, None]))
    key_rot = lower_section(rotate(key_linear.reshape(seqs, length, KV_HEADS, HEAD), cosine[:, :, None], sine[:, :, None]))
    values = value_rows.reshape(seqs, length, KV_HEADS, HEAD)
    attended_output = lax.map(jax.checkpoint(attend), (query_rot, key_rot, values, seg_ids))
    attended_output = lower_section_backward(lower_section(attended_output.reshape(seqs, length, HEADS * HEAD)))
    middle_hidden = layer_input + lower_section_backward(highest_precision('imb,bz->imz', attended_output, output_projection_weight))
    second_normalized = lower_section(normalize(middle_hidden, gains[1]))
    gate_activation = lower_section_backward(highest_precision('otg,gx->otx', second_normalized, gate_projection_weight[0]))
    up_projection_value = lower_section_backward(highest_precision('otg,gx->otx', second_normalized, gate_projection_weight[1]))
    inner_hidden = lower_section(jax.nn.silu(gate_activation) * up_projection_value)
    return middle_hidden + lower_section_backward(highest_precision('ygp,po->ygo', inner_hidden, down_projection_weight))

def reference(section_in, segments, positions, query_weight, kv_weight, output_weight, gate_up, down_weight, norm_gains, query_bias, kv_bias, out_grad):
    weights = tuple((w.astype(jnp.float32) for w in (query_weight, kv_weight, output_weight, gate_up, down_weight, norm_gains, query_bias, kv_bias)))

    def both(inputs, params, bridge, seg_ids, places):
        first_w = tuple((w[0] for w in params))
        second_w = tuple((w[1] for w in params))
        out_one = layer(inputs, first_w, seg_ids, places)
        middle_hidden = lower_section_backward(lower_section(out_one) + bridge)
        out_two = layer(middle_hidden, second_w, seg_ids, places)
        return (out_one, out_two)

    def step(totals, batch):
        inputs, seg_ids, places, cotangent = batch
        bridge = jnp.zeros(inputs.shape, jnp.float32)
        outs, pullback = jax.vjp(lambda a, w, b: both(a, w, b, seg_ids, places), inputs.astype(jnp.float32), weights, bridge)
        grad_in, grad_w, grad_bridge = pullback((jnp.zeros_like(outs[0]), cotangent.astype(jnp.float32)))
        totals = jax.tree.map(jnp.add, totals, grad_w)
        return (totals, (outs[0].astype(jnp.bfloat16), outs[1].astype(jnp.bfloat16), grad_in.astype(jnp.bfloat16), grad_bridge.astype(jnp.bfloat16)))
    zeros = jax.tree.map(jnp.zeros_like, weights)
    totals, results = lax.scan(step, zeros, (section_in, segments, positions, out_grad))
    first_out, second_out, first_grad, second_grad = results
    section_out = jnp.stack([first_out, second_out])
    input_grad = jnp.stack([first_grad, second_grad])
    return (section_out, input_grad, totals[0], totals[1], totals[2], totals[3], totals[4], totals[5], totals[6], totals[7])
```

```python
import jax
import jax.numpy as jnp
from jax import lax
from jax.sharding import PartitionSpec as P

HEADS = 12
KV_HEADS = 2
HEAD = 128

EPS = 1e-06
ROPE_BASE = 1000000.0
NEG = -1e30
SCALE = HEAD ** (-0.5)
CHUNKS = 2

F32 = jnp.float32
BF16 = jnp.bfloat16


def dot(form, left, right):
    return jnp.einsum(form, left, right, preferred_element_type=F32)


def swap(value):
    return lax.ppermute(value, "section", [(0, 1), (1, 0)])


def chain_sum(part):
    count = lax.axis_size("tp")
    place = lax.axis_index("tp")
    middle = count // 2
    total = part
    for hop in range(middle - 1):
        got = lax.ppermute(total, "tp", [(hop, hop + 1), (count - 1 - hop, count - 2 - hop)])
        total = (total.astype(F32) + got.astype(F32)).astype(BF16)
    got = lax.ppermute(total, "tp", [(middle - 1, middle), (middle, middle - 1)])
    total = (total.astype(F32) + got.astype(F32)).astype(BF16)
    for hop in range(middle - 1):
        low, high = middle - 1 - hop, middle + hop
        got = lax.ppermute(total, "tp", [(low, low - 1), (high, high + 1)])
        total = jnp.where((place == low - 1) | (place == high + 1), got, total)
    return total


def tp_sum(part):
    rows = part.shape[0] // CHUNKS
    return jnp.concatenate([chain_sum(part[c * rows : (c + 1) * rows]) for c in range(CHUNKS)], axis=0)


def rotate(values, cosine, sine):
    half = values.shape[-1] // 2
    turned = jnp.concatenate([-values[..., half:], values[..., :half]], axis=-1)
    return values * cosine + turned * sine


def unrotate(grads, cosine, sine):
    half = grads.shape[-1] // 2
    scaled = grads * sine
    turned = jnp.concatenate([scaled[..., half:], -scaled[..., :half]], axis=-1)
    return grads * cosine + turned


def rope_tables(places):
    steps = jnp.arange(HEAD // 2, dtype=F32) * (2.0 / HEAD)
    inverse = ROPE_BASE ** (-steps)
    angles = places.astype(F32)[..., None] * inverse
    angles = jnp.concatenate([angles, angles], axis=-1)
    return (jnp.cos(angles), jnp.sin(angles))


def normalize(rows_in, gain):
    factor = lax.rsqrt(jnp.mean(rows_in * rows_in, axis=-1, keepdims=True) + EPS)
    return (factor, (rows_in * factor * gain).astype(BF16))


def norm_back(grad_out, rows_in, factor, gain):
    unit = rows_in * factor
    gain_grad = jnp.sum(grad_out * unit, axis=0)
    weighted = grad_out * gain
    return (
        factor * (weighted - unit * jnp.mean(weighted * unit, axis=-1, keepdims=True)),
        gain_grad,
    )


def over_ctx(value):
    if lax.axis_size("ctx") == 2:
        other = lax.ppermute(value, "ctx", [(0, 1), (1, 0)])
        return jnp.concatenate([value, other], axis=value.ndim - 2)
    return lax.all_gather(value, "ctx", axis=value.ndim - 2, tiled=True)


def back_over_ctx(grads):
    span = grads.shape[-2] // lax.axis_size("ctx")
    grads = grads.astype(BF16)
    if lax.axis_size("ctx") == 2:
        other = lax.ppermute(grads[..., span:, :], "ctx", [(0, 1), (1, 0)])
        return grads[..., :span, :].astype(F32) + other.astype(F32)
    return lax.psum_scatter(grads, "ctx", scatter_dimension=grads.ndim - 2, tiled=True).astype(F32)


def attention_forward(layer_in, tables, mask, weights):
    span = layer_in.shape[0]
    wq, wkv, wo, gains, q_bias, kv_bias = weights
    heads_here = wq.shape[1] // HEAD
    cosine, sine = tables
    rows_in = layer_in.astype(F32)
    factor, normed = normalize(rows_in, gains[0])
    query = dot("rd,de->re", normed, wq) + q_bias.reshape(-1)
    query = rotate(query.reshape(span, heads_here, HEAD), cosine[:, None], sine[:, None]).astype(BF16)
    kv_lin = dot("rd,de->re", normed, wkv) + kv_bias.reshape(-1)
    key = rotate(kv_lin[:, :HEAD], cosine, sine).astype(BF16)
    kv = over_ctx(jnp.stack([key, kv_lin[:, HEAD:].astype(BF16)]))
    scores = jnp.where(mask, dot("ihd,jd->hij", query, kv[0]) * SCALE, NEG)
    top = jnp.max(scores, axis=-1, keepdims=True)
    log_total = top + jnp.log(jnp.sum(jnp.exp(scores - top), axis=-1, keepdims=True))
    probs = jnp.exp(scores - log_total).astype(BF16)
    attended = dot("hij,jd->ihd", probs, kv[1]).reshape(span, heads_here * HEAD).astype(BF16)
    part = dot("re,de->rd", attended, wo).astype(BF16)
    return part, dict(layer_in=layer_in, factor=factor, normed=normed, query=query, kv=kv, log_total=log_total, attended=attended)


def ffn_forward(layer_in, attn_out, gains, w_own, w_other, w_down, first):
    middle = layer_in.astype(F32) + attn_out.astype(F32)
    factor, normed = normalize(middle, gains[1])
    own = dot("rd,df->rf", normed, w_own)
    other = dot("rd,df->rf", normed, w_other)
    gate, up = jnp.where(first, own, other), jnp.where(first, other, own)
    inner = (jax.nn.silu(gate) * up).astype(BF16)
    part = dot("rf,df->rd", inner, w_down).astype(BF16)
    return part, dict(attn_out=attn_out, factor_two=factor, normed_two=normed, own=own.astype(BF16), other=other.astype(BF16), inner=inner)


def ffn_backward(ffn_grad, kept, w_own, w_other, w_down, first):
    inner_grad = dot("rd,df->rf", ffn_grad, w_down)
    own, other = kept["own"].astype(F32), kept["other"].astype(F32)
    gate, up = jnp.where(first, own, other), jnp.where(first, other, own)
    sig = jax.nn.sigmoid(gate)
    gate_grad = inner_grad * up * sig * (1.0 + gate * (1.0 - sig))
    up_grad = inner_grad * gate * sig
    own_grad = jnp.where(first, gate_grad, up_grad).astype(BF16)
    other_grad = jnp.where(first, up_grad, gate_grad).astype(BF16)
    part = dot("rf,df->rd", own_grad, w_own) + dot("rf,df->rd", other_grad, w_other)
    return part.astype(BF16), own_grad, other_grad


def attention_backward(upstream, normed_two_grad, kept, tables, mask, weights):
    wq, wkv, wo, gains, q_bias, kv_bias = weights
    heads_here = wq.shape[1] // HEAD
    span = upstream.shape[0]
    cosine, sine = tables
    middle = kept["layer_in"].astype(F32) + kept["attn_out"].astype(F32)
    norm_grad, gain_two = norm_back(normed_two_grad.astype(F32), middle, kept["factor_two"], gains[1])
    middle_grad = upstream.astype(F32) + norm_grad
    attn_grad = middle_grad.astype(BF16)
    heads_grad = dot("rd,de->re", attn_grad, wo).astype(BF16).reshape(span, heads_here, HEAD)
    query, kv = kept["query"], kept["kv"]
    scores = jnp.where(mask, dot("ihd,jd->hij", query, kv[0]) * SCALE, NEG)
    probs = jnp.exp(scores - kept["log_total"])
    prob_grad = dot("ihd,jd->hij", heads_grad, kv[1])
    attended = kept["attended"].reshape(span, heads_here, HEAD)
    row_sum = jnp.sum(attended.astype(F32) * heads_grad.astype(F32), axis=-1).T[..., None]
    score_grad = (probs * (prob_grad - row_sum)).astype(BF16)
    query_grad = dot("hij,jd->ihd", score_grad, kv[0]) * SCALE
    key_grad = dot("hij,ihd->jd", score_grad, query) * SCALE
    value_grad = dot("hij,ihd->jd", probs.astype(BF16), heads_grad)
    kv_grad = back_over_ctx(jnp.stack([key_grad, value_grad]))
    q_lin_grad = unrotate(query_grad, cosine[:, None], sine[:, None]).reshape(span, heads_here * HEAD).astype(BF16)
    k_lin_grad = unrotate(kv_grad[0], cosine, sine)
    lin_grad = jnp.concatenate([q_lin_grad, k_lin_grad.astype(BF16), kv_grad[1].astype(BF16)], axis=-1)
    part = dot("re,de->rd", lin_grad, jnp.concatenate([wq, wkv], axis=-1)).astype(BF16)
    return part, middle_grad, attn_grad, lin_grad, gain_two


def input_backward(normed_one_grad, middle_grad, kept, gains):
    norm_grad, gain_one = norm_back(
        normed_one_grad.astype(F32), kept["layer_in"].astype(F32), kept["factor"], gains[0]
    )
    return (middle_grad + norm_grad).astype(BF16), gain_one


def local(
    section_in,
    segments,
    positions,
    query_weight,
    kv_weight,
    output_weight,
    gate_up,
    down_weight,
    norm_gains,
    query_bias,
    kv_bias,
    out_grad,
):
    sec = lax.axis_index("section")
    first = sec == 0
    group = HEADS // KV_HEADS
    heads_here = HEADS // lax.axis_size("tp")
    head_pick = lax.axis_index("tp") * heads_here // group
    shards = lax.axis_size("dp") * lax.axis_size("ctx")
    ranks = ("dp", "ctx")
    seqs, span, width = section_in.shape[1:]
    shard = query_weight.shape[1]
    q_cols = query_weight.shape[2]
    ff = gate_up.shape[3]

    def per_layer(mine, theirs):
        return jnp.where(first, mine, theirs), jnp.where(first, theirs, mine)

    packed = jnp.concatenate([query_weight[0], kv_weight[0, 0], kv_weight[0, 1], output_weight[0].T], axis=1)
    packed = lax.all_gather(packed, ranks, axis=0, tiled=True)
    packed = per_layer(packed, swap(packed))
    small = jnp.concatenate([norm_gains[0].reshape(-1), query_bias[0].reshape(-1), kv_bias[0].reshape(-1)])
    small = lax.all_gather(small, ("section",) + ranks, axis=0).reshape(2, shards, -1)
    attn_weights = []
    kv_width = KV_HEADS * HEAD
    for layer in range(2):
        p, s = packed[layer], small[layer]
        wq = p[:, :q_cols]
        wk = lax.dynamic_slice_in_dim(p[:, q_cols : q_cols + kv_width], head_pick * HEAD, HEAD, 1)
        wv = lax.dynamic_slice_in_dim(p[:, q_cols + kv_width : q_cols + 2 * kv_width], head_pick * HEAD, HEAD, 1)
        wo = p[:, q_cols + 2 * kv_width :]
        gains = s[:, : 2 * shard].reshape(shards, 2, shard).transpose(1, 0, 2).reshape(2, width)
        piece = HEAD // shards
        q_b = s[:, 2 * shard : 2 * shard + heads_here * piece].reshape(shards, heads_here, piece)
        q_b = q_b.transpose(1, 0, 2).reshape(heads_here, HEAD)
        kv_b = s[:, 2 * shard + heads_here * piece :].reshape(shards, 2, KV_HEADS, piece)
        kv_b = kv_b.transpose(1, 2, 0, 3).reshape(2, KV_HEADS, HEAD)
        kv_b = lax.dynamic_slice_in_dim(kv_b, head_pick, 1, 1)
        attn_weights.append((wq, jnp.concatenate([wk, wv], axis=1), wo, gains.astype(F32), q_b.astype(F32), kv_b.astype(F32)))

    half = shard // 2
    mine = lax.dynamic_index_in_dim(gate_up[0], sec, 0, keepdims=False)
    theirs = swap(lax.dynamic_index_in_dim(gate_up[0], 1 - sec, 0, keepdims=False))
    gate_up_shards = per_layer(mine, theirs)
    down_t = down_weight[0].T
    mine = lax.dynamic_slice_in_dim(down_t, sec * half, half, 0)
    theirs = swap(lax.dynamic_slice_in_dim(down_t, (1 - sec) * half, half, 0))
    down_shards = per_layer(mine, theirs)
    ffn_weights = []
    for layer in range(2):
        own = lax.all_gather(gate_up_shards[layer], ranks, axis=0, tiled=True)
        other = swap(own)
        down_own = lax.all_gather(down_shards[layer], ranks, axis=0)
        down_other = swap(down_own)
        down = jnp.stack(per_layer(down_own, down_other), axis=1).reshape(width, ff)
        ffn_weights.append((own, other, down))

    micro = sec
    seg = lax.dynamic_index_in_dim(segments, micro, 0, keepdims=False)
    pos = lax.dynamic_index_in_dim(positions, micro, 0, keepdims=False)
    hidden = lax.dynamic_index_in_dim(section_in, micro, 0, keepdims=False)
    grad_top = lax.dynamic_index_in_dim(out_grad, micro, 0, keepdims=False)
    rows_at = lax.axis_index("ctx") * span + jnp.arange(span)
    count = lax.axis_size("ctx")
    if count == 2:
        keys_at = jnp.concatenate([rows_at, (1 - lax.axis_index("ctx")) * span + jnp.arange(span)])
    else:
        keys_at = jnp.arange(count * span)
    seg_keys = over_ctx(seg[..., None])[..., 0]
    masks, tables = [], []
    for s in range(seqs):
        causal = keys_at[None, :] <= rows_at[:, None]
        masks.append((causal & (seg[s][:, None] == seg_keys[s][None, :]))[None])
        tables.append(rope_tables(pos[s]))

    kept = [[None] * seqs for _ in range(2)]
    layer_in = [hidden[s] for s in range(seqs)]
    outs = []
    for layer in range(2):
        weights = attn_weights[layer]
        parts = [None] * seqs
        for s in range(seqs):
            parts[s], kept[layer][s] = attention_forward(layer_in[s], tables[s], masks[s], weights)
        attn_out = [tp_sum(parts[s]) for s in range(seqs)]
        for s in range(seqs):
            parts[s], more = ffn_forward(layer_in[s], attn_out[s], weights[3], *ffn_weights[layer], first)
            kept[layer][s].update(more)
        next_in = []
        for s in range(seqs):
            ffn_out = tp_sum(parts[s]).astype(F32)
            middle = layer_in[s].astype(F32) + attn_out[s].astype(F32)
            next_in.append((middle + ffn_out).astype(BF16))
        layer_in = next_in
        outs.append(jnp.stack(layer_in))

    def to_section(values):
        low = lax.ppermute(values[0], "section", [(1, 0)])
        high = lax.ppermute(values[1], "section", [(0, 1)])
        return jnp.stack([jnp.where(first, values[0], high), jnp.where(first, low, values[1])])

    section_out = to_section(outs)

    upstream = [grad_top[s] for s in range(seqs)]
    in_grads = [None, None]
    gate_up_grads, down_grads, packed_grads = [None, None], [None, None], [None, None]
    for layer in (1, 0):
        weights = attn_weights[layer]
        w_own, w_other, w_down = ffn_weights[layer]
        k = kept[layer]
        parts, own_grads, other_grads = zip(
            *[ffn_backward(upstream[s], k[s], w_own, w_other, w_down, first) for s in range(seqs)]
        )
        normed_two_grad = [tp_sum(p) for p in parts]
        normed_two = jnp.concatenate([k[s]["normed_two"] for s in range(seqs)])
        own_w = dot("rd,rf->df", normed_two, jnp.concatenate(own_grads)).astype(BF16)
        other_w = dot("rd,rf->df", normed_two, jnp.concatenate(other_grads)).astype(BF16)
        own_w = (own_w.astype(F32) + swap(other_w).astype(F32)).astype(BF16)
        gate_up_grads[layer] = lax.psum_scatter(own_w, ranks, scatter_dimension=0, tiled=True)
        down_w = dot("rd,rf->df", jnp.concatenate(upstream), jnp.concatenate([k[s]["inner"] for s in range(seqs)])).astype(BF16)
        down_w = down_w.reshape(shards, 2, half, ff)
        down_own = lax.dynamic_index_in_dim(down_w, sec, 1, keepdims=False)
        down_other = lax.dynamic_index_in_dim(down_w, 1 - sec, 1, keepdims=False)
        down_own = (down_own.astype(F32) + swap(down_other).astype(F32)).astype(BF16)
        down_grads[layer] = lax.psum_scatter(
            down_own.reshape(shards * half, ff), ranks, scatter_dimension=0, tiled=True
        )

        results = [
            attention_backward(upstream[s], normed_two_grad[s], k[s], tables[s], masks[s], weights) for s in range(seqs)
        ]
        parts, middle_grads, attn_grads, lin_grads, gains_two = zip(*results)
        normed_one_grad = [tp_sum(p) for p in parts]
        lin_grad = jnp.concatenate(lin_grads)
        normed_one = jnp.concatenate([k[s]["normed"] for s in range(seqs)])
        lin_w = dot("rd,re->de", normed_one, lin_grad)
        attended = jnp.concatenate([k[s]["attended"] for s in range(seqs)])
        out_w = dot("rd,re->de", jnp.concatenate(attn_grads), attended)
        results = [input_backward(normed_one_grad[s], middle_grads[s], k[s], weights[3]) for s in range(seqs)]
        upstream = [r[0] for r in results]
        in_grads[layer] = jnp.stack(upstream)
        gain_cols = jnp.stack([sum(r[1] for r in results), sum(gains_two)], axis=1)
        bias = jnp.sum(lin_grad.astype(F32), axis=0)
        piece = HEAD // shards
        bias = bias.reshape(heads_here + 2, shards, piece).transpose(1, 0, 2).reshape(shards, (heads_here + 2) * piece)
        bias = jnp.pad(bias, ((0, 0), (0, -bias.shape[1] % shard)))
        bias = bias.reshape(shards, -1, shard).transpose(0, 2, 1).reshape(width, -1)
        extra = jnp.concatenate([gain_cols, bias], axis=1)
        extra = jnp.pad(extra, ((0, 0), (0, HEAD - extra.shape[1])))
        packed_grads[layer] = jnp.concatenate([lin_w, out_w, extra], axis=1).astype(BF16)

    input_grad = to_section(in_grads)

    low = lax.ppermute(packed_grads[0], "section", [(1, 0)])
    high = lax.ppermute(packed_grads[1], "section", [(0, 1)])
    packed_total = jnp.where(
        first, packed_grads[0].astype(F32) + low.astype(F32), packed_grads[1].astype(F32) + high.astype(F32)
    ).astype(BF16)
    packed_total = lax.psum_scatter(packed_total, ranks, scatter_dimension=0, tiled=True).astype(F32)
    q_grad = packed_total[:, :q_cols]
    kv_narrow = packed_total[:, q_cols : q_cols + 2 * HEAD].reshape(shard, 2, HEAD)
    o_grad = packed_total[:, q_cols + 2 * HEAD : 2 * q_cols + 2 * HEAD].T
    extra = packed_total[:, 2 * q_cols + 2 * HEAD :]
    gains_grad = extra[:, :2].T
    piece = HEAD // shards
    bias_cols = -(-(heads_here + 2) * piece // shard)
    bias = extra[:, 2 : 2 + bias_cols].T.reshape(-1)[: (heads_here + 2) * piece].reshape(heads_here + 2, piece)
    q_bias_grad = bias[:heads_here]
    kv_full = jnp.zeros((shard, 2, KV_HEADS, HEAD), F32)
    kv_full = lax.dynamic_update_slice_in_dim(kv_full, kv_narrow[:, :, None], head_pick, 2)
    bias_full = jnp.zeros((2, KV_HEADS, piece), F32)
    bias_full = lax.dynamic_update_slice_in_dim(bias_full, bias[heads_here:, None], head_pick, 1)
    flat = bias_full.reshape(-1)
    flat = jnp.pad(flat, (0, -flat.shape[0] % (2 * KV_HEADS * HEAD)))
    flat_rows = flat.shape[0] // (2 * KV_HEADS * HEAD)
    joined = jnp.concatenate([kv_full.reshape(shard, -1), flat.reshape(flat_rows, -1)]).astype(BF16)
    joined = chain_sum(joined).astype(F32)
    kv_grad = joined[:shard].reshape(shard, 2, KV_HEADS * HEAD).transpose(1, 0, 2)
    kv_bias_grad = joined[shard:].reshape(-1)[: 2 * KV_HEADS * piece].reshape(2, KV_HEADS, piece)

    def collect(values):
        kept_half = jnp.where(first, values[0], values[1])
        other = swap(jnp.where(first, values[1], values[0]))
        return jnp.where(first, kept_half, other), jnp.where(first, other, kept_half)

    gate_up_grad = jnp.stack(collect(gate_up_grads)).astype(F32)
    down_grad = jnp.concatenate(collect(down_grads), axis=0).T.astype(F32)
    return (
        section_out[None],
        input_grad[None],
        q_grad[None],
        kv_grad[None],
        o_grad[None],
        gate_up_grad[None],
        down_grad[None],
        gains_grad[None],
        q_bias_grad[None],
        kv_bias_grad[None],
    )


def solution(mesh):
    in_specs = (
        P(None, "dp", "ctx", None),
        P(None, "dp", "ctx"),
        P(None, "dp", "ctx"),
        P("section", ("dp", "ctx"), "tp"),
        P("section", None, ("dp", "ctx"), None),
        P("section", "tp", ("dp", "ctx")),
        P("section", None, ("dp", "ctx"), "tp"),
        P("section", "tp", ("dp", "ctx")),
        P("section", None, ("dp", "ctx")),
        P("section", "tp", ("dp", "ctx")),
        P("section", None, None, ("dp", "ctx")),
        P(None, "dp", "ctx", None),
    )
    out_specs = (
        P("section", None, "dp", "ctx", None),
        P("section", None, "dp", "ctx", None),
        P("section", ("dp", "ctx"), "tp"),
        P("section", None, ("dp", "ctx"), None),
        P("section", "tp", ("dp", "ctx")),
        P("section", None, ("dp", "ctx"), "tp"),
        P("section", "tp", ("dp", "ctx")),
        P("section", None, ("dp", "ctx")),
        P("section", "tp", ("dp", "ctx")),
        P("section", None, None, ("dp", "ctx")),
    )
    return jax.shard_map(local, mesh=mesh, in_specs=in_specs, out_specs=out_specs, check_vma=False)
```

```python
import jax
import jax.numpy as jnp
from jax import lax
from jax.experimental import pallas as pl
from jax.experimental.pallas import tpu as pltpu
from jax.sharding import PartitionSpec as P

HEADS = 12
KV_HEADS = 2
HEAD = 128

EPS = 1e-06
ROPE_BASE = 1000000.0
NEG = -1e30
SCALE = HEAD ** (-0.5)
CHUNKS = 8
MESH = pl.DeviceIdType.MESH

F32 = jnp.float32
BF16 = jnp.bfloat16


def dot(form, left, right):
    return jnp.einsum(form, left, right, preferred_element_type=F32)


def swap(value):
    return lax.ppermute(value, "section", [(0, 1), (1, 0)])


def chain_sum(part):
    count = lax.axis_size("tp")
    place = lax.axis_index("tp")
    middle = count // 2
    total = part
    for hop in range(middle - 1):
        got = lax.ppermute(total, "tp", [(hop, hop + 1), (count - 1 - hop, count - 2 - hop)])
        total = (total.astype(F32) + got.astype(F32)).astype(BF16)
    got = lax.ppermute(total, "tp", [(middle - 1, middle), (middle, middle - 1)])
    total = (total.astype(F32) + got.astype(F32)).astype(BF16)
    for hop in range(middle - 1):
        low, high = middle - 1 - hop, middle + hop
        got = lax.ppermute(total, "tp", [(low, low - 1), (high, high + 1)])
        total = jnp.where((place == low - 1) | (place == high + 1), got, total)
    return total


class Chain:
    def __init__(self, part, total, from_end, from_peer, joined, sems):
        self.part, self.total = part, total
        self.from_end, self.from_peer, self.joined = from_end, from_peer, joined
        self.sems = sems
        self.rows = part.shape[0] // CHUNKS
        place = lax.axis_index("tp")
        self.is_middle = (place == 1) | (place == 2)
        self.inner = jnp.where(place < 2, place + 1, place - 1)
        self.outer = jnp.where(place < 2, place - 1, place + 1)

    def greet(self):
        barrier = pltpu.get_barrier_semaphore()
        pl.semaphore_signal(barrier, inc=1, device_id={"tp": self.inner}, device_id_type=MESH)

        @pl.when(self.is_middle)
        def _():
            pl.semaphore_signal(barrier, inc=1, device_id={"tp": self.outer}, device_id_type=MESH)
            pl.semaphore_wait(barrier, 2)

        @pl.when(jnp.logical_not(self.is_middle))
        def _():
            pl.semaphore_wait(barrier, 1)

    def at(self, ref, c):
        return ref.at[pl.ds(c * self.rows, self.rows)]

    def copy(self, source, target, c, step, place):
        return pltpu.make_async_remote_copy(
            src_ref=self.at(source, c),
            dst_ref=self.at(target, c),
            send_sem=self.sems.at[2 * step, c],
            recv_sem=self.sems.at[2 * step + 1, c],
            device_id={"tp": place},
            device_id_type=MESH,
        )

    def inward(self, c):
        return self.copy(self.part, self.from_end, c, 0, self.inner)

    def across(self, c):
        return self.copy(self.joined, self.from_peer, c, 1, self.inner)

    def outward(self, c):
        return self.copy(self.total, self.total, c, 2, self.outer)

    def start(self):
        self.greet()

        @pl.when(jnp.logical_not(self.is_middle))
        def _():
            @pl.loop(0, CHUNKS)
            def _(c):
                self.inward(c).start()

    def join(self, c):
        self.inward(c).wait_recv()
        self.at(self.joined, c)[...] = self.at(self.part, c)[...] + self.at(self.from_end, c)[...]
        self.across(c).start()

    def close(self, c):
        self.across(c).wait_recv()
        self.at(self.total, c)[...] = self.at(self.joined, c)[...] + self.at(self.from_peer, c)[...]
        self.outward(c).start()

    def finish(self):
        @pl.when(self.is_middle)
        def _():
            @pl.loop(0, CHUNKS)
            def _(c):
                self.across(c).wait_send()
                self.outward(c).wait_send()

        @pl.when(jnp.logical_not(self.is_middle))
        def _():
            @pl.loop(0, CHUNKS)
            def _(c):
                self.inward(c).wait_send()
                self.outward(c).wait_recv()


def sum_kernel(part, total, from_end, from_peer, joined, sems):
    chain = Chain(part, total, from_end, from_peer, joined, sems)
    chain.start()

    @pl.when(chain.is_middle)
    def _():
        chain.join(0)

        @pl.loop(1, CHUNKS)
        def _(c):
            chain.join(c)
            chain.close(c - 1)

        chain.close(CHUNKS - 1)

    chain.finish()


def tp_sum(part):
    shape = part.shape
    return pl.pallas_call(
        sum_kernel,
        out_shape=jax.ShapeDtypeStruct(shape, BF16),
        in_specs=[pl.BlockSpec(memory_space=pltpu.VMEM)],
        out_specs=pl.BlockSpec(memory_space=pltpu.VMEM),
        scratch_shapes=[pltpu.VMEM(shape, BF16)] * 3 + [pltpu.SemaphoreType.DMA((6, CHUNKS))],
        compiler_params=pltpu.CompilerParams(collective_id=0, has_side_effects=True, vmem_limit_bytes=32 << 20),
        cost_estimate=pl.CostEstimate(flops=0, bytes_accessed=64 << 20, transcendentals=0),
    )(part)


def rotate(values, cosine, sine):
    half = values.shape[-1] // 2
    turned = jnp.concatenate([-values[..., half:], values[..., :half]], axis=-1)
    return values * cosine + turned * sine


def unrotate(grads, cosine, sine):
    half = grads.shape[-1] // 2
    scaled = grads * sine
    turned = jnp.concatenate([scaled[..., half:], -scaled[..., :half]], axis=-1)
    return grads * cosine + turned


def rope_tables(places):
    steps = jnp.arange(HEAD // 2, dtype=F32) * (2.0 / HEAD)
    inverse = ROPE_BASE ** (-steps)
    angles = places.astype(F32)[..., None] * inverse
    angles = jnp.concatenate([angles, angles], axis=-1)
    return (jnp.cos(angles), jnp.sin(angles))


def normalize(rows_in, gain):
    factor = lax.rsqrt(jnp.mean(rows_in * rows_in, axis=-1, keepdims=True) + EPS)
    return (factor, (rows_in * factor * gain).astype(BF16))


def norm_back(grad_out, rows_in, factor, gain):
    unit = rows_in * factor
    gain_grad = jnp.sum(grad_out * unit, axis=0)
    weighted = grad_out * gain
    return (
        factor * (weighted - unit * jnp.mean(weighted * unit, axis=-1, keepdims=True)),
        gain_grad,
    )


def over_ctx(value):
    if lax.axis_size("ctx") == 2:
        other = lax.ppermute(value, "ctx", [(0, 1), (1, 0)])
        return jnp.concatenate([value, other], axis=value.ndim - 2)
    return lax.all_gather(value, "ctx", axis=value.ndim - 2, tiled=True)


def back_over_ctx(grads):
    span = grads.shape[-2] // lax.axis_size("ctx")
    grads = grads.astype(BF16)
    if lax.axis_size("ctx") == 2:
        other = lax.ppermute(grads[..., span:, :], "ctx", [(0, 1), (1, 0)])
        return grads[..., :span, :].astype(F32) + other.astype(F32)
    return lax.psum_scatter(grads, "ctx", scatter_dimension=grads.ndim - 2, tiled=True).astype(F32)


def attention_forward(layer_in, tables, mask, weights):
    span = layer_in.shape[0]
    wq, wkv, wo, gains, q_bias, kv_bias = weights
    heads_here = wq.shape[1] // HEAD
    cosine, sine = tables
    rows_in = layer_in.astype(F32)
    factor, normed = normalize(rows_in, gains[0])
    query = dot("rd,de->re", normed, wq) + q_bias.reshape(-1)
    query = rotate(query.reshape(span, heads_here, HEAD), cosine[:, None], sine[:, None]).astype(BF16)
    kv_lin = dot("rd,de->re", normed, wkv) + kv_bias.reshape(-1)
    key = rotate(kv_lin[:, :HEAD], cosine, sine).astype(BF16)
    kv = over_ctx(jnp.stack([key, kv_lin[:, HEAD:].astype(BF16)]))
    scores = jnp.where(mask, dot("ihd,jd->hij", query, kv[0]) * SCALE, NEG)
    top = jnp.max(scores, axis=-1, keepdims=True)
    log_total = top + jnp.log(jnp.sum(jnp.exp(scores - top), axis=-1, keepdims=True))
    probs = jnp.exp(scores - log_total).astype(BF16)
    attended = dot("hij,jd->ihd", probs, kv[1]).reshape(span, heads_here * HEAD).astype(BF16)
    part = dot("re,de->rd", attended, wo).astype(BF16)
    return part, dict(layer_in=layer_in, factor=factor, normed=normed, query=query, kv=kv, log_total=log_total, attended=attended)


def ffn_forward(layer_in, attn_out, gains, w_own, w_other, w_down, first):
    middle = layer_in.astype(F32) + attn_out.astype(F32)
    factor, normed = normalize(middle, gains[1])
    own = dot("rd,df->rf", normed, w_own)
    other = dot("rd,df->rf", normed, w_other)
    gate, up = jnp.where(first, own, other), jnp.where(first, other, own)
    inner = (jax.nn.silu(gate) * up).astype(BF16)
    part = dot("rf,df->rd", inner, w_down).astype(BF16)
    return part, dict(attn_out=attn_out, factor_two=factor, normed_two=normed, own=own.astype(BF16), other=other.astype(BF16), inner=inner)


def ffn_backward(ffn_grad, kept, w_own, w_other, w_down, first):
    inner_grad = dot("rd,df->rf", ffn_grad, w_down)
    own, other = kept["own"].astype(F32), kept["other"].astype(F32)
    gate, up = jnp.where(first, own, other), jnp.where(first, other, own)
    sig = jax.nn.sigmoid(gate)
    gate_grad = inner_grad * up * sig * (1.0 + gate * (1.0 - sig))
    up_grad = inner_grad * gate * sig
    own_grad = jnp.where(first, gate_grad, up_grad).astype(BF16)
    other_grad = jnp.where(first, up_grad, gate_grad).astype(BF16)
    part = dot("rf,df->rd", own_grad, w_own) + dot("rf,df->rd", other_grad, w_other)
    return part.astype(BF16), own_grad, other_grad


def attention_backward(upstream, normed_two_grad, kept, tables, mask, weights):
    wq, wkv, wo, gains, q_bias, kv_bias = weights
    heads_here = wq.shape[1] // HEAD
    span = upstream.shape[0]
    cosine, sine = tables
    middle = kept["layer_in"].astype(F32) + kept["attn_out"].astype(F32)
    norm_grad, gain_two = norm_back(normed_two_grad.astype(F32), middle, kept["factor_two"], gains[1])
    middle_grad = upstream.astype(F32) + norm_grad
    attn_grad = middle_grad.astype(BF16)
    heads_grad = dot("rd,de->re", attn_grad, wo).astype(BF16).reshape(span, heads_here, HEAD)
    query, kv = kept["query"], kept["kv"]
    scores = jnp.where(mask, dot("ihd,jd->hij", query, kv[0]) * SCALE, NEG)
    probs = jnp.exp(scores - kept["log_total"])
    prob_grad = dot("ihd,jd->hij", heads_grad, kv[1])
    attended = kept["attended"].reshape(span, heads_here, HEAD)
    row_sum = jnp.sum(attended.astype(F32) * heads_grad.astype(F32), axis=-1).T[..., None]
    score_grad = (probs * (prob_grad - row_sum)).astype(BF16)
    query_grad = dot("hij,jd->ihd", score_grad, kv[0]) * SCALE
    key_grad = dot("hij,ihd->jd", score_grad, query) * SCALE
    value_grad = dot("hij,ihd->jd", probs.astype(BF16), heads_grad)
    kv_grad = back_over_ctx(jnp.stack([key_grad, value_grad]))
    q_lin_grad = unrotate(query_grad, cosine[:, None], sine[:, None]).reshape(span, heads_here * HEAD).astype(BF16)
    k_lin_grad = unrotate(kv_grad[0], cosine, sine)
    lin_grad = jnp.concatenate([q_lin_grad, k_lin_grad.astype(BF16), kv_grad[1].astype(BF16)], axis=-1)
    part = dot("re,de->rd", lin_grad, jnp.concatenate([wq, wkv], axis=-1)).astype(BF16)
    return part, middle_grad, attn_grad, lin_grad, gain_two


def input_backward(normed_one_grad, middle_grad, kept, gains):
    norm_grad, gain_one = norm_back(
        normed_one_grad.astype(F32), kept["layer_in"].astype(F32), kept["factor"], gains[0]
    )
    return (middle_grad + norm_grad).astype(BF16), gain_one


def local(
    section_in,
    segments,
    positions,
    query_weight,
    kv_weight,
    output_weight,
    gate_up,
    down_weight,
    norm_gains,
    query_bias,
    kv_bias,
    out_grad,
):
    sec = lax.axis_index("section")
    first = sec == 0
    group = HEADS // KV_HEADS
    heads_here = HEADS // lax.axis_size("tp")
    head_pick = lax.axis_index("tp") * heads_here // group
    shards = lax.axis_size("dp") * lax.axis_size("ctx")
    ranks = ("dp", "ctx")
    seqs, span, width = section_in.shape[1:]
    shard = query_weight.shape[1]
    q_cols = query_weight.shape[2]
    ff = gate_up.shape[3]

    def per_layer(mine, theirs):
        return jnp.where(first, mine, theirs), jnp.where(first, theirs, mine)

    packed = jnp.concatenate([query_weight[0], kv_weight[0, 0], kv_weight[0, 1], output_weight[0].T], axis=1)
    packed = lax.all_gather(packed, ranks, axis=0, tiled=True)
    packed = per_layer(packed, swap(packed))
    small = jnp.concatenate([norm_gains[0].reshape(-1), query_bias[0].reshape(-1), kv_bias[0].reshape(-1)])
    small = lax.all_gather(small, ("section",) + ranks, axis=0).reshape(2, shards, -1)
    attn_weights = []
    kv_width = KV_HEADS * HEAD
    for layer in range(2):
        p, s = packed[layer], small[layer]
        wq = p[:, :q_cols]
        wk = lax.dynamic_slice_in_dim(p[:, q_cols : q_cols + kv_width], head_pick * HEAD, HEAD, 1)
        wv = lax.dynamic_slice_in_dim(p[:, q_cols + kv_width : q_cols + 2 * kv_width], head_pick * HEAD, HEAD, 1)
        wo = p[:, q_cols + 2 * kv_width :]
        gains = s[:, : 2 * shard].reshape(shards, 2, shard).transpose(1, 0, 2).reshape(2, width)
        piece = HEAD // shards
        q_b = s[:, 2 * shard : 2 * shard + heads_here * piece].reshape(shards, heads_here, piece)
        q_b = q_b.transpose(1, 0, 2).reshape(heads_here, HEAD)
        kv_b = s[:, 2 * shard + heads_here * piece :].reshape(shards, 2, KV_HEADS, piece)
        kv_b = kv_b.transpose(1, 2, 0, 3).reshape(2, KV_HEADS, HEAD)
        kv_b = lax.dynamic_slice_in_dim(kv_b, head_pick, 1, 1)
        attn_weights.append((wq, jnp.concatenate([wk, wv], axis=1), wo, gains.astype(F32), q_b.astype(F32), kv_b.astype(F32)))

    half = shard // 2
    mine = lax.dynamic_index_in_dim(gate_up[0], sec, 0, keepdims=False)
    theirs = swap(lax.dynamic_index_in_dim(gate_up[0], 1 - sec, 0, keepdims=False))
    gate_up_shards = per_layer(mine, theirs)
    down_t = down_weight[0].T
    mine = lax.dynamic_slice_in_dim(down_t, sec * half, half, 0)
    theirs = swap(lax.dynamic_slice_in_dim(down_t, (1 - sec) * half, half, 0))
    down_shards = per_layer(mine, theirs)
    ffn_weights = []
    for layer in range(2):
        own = lax.all_gather(gate_up_shards[layer], ranks, axis=0, tiled=True)
        other = swap(own)
        down_own = lax.all_gather(down_shards[layer], ranks, axis=0)
        down_other = swap(down_own)
        down = jnp.stack(per_layer(down_own, down_other), axis=1).reshape(width, ff)
        ffn_weights.append((own, other, down))

    micro = sec
    seg = lax.dynamic_index_in_dim(segments, micro, 0, keepdims=False)
    pos = lax.dynamic_index_in_dim(positions, micro, 0, keepdims=False)
    hidden = lax.dynamic_index_in_dim(section_in, micro, 0, keepdims=False)
    grad_top = lax.dynamic_index_in_dim(out_grad, micro, 0, keepdims=False)
    rows_at = lax.axis_index("ctx") * span + jnp.arange(span)
    count = lax.axis_size("ctx")
    if count == 2:
        keys_at = jnp.concatenate([rows_at, (1 - lax.axis_index("ctx")) * span + jnp.arange(span)])
    else:
        keys_at = jnp.arange(count * span)
    seg_keys = over_ctx(seg[..., None])[..., 0]
    masks, tables = [], []
    for s in range(seqs):
        causal = keys_at[None, :] <= rows_at[:, None]
        masks.append((causal & (seg[s][:, None] == seg_keys[s][None, :]))[None])
        tables.append(rope_tables(pos[s]))

    kept = [[None] * seqs for _ in range(2)]
    layer_in = [hidden[s] for s in range(seqs)]
    outs = []
    for layer in range(2):
        weights = attn_weights[layer]
        parts = [None] * seqs
        for s in range(seqs):
            parts[s], kept[layer][s] = attention_forward(layer_in[s], tables[s], masks[s], weights)
        attn_out = [tp_sum(parts[s]) for s in range(seqs)]
        for s in range(seqs):
            parts[s], more = ffn_forward(layer_in[s], attn_out[s], weights[3], *ffn_weights[layer], first)
            kept[layer][s].update(more)
        next_in = []
        for s in range(seqs):
            ffn_out = tp_sum(parts[s]).astype(F32)
            middle = layer_in[s].astype(F32) + attn_out[s].astype(F32)
            next_in.append((middle + ffn_out).astype(BF16))
        layer_in = next_in
        outs.append(jnp.stack(layer_in))

    def to_section(values):
        low = lax.ppermute(values[0], "section", [(1, 0)])
        high = lax.ppermute(values[1], "section", [(0, 1)])
        return jnp.stack([jnp.where(first, values[0], high), jnp.where(first, low, values[1])])

    section_out = to_section(outs)

    upstream = [grad_top[s] for s in range(seqs)]
    in_grads = [None, None]
    gate_up_grads, down_grads, packed_grads = [None, None], [None, None], [None, None]
    for layer in (1, 0):
        weights = attn_weights[layer]
        w_own, w_other, w_down = ffn_weights[layer]
        k = kept[layer]
        parts, own_grads, other_grads = zip(
            *[ffn_backward(upstream[s], k[s], w_own, w_other, w_down, first) for s in range(seqs)]
        )
        normed_two_grad = [tp_sum(p) for p in parts]
        normed_two = jnp.concatenate([k[s]["normed_two"] for s in range(seqs)])
        own_w = dot("rd,rf->df", normed_two, jnp.concatenate(own_grads)).astype(BF16)
        other_w = dot("rd,rf->df", normed_two, jnp.concatenate(other_grads)).astype(BF16)
        own_w = (own_w.astype(F32) + swap(other_w).astype(F32)).astype(BF16)
        own_w, normed_two_grad = lax.optimization_barrier((own_w, normed_two_grad))
        gate_up_grads[layer] = lax.psum_scatter(own_w, ranks, scatter_dimension=0, tiled=True)
        down_w = dot("rd,rf->df", jnp.concatenate(upstream), jnp.concatenate([k[s]["inner"] for s in range(seqs)])).astype(BF16)
        down_w = down_w.reshape(shards, 2, half, ff)
        down_own = lax.dynamic_index_in_dim(down_w, sec, 1, keepdims=False)
        down_other = lax.dynamic_index_in_dim(down_w, 1 - sec, 1, keepdims=False)
        down_own = (down_own.astype(F32) + swap(down_other).astype(F32)).astype(BF16)
        down_own, normed_two_grad = lax.optimization_barrier((down_own, normed_two_grad))
        down_grads[layer] = lax.psum_scatter(
            down_own.reshape(shards * half, ff), ranks, scatter_dimension=0, tiled=True
        )

        results = [
            attention_backward(upstream[s], normed_two_grad[s], k[s], tables[s], masks[s], weights) for s in range(seqs)
        ]
        parts, middle_grads, attn_grads, lin_grads, gains_two = zip(*results)
        normed_one_grad = [tp_sum(p) for p in parts]
        lin_grad = jnp.concatenate(lin_grads)
        normed_one = jnp.concatenate([k[s]["normed"] for s in range(seqs)])
        lin_w = dot("rd,re->de", normed_one, lin_grad)
        attended = jnp.concatenate([k[s]["attended"] for s in range(seqs)])
        out_w = dot("rd,re->de", jnp.concatenate(attn_grads), attended)
        results = [input_backward(normed_one_grad[s], middle_grads[s], k[s], weights[3]) for s in range(seqs)]
        upstream = [r[0] for r in results]
        in_grads[layer] = jnp.stack(upstream)
        gain_cols = jnp.stack([sum(r[1] for r in results), sum(gains_two)], axis=1)
        bias = jnp.sum(lin_grad.astype(F32), axis=0)
        piece = HEAD // shards
        bias = bias.reshape(heads_here + 2, shards, piece).transpose(1, 0, 2).reshape(shards, (heads_here + 2) * piece)
        bias = jnp.pad(bias, ((0, 0), (0, -bias.shape[1] % shard)))
        bias = bias.reshape(shards, -1, shard).transpose(0, 2, 1).reshape(width, -1)
        extra = jnp.concatenate([gain_cols, bias], axis=1)
        extra = jnp.pad(extra, ((0, 0), (0, HEAD - extra.shape[1])))
        packed_grads[layer] = jnp.concatenate([lin_w, out_w, extra], axis=1).astype(BF16)

    input_grad = to_section(in_grads)

    low = lax.ppermute(packed_grads[0], "section", [(1, 0)])
    high = lax.ppermute(packed_grads[1], "section", [(0, 1)])
    packed_total = jnp.where(
        first, packed_grads[0].astype(F32) + low.astype(F32), packed_grads[1].astype(F32) + high.astype(F32)
    ).astype(BF16)
    packed_total = lax.psum_scatter(packed_total, ranks, scatter_dimension=0, tiled=True).astype(F32)
    q_grad = packed_total[:, :q_cols]
    kv_narrow = packed_total[:, q_cols : q_cols + 2 * HEAD].reshape(shard, 2, HEAD)
    o_grad = packed_total[:, q_cols + 2 * HEAD : 2 * q_cols + 2 * HEAD].T
    extra = packed_total[:, 2 * q_cols + 2 * HEAD :]
    gains_grad = extra[:, :2].T
    piece = HEAD // shards
    bias_cols = -(-(heads_here + 2) * piece // shard)
    bias = extra[:, 2 : 2 + bias_cols].T.reshape(-1)[: (heads_here + 2) * piece].reshape(heads_here + 2, piece)
    q_bias_grad = bias[:heads_here]
    kv_full = jnp.zeros((shard, 2, KV_HEADS, HEAD), F32)
    kv_full = lax.dynamic_update_slice_in_dim(kv_full, kv_narrow[:, :, None], head_pick, 2)
    bias_full = jnp.zeros((2, KV_HEADS, piece), F32)
    bias_full = lax.dynamic_update_slice_in_dim(bias_full, bias[heads_here:, None], head_pick, 1)
    flat = bias_full.reshape(-1)
    flat = jnp.pad(flat, (0, -flat.shape[0] % (2 * KV_HEADS * HEAD)))
    flat_rows = flat.shape[0] // (2 * KV_HEADS * HEAD)
    joined = jnp.concatenate([kv_full.reshape(shard, -1), flat.reshape(flat_rows, -1)]).astype(BF16)
    joined = chain_sum(joined).astype(F32)
    kv_grad = joined[:shard].reshape(shard, 2, KV_HEADS * HEAD).transpose(1, 0, 2)
    kv_bias_grad = joined[shard:].reshape(-1)[: 2 * KV_HEADS * piece].reshape(2, KV_HEADS, piece)

    def collect(values):
        kept_half = jnp.where(first, values[0], values[1])
        other = swap(jnp.where(first, values[1], values[0]))
        return jnp.where(first, kept_half, other), jnp.where(first, other, kept_half)

    gate_up_grad = jnp.stack(collect(gate_up_grads)).astype(F32)
    down_grad = jnp.concatenate(collect(down_grads), axis=0).T.astype(F32)
    return (
        section_out[None],
        input_grad[None],
        q_grad[None],
        kv_grad[None],
        o_grad[None],
        gate_up_grad[None],
        down_grad[None],
        gains_grad[None],
        q_bias_grad[None],
        kv_bias_grad[None],
    )


def solution(mesh):
    in_specs = (
        P(None, "dp", "ctx", None),
        P(None, "dp", "ctx"),
        P(None, "dp", "ctx"),
        P("section", ("dp", "ctx"), "tp"),
        P("section", None, ("dp", "ctx"), None),
        P("section", "tp", ("dp", "ctx")),
        P("section", None, ("dp", "ctx"), "tp"),
        P("section", "tp", ("dp", "ctx")),
        P("section", None, ("dp", "ctx")),
        P("section", "tp", ("dp", "ctx")),
        P("section", None, None, ("dp", "ctx")),
        P(None, "dp", "ctx", None),
    )
    out_specs = (
        P("section", None, "dp", "ctx", None),
        P("section", None, "dp", "ctx", None),
        P("section", ("dp", "ctx"), "tp"),
        P("section", None, ("dp", "ctx"), None),
        P("section", "tp", ("dp", "ctx")),
        P("section", None, ("dp", "ctx"), "tp"),
        P("section", "tp", ("dp", "ctx")),
        P("section", None, ("dp", "ctx")),
        P("section", "tp", ("dp", "ctx")),
        P("section", None, None, ("dp", "ctx")),
    )
    return jax.shard_map(local, mesh=mesh, in_specs=in_specs, out_specs=out_specs, check_vma=False)
```

```python
import jax
import jax.numpy as jnp
from jax import lax
from jax.experimental import pallas as pl
from jax.experimental.pallas import tpu as pltpu
from jax.sharding import PartitionSpec as P

HEADS = 12
KV_HEADS = 2
HEAD = 128

EPS = 1e-06
ROPE_BASE = 1000000.0
NEG = -1e30
SCALE = HEAD ** (-0.5)
TILE = 256
MESH = pl.DeviceIdType.MESH

F32 = jnp.float32
BF16 = jnp.bfloat16


def dot(form, left, right):
    return jnp.einsum(form, left, right, preferred_element_type=F32)


def swap(value):
    return lax.ppermute(value, "section", [(0, 1), (1, 0)])


def chain_sum(part):
    count = lax.axis_size("tp")
    place = lax.axis_index("tp")
    middle = count // 2
    total = part
    for hop in range(middle - 1):
        got = lax.ppermute(total, "tp", [(hop, hop + 1), (count - 1 - hop, count - 2 - hop)])
        total = (total.astype(F32) + got.astype(F32)).astype(BF16)
    got = lax.ppermute(total, "tp", [(middle - 1, middle), (middle, middle - 1)])
    total = (total.astype(F32) + got.astype(F32)).astype(BF16)
    for hop in range(middle - 1):
        low, high = middle - 1 - hop, middle + hop
        got = lax.ppermute(total, "tp", [(low, low - 1), (high, high + 1)])
        total = jnp.where((place == low - 1) | (place == high + 1), got, total)
    return total


class Chain:
    def __init__(self, part, total, from_end, from_peer, joined, sems):
        self.part, self.total = part, total
        self.from_end, self.from_peer, self.joined = from_end, from_peer, joined
        self.sems = sems
        self.chunks = sems.shape[1]
        self.rows = part.shape[0] // self.chunks
        place = lax.axis_index("tp")
        self.is_middle = (place == 1) | (place == 2)
        self.inner = jnp.where(place < 2, place + 1, place - 1)
        self.outer = jnp.where(place < 2, place - 1, place + 1)

    def greet(self, others=0):
        barrier = pltpu.get_barrier_semaphore()
        pl.semaphore_signal(barrier, inc=1, device_id={"tp": self.inner}, device_id_type=MESH)

        @pl.when(self.is_middle)
        def _():
            pl.semaphore_signal(barrier, inc=1, device_id={"tp": self.outer}, device_id_type=MESH)
            pl.semaphore_wait(barrier, 2 + others)

        @pl.when(jnp.logical_not(self.is_middle))
        def _():
            pl.semaphore_wait(barrier, 1 + others)

    def at(self, ref, c):
        return ref.at[pl.ds(pl.multiple_of(c * self.rows, self.rows), self.rows)]

    def copy(self, source, target, c, step, place):
        return pltpu.make_async_remote_copy(
            src_ref=self.at(source, c),
            dst_ref=self.at(target, c),
            send_sem=self.sems.at[2 * step, c],
            recv_sem=self.sems.at[2 * step + 1, c],
            device_id={"tp": place},
            device_id_type=MESH,
        )

    def inward(self, c):
        return self.copy(self.part, self.from_end, c, 0, self.inner)

    def across(self, c):
        return self.copy(self.joined, self.from_peer, c, 1, self.inner)

    def outward(self, c):
        return self.copy(self.total, self.total, c, 2, self.outer)

    def start(self):
        @pl.when(jnp.logical_not(self.is_middle))
        def _():
            @pl.loop(0, self.chunks)
            def _(c):
                self.inward(c).start()

    def join(self, c):
        self.inward(c).wait_recv()
        self.at(self.joined, c)[...] = self.at(self.part, c)[...] + self.at(self.from_end, c)[...]
        self.across(c).start()

    def close(self, c):
        self.across(c).wait_recv()
        self.at(self.total, c)[...] = self.at(self.joined, c)[...] + self.at(self.from_peer, c)[...]
        self.outward(c).start()

    def step(self, c):
        @pl.when(self.is_middle & (c < self.chunks))
        def _():
            self.join(c)

            @pl.when(c > 0)
            def _():
                self.close(c - 1)

    def finish(self, done):
        @pl.when(self.is_middle)
        def _():
            if done < self.chunks:

                @pl.loop(done, self.chunks)
                def _(c):
                    self.step(c)

            self.close(self.chunks - 1)

            @pl.loop(0, self.chunks)
            def _(c):
                self.across(c).wait_send()
                self.outward(c).wait_send()

        @pl.when(jnp.logical_not(self.is_middle))
        def _():
            @pl.loop(0, self.chunks)
            def _(c):
                self.inward(c).wait_send()
                self.outward(c).wait_recv()


def chain_chunks(rows):
    return min(16, rows // 16)


def chain_scratch(shape):
    return [pltpu.VMEM(shape, BF16)] * 3 + [pltpu.SemaphoreType.DMA((6, chain_chunks(shape[0])))]


VMEM = pl.BlockSpec(memory_space=pltpu.VMEM)
ANY = pl.BlockSpec(memory_space=pl.ANY)


def params(collective_id):
    return pltpu.CompilerParams(collective_id=collective_id, has_side_effects=True, vmem_limit_bytes=58 << 20)


def cost(flops):
    return pl.CostEstimate(flops=flops, bytes_accessed=100 << 20, transcendentals=0)


def sum_kernel(part, total, *scratch):
    chain = Chain(part, total, *scratch)
    chain.greet()
    chain.start()
    chain.finish(0)


def tp_sum(part):
    shape = part.shape
    return pl.pallas_call(
        sum_kernel,
        out_shape=jax.ShapeDtypeStruct(shape, BF16),
        in_specs=[VMEM],
        out_specs=VMEM,
        scratch_shapes=chain_scratch(shape),
        compiler_params=params(0),
        cost_estimate=cost(0),
    )(part)


def mm(left, right):
    return jnp.dot(left, right, preferred_element_type=F32)


def mm_t(left, right):
    return lax.dot_general(left, right, (((1,), (1,)), ((), ())), preferred_element_type=F32)


def tile_at(ref, j, size=TILE):
    return ref.at[:, pl.ds(pl.multiple_of(j * size, size), size)]


def rows_at(ref, j, size=TILE):
    return ref.at[pl.ds(pl.multiple_of(j * size, size), size)]


def copy_either(first, one, two, target, sem, start):
    @pl.when(first)
    def _():
        copy = pltpu.make_async_copy(one, target, sem)
        copy.start() if start else copy.wait()

    @pl.when(jnp.logical_not(first))
    def _():
        copy = pltpu.make_async_copy(two, target, sem)
        copy.start() if start else copy.wait()


def normalize_rows(source, gain, target, block):
    @pl.loop(0, target.shape[0] // block)
    def _(i):
        rows = pl.ds(pl.multiple_of(i * block, block), block)
        values = source(rows)
        factor = lax.rsqrt(jnp.mean(values * values, axis=-1, keepdims=True) + EPS)
        target[rows] = (values * factor * gain[...]).astype(BF16)


def ffn_forward_kernel(
    layer_in, attn_out, gain, part, w_own, w_other, w_down,
    normed, gate_out, up_out, inner_out, result, total,
    gate_w, up_w, down_w, gate, up, inner, one, two, w_sems, out_sems, *chain_refs,
):
    first = lax.axis_index("section") == 0
    tiles, outs = gate_w.shape[1] // TILE, gate_w.shape[0] // TILE

    @pl.loop(0, tiles)
    def _(j):
        copy_either(first, tile_at(w_own, j), tile_at(w_other, j), tile_at(gate_w, j), w_sems.at[0, j], True)
        copy_either(first, tile_at(w_other, j), tile_at(w_own, j), tile_at(up_w, j), w_sems.at[1, j], True)

    @pl.loop(0, outs)
    def _(n):
        pltpu.make_async_copy(rows_at(w_down, n), rows_at(down_w, n), w_sems.at[2, n]).start()

    chain = Chain(part, total, *chain_refs)
    chain.greet()
    chain.start()
    normalize_rows(lambda rows: layer_in[rows].astype(F32) + attn_out[rows].astype(F32), gain, normed, 16)

    @pl.loop(0, tiles)
    def _(j):
        copy_either(first, tile_at(w_own, j), tile_at(w_other, j), tile_at(gate_w, j), w_sems.at[0, j], False)
        one[...] = mm(normed[...], tile_at(gate_w, j)[...])
        copy_either(first, tile_at(w_other, j), tile_at(w_own, j), tile_at(up_w, j), w_sems.at[1, j], False)
        two[...] = mm(normed[...], tile_at(up_w, j)[...])
        columns = pl.ds(pl.multiple_of(j * TILE, TILE), TILE)

        @pl.loop(0, one.shape[0] // 32)
        def _(i):
            rows = pl.ds(pl.multiple_of(i * 32, 32), 32)
            g, u = one[rows], two[rows]
            gate[rows, columns] = g.astype(BF16)
            up[rows, columns] = u.astype(BF16)
            inner[rows, columns] = (g * jax.nn.sigmoid(g) * u).astype(BF16)

        for k, (source, target) in enumerate(((gate, gate_out), (up, up_out), (inner, inner_out))):
            pltpu.make_async_copy(tile_at(source, j), tile_at(target, j), out_sems.at[k, j]).start()
        chain.step(j)

    @pl.loop(0, outs)
    def _(n):
        pltpu.make_async_copy(rows_at(w_down, n), rows_at(down_w, n), w_sems.at[2, n]).wait()
        tile_at(result, n)[...] = mm_t(inner[...], rows_at(down_w, n)[...]).astype(BF16)
        chain.step(tiles + n)

    chain.finish(tiles + outs)

    @pl.loop(0, tiles)
    def _(j):
        for k, (source, target) in enumerate(((gate, gate_out), (up, up_out), (inner, inner_out))):
            pltpu.make_async_copy(tile_at(source, j), tile_at(target, j), out_sems.at[k, j]).wait()


def ffn_forward(layer_in, attn_out, gain, weights, part):
    rows, width = layer_in.shape
    ff = weights[0].shape[1]
    tiles = max(ff, width) // TILE
    narrow, wide = jax.ShapeDtypeStruct((rows, width), BF16), jax.ShapeDtypeStruct((rows, ff), BF16)
    return pl.pallas_call(
        ffn_forward_kernel,
        out_shape=[narrow, wide, wide, wide, narrow, narrow],
        in_specs=[VMEM] * 4 + [ANY] * 3,
        out_specs=[VMEM] + [ANY] * 3 + [VMEM] * 2,
        scratch_shapes=[pltpu.VMEM((width, ff), BF16)] * 3
        + [pltpu.VMEM((rows, ff), BF16)] * 3
        + [pltpu.VMEM((rows, TILE), F32)] * 2
        + [pltpu.SemaphoreType.DMA((3, tiles))] * 2
        + chain_scratch((rows, width)),
        compiler_params=params(1),
        cost_estimate=cost(6 * rows * width * ff),
    )(layer_in, attn_out, gain, part, *weights)


def ffn_backward_kernel(
    grad, part, gate_in, up_in, w_own, w_other, w_down,
    own_out, other_out, result, total,
    gate_w, up_w, down_w, gate, up, one, w_sems, in_sems, out_sems, *chain_refs,
):
    first = lax.axis_index("section") == 0
    tiles, outs = gate_w.shape[1] // TILE, gate_w.shape[0] // TILE

    @pl.loop(0, tiles)
    def _(j):
        pltpu.make_async_copy(tile_at(w_down, j), tile_at(down_w, j), w_sems.at[2, j]).start()
        pltpu.make_async_copy(tile_at(gate_in, j), tile_at(gate, j), in_sems.at[0, j]).start()
        pltpu.make_async_copy(tile_at(up_in, j), tile_at(up, j), in_sems.at[1, j]).start()

    @pl.loop(0, outs)
    def _(n):
        copy_either(first, rows_at(w_own, n), rows_at(w_other, n), rows_at(gate_w, n), w_sems.at[0, n], True)
        copy_either(first, rows_at(w_other, n), rows_at(w_own, n), rows_at(up_w, n), w_sems.at[1, n], True)

    chain = Chain(part, total, *chain_refs)
    chain.greet()
    chain.start()

    @pl.loop(0, tiles)
    def _(j):
        pltpu.make_async_copy(tile_at(w_down, j), tile_at(down_w, j), w_sems.at[2, j]).wait()
        one[...] = mm(grad[...], tile_at(down_w, j)[...])
        pltpu.make_async_copy(tile_at(gate_in, j), tile_at(gate, j), in_sems.at[0, j]).wait()
        pltpu.make_async_copy(tile_at(up_in, j), tile_at(up, j), in_sems.at[1, j]).wait()
        columns = pl.ds(pl.multiple_of(j * TILE, TILE), TILE)

        @pl.loop(0, one.shape[0] // 32)
        def _(i):
            rows = pl.ds(pl.multiple_of(i * 32, 32), 32)
            g, u, d = gate[rows, columns].astype(F32), up[rows, columns].astype(F32), one[rows]
            sig = jax.nn.sigmoid(g)
            d = d * sig
            gate[rows, columns] = (d * u * (1.0 + g * (1.0 - sig))).astype(BF16)
            up[rows, columns] = (d * g).astype(BF16)

        chain.step(j)

    def send(start):
        @pl.loop(0, tiles)
        def _(j):
            for source, target, k in ((own_out, other_out, 0), (other_out, own_out, 1)):
                held = tile_at(gate if k == 0 else up, j)

                @pl.when(first)
                def _():
                    copy = pltpu.make_async_copy(held, tile_at(source, j), out_sems.at[k, j])
                    copy.start() if start else copy.wait()

                @pl.when(jnp.logical_not(first))
                def _():
                    copy = pltpu.make_async_copy(held, tile_at(target, j), out_sems.at[k, j])
                    copy.start() if start else copy.wait()

    send(True)

    @pl.loop(0, outs)
    def _(n):
        copy_either(first, rows_at(w_own, n), rows_at(w_other, n), rows_at(gate_w, n), w_sems.at[0, n], False)
        one[...] = mm_t(gate[...], rows_at(gate_w, n)[...])
        copy_either(first, rows_at(w_other, n), rows_at(w_own, n), rows_at(up_w, n), w_sems.at[1, n], False)
        tile_at(result, n)[...] = (one[...] + mm_t(up[...], rows_at(up_w, n)[...])).astype(BF16)
        chain.step(tiles + n)

    chain.finish(tiles + outs)
    send(False)


def ffn_backward(grad, gate, up, weights, part):
    rows, width = grad.shape
    ff = weights[0].shape[1]
    tiles = max(ff, width) // TILE
    narrow, wide = jax.ShapeDtypeStruct((rows, width), BF16), jax.ShapeDtypeStruct((rows, ff), BF16)
    return pl.pallas_call(
        ffn_backward_kernel,
        out_shape=[wide, wide, narrow, narrow],
        in_specs=[VMEM] * 2 + [ANY] * 5,
        out_specs=[ANY] * 2 + [VMEM] * 2,
        scratch_shapes=[pltpu.VMEM((width, ff), BF16)] * 3
        + [pltpu.VMEM((rows, ff), BF16)] * 2
        + [pltpu.VMEM((rows, TILE), F32)]
        + [pltpu.SemaphoreType.DMA((3, tiles))] * 3
        + chain_scratch((rows, width)),
        compiler_params=params(2),
        cost_estimate=cost(6 * rows * width * ff),
    )(grad, part, gate, up, *weights)


def rotate(values, cosine, sine):
    half = values.shape[-1] // 2
    turned = jnp.concatenate([-values[..., half:], values[..., :half]], axis=-1)
    return values * cosine + turned * sine


def unrotate(grads, cosine, sine):
    half = grads.shape[-1] // 2
    scaled = grads * sine
    turned = jnp.concatenate([scaled[..., half:], -scaled[..., :half]], axis=-1)
    return grads * cosine + turned


def rope_tables(places):
    steps = jnp.arange(HEAD // 2, dtype=F32) * (2.0 / HEAD)
    inverse = ROPE_BASE ** (-steps)
    angles = places.astype(F32)[..., None] * inverse
    angles = jnp.concatenate([angles, angles], axis=-1)
    return (jnp.cos(angles), jnp.sin(angles))


def normalize(rows_in, gain):
    factor = lax.rsqrt(jnp.mean(rows_in * rows_in, axis=-1, keepdims=True) + EPS)
    return (factor, (rows_in * factor * gain).astype(BF16))


def norm_back(grad_out, rows_in, factor, gain):
    unit = rows_in * factor
    gain_grad = jnp.sum(grad_out * unit, axis=0)
    weighted = grad_out * gain
    return (
        factor * (weighted - unit * jnp.mean(weighted * unit, axis=-1, keepdims=True)),
        gain_grad,
    )


def over_ctx(value):
    if lax.axis_size("ctx") == 2:
        other = lax.ppermute(value, "ctx", [(0, 1), (1, 0)])
        return jnp.concatenate([value, other], axis=value.ndim - 2)
    return lax.all_gather(value, "ctx", axis=value.ndim - 2, tiled=True)


def back_over_ctx(grads):
    span = grads.shape[-2] // lax.axis_size("ctx")
    grads = grads.astype(BF16)
    if lax.axis_size("ctx") == 2:
        other = lax.ppermute(grads[..., span:, :], "ctx", [(0, 1), (1, 0)])
        return grads[..., :span, :].astype(F32) + other.astype(F32)
    return lax.psum_scatter(grads, "ctx", scatter_dimension=grads.ndim - 2, tiled=True).astype(F32)


def attention_forward(layer_in, tables, mask, weights):
    span = layer_in.shape[0]
    wq, wkv, wo, gains, q_bias, kv_bias = weights
    heads_here = wq.shape[1] // HEAD
    cosine, sine = tables
    rows_in = layer_in.astype(F32)
    factor, normed = normalize(rows_in, gains[0])
    query = dot("rd,de->re", normed, wq) + q_bias.reshape(-1)
    query = rotate(query.reshape(span, heads_here, HEAD), cosine[:, None], sine[:, None]).astype(BF16)
    kv_lin = dot("rd,de->re", normed, wkv) + kv_bias.reshape(-1)
    key = rotate(kv_lin[:, :HEAD], cosine, sine).astype(BF16)
    kv = over_ctx(jnp.stack([key, kv_lin[:, HEAD:].astype(BF16)]))
    scores = jnp.where(mask, dot("ihd,jd->hij", query, kv[0]) * SCALE, NEG)
    top = jnp.max(scores, axis=-1, keepdims=True)
    log_total = top + jnp.log(jnp.sum(jnp.exp(scores - top), axis=-1, keepdims=True))
    probs = jnp.exp(scores - log_total).astype(BF16)
    attended = dot("hij,jd->ihd", probs, kv[1]).reshape(span, heads_here * HEAD).astype(BF16)
    part = dot("re,de->rd", attended, wo).astype(BF16)
    return part, dict(layer_in=layer_in, factor=factor, normed=normed, query=query, kv=kv, log_total=log_total, attended=attended)


def attention_backward(upstream, normed_two_grad, kept, tables, mask, weights):
    wq, wkv, wo, gains, q_bias, kv_bias = weights
    heads_here = wq.shape[1] // HEAD
    span = upstream.shape[0]
    cosine, sine = tables
    middle = kept["layer_in"].astype(F32) + kept["attn_out"].astype(F32)
    factor_two = lax.rsqrt(jnp.mean(middle * middle, axis=-1, keepdims=True) + EPS)
    norm_grad, gain_two = norm_back(normed_two_grad.astype(F32), middle, factor_two, gains[1])
    middle_grad = upstream.astype(F32) + norm_grad
    attn_grad = middle_grad.astype(BF16)
    heads_grad = dot("rd,de->re", attn_grad, wo).astype(BF16).reshape(span, heads_here, HEAD)
    query, kv = kept["query"], kept["kv"]
    scores = jnp.where(mask, dot("ihd,jd->hij", query, kv[0]) * SCALE, NEG)
    probs = jnp.exp(scores - kept["log_total"])
    prob_grad = dot("ihd,jd->hij", heads_grad, kv[1])
    attended = kept["attended"].reshape(span, heads_here, HEAD)
    row_sum = jnp.sum(attended.astype(F32) * heads_grad.astype(F32), axis=-1).T[..., None]
    score_grad = (probs * (prob_grad - row_sum)).astype(BF16)
    query_grad = dot("hij,jd->ihd", score_grad, kv[0]) * SCALE
    key_grad = dot("hij,ihd->jd", score_grad, query) * SCALE
    value_grad = dot("hij,ihd->jd", probs.astype(BF16), heads_grad)
    kv_grad = back_over_ctx(jnp.stack([key_grad, value_grad]))
    q_lin_grad = unrotate(query_grad, cosine[:, None], sine[:, None]).reshape(span, heads_here * HEAD).astype(BF16)
    k_lin_grad = unrotate(kv_grad[0], cosine, sine)
    lin_grad = jnp.concatenate([q_lin_grad, k_lin_grad.astype(BF16), kv_grad[1].astype(BF16)], axis=-1)
    part = dot("re,de->rd", lin_grad, jnp.concatenate([wq, wkv], axis=-1)).astype(BF16)
    return part, middle_grad, attn_grad, lin_grad, gain_two


def input_backward(normed_one_grad, middle_grad, kept, gains):
    norm_grad, gain_one = norm_back(
        normed_one_grad.astype(F32), kept["layer_in"].astype(F32), kept["factor"], gains[0]
    )
    return (middle_grad + norm_grad).astype(BF16), gain_one


def local(
    section_in,
    segments,
    positions,
    query_weight,
    kv_weight,
    output_weight,
    gate_up,
    down_weight,
    norm_gains,
    query_bias,
    kv_bias,
    out_grad,
):
    sec = lax.axis_index("section")
    first = sec == 0
    group = HEADS // KV_HEADS
    heads_here = HEADS // lax.axis_size("tp")
    head_pick = lax.axis_index("tp") * heads_here // group
    shards = lax.axis_size("dp") * lax.axis_size("ctx")
    ranks = ("dp", "ctx")
    seqs, span, width = section_in.shape[1:]
    shard = query_weight.shape[1]
    q_cols = query_weight.shape[2]
    ff = gate_up.shape[3]

    def per_layer(mine, theirs):
        return jnp.where(first, mine, theirs), jnp.where(first, theirs, mine)

    piece = HEAD // shards
    biases = jnp.concatenate([query_bias[0].reshape(-1), kv_bias[0].reshape(-1)])
    n_biases = biases.shape[0]
    biases = jnp.pad(biases, (0, -n_biases % shard)).reshape(-1, shard).T
    extra = jnp.concatenate([norm_gains[0].T, biases], axis=1)
    n_extra = extra.shape[1]
    extra = jnp.pad(extra, ((0, 0), (0, HEAD - n_extra)))
    packed = jnp.concatenate([query_weight[0], kv_weight[0, 0], kv_weight[0, 1], output_weight[0].T, extra], axis=1)
    packed = lax.all_gather(packed, ranks, axis=0, tiled=True)
    packed_mine = packed
    packed = per_layer(packed, swap(packed))
    attn_weights = []
    kv_width = KV_HEADS * HEAD
    for layer in range(2):
        p = packed[layer]
        wq = p[:, :q_cols]
        wk = lax.dynamic_slice_in_dim(p[:, q_cols : q_cols + kv_width], head_pick * HEAD, HEAD, 1)
        wv = lax.dynamic_slice_in_dim(p[:, q_cols + kv_width : q_cols + 2 * kv_width], head_pick * HEAD, HEAD, 1)
        wo = p[:, q_cols + 2 * kv_width : 2 * q_cols + 2 * kv_width]
        s = p[:, 2 * q_cols + 2 * kv_width :]
        gains = s[:, :2].T
        s = s[:, 2:n_extra].T.reshape(-1, shards, shard).transpose(1, 0, 2).reshape(shards, -1)[:, :n_biases]
        q_b = s[:, : heads_here * piece].reshape(shards, heads_here, piece).transpose(1, 0, 2).reshape(heads_here, HEAD)
        kv_b = s[:, heads_here * piece :].reshape(shards, 2, KV_HEADS, piece)
        kv_b = kv_b.transpose(1, 2, 0, 3).reshape(2, KV_HEADS, HEAD)
        kv_b = lax.dynamic_slice_in_dim(kv_b, head_pick, 1, 1)
        attn_weights.append((wq, jnp.concatenate([wk, wv], axis=1), wo, gains.astype(F32), q_b.astype(F32), kv_b.astype(F32)))

    half = shard // 2
    spare = -ff % TILE
    wide = jnp.pad(gate_up[0], ((0, 0), (0, 0), (0, spare)))
    mine = lax.dynamic_index_in_dim(wide, sec, 0, keepdims=False)
    theirs = swap(lax.dynamic_index_in_dim(wide, 1 - sec, 0, keepdims=False))
    gate_up_shards = per_layer(mine, theirs)
    down_t = jnp.pad(down_weight[0].T, ((0, 0), (0, spare)))
    mine = lax.dynamic_slice_in_dim(down_t, sec * half, half, 0)
    theirs = swap(lax.dynamic_slice_in_dim(down_t, (1 - sec) * half, half, 0))
    down_shards = per_layer(mine, theirs)

    def after(value, event):
        return lax.optimization_barrier((value, event))[0]

    def gather_ffn(layer, event):
        own = lax.all_gather(after(gate_up_shards[layer], event), ranks, axis=0, tiled=True)
        down_own = lax.all_gather(after(down_shards[layer], own), ranks, axis=0)
        return own, down_own

    def share_ffn(own, down_own):
        down = jnp.stack(per_layer(down_own, swap(down_own)), axis=1).reshape(width, ff + spare)
        return own, swap(own), down

    gathered_low = gather_ffn(0, packed_mine)
    gathered_high = gather_ffn(1, gathered_low[1])
    ffn_weights = [share_ffn(*gathered_low), None]

    micro = sec
    seg = lax.dynamic_index_in_dim(segments, micro, 0, keepdims=False)
    pos = lax.dynamic_index_in_dim(positions, micro, 0, keepdims=False)
    hidden = lax.dynamic_index_in_dim(section_in, micro, 0, keepdims=False)
    grad_top = lax.dynamic_index_in_dim(out_grad, micro, 0, keepdims=False)
    rows_at = lax.axis_index("ctx") * span + jnp.arange(span)
    count = lax.axis_size("ctx")
    if count == 2:
        keys_at = jnp.concatenate([rows_at, (1 - lax.axis_index("ctx")) * span + jnp.arange(span)])
    else:
        keys_at = jnp.arange(count * span)
    seg_keys = over_ctx(seg[..., None])[..., 0]
    masks, tables = [], []
    for s in range(seqs):
        causal = keys_at[None, :] <= rows_at[:, None]
        masks.append((causal & (seg[s][:, None] == seg_keys[s][None, :]))[None])
        tables.append(rope_tables(pos[s]))

    kept = [[None, None] for _ in range(2)]
    layer_in = [hidden[0], hidden[1]]
    outs = []
    for layer in range(2):
        weights, k = attn_weights[layer], kept[layer]
        part_a, k[0] = attention_forward(layer_in[0], tables[0], masks[0], weights)
        part_b, k[1] = attention_forward(layer_in[1], tables[1], masks[1], weights)
        attn_a = tp_sum(part_a)
        gain = weights[3][1:]
        normed_a, gate, up, inner, part_a, attn_b = ffn_forward(layer_in[0], attn_a, gain, ffn_weights[layer], part_b)
        k[0].update(attn_out=attn_a, normed_two=normed_a, gate=gate, up=up, inner=inner)
        normed_b, gate, up, inner, part_b, ffn_a = ffn_forward(layer_in[1], attn_b, gain, ffn_weights[layer], part_a)
        k[1].update(attn_out=attn_b, normed_two=normed_b, gate=gate, up=up, inner=inner)
        if layer == 0:
            ffn_b = tp_sum(part_b)
        else:
            upstream = [grad_top[0], grad_top[1]]
            own_a, other_a, grad_a, ffn_b = ffn_backward(upstream[0], k[0]["gate"], k[0]["up"], ffn_weights[1], part_b)
        layer_in = [
            (layer_in[s].astype(F32) + k[s]["attn_out"].astype(F32) + out.astype(F32)).astype(BF16)
            for s, out in enumerate((ffn_a, ffn_b))
        ]
        outs.append(jnp.stack(layer_in))
        if layer == 0:
            layer_in[0], gathered_high = lax.optimization_barrier((layer_in[0], gathered_high))
            ffn_weights[1] = share_ffn(*gathered_high)

    def to_section(values):
        low = lax.ppermute(values[0], "section", [(1, 0)])
        high = lax.ppermute(values[1], "section", [(0, 1)])
        return jnp.stack([jnp.where(first, values[0], high), jnp.where(first, low, values[1])])

    section_out = to_section(outs)

    in_grads = [None, None]
    gate_up_grads, down_grads, packed_grads = [None, None], [None, None], [None, None]
    waiting = None
    for layer in (1, 0):
        weights, k = attn_weights[layer], kept[layer]
        if layer == 0:
            own_a, other_a, grad_a, sum_b = ffn_backward(upstream[0], k[0]["gate"], k[0]["up"], ffn_weights[0], parts[1])
            upstream[1], gain_b = input_backward(sum_b, middle_grads[1], kept[1][1], attn_weights[1][3])
            waiting(upstream, gain_a + gain_b)
        own_b, other_b, grad_b, sum_a = ffn_backward(upstream[1], k[1]["gate"], k[1]["up"], ffn_weights[layer], grad_a)
        normed_two_grad = [sum_a, tp_sum(grad_b)]
        own_grads, other_grads = (own_a, own_b), (other_a, other_b)
        normed_two = jnp.concatenate([k[s]["normed_two"] for s in range(seqs)])
        own_w = dot("rd,rf->df", normed_two, jnp.concatenate(own_grads)).astype(BF16)
        other_w = dot("rd,rf->df", normed_two, jnp.concatenate(other_grads)).astype(BF16)
        own_w = (own_w.astype(F32) + swap(other_w).astype(F32)).astype(BF16)
        own_w, normed_two_grad = lax.optimization_barrier((own_w, normed_two_grad))
        gate_up_grads[layer] = lax.psum_scatter(own_w, ranks, scatter_dimension=0, tiled=True)
        down_w = dot("rd,rf->df", jnp.concatenate(upstream), jnp.concatenate([k[s]["inner"] for s in range(seqs)])).astype(BF16)
        down_w = down_w.reshape(shards, 2, half, ff + spare)
        down_own = lax.dynamic_index_in_dim(down_w, sec, 1, keepdims=False)
        down_other = lax.dynamic_index_in_dim(down_w, 1 - sec, 1, keepdims=False)
        down_own = (down_own.astype(F32) + swap(down_other).astype(F32)).astype(BF16)
        down_own, normed_two_grad = lax.optimization_barrier((down_own, normed_two_grad))
        down_grads[layer] = lax.psum_scatter(
            down_own.reshape(shards * half, ff + spare), ranks, scatter_dimension=0, tiled=True
        )

        results = [
            attention_backward(upstream[s], normed_two_grad[s], k[s], tables[s], masks[s], weights) for s in range(seqs)
        ]
        parts, middle_grads, attn_grads, lin_grads, gains_two = zip(*results)
        lin_grad = jnp.concatenate(lin_grads)
        normed_one = jnp.concatenate([k[s]["normed"] for s in range(seqs)])
        lin_w = dot("rd,re->de", normed_one, lin_grad)
        attended = jnp.concatenate([k[s]["attended"] for s in range(seqs)])
        out_w = dot("rd,re->de", jnp.concatenate(attn_grads), attended)
        bias = jnp.sum(lin_grad.astype(F32), axis=0)

        def finish(upstream, gain_one, layer=layer, lin_w=lin_w, out_w=out_w, bias=bias, gains_two=gains_two):
            in_grads[layer] = jnp.stack(upstream)
            gain_cols = jnp.stack([gain_one, sum(gains_two)], axis=1)
            bias = bias.reshape(heads_here + 2, shards, piece).transpose(1, 0, 2).reshape(shards, (heads_here + 2) * piece)
            bias = jnp.pad(bias, ((0, 0), (0, -bias.shape[1] % shard)))
            bias = bias.reshape(shards, -1, shard).transpose(0, 2, 1).reshape(width, -1)
            extra = jnp.concatenate([gain_cols, bias], axis=1)
            extra = jnp.pad(extra, ((0, 0), (0, HEAD - extra.shape[1])))
            packed_grads[layer] = jnp.concatenate([lin_w, out_w, extra], axis=1).astype(BF16)

        waiting = finish
        upstream = [None, None]
        upstream[0], gain_a = input_backward(tp_sum(parts[0]), middle_grads[0], k[0], weights[3])
    upstream[1], gain_b = input_backward(tp_sum(parts[1]), middle_grads[1], kept[0][1], attn_weights[0][3])
    waiting(upstream, gain_a + gain_b)

    input_grad = to_section(in_grads)

    low = lax.ppermute(packed_grads[0], "section", [(1, 0)])
    high = lax.ppermute(packed_grads[1], "section", [(0, 1)])
    packed_total = jnp.where(
        first, packed_grads[0].astype(F32) + low.astype(F32), packed_grads[1].astype(F32) + high.astype(F32)
    ).astype(BF16)
    packed_total = lax.psum_scatter(packed_total, ranks, scatter_dimension=0, tiled=True).astype(F32)
    q_grad = packed_total[:, :q_cols]
    kv_narrow = packed_total[:, q_cols : q_cols + 2 * HEAD].reshape(shard, 2, HEAD)
    o_grad = packed_total[:, q_cols + 2 * HEAD : 2 * q_cols + 2 * HEAD].T
    extra = packed_total[:, 2 * q_cols + 2 * HEAD :]
    gains_grad = extra[:, :2].T
    bias_cols = -(-(heads_here + 2) * piece // shard)
    bias = extra[:, 2 : 2 + bias_cols].T.reshape(-1)[: (heads_here + 2) * piece].reshape(heads_here + 2, piece)
    q_bias_grad = bias[:heads_here]
    kv_full = jnp.zeros((shard, 2, KV_HEADS, HEAD), F32)
    kv_full = lax.dynamic_update_slice_in_dim(kv_full, kv_narrow[:, :, None], head_pick, 2)
    bias_full = jnp.zeros((2, KV_HEADS, piece), F32)
    bias_full = lax.dynamic_update_slice_in_dim(bias_full, bias[heads_here:, None], head_pick, 1)
    flat = bias_full.reshape(-1)
    flat = jnp.pad(flat, (0, -flat.shape[0] % (2 * KV_HEADS * HEAD)))
    flat_rows = flat.shape[0] // (2 * KV_HEADS * HEAD)
    joined = jnp.concatenate([kv_full.reshape(shard, -1), flat.reshape(flat_rows, -1)]).astype(BF16)
    joined = chain_sum(joined).astype(F32)
    kv_grad = joined[:shard].reshape(shard, 2, KV_HEADS * HEAD).transpose(1, 0, 2)
    kv_bias_grad = joined[shard:].reshape(-1)[: 2 * KV_HEADS * piece].reshape(2, KV_HEADS, piece)

    def collect(values):
        kept_half = jnp.where(first, values[0], values[1])
        other = swap(jnp.where(first, values[1], values[0]))
        return jnp.where(first, kept_half, other), jnp.where(first, other, kept_half)

    gate_up_grad = jnp.stack(collect(gate_up_grads))[..., :ff].astype(F32)
    down_grad = jnp.concatenate(collect(down_grads), axis=0)[:, :ff].T.astype(F32)
    return (
        section_out[None],
        input_grad[None],
        q_grad[None],
        kv_grad[None],
        o_grad[None],
        gate_up_grad[None],
        down_grad[None],
        gains_grad[None],
        q_bias_grad[None],
        kv_bias_grad[None],
    )


def solution(mesh):
    in_specs = (
        P(None, "dp", "ctx", None),
        P(None, "dp", "ctx"),
        P(None, "dp", "ctx"),
        P("section", ("dp", "ctx"), "tp"),
        P("section", None, ("dp", "ctx"), None),
        P("section", "tp", ("dp", "ctx")),
        P("section", None, ("dp", "ctx"), "tp"),
        P("section", "tp", ("dp", "ctx")),
        P("section", None, ("dp", "ctx")),
        P("section", "tp", ("dp", "ctx")),
        P("section", None, None, ("dp", "ctx")),
        P(None, "dp", "ctx", None),
    )
    out_specs = (
        P("section", None, "dp", "ctx", None),
        P("section", None, "dp", "ctx", None),
        P("section", ("dp", "ctx"), "tp"),
        P("section", None, ("dp", "ctx"), None),
        P("section", "tp", ("dp", "ctx")),
        P("section", None, ("dp", "ctx"), "tp"),
        P("section", "tp", ("dp", "ctx")),
        P("section", None, ("dp", "ctx")),
        P("section", "tp", ("dp", "ctx")),
        P("section", None, None, ("dp", "ctx")),
    )
    return jax.shard_map(local, mesh=mesh, in_specs=in_specs, out_specs=out_specs, check_vma=False)
```

```python
import functools

import jax
import jax.numpy as jnp
from jax import lax
from jax.experimental import pallas as pl
from jax.experimental.pallas import tpu as pltpu
from jax.sharding import PartitionSpec as P

HEADS = 12
KV_HEADS = 2
HEAD = 128

EPS = 1e-06
ROPE_BASE = 1000000.0
NEG = -1e30
SCALE = HEAD ** (-0.5)
TILE = 256
MESH = pl.DeviceIdType.MESH

F32 = jnp.float32
BF16 = jnp.bfloat16


def dot(form, left, right):
    return jnp.einsum(form, left, right, preferred_element_type=F32)


def swap(value):
    return lax.ppermute(value, "section", [(0, 1), (1, 0)])


def chain_sum(part):
    count = lax.axis_size("tp")
    place = lax.axis_index("tp")
    middle = count // 2
    total = part
    for hop in range(middle - 1):
        got = lax.ppermute(total, "tp", [(hop, hop + 1), (count - 1 - hop, count - 2 - hop)])
        total = (total.astype(F32) + got.astype(F32)).astype(BF16)
    got = lax.ppermute(total, "tp", [(middle - 1, middle), (middle, middle - 1)])
    total = (total.astype(F32) + got.astype(F32)).astype(BF16)
    for hop in range(middle - 1):
        low, high = middle - 1 - hop, middle + hop
        got = lax.ppermute(total, "tp", [(low, low - 1), (high, high + 1)])
        total = jnp.where((place == low - 1) | (place == high + 1), got, total)
    return total


class Chain:
    def __init__(self, part, total, from_end, from_peer, joined, sems):
        self.part, self.total = part, total
        self.from_end, self.from_peer, self.joined = from_end, from_peer, joined
        self.sems = sems
        self.chunks = sems.shape[1]
        self.rows = part.shape[0] // self.chunks
        place = lax.axis_index("tp")
        self.is_middle = (place == 1) | (place == 2)
        self.inner = jnp.where(place < 2, place + 1, place - 1)
        self.outer = jnp.where(place < 2, place - 1, place + 1)

    def greet(self, others=0):
        barrier = pltpu.get_barrier_semaphore()
        pl.semaphore_signal(barrier, inc=1, device_id={"tp": self.inner}, device_id_type=MESH)

        @pl.when(self.is_middle)
        def _():
            pl.semaphore_signal(barrier, inc=1, device_id={"tp": self.outer}, device_id_type=MESH)
            pl.semaphore_wait(barrier, 2 + others)

        @pl.when(jnp.logical_not(self.is_middle))
        def _():
            pl.semaphore_wait(barrier, 1 + others)

    def at(self, ref, c):
        return ref.at[pl.ds(pl.multiple_of(c * self.rows, self.rows), self.rows)]

    def copy(self, source, target, c, step, place):
        return pltpu.make_async_remote_copy(
            src_ref=self.at(source, c),
            dst_ref=self.at(target, c),
            send_sem=self.sems.at[2 * step, c],
            recv_sem=self.sems.at[2 * step + 1, c],
            device_id={"tp": place},
            device_id_type=MESH,
        )

    def inward(self, c):
        return self.copy(self.part, self.from_end, c, 0, self.inner)

    def across(self, c):
        return self.copy(self.joined, self.from_peer, c, 1, self.inner)

    def outward(self, c):
        return self.copy(self.total, self.total, c, 2, self.outer)

    def start(self):
        @pl.when(jnp.logical_not(self.is_middle))
        def _():
            @pl.loop(0, self.chunks)
            def _(c):
                self.inward(c).start()

    def join(self, c):
        self.inward(c).wait_recv()
        self.at(self.joined, c)[...] = self.at(self.part, c)[...] + self.at(self.from_end, c)[...]
        self.across(c).start()

    def close(self, c):
        self.across(c).wait_recv()
        self.at(self.total, c)[...] = self.at(self.joined, c)[...] + self.at(self.from_peer, c)[...]
        self.outward(c).start()

    def step(self, c):
        @pl.when(self.is_middle & (c < self.chunks))
        def _():
            self.join(c)

            @pl.when(c > 0)
            def _():
                self.close(c - 1)

    def finish(self, done):
        @pl.when(self.is_middle)
        def _():
            if done < self.chunks:

                @pl.loop(done, self.chunks)
                def _(c):
                    self.step(c)

            self.close(self.chunks - 1)

            @pl.loop(0, self.chunks)
            def _(c):
                self.across(c).wait_send()
                self.outward(c).wait_send()

        @pl.when(jnp.logical_not(self.is_middle))
        def _():
            @pl.loop(0, self.chunks)
            def _(c):
                self.inward(c).wait_send()
                self.outward(c).wait_recv()


def chain_chunks(rows):
    return min(16, rows // 16)


def chain_scratch(shape):
    return [pltpu.VMEM(shape, BF16)] * 3 + [pltpu.SemaphoreType.DMA((6, chain_chunks(shape[0])))]


VMEM = pl.BlockSpec(memory_space=pltpu.VMEM)
ANY = pl.BlockSpec(memory_space=pl.ANY)


def params(collective_id):
    return pltpu.CompilerParams(collective_id=collective_id, has_side_effects=True, vmem_limit_bytes=58 << 20)


def cost(flops):
    return pl.CostEstimate(flops=flops, bytes_accessed=100 << 20, transcendentals=0)


def sum_kernel(part, total, *scratch):
    chain = Chain(part, total, *scratch)
    chain.greet()
    chain.start()
    chain.finish(0)


def tp_sum(part):
    shape = part.shape
    return pl.pallas_call(
        sum_kernel,
        out_shape=jax.ShapeDtypeStruct(shape, BF16),
        in_specs=[VMEM],
        out_specs=VMEM,
        scratch_shapes=chain_scratch(shape),
        compiler_params=params(0),
        cost_estimate=cost(0),
    )(part)


def mm(left, right):
    return jnp.dot(left, right, preferred_element_type=F32)


def mm_t(left, right):
    return lax.dot_general(left, right, (((1,), (1,)), ((), ())), preferred_element_type=F32)


def tile_at(ref, j, size=TILE):
    return ref.at[:, pl.ds(pl.multiple_of(j * size, size), size)]


def rows_at(ref, j, size=TILE):
    return ref.at[pl.ds(pl.multiple_of(j * size, size), size)]


def copy_either(first, one, two, target, sem, start):
    @pl.when(first)
    def _():
        copy = pltpu.make_async_copy(one, target, sem)
        copy.start() if start else copy.wait()

    @pl.when(jnp.logical_not(first))
    def _():
        copy = pltpu.make_async_copy(two, target, sem)
        copy.start() if start else copy.wait()


def normalize_rows(source, gain, target, block=64):
    @pl.loop(0, target.shape[0] // block)
    def _(i):
        rows = pl.ds(pl.multiple_of(i * block, block), block)
        values = source(rows)
        factor = lax.rsqrt(jnp.mean(values * values, axis=-1, keepdims=True) + EPS)
        target[rows] = (values * factor * gain[...]).astype(BF16)


def ffn_forward_kernel(
    layer_in, attn_out, gain, part, w_own, w_other, w_down,
    normed, gate_out, up_out, inner_out, result, total,
    gate_w, up_w, down_w, gate, up, inner, w_sems, out_sems, *chain_refs,
):
    first = lax.axis_index("section") == 0
    tiles, outs = gate_w.shape[1] // TILE, gate_w.shape[0] // TILE

    @pl.loop(0, tiles)
    def _(j):
        copy_either(first, tile_at(w_own, j), tile_at(w_other, j), tile_at(gate_w, j), w_sems.at[0, j], True)
        copy_either(first, tile_at(w_other, j), tile_at(w_own, j), tile_at(up_w, j), w_sems.at[1, j], True)

    @pl.loop(0, outs)
    def _(n):
        pltpu.make_async_copy(rows_at(w_down, n), rows_at(down_w, n), w_sems.at[2, n]).start()

    chain = Chain(part, total, *chain_refs)
    chain.greet()
    chain.start()
    normalize_rows(lambda rows: layer_in[rows].astype(F32) + attn_out[rows].astype(F32), gain, normed)

    @pl.loop(0, tiles)
    def _(j):
        copy_either(first, tile_at(w_own, j), tile_at(w_other, j), tile_at(gate_w, j), w_sems.at[0, j], False)
        copy_either(first, tile_at(w_other, j), tile_at(w_own, j), tile_at(up_w, j), w_sems.at[1, j], False)
        g = mm(normed[...], tile_at(gate_w, j)[...])
        u = mm(normed[...], tile_at(up_w, j)[...])
        tile_at(gate, j)[...] = g.astype(BF16)
        tile_at(up, j)[...] = u.astype(BF16)
        tile_at(inner, j)[...] = (g * jax.nn.sigmoid(g) * u).astype(BF16)

        for k, (source, target) in enumerate(((gate, gate_out), (up, up_out), (inner, inner_out))):
            pltpu.make_async_copy(tile_at(source, j), tile_at(target, j), out_sems.at[k, j]).start()
        chain.step(j)

    @pl.loop(0, outs)
    def _(n):
        pltpu.make_async_copy(rows_at(w_down, n), rows_at(down_w, n), w_sems.at[2, n]).wait()
        tile_at(result, n)[...] = mm_t(inner[...], rows_at(down_w, n)[...]).astype(BF16)
        chain.step(tiles + n)

    chain.finish(tiles + outs)

    @pl.loop(0, tiles)
    def _(j):
        for k, (source, target) in enumerate(((gate, gate_out), (up, up_out), (inner, inner_out))):
            pltpu.make_async_copy(tile_at(source, j), tile_at(target, j), out_sems.at[k, j]).wait()


def ffn_forward(layer_in, attn_out, gain, weights, part):
    rows, width = layer_in.shape
    ff = weights[0].shape[1]
    tiles = max(ff, width) // TILE
    narrow, wide = jax.ShapeDtypeStruct((rows, width), BF16), jax.ShapeDtypeStruct((rows, ff), BF16)
    return pl.pallas_call(
        ffn_forward_kernel,
        out_shape=[narrow, wide, wide, wide, narrow, narrow],
        in_specs=[VMEM] * 4 + [ANY] * 3,
        out_specs=[VMEM] + [ANY] * 3 + [VMEM] * 2,
        scratch_shapes=[pltpu.VMEM((width, ff), BF16)] * 3
        + [pltpu.VMEM((rows, ff), BF16)] * 3
        + [pltpu.SemaphoreType.DMA((3, tiles))] * 2
        + chain_scratch((rows, width)),
        compiler_params=params(1),
        cost_estimate=cost(6 * rows * width * ff),
    )(layer_in, attn_out, gain, part, *weights)


def ffn_backward_kernel(
    grad, part, gate_in, up_in, w_own, w_other, w_down,
    own_out, other_out, result, total,
    gate_w, up_w, down_w, gate, up, w_sems, in_sems, out_sems, *chain_refs,
):
    first = lax.axis_index("section") == 0
    tiles, outs = gate_w.shape[1] // TILE, gate_w.shape[0] // TILE

    @pl.loop(0, tiles)
    def _(j):
        pltpu.make_async_copy(tile_at(w_down, j), tile_at(down_w, j), w_sems.at[2, j]).start()
        pltpu.make_async_copy(tile_at(gate_in, j), tile_at(gate, j), in_sems.at[0, j]).start()
        pltpu.make_async_copy(tile_at(up_in, j), tile_at(up, j), in_sems.at[1, j]).start()

    @pl.loop(0, outs)
    def _(n):
        copy_either(first, rows_at(w_own, n), rows_at(w_other, n), rows_at(gate_w, n), w_sems.at[0, n], True)
        copy_either(first, rows_at(w_other, n), rows_at(w_own, n), rows_at(up_w, n), w_sems.at[1, n], True)

    chain = Chain(part, total, *chain_refs)
    chain.greet()
    chain.start()

    @pl.loop(0, tiles)
    def _(j):
        pltpu.make_async_copy(tile_at(w_down, j), tile_at(down_w, j), w_sems.at[2, j]).wait()
        pltpu.make_async_copy(tile_at(gate_in, j), tile_at(gate, j), in_sems.at[0, j]).wait()
        pltpu.make_async_copy(tile_at(up_in, j), tile_at(up, j), in_sems.at[1, j]).wait()
        d = mm(grad[...], tile_at(down_w, j)[...])
        g, u = tile_at(gate, j)[...].astype(F32), tile_at(up, j)[...].astype(F32)
        sig = jax.nn.sigmoid(g)
        d = d * sig
        tile_at(gate, j)[...] = (d * u * (1.0 + g * (1.0 - sig))).astype(BF16)
        tile_at(up, j)[...] = (d * g).astype(BF16)

        chain.step(j)

    def send(start):
        @pl.loop(0, tiles)
        def _(j):
            for source, target, k in ((own_out, other_out, 0), (other_out, own_out, 1)):
                held = tile_at(gate if k == 0 else up, j)

                @pl.when(first)
                def _():
                    copy = pltpu.make_async_copy(held, tile_at(source, j), out_sems.at[k, j])
                    copy.start() if start else copy.wait()

                @pl.when(jnp.logical_not(first))
                def _():
                    copy = pltpu.make_async_copy(held, tile_at(target, j), out_sems.at[k, j])
                    copy.start() if start else copy.wait()

    send(True)

    @pl.loop(0, outs)
    def _(n):
        copy_either(first, rows_at(w_own, n), rows_at(w_other, n), rows_at(gate_w, n), w_sems.at[0, n], False)
        copy_either(first, rows_at(w_other, n), rows_at(w_own, n), rows_at(up_w, n), w_sems.at[1, n], False)
        sum_two = mm_t(gate[...], rows_at(gate_w, n)[...]) + mm_t(up[...], rows_at(up_w, n)[...])
        tile_at(result, n)[...] = sum_two.astype(BF16)
        chain.step(tiles + n)

    chain.finish(tiles + outs)
    send(False)


def ffn_backward(grad, gate, up, weights, part):
    rows, width = grad.shape
    ff = weights[0].shape[1]
    tiles = max(ff, width) // TILE
    narrow, wide = jax.ShapeDtypeStruct((rows, width), BF16), jax.ShapeDtypeStruct((rows, ff), BF16)
    return pl.pallas_call(
        ffn_backward_kernel,
        out_shape=[wide, wide, narrow, narrow],
        in_specs=[VMEM] * 2 + [ANY] * 5,
        out_specs=[ANY] * 2 + [VMEM] * 2,
        scratch_shapes=[pltpu.VMEM((width, ff), BF16)] * 3
        + [pltpu.VMEM((rows, ff), BF16)] * 2
        + [pltpu.SemaphoreType.DMA((3, tiles))] * 3
        + chain_scratch((rows, width)),
        compiler_params=params(2),
        cost_estimate=cost(6 * rows * width * ff),
    )(grad, part, gate, up, *weights)


def roped(values, cosine, sine):
    return values * cosine + pltpu.roll(values, HEAD // 2, 1) * sine


def unroped(grads, cosine, sine):
    return grads * cosine + pltpu.roll(grads * sine, HEAD // 2, 1)


def mm_0(left, right):
    return lax.dot_general(left, right, (((0,), (0,)), ((), ())), preferred_element_type=F32)


def greet_ctx(count):
    me = lax.axis_index("ctx")
    barrier = pltpu.get_barrier_semaphore()
    for step in range(1, count):
        pl.semaphore_signal(barrier, inc=1, device_id={"ctx": lax.rem(me + step, count)}, device_id_type=MESH)


def allowed_keys(seg_rows, seg_keys, i, block):
    rows, keys = seg_rows.shape[0], seg_keys.shape[1]
    first_row = lax.axis_index("ctx") * rows + i * block
    row_at = first_row + lax.broadcasted_iota(jnp.int32, (block, keys), 0)
    key_at = lax.broadcasted_iota(jnp.int32, (block, keys), 1)
    own = seg_rows[pl.ds(pl.multiple_of(i * block, block), block)]
    return (key_at <= row_at) & (own == seg_keys[...])


def attention_forward_kernel(chained, heads, *refs):
    layer_in, gain, w_lin, w_out, bias, cosine, sine, seg_rows, seg_keys = refs[:9]
    refs = refs[9:]
    if chained:
        part, refs = refs[0], refs[1:]
    normed, query, kv, lse, attended, result = refs[:6]
    refs = refs[6:]
    if chained:
        total, refs = refs[0], refs[1:]
    kv_sems, refs = refs[0], refs[1:]
    rows, q_cols = query.shape
    count = kv.shape[0] // rows
    me = lax.axis_index("ctx")
    block = min(256, rows)

    greet_ctx(count)
    if chained:
        chain = Chain(part, total, *refs)
        chain.greet(count - 1)
        chain.start()
    else:
        pl.semaphore_wait(pltpu.get_barrier_semaphore(), count - 1)

    def step(first, last):
        if chained:
            for c in range(first, last):
                chain.step(c)

    normalize_rows(lambda r: layer_in[r].astype(F32), gain, normed)
    mine = kv.at[pl.ds(pl.multiple_of(me * rows, rows), rows)]
    lin = mm(normed[...], w_lin[:, q_cols:]) + bias[:, q_cols:]
    mine[:, :HEAD] = roped(lin[:, :HEAD], cosine[...], sine[...]).astype(BF16)
    mine[:, HEAD:] = lin[:, HEAD:].astype(BF16)

    def passing(offset):
        return pltpu.make_async_remote_copy(
            src_ref=mine,
            dst_ref=mine,
            send_sem=kv_sems.at[0, offset],
            recv_sem=kv_sems.at[1, offset],
            device_id={"ctx": lax.rem(me + offset, count)},
            device_id_type=MESH,
        )

    for offset in range(1, count):
        passing(offset).start()
    step(0, 2)
    lin = mm(normed[...], w_lin[:, :q_cols]) + bias[:, :q_cols]
    for h in range(heads):
        columns = slice(h * HEAD, (h + 1) * HEAD)
        query[:, columns] = roped(lin[:, columns], cosine[...], sine[...]).astype(BF16)
    step(2, 4)
    for offset in range(1, count):
        passing(offset).wait_recv()

    @pl.loop(0, rows // block)
    def _(i):
        at = pl.ds(pl.multiple_of(i * block, block), block)
        allowed = allowed_keys(seg_rows, seg_keys, i, block)
        lane = lax.broadcasted_iota(jnp.int32, (block, HEAD), 1)
        logs = jnp.zeros((block, HEAD), F32)
        for h in range(heads):
            columns = slice(h * HEAD, (h + 1) * HEAD)
            scores = jnp.where(allowed, mm_t(query[at, columns], kv[:, :HEAD]) * SCALE, NEG)
            top = jnp.max(scores, axis=-1, keepdims=True)
            probs = jnp.exp(scores - top)
            sums = jnp.sum(probs, axis=-1, keepdims=True)
            probs = (probs * (1.0 / sums)).astype(BF16)
            attended[at, columns] = mm(probs, kv[:, HEAD:]).astype(BF16)
            logs = jnp.where(lane == h, top + jnp.log(sums), logs)
        lse[at] = logs
        if chained:
            for c in range(3):
                chain.step(4 + 3 * i + c)

    base = 4 + 3 * (rows // block)

    @pl.loop(0, result.shape[1] // TILE)
    def _(n):
        tile_at(result, n)[...] = mm_t(attended[...], rows_at(w_out, n)[...]).astype(BF16)
        if chained:
            chain.step(base + n)

    for offset in range(1, count):
        passing(offset).wait_send()
    if chained:
        chain.finish(base + result.shape[1] // TILE)


def attention_forward(layer_in, weights, tables, segs, part=None):
    w_lin, w_out, gains, bias = weights
    rows, width = layer_in.shape
    q_cols = w_out.shape[1]
    keys = segs[1].shape[1]
    count = keys // rows
    chained = part is not None
    narrow = jax.ShapeDtypeStruct((rows, width), BF16)
    heads_out = jax.ShapeDtypeStruct((rows, q_cols), BF16)
    kv_out = jax.ShapeDtypeStruct((keys, 2 * HEAD), BF16)
    lse_out = jax.ShapeDtypeStruct((rows, HEAD), F32)
    outs = [narrow, heads_out, kv_out, lse_out, heads_out, narrow] + [narrow] * chained
    args = (layer_in, gains[:1], w_lin, w_out, bias, *tables, *segs) + ((part,) if chained else ())
    return pl.pallas_call(
        functools.partial(attention_forward_kernel, chained, q_cols // HEAD),
        out_shape=outs,
        in_specs=[VMEM] * len(args),
        out_specs=[VMEM] * len(outs),
        scratch_shapes=[pltpu.SemaphoreType.DMA((2, count))] + (chain_scratch((rows, width)) if chained else []),
        compiler_params=params(3 + chained),
        cost_estimate=cost(2 * rows * (width * (2 * q_cols + 2 * HEAD) + 2 * keys * q_cols)),
    )(*args)


def attention_backward_kernel(
    upstream, sum_in, layer_in, attn_out, gain, w_lin, w_out, query, kv, lse, attended,
    cosine, sine, seg_rows, seg_keys, part,
    middle_grad, attn_grad, lin, gain_grad, result, total,
    heads_grad, kv_grad, sent, got, kv_sems, *chain_refs,
):
    rows, q_cols = query.shape
    heads = q_cols // HEAD
    count = kv.shape[0] // rows
    me = lax.axis_index("ctx")
    block = min(256, rows)
    greet_ctx(count)
    chain = Chain(part, total, *chain_refs)
    chain.greet(count - 1)
    chain.start()
    gain_grad[...] = jnp.zeros_like(gain_grad)
    kv_grad[...] = jnp.zeros_like(kv_grad)

    @pl.loop(0, rows // 64)
    def _(i):
        at = pl.ds(pl.multiple_of(i * 64, 64), 64)
        middle = layer_in[at].astype(F32) + attn_out[at].astype(F32)
        factor = lax.rsqrt(jnp.mean(middle * middle, axis=-1, keepdims=True) + EPS)
        unit = middle * factor
        grad = sum_in[at].astype(F32)
        per_row = grad * unit
        weighted = grad * gain[...]
        mean = jnp.mean(per_row * gain[...], axis=-1, keepdims=True)
        out = upstream[at].astype(F32) + factor * (weighted - unit * mean)
        middle_grad[at] = out
        attn_grad[at] = out.astype(BF16)
        gain_grad[...] += jnp.sum(per_row.reshape(8, 8, per_row.shape[1]), axis=0)

    chain.step(0)
    chain.step(1)
    heads_grad[...] = mm(attn_grad[...], w_out[...]).astype(BF16)
    chain.step(2)
    chain.step(3)

    @pl.loop(0, rows // block)
    def _(i):
        at = pl.ds(pl.multiple_of(i * block, block), block)
        allowed = allowed_keys(seg_rows, seg_keys, i, block)
        for h in range(heads):
            columns = slice(h * HEAD, (h + 1) * HEAD)
            scores = mm_t(query[at, columns], kv[:, :HEAD]) * SCALE - lse[at, h : h + 1]
            probs = jnp.exp(jnp.where(allowed, scores, NEG))
            grad = heads_grad[at, columns]
            row_sum = jnp.sum(attended[at, columns].astype(F32) * grad.astype(F32), axis=-1, keepdims=True)
            score_grad = (probs * (mm_t(grad, kv[:, HEAD:]) - row_sum)).astype(BF16)
            q_grad = mm(score_grad, kv[:, :HEAD]) * SCALE
            lin[at, columns] = unroped(q_grad, cosine[at], sine[at]).astype(BF16)
            kv_grad[:, :HEAD] += mm_0(score_grad, query[at, columns])
            kv_grad[:, HEAD:] += mm_0(probs.astype(BF16), grad)
            chain.step(4 + heads * i + h)

    def passing(offset):
        return pltpu.make_async_remote_copy(
            src_ref=sent.at[offset - 1],
            dst_ref=got.at[offset - 1],
            send_sem=kv_sems.at[0, offset],
            recv_sem=kv_sems.at[1, offset],
            device_id={"ctx": lax.rem(me + offset, count)},
            device_id_type=MESH,
        )

    for offset in range(1, count):
        peer = pl.ds(pl.multiple_of(lax.rem(me + offset, count) * rows, rows), rows)
        sent[offset - 1, :, :HEAD] = (kv_grad[peer, :HEAD] * SCALE).astype(BF16)
        sent[offset - 1, :, HEAD:] = kv_grad[peer, HEAD:].astype(BF16)
        passing(offset).start()
    mine = pl.ds(pl.multiple_of(me * rows, rows), rows)
    k_grad, v_grad = kv_grad[mine, :HEAD] * SCALE, kv_grad[mine, HEAD:]
    for offset in range(1, count):
        passing(offset).wait_recv()
        k_grad = k_grad + got[offset - 1, :, :HEAD].astype(F32)
        v_grad = v_grad + got[offset - 1, :, HEAD:].astype(F32)
    lin[:, q_cols : q_cols + HEAD] = unroped(k_grad, cosine[...], sine[...]).astype(BF16)
    lin[:, q_cols + HEAD :] = v_grad.astype(BF16)
    base = 4 + heads * (rows // block)

    @pl.loop(0, result.shape[1] // TILE)
    def _(n):
        tile_at(result, n)[...] = mm_t(lin[...], rows_at(w_lin, n)[...]).astype(BF16)
        chain.step(base + n)

    for offset in range(1, count):
        passing(offset).wait_send()
    chain.finish(base + result.shape[1] // TILE)


def attention_backward(upstream, sum_in, kept, weights, tables, segs, part):
    w_lin, w_out, gains, bias = weights
    rows, width = upstream.shape
    q_cols = w_out.shape[1]
    keys = segs[1].shape[1]
    count = keys // rows
    narrow = jax.ShapeDtypeStruct((rows, width), BF16)
    outs = [
        jax.ShapeDtypeStruct((rows, width), F32),
        narrow,
        jax.ShapeDtypeStruct((rows, q_cols + 2 * HEAD), BF16),
        jax.ShapeDtypeStruct((8, width), F32),
        narrow,
        narrow,
    ]
    args = (upstream, sum_in, kept["layer_in"], kept["attn_out"], gains[1:], w_lin, w_out)
    args += (kept["query"], kept["kv"], kept["lse"], kept["attended"], *tables, *segs, part)
    return pl.pallas_call(
        attention_backward_kernel,
        out_shape=outs,
        in_specs=[VMEM] * len(args),
        out_specs=[VMEM] * len(outs),
        scratch_shapes=[
            pltpu.VMEM((rows, q_cols), BF16),
            pltpu.VMEM((keys, 2 * HEAD), F32),
            pltpu.VMEM((max(count - 1, 1), rows, 2 * HEAD), BF16),
            pltpu.VMEM((max(count - 1, 1), rows, 2 * HEAD), BF16),
            pltpu.SemaphoreType.DMA((2, count)),
        ]
        + chain_scratch((rows, width)),
        compiler_params=params(5),
        cost_estimate=cost(2 * rows * (width * (2 * q_cols + 2 * HEAD) + 5 * keys * q_cols)),
    )(*args)


def rope_tables(places):
    steps = jnp.arange(HEAD // 2, dtype=F32) * (2.0 / HEAD)
    inverse = ROPE_BASE ** (-steps)
    angles = places.astype(F32)[..., None] * inverse
    angles = jnp.concatenate([angles, angles], axis=-1)
    return (jnp.cos(angles), jnp.sin(angles))


def norm_back(grad_out, rows_in, factor, gain):
    unit = rows_in * factor
    gain_grad = jnp.sum(grad_out * unit, axis=0)
    weighted = grad_out * gain
    return (
        factor * (weighted - unit * jnp.mean(weighted * unit, axis=-1, keepdims=True)),
        gain_grad,
    )


def over_ctx(value):
    if lax.axis_size("ctx") == 2:
        other = lax.ppermute(value, "ctx", [(0, 1), (1, 0)])
        low = lax.axis_index("ctx") == 0
        return jnp.concatenate([jnp.where(low, value, other), jnp.where(low, other, value)], axis=-1)
    return lax.all_gather(value, "ctx", axis=value.ndim - 1, tiled=True)


def input_backward(normed_one_grad, middle_grad, kept, gains):
    layer_in = kept["layer_in"].astype(F32)
    factor = lax.rsqrt(jnp.mean(layer_in * layer_in, axis=-1, keepdims=True) + EPS)
    norm_grad, gain_one = norm_back(normed_one_grad.astype(F32), layer_in, factor, gains[0])
    return (middle_grad + norm_grad).astype(BF16), gain_one


def local(
    section_in,
    segments,
    positions,
    query_weight,
    kv_weight,
    output_weight,
    gate_up,
    down_weight,
    norm_gains,
    query_bias,
    kv_bias,
    out_grad,
):
    sec = lax.axis_index("section")
    first = sec == 0
    group = HEADS // KV_HEADS
    heads_here = HEADS // lax.axis_size("tp")
    head_pick = lax.axis_index("tp") * heads_here // group
    shards = lax.axis_size("dp") * lax.axis_size("ctx")
    ranks = ("dp", "ctx")
    seqs, span, width = section_in.shape[1:]
    shard = query_weight.shape[1]
    q_cols = query_weight.shape[2]
    ff = gate_up.shape[3]

    def per_layer(mine, theirs):
        return jnp.where(first, mine, theirs), jnp.where(first, theirs, mine)

    piece = HEAD // shards
    biases = jnp.concatenate([query_bias[0].reshape(-1), kv_bias[0].reshape(-1)])
    n_biases = biases.shape[0]
    biases = jnp.pad(biases, (0, -n_biases % shard)).reshape(-1, shard).T
    extra = jnp.concatenate([norm_gains[0].T, biases], axis=1)
    n_extra = extra.shape[1]
    extra = jnp.pad(extra, ((0, 0), (0, HEAD - n_extra)))
    packed = jnp.concatenate([query_weight[0], kv_weight[0, 0], kv_weight[0, 1], output_weight[0].T, extra], axis=1)
    packed = lax.all_gather(packed, ranks, axis=0, tiled=True)
    packed_mine = packed
    packed = per_layer(packed, swap(packed))
    attn_weights = []
    kv_width = KV_HEADS * HEAD
    for layer in range(2):
        p = packed[layer]
        wq = p[:, :q_cols]
        wk = lax.dynamic_slice_in_dim(p[:, q_cols : q_cols + kv_width], head_pick * HEAD, HEAD, 1)
        wv = lax.dynamic_slice_in_dim(p[:, q_cols + kv_width : q_cols + 2 * kv_width], head_pick * HEAD, HEAD, 1)
        wo = p[:, q_cols + 2 * kv_width : 2 * q_cols + 2 * kv_width]
        s = p[:, 2 * q_cols + 2 * kv_width :]
        gains = s[:, :2].T
        s = s[:, 2:n_extra].T.reshape(-1, shards, shard).transpose(1, 0, 2).reshape(shards, -1)[:, :n_biases]
        q_b = s[:, : heads_here * piece].reshape(shards, heads_here, piece).transpose(1, 0, 2).reshape(heads_here, HEAD)
        kv_b = s[:, heads_here * piece :].reshape(shards, 2, KV_HEADS, piece)
        kv_b = kv_b.transpose(1, 2, 0, 3).reshape(2, KV_HEADS, HEAD)
        kv_b = lax.dynamic_slice_in_dim(kv_b, head_pick, 1, 1)
        bias = jnp.concatenate([q_b.reshape(1, -1), kv_b.reshape(1, -1)], axis=1).astype(F32)
        attn_weights.append((jnp.concatenate([wq, wk, wv], axis=1), wo, gains.astype(F32), bias))

    half = shard // 2
    spare = -ff % TILE
    wide = jnp.pad(gate_up[0], ((0, 0), (0, 0), (0, spare)))
    mine = lax.dynamic_index_in_dim(wide, sec, 0, keepdims=False)
    theirs = swap(lax.dynamic_index_in_dim(wide, 1 - sec, 0, keepdims=False))
    gate_up_shards = per_layer(mine, theirs)
    down_t = jnp.pad(down_weight[0].T, ((0, 0), (0, spare)))
    mine = lax.dynamic_slice_in_dim(down_t, sec * half, half, 0)
    theirs = swap(lax.dynamic_slice_in_dim(down_t, (1 - sec) * half, half, 0))
    down_shards = per_layer(mine, theirs)

    def after(value, event):
        return lax.optimization_barrier((value, event))[0]

    def gather_own(layer, event):
        return lax.all_gather(after(gate_up_shards[layer], event), ranks, axis=0, tiled=True)

    def gather_down(layer, event):
        return lax.all_gather(after(down_shards[layer], event), ranks, axis=0)

    def share_ffn(own, down_own, event):
        own, down_own, event = lax.optimization_barrier((own, down_own, event))
        down = jnp.stack(per_layer(down_own, swap(down_own)), axis=1).reshape(width, ff + spare)
        return (own, swap(own), down), event

    micro = sec
    seg = lax.dynamic_index_in_dim(segments, micro, 0, keepdims=False)
    pos = lax.dynamic_index_in_dim(positions, micro, 0, keepdims=False)
    hidden = lax.dynamic_index_in_dim(section_in, micro, 0, keepdims=False)
    grad_top = lax.dynamic_index_in_dim(out_grad, micro, 0, keepdims=False)
    seg_keys = over_ctx(seg)
    segs, tables = [], []
    for q in range(seqs):
        segs.append((seg[q][:, None], seg_keys[q][None]))
        cosine, sine = rope_tables(pos[q])
        tables.append((cosine, jnp.where(jnp.arange(HEAD) < HEAD // 2, -sine, sine)))

    kept = [[dict(), dict()] for _ in range(2)]
    names = ("normed", "query", "kv", "lse", "attended")
    layer_in = [hidden[0], hidden[1]]
    outs = []
    ffn_weights = [None, None]
    own_low = gather_own(0, packed_mine)
    for layer in range(2):
        weights, k = attn_weights[layer], kept[layer]
        gains = weights[2]
        k[0]["layer_in"] = layer_in[0]
        if layer == 0:
            *more, part_a = attention_forward(layer_in[0], weights, tables[0], segs[0])
            down_low = gather_down(0, part_a)
        else:
            *more, part_a, ffn_b = attention_forward(layer_in[0], weights, tables[0], segs[0], part_b)
            layer_in[1] = (layer_in[1].astype(F32) + kept[0][1]["attn_out"].astype(F32) + ffn_b.astype(F32)).astype(BF16)
            outs.append(jnp.stack(layer_in))
        k[0].update(zip(names, more))
        k[1]["layer_in"] = layer_in[1]
        *more, part_b, attn_a = attention_forward(layer_in[1], weights, tables[1], segs[1], part_a)
        k[1].update(zip(names, more))
        if layer == 0:
            ffn_weights[0], attn_a = share_ffn(own_low, down_low, attn_a)
            own_high = gather_own(1, attn_a)
        gain = gains[1:]
        normed_a, gate, up, inner, part_a, attn_b = ffn_forward(layer_in[0], attn_a, gain, ffn_weights[layer], part_b)
        k[0].update(attn_out=attn_a, normed_two=normed_a, gate=gate, up=up, inner=inner)
        if layer == 0:
            down_high = gather_down(1, part_a)
        normed_b, gate, up, inner, part_b, ffn_a = ffn_forward(layer_in[1], attn_b, gain, ffn_weights[layer], part_a)
        k[1].update(attn_out=attn_b, normed_two=normed_b, gate=gate, up=up, inner=inner)
        layer_a = (layer_in[0].astype(F32) + attn_a.astype(F32) + ffn_a.astype(F32)).astype(BF16)
        if layer == 0:
            ffn_weights[1], layer_a = share_ffn(own_high, down_high, layer_a)
        layer_in = [layer_a, layer_in[1]]
    upstream = [grad_top[0], grad_top[1]]
    k = kept[1]
    own_a, other_a, grad_a, ffn_b = ffn_backward(upstream[0], k[0]["gate"], k[0]["up"], ffn_weights[1], part_b)
    layer_in[1] = (layer_in[1].astype(F32) + k[1]["attn_out"].astype(F32) + ffn_b.astype(F32)).astype(BF16)
    outs.append(jnp.stack(layer_in))

    def to_section(values):
        low = lax.ppermute(values[0], "section", [(1, 0)])
        high = lax.ppermute(values[1], "section", [(0, 1)])
        return jnp.stack([jnp.where(first, values[0], high), jnp.where(first, low, values[1])])

    section_out = to_section(outs)

    in_grads = [None, None]
    gate_up_grads, down_grads, packed_grads = [None, None], [None, None], [None, None]
    waiting = None
    for layer in (1, 0):
        weights, k = attn_weights[layer], kept[layer]
        if layer == 0:
            own_a, other_a, grad_a, sum_b = ffn_backward(upstream[0], k[0]["gate"], k[0]["up"], ffn_weights[0], parts[1])
            upstream[1], gain_b = input_backward(sum_b, middle_grads[1], kept[1][1], attn_weights[1][2])
            grad_a, down_grads[1] = lax.optimization_barrier((grad_a, down_grads[1]))
            waiting(upstream, gain_a + gain_b)
        own_b, other_b, grad_b, sum_a = ffn_backward(upstream[1], k[1]["gate"], k[1]["up"], ffn_weights[layer], grad_a)
        own_grads, other_grads = (own_a, own_b), (other_a, other_b)
        normed_two = jnp.concatenate([k[q]["normed_two"] for q in range(seqs)])
        own_w = dot("rd,rf->df", normed_two, jnp.concatenate(own_grads)).astype(BF16)
        other_w = dot("rd,rf->df", normed_two, jnp.concatenate(other_grads)).astype(BF16)
        own_w = (own_w.astype(F32) + swap(other_w).astype(F32)).astype(BF16)
        own_w, sum_a = lax.optimization_barrier((own_w, sum_a))
        gate_up_grads[layer] = lax.psum_scatter(own_w, ranks, scatter_dimension=0, tiled=True)
        down_w = dot("rd,rf->df", jnp.concatenate(upstream), jnp.concatenate([k[q]["inner"] for q in range(seqs)])).astype(BF16)
        down_w = down_w.reshape(shards, 2, half, ff + spare)
        down_own = lax.dynamic_index_in_dim(down_w, sec, 1, keepdims=False)
        down_other = lax.dynamic_index_in_dim(down_w, 1 - sec, 1, keepdims=False)
        down_own = (down_own.astype(F32) + swap(down_other).astype(F32)).astype(BF16)
        down_own, sum_a = lax.optimization_barrier((down_own, sum_a))
        down_grads[layer] = lax.psum_scatter(
            down_own.reshape(shards * half, ff + spare), ranks, scatter_dimension=0, tiled=True
        )

        first_a = attention_backward(upstream[0], sum_a, k[0], weights, tables[0], segs[0], grad_b)
        first_b = attention_backward(upstream[1], first_a[-1], k[1], weights, tables[1], segs[1], first_a[-2])
        middle_grads, attn_grads, lin_grads, gains_two, parts, sums = zip(first_a, first_b)
        gains_two = [jnp.sum(g, axis=0) for g in gains_two]
        sum_a, sum_b = sums[1], None
        lin_grad = jnp.concatenate(lin_grads)
        normed_one = jnp.concatenate([k[q]["normed"] for q in range(seqs)])
        lin_w = dot("rd,re->de", normed_one, lin_grad)
        attended = jnp.concatenate([k[q]["attended"] for q in range(seqs)])
        out_w = dot("rd,re->de", jnp.concatenate(attn_grads), attended)
        bias = jnp.sum(lin_grad.astype(F32), axis=0)

        def finish(upstream, gain_one, layer=layer, lin_w=lin_w, out_w=out_w, bias=bias, gains_two=gains_two):
            in_grads[layer] = jnp.stack(upstream)
            gain_cols = jnp.stack([gain_one, sum(gains_two)], axis=1)
            bias = bias.reshape(heads_here + 2, shards, piece).transpose(1, 0, 2).reshape(shards, (heads_here + 2) * piece)
            bias = jnp.pad(bias, ((0, 0), (0, -bias.shape[1] % shard)))
            bias = bias.reshape(shards, -1, shard).transpose(0, 2, 1).reshape(width, -1)
            extra = jnp.concatenate([gain_cols, bias], axis=1)
            extra = jnp.pad(extra, ((0, 0), (0, HEAD - extra.shape[1])))
            packed_grads[layer] = jnp.concatenate([lin_w, out_w, extra], axis=1).astype(BF16)

        waiting = finish
        upstream = [None, None]
        upstream[0], gain_a = input_backward(sum_a, middle_grads[0], k[0], weights[2])
        if layer == 1:
            upstream[0], gate_up_grads[1] = lax.optimization_barrier((upstream[0], gate_up_grads[1]))
    last_part, gate_up_grads[0] = lax.optimization_barrier((parts[1], gate_up_grads[0]))
    sum_b, down_grads[0] = lax.optimization_barrier((tp_sum(last_part), down_grads[0]))
    upstream[1], gain_b = input_backward(sum_b, middle_grads[1], kept[0][1], attn_weights[0][2])
    waiting(upstream, gain_a + gain_b)

    input_grad = to_section(in_grads)

    low = lax.ppermute(packed_grads[0], "section", [(1, 0)])
    high = lax.ppermute(packed_grads[1], "section", [(0, 1)])
    packed_total = jnp.where(
        first, packed_grads[0].astype(F32) + low.astype(F32), packed_grads[1].astype(F32) + high.astype(F32)
    ).astype(BF16)
    packed_total = lax.psum_scatter(packed_total, ranks, scatter_dimension=0, tiled=True).astype(F32)
    q_grad = packed_total[:, :q_cols]
    kv_narrow = packed_total[:, q_cols : q_cols + 2 * HEAD].reshape(shard, 2, HEAD)
    o_grad = packed_total[:, q_cols + 2 * HEAD : 2 * q_cols + 2 * HEAD].T
    extra = packed_total[:, 2 * q_cols + 2 * HEAD :]
    gains_grad = extra[:, :2].T
    bias_cols = -(-(heads_here + 2) * piece // shard)
    bias = extra[:, 2 : 2 + bias_cols].T.reshape(-1)[: (heads_here + 2) * piece].reshape(heads_here + 2, piece)
    q_bias_grad = bias[:heads_here]
    kv_full = jnp.zeros((shard, 2, KV_HEADS, HEAD), F32)
    kv_full = lax.dynamic_update_slice_in_dim(kv_full, kv_narrow[:, :, None], head_pick, 2)
    bias_full = jnp.zeros((2, KV_HEADS, piece), F32)
    bias_full = lax.dynamic_update_slice_in_dim(bias_full, bias[heads_here:, None], head_pick, 1)
    flat = bias_full.reshape(-1)
    flat = jnp.pad(flat, (0, -flat.shape[0] % (2 * KV_HEADS * HEAD)))
    flat_rows = flat.shape[0] // (2 * KV_HEADS * HEAD)
    joined = jnp.concatenate([kv_full.reshape(shard, -1), flat.reshape(flat_rows, -1)]).astype(BF16)
    joined = chain_sum(joined).astype(F32)
    kv_grad = joined[:shard].reshape(shard, 2, KV_HEADS * HEAD).transpose(1, 0, 2)
    kv_bias_grad = joined[shard:].reshape(-1)[: 2 * KV_HEADS * piece].reshape(2, KV_HEADS, piece)

    def collect(values):
        kept_half = jnp.where(first, values[0], values[1])
        other = swap(jnp.where(first, values[1], values[0]))
        return jnp.where(first, kept_half, other), jnp.where(first, other, kept_half)

    gate_up_grad = jnp.stack(collect(gate_up_grads))[..., :ff].astype(F32)
    down_grad = jnp.concatenate(collect(down_grads), axis=0)[:, :ff].T.astype(F32)
    return (
        section_out[None],
        input_grad[None],
        q_grad[None],
        kv_grad[None],
        o_grad[None],
        gate_up_grad[None],
        down_grad[None],
        gains_grad[None],
        q_bias_grad[None],
        kv_bias_grad[None],
    )


def solution(mesh):
    in_specs = (
        P(None, "dp", "ctx", None),
        P(None, "dp", "ctx"),
        P(None, "dp", "ctx"),
        P("section", ("dp", "ctx"), "tp"),
        P("section", None, ("dp", "ctx"), None),
        P("section", "tp", ("dp", "ctx")),
        P("section", None, ("dp", "ctx"), "tp"),
        P("section", "tp", ("dp", "ctx")),
        P("section", None, ("dp", "ctx")),
        P("section", "tp", ("dp", "ctx")),
        P("section", None, None, ("dp", "ctx")),
        P(None, "dp", "ctx", None),
    )
    out_specs = (
        P("section", None, "dp", "ctx", None),
        P("section", None, "dp", "ctx", None),
        P("section", ("dp", "ctx"), "tp"),
        P("section", None, ("dp", "ctx"), None),
        P("section", "tp", ("dp", "ctx")),
        P("section", None, ("dp", "ctx"), "tp"),
        P("section", "tp", ("dp", "ctx")),
        P("section", None, ("dp", "ctx")),
        P("section", "tp", ("dp", "ctx")),
        P("section", None, None, ("dp", "ctx")),
    )
    return jax.shard_map(local, mesh=mesh, in_specs=in_specs, out_specs=out_specs, check_vma=False)
```

```python
import functools

import jax
import jax.numpy as jnp
from jax import lax
from jax.experimental import pallas as pl
from jax.experimental.pallas import tpu as pltpu
from jax.sharding import PartitionSpec as P

HEADS = 12
KV_HEADS = 2
HEAD = 128

EPS = 1e-06
ROPE_BASE = 1000000.0
NEG = -1e30
SCALE = HEAD ** (-0.5)
TILE = 768
MESH = pl.DeviceIdType.MESH

F32 = jnp.float32
BF16 = jnp.bfloat16


def dot(form, left, right):
    return jnp.einsum(form, left, right, preferred_element_type=F32)


def swap(value):
    return lax.ppermute(value, "section", [(0, 1), (1, 0)])


def chain_sum(part):
    count = lax.axis_size("tp")
    place = lax.axis_index("tp")
    middle = count // 2
    total = part
    for hop in range(middle - 1):
        got = lax.ppermute(total, "tp", [(hop, hop + 1), (count - 1 - hop, count - 2 - hop)])
        total = (total.astype(F32) + got.astype(F32)).astype(BF16)
    got = lax.ppermute(total, "tp", [(middle - 1, middle), (middle, middle - 1)])
    total = (total.astype(F32) + got.astype(F32)).astype(BF16)
    for hop in range(middle - 1):
        low, high = middle - 1 - hop, middle + hop
        got = lax.ppermute(total, "tp", [(low, low - 1), (high, high + 1)])
        total = jnp.where((place == low - 1) | (place == high + 1), got, total)
    return total


class Chain:
    def __init__(self, part, total, from_end, from_peer, joined, sems):
        self.part, self.total = part, total
        self.from_end, self.from_peer, self.joined = from_end, from_peer, joined
        self.sems = sems
        self.chunks = sems.shape[1]
        self.rows = part.shape[0] // self.chunks
        place = lax.axis_index("tp")
        self.is_middle = (place == 1) | (place == 2)
        self.inner = jnp.where(place < 2, place + 1, place - 1)
        self.outer = jnp.where(place < 2, place - 1, place + 1)

    def greet(self, others=0):
        barrier = pltpu.get_barrier_semaphore()
        pl.semaphore_signal(barrier, inc=1, device_id={"tp": self.inner}, device_id_type=MESH)

        @pl.when(self.is_middle)
        def _():
            pl.semaphore_signal(barrier, inc=1, device_id={"tp": self.outer}, device_id_type=MESH)
            pl.semaphore_wait(barrier, 2 + others)

        @pl.when(jnp.logical_not(self.is_middle))
        def _():
            pl.semaphore_wait(barrier, 1 + others)

    def at(self, ref, c):
        return ref.at[pl.ds(pl.multiple_of(c * self.rows, self.rows), self.rows)]

    def copy(self, source, target, c, step, place):
        return pltpu.make_async_remote_copy(
            src_ref=self.at(source, c),
            dst_ref=self.at(target, c),
            send_sem=self.sems.at[2 * step, c],
            recv_sem=self.sems.at[2 * step + 1, c],
            device_id={"tp": place},
            device_id_type=MESH,
        )

    def inward(self, c):
        return self.copy(self.part, self.from_end, c, 0, self.inner)

    def across(self, c):
        return self.copy(self.joined, self.from_peer, c, 1, self.inner)

    def outward(self, c):
        return self.copy(self.total, self.total, c, 2, self.outer)

    def start(self):
        @pl.when(jnp.logical_not(self.is_middle))
        def _():
            @pl.loop(0, self.chunks)
            def _(c):
                self.inward(c).start()

    def join(self, c):
        self.inward(c).wait_recv()
        self.at(self.joined, c)[...] = self.at(self.part, c)[...] + self.at(self.from_end, c)[...]
        self.across(c).start()

    def close(self, c):
        self.across(c).wait_recv()
        self.at(self.total, c)[...] = self.at(self.joined, c)[...] + self.at(self.from_peer, c)[...]
        self.outward(c).start()

    def step(self, c):
        @pl.when(self.is_middle & (c < self.chunks))
        def _():
            self.join(c)

            @pl.when(c > 0)
            def _():
                self.close(c - 1)

    def finish(self, done):
        @pl.when(self.is_middle)
        def _():
            if done < self.chunks:

                @pl.loop(done, self.chunks)
                def _(c):
                    self.step(c)

            self.close(self.chunks - 1)

            @pl.loop(0, self.chunks)
            def _(c):
                self.across(c).wait_send()
                self.outward(c).wait_send()

        @pl.when(jnp.logical_not(self.is_middle))
        def _():
            @pl.loop(0, self.chunks)
            def _(c):
                self.inward(c).wait_send()
                self.outward(c).wait_recv()


def chain_chunks(rows):
    return min(16, rows // 16)


def chain_scratch(shape):
    return [pltpu.VMEM(shape, BF16)] * 3 + [pltpu.SemaphoreType.DMA((6, chain_chunks(shape[0])))]


VMEM = pl.BlockSpec(memory_space=pltpu.VMEM)
ANY = pl.BlockSpec(memory_space=pl.ANY)


def params(collective_id):
    return pltpu.CompilerParams(collective_id=collective_id, has_side_effects=True, vmem_limit_bytes=58 << 20)


def cost():
    return pl.CostEstimate(flops=1 << 20, bytes_accessed=1 << 20, transcendentals=0)


def sum_kernel(part, total, *scratch):
    chain = Chain(part, total, *scratch)
    chain.greet()
    chain.start()
    chain.finish(0)


def tp_sum(part):
    shape = part.shape
    return pl.pallas_call(
        sum_kernel,
        out_shape=jax.ShapeDtypeStruct(shape, BF16),
        in_specs=[VMEM],
        out_specs=VMEM,
        scratch_shapes=chain_scratch(shape),
        compiler_params=params(0),
        cost_estimate=cost(),
    )(part)


def mm(left, right):
    return jnp.dot(left, right, preferred_element_type=F32)


def mm_t(left, right):
    return lax.dot_general(left, right, (((1,), (1,)), ((), ())), preferred_element_type=F32)


def tile_at(ref, j, size=TILE):
    return ref.at[:, pl.ds(pl.multiple_of(j * size, size), size)]


def rows_at(ref, j, size=TILE):
    return ref.at[pl.ds(pl.multiple_of(j * size, size), size)]


def copy_either(first, one, two, target, sem, start):
    @pl.when(first)
    def _():
        copy = pltpu.make_async_copy(one, target, sem)
        copy.start() if start else copy.wait()

    @pl.when(jnp.logical_not(first))
    def _():
        copy = pltpu.make_async_copy(two, target, sem)
        copy.start() if start else copy.wait()


def normalize_rows(source, gain, target, block=64):
    @pl.loop(0, target.shape[0] // block)
    def _(i):
        rows = pl.ds(pl.multiple_of(i * block, block), block)
        values = source(rows)
        factor = lax.rsqrt(jnp.mean(values * values, axis=-1, keepdims=True) + EPS)
        target[rows] = (values * factor * gain[...]).astype(BF16)


def ffn_forward_kernel(chained, *refs):
    layer_in, attn_out, gain, w_own, w_other, w_down = refs[:6]
    refs = refs[6:]
    if chained:
        part, refs = refs[0], refs[1:]
    normed, gate_out, up_out, inner_out, result = refs[:5]
    refs = refs[5:]
    if chained:
        total, refs = refs[0], refs[1:]
    gate_w, up_w, down_w, gate, up, inner, one, two, w_sems, out_sems, *chain_refs = refs
    first = lax.axis_index("section") == 0
    tiles, outs = gate_w.shape[1] // TILE, gate_w.shape[0] // TILE

    @pl.loop(0, tiles)
    def _(j):
        copy_either(first, tile_at(w_own, j), tile_at(w_other, j), tile_at(gate_w, j), w_sems.at[0, j], True)
        copy_either(first, tile_at(w_other, j), tile_at(w_own, j), tile_at(up_w, j), w_sems.at[1, j], True)

    @pl.loop(0, outs)
    def _(n):
        pltpu.make_async_copy(rows_at(w_down, n), rows_at(down_w, n), w_sems.at[2, n]).start()

    if chained:
        chain = Chain(part, total, *chain_refs)
        chain.greet()
        chain.start()

    def step(base, *places):
        if chained:
            for place in places:
                chain.step(base + place)

    normalize_rows(lambda rows: layer_in[rows].astype(F32) + attn_out[rows].astype(F32), gain, normed)
    block = min(64, one.shape[0])

    @pl.loop(0, tiles)
    def _(j):
        copy_either(first, tile_at(w_own, j), tile_at(w_other, j), tile_at(gate_w, j), w_sems.at[0, j], False)
        one[...] = mm(normed[...], tile_at(gate_w, j)[...])
        step(4 * j, 0, 1)
        copy_either(first, tile_at(w_other, j), tile_at(w_own, j), tile_at(up_w, j), w_sems.at[1, j], False)
        two[...] = mm(normed[...], tile_at(up_w, j)[...])
        step(4 * j, 2)
        columns = pl.ds(pl.multiple_of(j * TILE, TILE), TILE)

        @pl.loop(0, one.shape[0] // block)
        def _(i):
            rows = pl.ds(pl.multiple_of(i * block, block), block)
            g, u = one[rows], two[rows]
            gate[rows, columns] = g.astype(BF16)
            up[rows, columns] = u.astype(BF16)
            inner[rows, columns] = (g * jax.nn.sigmoid(g) * u).astype(BF16)

        step(4 * j, 3)
        for k, (source, target) in enumerate(((gate, gate_out), (up, up_out), (inner, inner_out))):
            pltpu.make_async_copy(tile_at(source, j), tile_at(target, j), out_sems.at[k, j]).start()

    @pl.loop(0, outs)
    def _(n):
        pltpu.make_async_copy(rows_at(w_down, n), rows_at(down_w, n), w_sems.at[2, n]).wait()
        tile_at(result, n)[...] = mm_t(inner[...], rows_at(down_w, n)[...]).astype(BF16)
        step(4 * tiles + 2 * n, 0, 1)

    if chained:
        chain.finish(4 * tiles + 2 * outs)

    @pl.loop(0, tiles)
    def _(j):
        for k, (source, target) in enumerate(((gate, gate_out), (up, up_out), (inner, inner_out))):
            pltpu.make_async_copy(tile_at(source, j), tile_at(target, j), out_sems.at[k, j]).wait()


def ffn_forward(layer_in, attn_out, gain, weights, part=None):
    rows, width = layer_in.shape
    ff = weights[0].shape[1]
    tiles = max(ff, width) // TILE
    chained = part is not None
    narrow, wide = jax.ShapeDtypeStruct((rows, width), BF16), jax.ShapeDtypeStruct((rows, ff), BF16)
    return pl.pallas_call(
        functools.partial(ffn_forward_kernel, chained),
        out_shape=[narrow, wide, wide, wide, narrow] + [narrow] * chained,
        in_specs=[VMEM] * 3 + [ANY] * 3 + [VMEM] * chained,
        out_specs=[VMEM] + [ANY] * 3 + [VMEM] * (1 + chained),
        scratch_shapes=[pltpu.VMEM((width, ff), BF16)] * 3
        + [pltpu.VMEM((rows, ff), BF16)] * 3
        + [pltpu.VMEM((rows, TILE), F32)] * 2
        + [pltpu.SemaphoreType.DMA((3, tiles))] * 2
        + (chain_scratch((rows, width)) if chained else []),
        compiler_params=params(1) if chained else pltpu.CompilerParams(vmem_limit_bytes=58 << 20),
        cost_estimate=cost(),
    )(layer_in, attn_out, gain, *weights, *((part,) if chained else ()))


def ffn_backward_kernel(
    grad, part, gate_in, up_in, w_own, w_other, w_down,
    own_out, other_out, result, total,
    gate_w, up_w, down_w, gate, up, one, w_sems, in_sems, out_sems, *chain_refs,
):
    first = lax.axis_index("section") == 0
    tiles, outs = gate_w.shape[1] // TILE, gate_w.shape[0] // TILE

    @pl.loop(0, tiles)
    def _(j):
        pltpu.make_async_copy(tile_at(w_down, j), tile_at(down_w, j), w_sems.at[2, j]).start()
        pltpu.make_async_copy(tile_at(gate_in, j), tile_at(gate, j), in_sems.at[0, j]).start()
        pltpu.make_async_copy(tile_at(up_in, j), tile_at(up, j), in_sems.at[1, j]).start()

    @pl.loop(0, outs)
    def _(n):
        copy_either(first, rows_at(w_own, n), rows_at(w_other, n), rows_at(gate_w, n), w_sems.at[0, n], True)
        copy_either(first, rows_at(w_other, n), rows_at(w_own, n), rows_at(up_w, n), w_sems.at[1, n], True)

    chain = Chain(part, total, *chain_refs)
    chain.greet()
    chain.start()
    block = min(64, one.shape[0])

    @pl.loop(0, tiles)
    def _(j):
        pltpu.make_async_copy(tile_at(w_down, j), tile_at(down_w, j), w_sems.at[2, j]).wait()
        pltpu.make_async_copy(tile_at(gate_in, j), tile_at(gate, j), in_sems.at[0, j]).wait()
        pltpu.make_async_copy(tile_at(up_in, j), tile_at(up, j), in_sems.at[1, j]).wait()
        one[...] = mm(grad[...], tile_at(down_w, j)[...])
        chain.step(3 * j)
        chain.step(3 * j + 1)
        columns = pl.ds(pl.multiple_of(j * TILE, TILE), TILE)

        @pl.loop(0, one.shape[0] // block)
        def _(i):
            rows = pl.ds(pl.multiple_of(i * block, block), block)
            g, u, d = gate[rows, columns].astype(F32), up[rows, columns].astype(F32), one[rows]
            sig = jax.nn.sigmoid(g)
            d = d * sig
            gate[rows, columns] = (d * u * (1.0 + g * (1.0 - sig))).astype(BF16)
            up[rows, columns] = (d * g).astype(BF16)

        chain.step(3 * j + 2)

    def send(start):
        @pl.loop(0, tiles)
        def _(j):
            for source, target, k in ((own_out, other_out, 0), (other_out, own_out, 1)):
                held = tile_at(gate if k == 0 else up, j)

                @pl.when(first)
                def _():
                    copy = pltpu.make_async_copy(held, tile_at(source, j), out_sems.at[k, j])
                    copy.start() if start else copy.wait()

                @pl.when(jnp.logical_not(first))
                def _():
                    copy = pltpu.make_async_copy(held, tile_at(target, j), out_sems.at[k, j])
                    copy.start() if start else copy.wait()

    send(True)

    @pl.loop(0, outs)
    def _(n):
        copy_either(first, rows_at(w_own, n), rows_at(w_other, n), rows_at(gate_w, n), w_sems.at[0, n], False)
        one[...] = mm_t(gate[...], rows_at(gate_w, n)[...])
        chain.step(3 * tiles + 4 * n)
        chain.step(3 * tiles + 4 * n + 1)
        copy_either(first, rows_at(w_other, n), rows_at(w_own, n), rows_at(up_w, n), w_sems.at[1, n], False)
        tile_at(result, n)[...] = (one[...] + mm_t(up[...], rows_at(up_w, n)[...])).astype(BF16)
        chain.step(3 * tiles + 4 * n + 2)
        chain.step(3 * tiles + 4 * n + 3)

    chain.finish(3 * tiles + 4 * outs)
    send(False)


def ffn_backward(grad, gate, up, weights, part):
    rows, width = grad.shape
    ff = weights[0].shape[1]
    tiles = max(ff, width) // TILE
    narrow, wide = jax.ShapeDtypeStruct((rows, width), BF16), jax.ShapeDtypeStruct((rows, ff), BF16)
    return pl.pallas_call(
        ffn_backward_kernel,
        out_shape=[wide, wide, narrow, narrow],
        in_specs=[VMEM] * 2 + [ANY] * 5,
        out_specs=[ANY] * 2 + [VMEM] * 2,
        scratch_shapes=[pltpu.VMEM((width, ff), BF16)] * 3
        + [pltpu.VMEM((rows, ff), BF16)] * 2
        + [pltpu.VMEM((rows, TILE), F32)]
        + [pltpu.SemaphoreType.DMA((3, tiles))] * 3
        + chain_scratch((rows, width)),
        compiler_params=params(2),
        cost_estimate=cost(),
    )(grad, part, gate, up, *weights)


def roped(values, cosine, sine):
    return values * cosine + pltpu.roll(values, HEAD // 2, 1) * sine


def unroped(grads, cosine, sine):
    return grads * cosine + pltpu.roll(grads * sine, HEAD // 2, 1)


def mm_0(left, right):
    return lax.dot_general(left, right, (((0,), (0,)), ((), ())), preferred_element_type=F32)


def greet_ctx(count):
    me = lax.axis_index("ctx")
    barrier = pltpu.get_barrier_semaphore()
    for step in range(1, count):
        pl.semaphore_signal(barrier, inc=1, device_id={"ctx": lax.rem(me + step, count)}, device_id_type=MESH)


def allowed_keys(seg_rows, seg_keys, i, block):
    rows, keys = seg_rows.shape[0], seg_keys.shape[1]
    first_row = lax.axis_index("ctx") * rows + i * block
    row_at = first_row + lax.broadcasted_iota(jnp.int32, (block, keys), 0)
    key_at = lax.broadcasted_iota(jnp.int32, (block, keys), 1)
    own = seg_rows[pl.ds(pl.multiple_of(i * block, block), block)]
    return (key_at <= row_at) & (own == seg_keys[...])


def attention_forward_kernel(chained, heads, *refs):
    layer_in, gain, w_lin, w_out, bias, cosine, sine, seg_rows, seg_keys = refs[:9]
    refs = refs[9:]
    if chained:
        part, refs = refs[0], refs[1:]
    normed, query, kv, lse, attended, result = refs[:6]
    refs = refs[6:]
    if chained:
        total, refs = refs[0], refs[1:]
    kv_sems, refs = refs[0], refs[1:]
    rows, q_cols = query.shape
    count = kv.shape[0] // rows
    me = lax.axis_index("ctx")
    block = min(256, rows)

    greet_ctx(count)
    if chained:
        chain = Chain(part, total, *refs)
        chain.greet(count - 1)
        chain.start()
    else:
        pl.semaphore_wait(pltpu.get_barrier_semaphore(), count - 1)

    def step(first, last):
        if chained:
            for c in range(first, last):
                chain.step(c)

    normalize_rows(lambda r: layer_in[r].astype(F32), gain, normed)
    mine = kv.at[pl.ds(pl.multiple_of(me * rows, rows), rows)]
    step(0, 1)
    lin = mm(normed[...], w_lin[...]) + bias[...]
    mine[:, :HEAD] = roped(lin[:, q_cols : q_cols + HEAD], cosine[...], sine[...]).astype(BF16)
    mine[:, HEAD:] = lin[:, q_cols + HEAD :].astype(BF16)

    def passing(offset):
        return pltpu.make_async_remote_copy(
            src_ref=mine,
            dst_ref=mine,
            send_sem=kv_sems.at[0, offset],
            recv_sem=kv_sems.at[1, offset],
            device_id={"ctx": lax.rem(me + offset, count)},
            device_id_type=MESH,
        )

    for offset in range(1, count):
        passing(offset).start()
    step(1, 3)
    for h in range(heads):
        columns = slice(h * HEAD, (h + 1) * HEAD)
        query[:, columns] = roped(lin[:, columns], cosine[...], sine[...]).astype(BF16)
    step(3, 4)
    for offset in range(1, count):
        passing(offset).wait_recv()

    @pl.loop(0, rows // block)
    def _(i):
        at = pl.ds(pl.multiple_of(i * block, block), block)
        allowed = allowed_keys(seg_rows, seg_keys, i, block)
        lane = lax.broadcasted_iota(jnp.int32, (block, HEAD), 1)
        logs = jnp.zeros((block, HEAD), F32)
        for h in range(heads):
            columns = slice(h * HEAD, (h + 1) * HEAD)
            scores = jnp.where(allowed, mm_t(query[at, columns], kv[:, :HEAD]) * SCALE, NEG)
            top = jnp.max(scores, axis=-1, keepdims=True)
            probs = jnp.exp(scores - top)
            sums = jnp.sum(probs, axis=-1, keepdims=True)
            probs = (probs * (1.0 / sums)).astype(BF16)
            attended[at, columns] = mm(probs, kv[:, HEAD:]).astype(BF16)
            logs = jnp.where(lane == h, top + jnp.log(sums), logs)
            if chained:
                chain.step(4 + heads * i + h)
        lse[at] = logs

    base = 4 + heads * (rows // block)

    @pl.loop(0, result.shape[1] // TILE)
    def _(n):
        tile_at(result, n)[...] = mm_t(attended[...], rows_at(w_out, n)[...]).astype(BF16)
        if chained:
            chain.step(base + 3 * n)
            chain.step(base + 3 * n + 1)
            chain.step(base + 3 * n + 2)

    for offset in range(1, count):
        passing(offset).wait_send()
    if chained:
        chain.finish(base + 3 * (result.shape[1] // TILE))


def attention_forward(layer_in, weights, tables, segs, part=None):
    w_lin, w_out, gains, bias = weights
    rows, width = layer_in.shape
    q_cols = w_out.shape[1]
    keys = segs[1].shape[1]
    count = keys // rows
    chained = part is not None
    narrow = jax.ShapeDtypeStruct((rows, width), BF16)
    heads_out = jax.ShapeDtypeStruct((rows, q_cols), BF16)
    kv_out = jax.ShapeDtypeStruct((keys, 2 * HEAD), BF16)
    lse_out = jax.ShapeDtypeStruct((rows, HEAD), F32)
    outs = [narrow, heads_out, kv_out, lse_out, heads_out, narrow] + [narrow] * chained
    args = (layer_in, gains[:1], w_lin, w_out, bias, *tables, *segs) + ((part,) if chained else ())
    return pl.pallas_call(
        functools.partial(attention_forward_kernel, chained, q_cols // HEAD),
        out_shape=outs,
        in_specs=[VMEM] * len(args),
        out_specs=[VMEM] * len(outs),
        scratch_shapes=[pltpu.SemaphoreType.DMA((2, count))] + (chain_scratch((rows, width)) if chained else []),
        compiler_params=params(3 + chained),
        cost_estimate=cost(),
    )(*args)


def attention_backward_kernel(
    upstream, sum_in, layer_in, attn_out, gain, w_lin, w_out, query, kv, lse, attended,
    cosine, sine, seg_rows, seg_keys, part,
    middle_grad, attn_grad, lin, gain_grad, result, total,
    heads_grad, kv_grad, sent, got, kv_sems, *chain_refs,
):
    rows, q_cols = query.shape
    heads = q_cols // HEAD
    count = kv.shape[0] // rows
    me = lax.axis_index("ctx")
    block = min(256, rows)
    greet_ctx(count)
    chain = Chain(part, total, *chain_refs)
    chain.greet(count - 1)
    chain.start()
    gain_grad[...] = jnp.zeros_like(gain_grad)
    kv_grad[...] = jnp.zeros_like(kv_grad)

    @pl.loop(0, rows // 64)
    def _(i):
        at = pl.ds(pl.multiple_of(i * 64, 64), 64)
        middle = layer_in[at].astype(F32) + attn_out[at].astype(F32)
        factor = lax.rsqrt(jnp.mean(middle * middle, axis=-1, keepdims=True) + EPS)
        unit = middle * factor
        grad = sum_in[at].astype(F32)
        per_row = grad * unit
        weighted = grad * gain[...]
        mean = jnp.mean(per_row * gain[...], axis=-1, keepdims=True)
        out = upstream[at].astype(F32) + factor * (weighted - unit * mean)
        middle_grad[at] = out
        attn_grad[at] = out.astype(BF16)
        gain_grad[...] += jnp.sum(per_row.reshape(8, 8, per_row.shape[1]), axis=0)

    chain.step(0)
    chain.step(1)
    heads_grad[...] = mm(attn_grad[...], w_out[...]).astype(BF16)
    chain.step(2)
    chain.step(3)

    @pl.loop(0, rows // block)
    def _(i):
        at = pl.ds(pl.multiple_of(i * block, block), block)
        allowed = allowed_keys(seg_rows, seg_keys, i, block)
        for h in range(heads):
            columns = slice(h * HEAD, (h + 1) * HEAD)
            scores = mm_t(query[at, columns], kv[:, :HEAD]) * SCALE - lse[at, h : h + 1]
            probs = jnp.exp(jnp.where(allowed, scores, NEG))
            grad = heads_grad[at, columns]
            row_sum = jnp.sum(attended[at, columns].astype(F32) * grad.astype(F32), axis=-1, keepdims=True)
            score_grad = (probs * (mm_t(grad, kv[:, HEAD:]) - row_sum)).astype(BF16)
            q_grad = mm(score_grad, kv[:, :HEAD]) * SCALE
            lin[at, columns] = unroped(q_grad, cosine[at], sine[at]).astype(BF16)
            kv_grad[:, :HEAD] += mm_0(score_grad, query[at, columns])
            kv_grad[:, HEAD:] += mm_0(probs.astype(BF16), grad)
            chain.step(4 + heads * i + h)

    def passing(offset):
        return pltpu.make_async_remote_copy(
            src_ref=sent.at[offset - 1],
            dst_ref=got.at[offset - 1],
            send_sem=kv_sems.at[0, offset],
            recv_sem=kv_sems.at[1, offset],
            device_id={"ctx": lax.rem(me + offset, count)},
            device_id_type=MESH,
        )

    for offset in range(1, count):
        peer = pl.ds(pl.multiple_of(lax.rem(me + offset, count) * rows, rows), rows)
        sent[offset - 1, :, :HEAD] = (kv_grad[peer, :HEAD] * SCALE).astype(BF16)
        sent[offset - 1, :, HEAD:] = kv_grad[peer, HEAD:].astype(BF16)
        passing(offset).start()
    mine = pl.ds(pl.multiple_of(me * rows, rows), rows)
    k_grad, v_grad = kv_grad[mine, :HEAD] * SCALE, kv_grad[mine, HEAD:]
    for offset in range(1, count):
        passing(offset).wait_recv()
        k_grad = k_grad + got[offset - 1, :, :HEAD].astype(F32)
        v_grad = v_grad + got[offset - 1, :, HEAD:].astype(F32)
    lin[:, q_cols : q_cols + HEAD] = unroped(k_grad, cosine[...], sine[...]).astype(BF16)
    lin[:, q_cols + HEAD :] = v_grad.astype(BF16)
    base = 4 + heads * (rows // block)

    @pl.loop(0, result.shape[1] // TILE)
    def _(n):
        tile_at(result, n)[...] = mm_t(lin[...], rows_at(w_lin, n)[...]).astype(BF16)
        chain.step(base + 2 * n)
        chain.step(base + 2 * n + 1)

    for offset in range(1, count):
        passing(offset).wait_send()
    chain.finish(base + 2 * (result.shape[1] // TILE))


def attention_backward(upstream, sum_in, kept, weights, tables, segs, part):
    w_lin, w_out, gains, bias = weights
    rows, width = upstream.shape
    q_cols = w_out.shape[1]
    keys = segs[1].shape[1]
    count = keys // rows
    narrow = jax.ShapeDtypeStruct((rows, width), BF16)
    outs = [
        jax.ShapeDtypeStruct((rows, width), F32),
        narrow,
        jax.ShapeDtypeStruct((rows, q_cols + 2 * HEAD), BF16),
        jax.ShapeDtypeStruct((8, width), F32),
        narrow,
        narrow,
    ]
    args = (upstream, sum_in, kept["layer_in"], kept["attn_out"], gains[1:], w_lin, w_out)
    args += (kept["query"], kept["kv"], kept["lse"], kept["attended"], *tables, *segs, part)
    return pl.pallas_call(
        attention_backward_kernel,
        out_shape=outs,
        in_specs=[VMEM] * len(args),
        out_specs=[VMEM] * len(outs),
        scratch_shapes=[
            pltpu.VMEM((rows, q_cols), BF16),
            pltpu.VMEM((keys, 2 * HEAD), F32),
            pltpu.VMEM((max(count - 1, 1), rows, 2 * HEAD), BF16),
            pltpu.VMEM((max(count - 1, 1), rows, 2 * HEAD), BF16),
            pltpu.SemaphoreType.DMA((2, count)),
        ]
        + chain_scratch((rows, width)),
        compiler_params=params(5),
        cost_estimate=cost(),
    )(*args)


def rope_tables(places):
    steps = jnp.arange(HEAD // 2, dtype=F32) * (2.0 / HEAD)
    inverse = ROPE_BASE ** (-steps)
    angles = places.astype(F32)[..., None] * inverse
    angles = jnp.concatenate([angles, angles], axis=-1)
    return (jnp.cos(angles), jnp.sin(angles))


def norm_back(grad_out, rows_in, factor, gain):
    unit = rows_in * factor
    gain_grad = jnp.sum(grad_out * unit, axis=0)
    weighted = grad_out * gain
    return (
        factor * (weighted - unit * jnp.mean(weighted * unit, axis=-1, keepdims=True)),
        gain_grad,
    )


def over_ctx(value):
    if lax.axis_size("ctx") == 2:
        other = lax.ppermute(value, "ctx", [(0, 1), (1, 0)])
        low = lax.axis_index("ctx") == 0
        return jnp.concatenate([jnp.where(low, value, other), jnp.where(low, other, value)], axis=-1)
    return lax.all_gather(value, "ctx", axis=value.ndim - 1, tiled=True)


def input_backward(normed_one_grad, middle_grad, kept, gains):
    layer_in = kept["layer_in"].astype(F32)
    factor = lax.rsqrt(jnp.mean(layer_in * layer_in, axis=-1, keepdims=True) + EPS)
    norm_grad, gain_one = norm_back(normed_one_grad.astype(F32), layer_in, factor, gains[0])
    return (middle_grad + norm_grad).astype(BF16), gain_one


def local(
    section_in,
    segments,
    positions,
    query_weight,
    kv_weight,
    output_weight,
    gate_up,
    down_weight,
    norm_gains,
    query_bias,
    kv_bias,
    out_grad,
):
    sec = lax.axis_index("section")
    first = sec == 0
    group = HEADS // KV_HEADS
    heads_here = HEADS // lax.axis_size("tp")
    head_pick = lax.axis_index("tp") * heads_here // group
    shards = lax.axis_size("dp") * lax.axis_size("ctx")
    ranks = ("dp", "ctx")
    seqs, span, width = section_in.shape[1:]
    shard = query_weight.shape[1]
    q_cols = query_weight.shape[2]
    ff = gate_up.shape[3]

    def per_layer(mine, theirs):
        return jnp.where(first, mine, theirs), jnp.where(first, theirs, mine)

    half = shard // 2
    kv_width = KV_HEADS * HEAD

    def halves(rows):
        mine = lax.dynamic_slice_in_dim(rows, sec * half, half, 0)
        return per_layer(mine, swap(lax.dynamic_slice_in_dim(rows, (1 - sec) * half, half, 0)))

    def joined(own):
        return jnp.stack(per_layer(own, swap(own)), axis=1).reshape(width, own.shape[-1])

    def after(value, event):
        return lax.optimization_barrier((value, event))[0]

    piece = HEAD // shards
    biases = jnp.concatenate([query_bias[0].reshape(-1), kv_bias[0].reshape(-1)])
    n_biases = biases.shape[0]
    biases = jnp.pad(biases, (0, -n_biases % shard)).reshape(-1, shard).T
    extra = jnp.concatenate([norm_gains[0].T, biases], axis=1)
    n_extra = extra.shape[1]
    extra = jnp.pad(extra, ((0, 0), (0, HEAD - n_extra)))
    packed = jnp.concatenate([query_weight[0], kv_weight[0, 0], kv_weight[0, 1], output_weight[0].T, extra], axis=1)
    packed_shards = halves(packed)
    spare = -ff % TILE
    wide = jnp.pad(gate_up[0], ((0, 0), (0, 0), (0, spare)))
    mine = lax.dynamic_index_in_dim(wide, sec, 0, keepdims=False)
    theirs = swap(lax.dynamic_index_in_dim(wide, 1 - sec, 0, keepdims=False))
    gate_up_shards = per_layer(mine, theirs)
    down_shards = halves(jnp.pad(down_weight[0].T, ((0, 0), (0, spare))))

    micro = sec
    seg = lax.dynamic_index_in_dim(segments, micro, 0, keepdims=False)
    pos = lax.dynamic_index_in_dim(positions, micro, 0, keepdims=False)
    hidden = lax.dynamic_index_in_dim(section_in, micro, 0, keepdims=False)
    seg_keys = over_ctx(seg)
    segs, tables = [], []
    for q in range(seqs):
        segs.append((seg[q][:, None], seg_keys[q][None]))
        cosine, sine = rope_tables(pos[q])
        tables.append((cosine, jnp.where(jnp.arange(HEAD) < HEAD // 2, -sine, sine)))
    hidden = [hidden[0], hidden[1]]

    packed_low = lax.all_gather(packed_shards[0], ranks, axis=0)
    packed_low, gate_up_shards, down_shards, packed_shards, segs, tables, hidden = lax.optimization_barrier(
        (packed_low, gate_up_shards, down_shards, packed_shards, segs, tables, hidden)
    )
    own_low = lax.all_gather(gate_up_shards[0], ranks, axis=0, tiled=True)

    def attention_weights(own):
        p = joined(own)
        wq = p[:, :q_cols]
        wk = lax.dynamic_slice_in_dim(p[:, q_cols : q_cols + kv_width], head_pick * HEAD, HEAD, 1)
        wv = lax.dynamic_slice_in_dim(p[:, q_cols + kv_width : q_cols + 2 * kv_width], head_pick * HEAD, HEAD, 1)
        wo = p[:, q_cols + 2 * kv_width : 2 * q_cols + 2 * kv_width]
        s = p[:, 2 * q_cols + 2 * kv_width :]
        gains = s[:, :2].T
        s = s[:, 2:n_extra].T.reshape(-1, shards, shard).transpose(1, 0, 2).reshape(shards, -1)[:, :n_biases]
        q_b = s[:, : heads_here * piece].reshape(shards, heads_here, piece).transpose(1, 0, 2).reshape(heads_here, HEAD)
        kv_b = s[:, heads_here * piece :].reshape(shards, 2, KV_HEADS, piece)
        kv_b = kv_b.transpose(1, 2, 0, 3).reshape(2, KV_HEADS, HEAD)
        kv_b = lax.dynamic_slice_in_dim(kv_b, head_pick, 1, 1)
        bias = jnp.concatenate([q_b.reshape(1, -1), kv_b.reshape(1, -1)], axis=1).astype(F32)
        return jnp.concatenate([wq, wk, wv], axis=1), wo, gains.astype(F32), bias

    def ffn_shared(own, down_own, event):
        own, down_own, event = lax.optimization_barrier((own, down_own, event))
        return (own, swap(own), joined(down_own)), event

    kept = [[dict(), dict()] for _ in range(2)]
    names = ("normed", "query", "kv", "lse", "attended")
    layer_in = list(hidden)
    outs = []
    ffn_weights = [None, None]
    attn_weights = [attention_weights(packed_low), None]
    for layer in range(2):
        weights, k = attn_weights[layer], kept[layer]
        gain = weights[2][1:]
        k[0]["layer_in"] = layer_in[0]
        if layer == 0:
            *more, part_a = attention_forward(layer_in[0], weights, tables[0], segs[0])
            down_low = lax.all_gather(after(down_shards[0], part_a), ranks, axis=0)
        else:
            *more, part_a, ffn_b = attention_forward(layer_in[0], weights, tables[0], segs[0], part_b)
            layer_in[1] = (layer_in[1].astype(F32) + kept[0][1]["attn_out"].astype(F32) + ffn_b.astype(F32)).astype(BF16)
            outs.append(jnp.stack(layer_in))
            part_a, own_high = lax.optimization_barrier((part_a, own_high))
            other_high = swap(own_high)
        k[0].update(zip(names, more))
        k[1]["layer_in"] = layer_in[1]
        *more, part_b, attn_a = attention_forward(layer_in[1], weights, tables[1], segs[1], part_a)
        k[1].update(zip(names, more))
        if layer == 0:
            part_b, own_low = lax.optimization_barrier((part_b, own_low))
            packed_high = lax.all_gather(after(packed_shards[1], part_b), ranks, axis=0)
            attn_b = tp_sum(part_b)
            ffn_weights[0], attn_b = ffn_shared(own_low, down_low, attn_b)
            own_high = lax.all_gather(after(gate_up_shards[1], attn_b), ranks, axis=0, tiled=True)
            normed_a, gate, up, inner, part_a = ffn_forward(layer_in[0], attn_a, gain, ffn_weights[0])
            down_high = lax.all_gather(after(down_shards[1], part_a), ranks, axis=0)
        else:
            part_b, down_high = lax.optimization_barrier((part_b, down_high))
            ffn_weights[1] = own_high, other_high, joined(down_high)
            normed_a, gate, up, inner, part_a, attn_b = ffn_forward(layer_in[0], attn_a, gain, ffn_weights[1], part_b)
        k[0].update(attn_out=attn_a, normed_two=normed_a, gate=gate, up=up, inner=inner)
        normed_b, gate, up, inner, part_b, ffn_a = ffn_forward(layer_in[1], attn_b, gain, ffn_weights[layer], part_a)
        k[1].update(attn_out=attn_b, normed_two=normed_b, gate=gate, up=up, inner=inner)
        layer_a = (layer_in[0].astype(F32) + attn_a.astype(F32) + ffn_a.astype(F32)).astype(BF16)
        if layer == 0:
            packed_high, layer_a = lax.optimization_barrier((packed_high, layer_a))
            attn_weights[1] = attention_weights(packed_high)
        layer_in = [layer_a, layer_in[1]]
    grad_top = lax.dynamic_index_in_dim(out_grad, micro, 0, keepdims=False)
    upstream = [grad_top[0], grad_top[1]]
    k = kept[1]
    own_a, other_a, grad_a, ffn_b = ffn_backward(upstream[0], k[0]["gate"], k[0]["up"], ffn_weights[1], part_b)
    layer_in[1] = (layer_in[1].astype(F32) + k[1]["attn_out"].astype(F32) + ffn_b.astype(F32)).astype(BF16)
    outs.append(jnp.stack(layer_in))

    def to_section(values):
        low = lax.ppermute(values[0], "section", [(1, 0)])
        high = lax.ppermute(values[1], "section", [(0, 1)])
        return jnp.stack([jnp.where(first, values[0], high), jnp.where(first, low, values[1])])

    section_out = to_section(outs)

    in_grads = [None, None]
    gate_up_grads, down_grads, packed_grads, gains_grads = [[None, None] for _ in range(4)]
    waiting = None
    for layer in (1, 0):
        weights, k = attn_weights[layer], kept[layer]
        if layer == 0:
            own_a, other_a, grad_a, sum_b = ffn_backward(upstream[0], k[0]["gate"], k[0]["up"], ffn_weights[0], parts[1])
            upstream[1], gain_b = input_backward(sum_b, middle_grads[1], kept[1][1], attn_weights[1][2])
            grad_a, down_grads[1] = lax.optimization_barrier((grad_a, down_grads[1]))
            waiting(upstream, gain_a + gain_b)
        own_b, other_b, grad_b, sum_a = ffn_backward(upstream[1], k[1]["gate"], k[1]["up"], ffn_weights[layer], grad_a)
        own_grads, other_grads = (own_a, own_b), (other_a, other_b)
        normed_two = jnp.concatenate([k[q]["normed_two"] for q in range(seqs)])
        own_w = dot("rd,rf->df", normed_two, jnp.concatenate(own_grads)).astype(BF16)
        other_w = dot("rd,rf->df", normed_two, jnp.concatenate(other_grads)).astype(BF16)
        own_w = (own_w.astype(F32) + swap(other_w).astype(F32)).astype(BF16)
        own_w, sum_a = lax.optimization_barrier((own_w, sum_a))
        gate_up_grads[layer] = lax.psum_scatter(own_w, ranks, scatter_dimension=0, tiled=True)
        down_w = dot("rd,rf->df", jnp.concatenate(upstream), jnp.concatenate([k[q]["inner"] for q in range(seqs)])).astype(BF16)
        down_w = down_w.reshape(shards, 2, half, ff + spare)
        down_own = lax.dynamic_index_in_dim(down_w, sec, 1, keepdims=False)
        down_other = lax.dynamic_index_in_dim(down_w, 1 - sec, 1, keepdims=False)
        down_own = (down_own.astype(F32) + swap(down_other).astype(F32)).astype(BF16)
        down_own, sum_a = lax.optimization_barrier((down_own, sum_a))
        down_grads[layer] = lax.psum_scatter(
            down_own.reshape(shards * half, ff + spare), ranks, scatter_dimension=0, tiled=True
        )

        first_a = attention_backward(upstream[0], sum_a, k[0], weights, tables[0], segs[0], grad_b)
        first_b = attention_backward(upstream[1], first_a[-1], k[1], weights, tables[1], segs[1], first_a[-2])
        middle_grads, attn_grads, lin_grads, gains_two, parts, sums = zip(first_a, first_b)
        gains_two = [jnp.sum(g, axis=0) for g in gains_two]
        sum_a, sum_b = sums[1], None
        lin_grad = jnp.concatenate(lin_grads)
        normed_one = jnp.concatenate([k[q]["normed"] for q in range(seqs)])
        lin_w = dot("rd,re->de", normed_one, lin_grad)
        attended = jnp.concatenate([k[q]["attended"] for q in range(seqs)])
        out_w = dot("rd,re->de", jnp.concatenate(attn_grads), attended)
        bias = jnp.sum(lin_grad.astype(F32), axis=0)
        bias = bias.reshape(heads_here + 2, shards, piece).transpose(1, 0, 2).reshape(shards, (heads_here + 2) * piece)
        bias = jnp.pad(bias, ((0, 0), (0, -bias.shape[1] % shard)))
        bias = bias.reshape(shards, -1, shard).transpose(0, 2, 1).reshape(width, -1)
        bias = jnp.pad(bias, ((0, 0), (0, HEAD - bias.shape[1])))
        packed_grads[layer] = jnp.concatenate([lin_w, out_w, bias], axis=1).astype(BF16)

        def finish(upstream, gain_one, layer=layer, gains_two=gains_two):
            in_grads[layer] = jnp.stack(upstream)
            gains_grads[layer] = jnp.stack([gain_one, sum(gains_two)])

        waiting = finish
        upstream = [None, None]
        upstream[0], gain_a = input_backward(sum_a, middle_grads[0], k[0], weights[2])
        if layer == 1:
            upstream[0], gate_up_grads[1] = lax.optimization_barrier((upstream[0], gate_up_grads[1]))
    low = lax.ppermute(packed_grads[0], "section", [(1, 0)])
    high = lax.ppermute(packed_grads[1], "section", [(0, 1)])
    packed_total = jnp.where(
        first, packed_grads[0].astype(F32) + low.astype(F32), packed_grads[1].astype(F32) + high.astype(F32)
    ).astype(BF16)
    last_part, gate_up_grads[0], packed_total = lax.optimization_barrier((parts[1], gate_up_grads[0], packed_total))
    packed_total = lax.psum_scatter(packed_total, ranks, scatter_dimension=0, tiled=True).astype(F32)
    sum_b, down_grads[0] = lax.optimization_barrier((tp_sum(last_part), down_grads[0]))
    upstream[1], gain_b = input_backward(sum_b, middle_grads[1], kept[0][1], attn_weights[0][2])
    waiting(upstream, gain_a + gain_b)
    input_grad = to_section(in_grads)
    low = lax.ppermute(gains_grads[0], "section", [(1, 0)])
    high = lax.ppermute(gains_grads[1], "section", [(0, 1)])
    gains_grad = jnp.where(first, gains_grads[0] + low, gains_grads[1] + high)
    for axis in ranks:
        if lax.axis_size(axis) == 2:
            gains_grad = gains_grad + lax.ppermute(gains_grad, axis, [(0, 1), (1, 0)])
        else:
            gains_grad = lax.psum(gains_grad, axis)
    at = (lax.axis_index("dp") * lax.axis_size("ctx") + lax.axis_index("ctx")) * shard
    gains_grad = lax.dynamic_slice_in_dim(gains_grad, at, shard, 1)
    q_grad = packed_total[:, :q_cols]
    kv_narrow = packed_total[:, q_cols : q_cols + 2 * HEAD].reshape(shard, 2, HEAD)
    o_grad = packed_total[:, q_cols + 2 * HEAD : 2 * q_cols + 2 * HEAD].T
    extra = packed_total[:, 2 * q_cols + 2 * HEAD :]
    bias_cols = -(-(heads_here + 2) * piece // shard)
    bias = extra[:, :bias_cols].T.reshape(-1)[: (heads_here + 2) * piece].reshape(heads_here + 2, piece)
    q_bias_grad = bias[:heads_here]
    kv_full = jnp.zeros((shard, 2, KV_HEADS, HEAD), F32)
    kv_full = lax.dynamic_update_slice_in_dim(kv_full, kv_narrow[:, :, None], head_pick, 2)
    bias_full = jnp.zeros((2, KV_HEADS, piece), F32)
    bias_full = lax.dynamic_update_slice_in_dim(bias_full, bias[heads_here:, None], head_pick, 1)
    flat = bias_full.reshape(-1)
    flat = jnp.pad(flat, (0, -flat.shape[0] % (2 * KV_HEADS * HEAD)))
    flat_rows = flat.shape[0] // (2 * KV_HEADS * HEAD)
    joined = jnp.concatenate([kv_full.reshape(shard, -1), flat.reshape(flat_rows, -1)]).astype(BF16)
    joined = chain_sum(joined).astype(F32)
    kv_grad = joined[:shard].reshape(shard, 2, KV_HEADS * HEAD).transpose(1, 0, 2)
    kv_bias_grad = joined[shard:].reshape(-1)[: 2 * KV_HEADS * piece].reshape(2, KV_HEADS, piece)

    def collect(values):
        kept_half = jnp.where(first, values[0], values[1])
        other = swap(jnp.where(first, values[1], values[0]))
        return jnp.where(first, kept_half, other), jnp.where(first, other, kept_half)

    gate_up_grad = jnp.stack(collect(gate_up_grads))[..., :ff].astype(F32)
    down_grad = jnp.concatenate(collect(down_grads), axis=0)[:, :ff].T.astype(F32)
    return (
        section_out[None],
        input_grad[None],
        q_grad[None],
        kv_grad[None],
        o_grad[None],
        gate_up_grad[None],
        down_grad[None],
        gains_grad[None],
        q_bias_grad[None],
        kv_bias_grad[None],
    )


def solution(mesh):
    in_specs = (
        P(None, "dp", "ctx", None),
        P(None, "dp", "ctx"),
        P(None, "dp", "ctx"),
        P("section", ("dp", "ctx"), "tp"),
        P("section", None, ("dp", "ctx"), None),
        P("section", "tp", ("dp", "ctx")),
        P("section", None, ("dp", "ctx"), "tp"),
        P("section", "tp", ("dp", "ctx")),
        P("section", None, ("dp", "ctx")),
        P("section", "tp", ("dp", "ctx")),
        P("section", None, None, ("dp", "ctx")),
        P(None, "dp", "ctx", None),
    )
    out_specs = (
        P("section", None, "dp", "ctx", None),
        P("section", None, "dp", "ctx", None),
        P("section", ("dp", "ctx"), "tp"),
        P("section", None, ("dp", "ctx"), None),
        P("section", "tp", ("dp", "ctx")),
        P("section", None, ("dp", "ctx"), "tp"),
        P("section", "tp", ("dp", "ctx")),
        P("section", None, ("dp", "ctx")),
        P("section", "tp", ("dp", "ctx")),
        P("section", None, None, ("dp", "ctx")),
    )
    return jax.shard_map(local, mesh=mesh, in_specs=in_specs, out_specs=out_specs, check_vma=False)
```

```python
import functools

import jax
import jax.numpy as jnp
from jax import lax
from jax.experimental import pallas as pl
from jax.experimental.pallas import tpu as pltpu
from jax.sharding import PartitionSpec as P

HEADS = 12
KV_HEADS = 2
HEAD = 128

EPS = 1e-06
ROPE_BASE = 1000000.0
NEG = -1e30
SCALE = HEAD ** (-0.5)
TILE = 768
VMEM_LIMIT = 60 << 20
MESH = pl.DeviceIdType.MESH

F32 = jnp.float32
BF16 = jnp.bfloat16


def dot(form, left, right):
    return jnp.einsum(form, left, right, preferred_element_type=F32)


def swap(value):
    return lax.ppermute(value, "section", [(0, 1), (1, 0)])


def chain_sum(part):
    count = lax.axis_size("tp")
    place = lax.axis_index("tp")
    middle = count // 2
    total = part
    for hop in range(middle - 1):
        got = lax.ppermute(total, "tp", [(hop, hop + 1), (count - 1 - hop, count - 2 - hop)])
        total = (total.astype(F32) + got.astype(F32)).astype(BF16)
    got = lax.ppermute(total, "tp", [(middle - 1, middle), (middle, middle - 1)])
    total = (total.astype(F32) + got.astype(F32)).astype(BF16)
    for hop in range(middle - 1):
        low, high = middle - 1 - hop, middle + hop
        got = lax.ppermute(total, "tp", [(low, low - 1), (high, high + 1)])
        total = jnp.where((place == low - 1) | (place == high + 1), got, total)
    return total


class Chain:
    def __init__(self, part, total, from_end, from_peer, sems):
        self.part, self.total = part, total
        self.from_end, self.from_peer = from_end, from_peer
        self.sems = sems
        self.chunks = sems.shape[1]
        self.rows = part.shape[0] // self.chunks
        self.is_middle, self.inner, self.outer = line_places()

    def at(self, ref, c):
        return ref.at[pl.ds(pl.multiple_of(c * self.rows, self.rows), self.rows)]

    def copy(self, source, target, c, step, place):
        return pltpu.make_async_remote_copy(
            src_ref=self.at(source, c),
            dst_ref=self.at(target, c),
            send_sem=self.sems.at[2 * step, c],
            recv_sem=self.sems.at[2 * step + 1, c],
            device_id={"tp": place},
            device_id_type=MESH,
        )

    def inward(self, c):
        return self.copy(self.part, self.from_end, c, 0, self.inner)

    def across(self, c):
        return self.copy(self.total, self.from_peer, c, 1, self.inner)

    def outward(self, c):
        return self.copy(self.total, self.total, c, 2, self.outer)

    def start(self):
        @pl.when(jnp.logical_not(self.is_middle))
        def _():
            @pl.loop(0, self.chunks)
            def _(c):
                self.inward(c).start()

    def join(self, c):
        self.inward(c).wait_recv()
        self.at(self.total, c)[...] = self.at(self.part, c)[...] + self.at(self.from_end, c)[...]
        self.across(c).start()

    def close(self, c):
        self.across(c).wait()
        self.at(self.total, c)[...] = self.at(self.total, c)[...] + self.at(self.from_peer, c)[...]
        self.outward(c).start()

    def step(self, c):
        @pl.when(self.is_middle & (c < self.chunks))
        def _():
            self.join(c)

            @pl.when(c > 0)
            def _():
                self.close(c - 1)

    def finish(self, done):
        @pl.when(self.is_middle)
        def _():
            if done < self.chunks:

                @pl.loop(done, self.chunks)
                def _(c):
                    self.step(c)

            self.close(self.chunks - 1)

            @pl.loop(0, self.chunks)
            def _(c):
                self.outward(c).wait_send()

        @pl.when(jnp.logical_not(self.is_middle))
        def _():
            @pl.loop(0, self.chunks)
            def _(c):
                self.inward(c).wait_send()
                self.outward(c).wait_recv()


def line_places():
    place = lax.axis_index("tp")
    is_middle = (place == 1) | (place == 2)
    return is_middle, jnp.where(place < 2, place + 1, place - 1), jnp.where(place < 2, place - 1, place + 1)


def greet(ctx_count=1):
    is_middle, inner, outer = line_places()
    me = lax.axis_index("ctx")
    barrier = pltpu.get_barrier_semaphore()
    for step in range(1, ctx_count):
        pl.semaphore_signal(barrier, inc=1, device_id={"ctx": lax.rem(me + step, ctx_count)}, device_id_type=MESH)
    pl.semaphore_signal(barrier, inc=1, device_id={"tp": inner}, device_id_type=MESH)

    @pl.when(is_middle)
    def _():
        pl.semaphore_signal(barrier, inc=1, device_id={"tp": outer}, device_id_type=MESH)
        pl.semaphore_wait(barrier, 1 + ctx_count)

    @pl.when(jnp.logical_not(is_middle))
    def _():
        pl.semaphore_wait(barrier, ctx_count)


def chain_scratch(shape):
    return [pltpu.VMEM(shape, BF16)] * 2 + [pltpu.SemaphoreType.DMA((6, min(8, shape[0] // 16)))]


CHAIN_REFS = 3
VMEM = pl.BlockSpec(memory_space=pltpu.VMEM)
ANY = pl.BlockSpec(memory_space=pl.ANY)


def params(collective_id):
    return pltpu.CompilerParams(collective_id=collective_id, has_side_effects=True, vmem_limit_bytes=VMEM_LIMIT)


def cost():
    return pl.CostEstimate(flops=1 << 20, bytes_accessed=1 << 20, transcendentals=0)


def sum_kernel(part, total, *scratch):
    chain = Chain(part, total, *scratch)
    greet()
    chain.start()
    chain.finish(0)


def tp_sum(part):
    shape = part.shape
    return pl.pallas_call(
        sum_kernel,
        out_shape=jax.ShapeDtypeStruct(shape, BF16),
        in_specs=[VMEM],
        out_specs=VMEM,
        scratch_shapes=chain_scratch(shape),
        compiler_params=params(0),
        cost_estimate=cost(),
    )(part)


class Taker:
    def __init__(self, refs):
        self.refs = list(refs)

    def __call__(self, count):
        taken, self.refs = self.refs[:count], self.refs[count:]
        return taken


def ticker(chain):
    return (lambda c: None) if chain is None else chain.step


def mm(left, right):
    return jnp.dot(left, right, preferred_element_type=F32)


def mm_t(left, right):
    return lax.dot_general(left, right, (((1,), (1,)), ((), ())), preferred_element_type=F32)


def mm_0(left, right):
    return lax.dot_general(left, right, (((0,), (0,)), ((), ())), preferred_element_type=F32)


def tile_at(ref, j, size=TILE):
    return ref.at[:, pl.ds(pl.multiple_of(j * size, size), size)]


def rows_at(ref, j, size=TILE):
    return ref.at[pl.ds(pl.multiple_of(j * size, size), size)]


def by_rows(rows, body, block=64):
    @pl.loop(0, rows // block)
    def _(i):
        body(pl.ds(pl.multiple_of(i * block, block), block))


def copy_either(first, one, two, target, sem, start):
    @pl.when(first)
    def _():
        copy = pltpu.make_async_copy(one, target, sem)
        copy.start() if start else copy.wait()

    @pl.when(jnp.logical_not(first))
    def _():
        copy = pltpu.make_async_copy(two, target, sem)
        copy.start() if start else copy.wait()


def send_either(first, source, one, two, sem, start):
    @pl.when(first)
    def _():
        copy = pltpu.make_async_copy(source, one, sem)
        copy.start() if start else copy.wait()

    @pl.when(jnp.logical_not(first))
    def _():
        copy = pltpu.make_async_copy(source, two, sem)
        copy.start() if start else copy.wait()


def norm_factor(values):
    return lax.rsqrt(jnp.mean(values * values, axis=-1, keepdims=True) + EPS)


def normalize_rows(source, gain, target):
    def body(rows):
        values = source(rows)
        target[rows] = (values * norm_factor(values) * gain[...]).astype(BF16)

    by_rows(target.shape[0], body)


def norm_back_rows(upstream, grad_in, source, gain, gain_grad, target):
    def body(rows):
        values = source(rows)
        factor = norm_factor(values)
        unit = values * factor
        grad = grad_in[rows].astype(F32)
        per_row = grad * unit
        mean = jnp.mean(per_row * gain[...], axis=-1, keepdims=True)
        target[rows] = (upstream[rows].astype(F32) + factor * (grad * gain[...] - unit * mean)).astype(BF16)
        gain_grad[...] += jnp.sum(per_row.reshape(-1, 8, per_row.shape[1]), axis=0)

    by_rows(target.shape[0], body)


class FfnWeights:
    def __init__(self, sources, targets, sems, by_columns):
        self.own, self.other, self.down_source = sources
        self.gate, self.up, self.down = targets
        self.sems = sems
        self.first = lax.axis_index("section") == 0
        self.wide = tile_at if by_columns else rows_at
        self.deep = rows_at if by_columns else tile_at
        self.tiles, self.outs = self.gate.shape[1] // TILE, self.gate.shape[0] // TILE
        self.wide_count, self.deep_count = (self.tiles, self.outs) if by_columns else (self.outs, self.tiles)

    def copy_gate(self, j, start):
        wide = self.wide
        copy_either(self.first, wide(self.own, j), wide(self.other, j), wide(self.gate, j), self.sems.at[0, j], start)

    def copy_up(self, j, start):
        wide = self.wide
        copy_either(self.first, wide(self.other, j), wide(self.own, j), wide(self.up, j), self.sems.at[1, j], start)

    def copy_down(self, j):
        return pltpu.make_async_copy(self.deep(self.down_source, j), self.deep(self.down, j), self.sems.at[2, j])

    def start_wide(self):
        @pl.loop(0, self.wide_count)
        def _(j):
            self.copy_gate(j, True)
            self.copy_up(j, True)

    def start_deep(self):
        @pl.loop(0, self.deep_count)
        def _(j):
            self.copy_down(j).start()


def ffn_forward_stage(weights, normed, outs, held, one, two, out_sems, result, tick, wait):
    gate, up, inner = held

    @pl.loop(0, weights.tiles)
    def _(j):
        if wait:
            weights.copy_gate(j, False)
        one[...] = mm(normed[...], tile_at(weights.gate, j)[...])
        tick(2 * j)
        if wait:
            weights.copy_up(j, False)
        two[...] = mm(normed[...], tile_at(weights.up, j)[...])
        columns = pl.ds(pl.multiple_of(j * TILE, TILE), TILE)

        def body(rows):
            g, u = one[rows], two[rows]
            gate[rows, columns] = g.astype(BF16)
            up[rows, columns] = u.astype(BF16)
            inner[rows, columns] = (g * jax.nn.sigmoid(g) * u).astype(BF16)

        by_rows(one.shape[0], body)
        tick(2 * j + 1)
        for k in range(3):
            pltpu.make_async_copy(tile_at(held[k], j), tile_at(outs[k], j), out_sems.at[k, j]).start()

    @pl.loop(0, weights.outs)
    def _(n):
        if wait:
            weights.copy_down(n).wait()
        tile_at(result, n)[...] = mm_t(inner[...], rows_at(weights.down, n)[...]).astype(BF16)
        tick(2 * weights.tiles + n)

    return 2 * weights.tiles + weights.outs


def wait_out(held, outs, out_sems):
    @pl.loop(0, held[0].shape[1] // TILE)
    def _(j):
        for k in range(len(held)):
            pltpu.make_async_copy(tile_at(held[k], j), tile_at(outs[k], j), out_sems.at[k, j]).wait()


def ffn_forward_kernel(lead, *refs):
    take = Taker(refs)
    layer_a, attn_a, layer_b, last_b, gain = take(5)
    sources = take(3)
    normed_a, *outs_a = take(4)
    normed_b, *outs_b = take(4)
    result_b, total_a = take(2)
    attn_b = take(1)[0] if lead else last_b
    targets, held = take(3), take(3)
    one, two, result_a, w_sems, out_sems = take(5)
    chain_a = Chain(result_a, total_a, *take(CHAIN_REFS))
    chain_b = Chain(last_b, attn_b, *take(CHAIN_REFS)) if lead else None
    weights = FfnWeights(sources, targets, w_sems, True)
    weights.start_wide()
    weights.start_deep()
    greet()
    if lead:
        chain_b.start()
    normalize_rows(lambda r: layer_a[r].astype(F32) + attn_a[r].astype(F32), gain, normed_a)
    done = ffn_forward_stage(weights, normed_a, outs_a, held, one, two, out_sems, result_a, ticker(chain_b), True)
    chain_a.start()
    if lead:
        chain_b.finish(done)
    normalize_rows(lambda r: layer_b[r].astype(F32) + attn_b[r].astype(F32), gain, normed_b)
    wait_out(held, outs_a, out_sems)
    done = ffn_forward_stage(weights, normed_b, outs_b, held, one, two, out_sems, result_b, ticker(chain_a), False)
    chain_a.finish(done)
    wait_out(held, outs_b, out_sems)


def ffn_forward(lead, layer_a, attn_a, layer_b, last_b, gain, weights):
    rows, width = layer_a.shape
    ff = weights[0].shape[1]
    tiles = max(ff, width) // TILE
    narrow, wide = jax.ShapeDtypeStruct((rows, width), BF16), jax.ShapeDtypeStruct((rows, ff), BF16)
    return pl.pallas_call(
        functools.partial(ffn_forward_kernel, lead),
        out_shape=[narrow, wide, wide, wide] * 2 + [narrow] * (2 + lead),
        in_specs=[VMEM] * 5 + [ANY] * 3,
        out_specs=([VMEM] + [ANY] * 3) * 2 + [VMEM] * (2 + lead),
        scratch_shapes=[pltpu.VMEM((width, ff), BF16)] * 3
        + [pltpu.VMEM((rows, ff), BF16)] * 3
        + [pltpu.VMEM((rows, TILE), F32)] * 2
        + [pltpu.VMEM((rows, width), BF16)]
        + [pltpu.SemaphoreType.DMA((3, tiles))] * 2
        + chain_scratch((rows, width)) * (1 + lead),
        compiler_params=params(1 + lead),
        cost_estimate=cost(),
    )(layer_a, attn_a, layer_b, last_b, gain, *weights)


def ffn_backward_stage(weights, grad, ins, outs, held, one, in_sems, out_sems, result, tick, wait):
    gate, up = held
    own_out, other_out = outs

    @pl.loop(0, weights.tiles)
    def _(j):
        if wait:
            weights.copy_down(j).wait()
        one[...] = mm(grad[...], tile_at(weights.down, j)[...])
        tick(j)
        for k in range(2):
            pltpu.make_async_copy(tile_at(ins[k], j), tile_at(held[k], j), in_sems.at[k, j]).wait()
        columns = pl.ds(pl.multiple_of(j * TILE, TILE), TILE)

        def body(rows):
            g, u, d = gate[rows, columns].astype(F32), up[rows, columns].astype(F32), one[rows]
            sig = jax.nn.sigmoid(g)
            d = d * sig
            gate[rows, columns] = (d * u * (1.0 + g * (1.0 - sig))).astype(BF16)
            up[rows, columns] = (d * g).astype(BF16)

        by_rows(one.shape[0], body)

    def sending(start):
        @pl.loop(0, weights.tiles)
        def _(j):
            own, other = tile_at(own_out, j), tile_at(other_out, j)
            send_either(weights.first, tile_at(gate, j), own, other, out_sems.at[0, j], start)
            send_either(weights.first, tile_at(up, j), other, own, out_sems.at[1, j], start)

    sending(True)

    @pl.loop(0, weights.outs)
    def _(n):
        if wait:
            weights.copy_gate(n, False)
            weights.copy_up(n, False)
        one[...] = mm_t(gate[...], rows_at(weights.gate, n)[...])
        tick(weights.tiles + 2 * n)
        tile_at(result, n)[...] = (one[...] + mm_t(up[...], rows_at(weights.up, n)[...])).astype(BF16)
        tick(weights.tiles + 2 * n + 1)

    return weights.tiles + 2 * weights.outs, lambda: sending(False)


def ffn_backward_kernel(low, *refs):
    take = Taker(refs)
    grad_a, grad_b, last_b = take(3)
    ins_a, ins_b, sources = take(2), take(2), take(3)
    if low:
        sum_a, layer_a, layer_b, gain = take(4)
    outs_a, outs_b = take(2), take(2)
    result_b, total_a, total_b = take(3)
    if low:
        made_a, made_b, gain_grad = take(3)
    targets, held = take(3), take(2)
    one, result_a, w_sems, in_sems, out_sems = take(5)
    chain_a = Chain(result_a, total_a, *take(CHAIN_REFS))
    chain_b = Chain(last_b, total_b, *take(CHAIN_REFS))
    weights = FfnWeights(sources, targets, w_sems, False)

    def fetch(ins):
        @pl.loop(0, weights.tiles)
        def _(j):
            for k in range(2):
                pltpu.make_async_copy(tile_at(ins[k], j), tile_at(held[k], j), in_sems.at[k, j]).start()

    weights.start_deep()
    fetch(ins_a)
    weights.start_wide()
    greet()
    chain_b.start()
    if low:
        gain_grad[...] = jnp.zeros_like(gain_grad)
        norm_back_rows(grad_a, sum_a, lambda r: layer_a[r].astype(F32), gain, gain_grad, made_a)
        grad_a = made_a
    done, sent_a = ffn_backward_stage(
        weights, grad_a, ins_a, outs_a, held, one, in_sems, out_sems, result_a, chain_b.step, True
    )
    chain_a.start()
    sent_a()
    fetch(ins_b)
    chain_b.finish(done)
    if low:
        norm_back_rows(grad_b, total_b, lambda r: layer_b[r].astype(F32), gain, gain_grad, made_b)
        grad_b = made_b
    done, sent_b = ffn_backward_stage(
        weights, grad_b, ins_b, outs_b, held, one, in_sems, out_sems, result_b, chain_a.step, False
    )
    chain_a.finish(done)
    sent_b()


def ffn_backward(grads, kept, weights, last_b, below=None):
    rows, width = last_b.shape
    ff = weights[0].shape[1]
    tiles = max(ff, width) // TILE
    low = below is not None
    narrow, wide = jax.ShapeDtypeStruct((rows, width), BF16), jax.ShapeDtypeStruct((rows, ff), BF16)
    more = [narrow, narrow, jax.ShapeDtypeStruct((8, width), F32)] if low else []
    return pl.pallas_call(
        functools.partial(ffn_backward_kernel, low),
        out_shape=[wide] * 4 + [narrow] * 3 + more,
        in_specs=[VMEM] * 3 + [ANY] * 7 + [VMEM] * (4 if low else 0),
        out_specs=[ANY] * 4 + [VMEM] * (3 + len(more)),
        scratch_shapes=[pltpu.VMEM((width, ff), BF16)] * 3
        + [pltpu.VMEM((rows, ff), BF16)] * 2
        + [pltpu.VMEM((rows, TILE), F32)]
        + [pltpu.VMEM((rows, width), BF16)]
        + [pltpu.SemaphoreType.DMA((3, tiles))]
        + [pltpu.SemaphoreType.DMA((2, tiles))] * 2
        + chain_scratch((rows, width)) * 2,
        compiler_params=params(3 + low),
        cost_estimate=cost(),
    )(*grads, last_b, kept[0]["gate"], kept[0]["up"], kept[1]["gate"], kept[1]["up"], *weights, *(below or ()))


def roped(values, cosine, sine):
    return values * cosine + pltpu.roll(values, HEAD // 2, 1) * sine


def unroped(grads, cosine, sine):
    return grads * cosine + pltpu.roll(grads * sine, HEAD // 2, 1)


def allowed_keys(seg_rows, seg_keys, i, block):
    rows, keys = seg_rows.shape[0], seg_keys.shape[1]
    first_row = lax.axis_index("ctx") * rows + i * block
    row_at = first_row + lax.broadcasted_iota(jnp.int32, (block, keys), 0)
    key_at = lax.broadcasted_iota(jnp.int32, (block, keys), 1)
    own = seg_rows[pl.ds(pl.multiple_of(i * block, block), block)]
    return (key_at <= row_at) & (own == seg_keys[...])


def attention_forward_stage(layer_in, gain, w_lin, w_out, bias, places, outs, result, kv_sems, tick):
    cosine, sine, seg_rows, seg_keys = places
    normed, query, kv, lse, attended = outs
    rows, q_cols = query.shape
    heads = q_cols // HEAD
    count = kv.shape[0] // rows
    me = lax.axis_index("ctx")
    block = min(256, rows)
    normalize_rows(lambda r: layer_in[r].astype(F32), gain, normed)
    mine = kv.at[pl.ds(pl.multiple_of(me * rows, rows), rows)]
    lin = mm(normed[...], w_lin[...]) + bias[...]
    mine[:, :HEAD] = roped(lin[:, q_cols : q_cols + HEAD], cosine[...], sine[...]).astype(BF16)
    mine[:, HEAD:] = lin[:, q_cols + HEAD :].astype(BF16)

    def passing(offset):
        return pltpu.make_async_remote_copy(
            src_ref=mine,
            dst_ref=mine,
            send_sem=kv_sems.at[0, offset],
            recv_sem=kv_sems.at[1, offset],
            device_id={"ctx": lax.rem(me + offset, count)},
            device_id_type=MESH,
        )

    for offset in range(1, count):
        passing(offset).start()
    for h in range(heads):
        columns = slice(h * HEAD, (h + 1) * HEAD)
        query[:, columns] = roped(lin[:, columns], cosine[...], sine[...]).astype(BF16)
    tick(0)
    for offset in range(1, count):
        passing(offset).wait_recv()

    @pl.loop(0, rows // block)
    def _(i):
        at = pl.ds(pl.multiple_of(i * block, block), block)
        allowed = allowed_keys(seg_rows, seg_keys, i, block)
        lane = lax.broadcasted_iota(jnp.int32, (block, HEAD), 1)
        logs = jnp.zeros((block, HEAD), F32)
        for h in range(heads):
            columns = slice(h * HEAD, (h + 1) * HEAD)
            scores = jnp.where(allowed, mm_t(query[at, columns], kv[:, :HEAD]) * SCALE, NEG)
            top = jnp.max(scores, axis=-1, keepdims=True)
            probs = jnp.exp(scores - top)
            sums = jnp.sum(probs, axis=-1, keepdims=True)
            probs = (probs * (1.0 / sums)).astype(BF16)
            attended[at, columns] = mm(probs, kv[:, HEAD:]).astype(BF16)
            logs = jnp.where(lane == h, top + jnp.log(sums), logs)
            tick(1 + heads * i + h)
        lse[at] = logs

    base = 1 + heads * (rows // block)

    @pl.loop(0, result.shape[1] // TILE)
    def _(n):
        tile_at(result, n)[...] = mm_t(attended[...], rows_at(w_out, n)[...]).astype(BF16)
        tick(base + n)

    for offset in range(1, count):
        passing(offset).wait_send()
    return base + result.shape[1] // TILE


def attention_forward_kernel(low, *refs):
    take = Taker(refs)
    gain, w_lin, w_out, bias = take(4)
    places_a, places_b = take(4), take(4)
    if low:
        layer_a, layer_b = take(2)
    else:
        adds_a, adds_b, (last_b,) = take(3), take(2), take(1)
    outs_a, outs_b = take(5), take(5)
    if low:
        total_a, total_b = take(2)
    else:
        result_b, total_a, last_sum_b, layer_a, layer_b = take(5)
    result_a, kv_sems_a, kv_sems_b = take(3)
    if low:
        (result_b,) = take(1)
    chain_a = Chain(result_a, total_a, *take(CHAIN_REFS))
    chain_b = Chain(result_b, total_b, *take(CHAIN_REFS)) if low else Chain(last_b, last_sum_b, *take(CHAIN_REFS))
    greet(kv_sems_a.shape[1])
    if not low:
        chain_b.start()

        def body(rows):
            layer_a[rows] = sum(ref[rows].astype(F32) for ref in adds_a).astype(BF16)

        by_rows(layer_a.shape[0], body)
    tick = ticker(None if low else chain_b)
    done = attention_forward_stage(layer_a, gain, w_lin, w_out, bias, places_a, outs_a, result_a, kv_sems_a, tick)
    chain_a.start()
    if not low:
        chain_b.finish(done)

        def body(rows):
            layer_b[rows] = sum(ref[rows].astype(F32) for ref in (*adds_b, last_sum_b)).astype(BF16)

        by_rows(layer_b.shape[0], body)
    done = attention_forward_stage(layer_b, gain, w_lin, w_out, bias, places_b, outs_b, result_b, kv_sems_b, chain_a.step)
    if low:
        chain_b.start()
    chain_a.finish(done)
    if low:
        chain_b.finish(0)


def attention_forward(weights, places, inputs):
    w_lin, w_out, gains, bias = weights
    rows, width = inputs[0].shape
    q_cols = w_out.shape[1]
    keys = places[0][3].shape[1]
    count = keys // rows
    low = len(inputs) == 2
    narrow = jax.ShapeDtypeStruct((rows, width), BF16)
    heads_out = jax.ShapeDtypeStruct((rows, q_cols), BF16)
    kv_out = jax.ShapeDtypeStruct((keys, 2 * HEAD), BF16)
    lse_out = jax.ShapeDtypeStruct((rows, HEAD), F32)
    outs = [narrow, heads_out, kv_out, lse_out, heads_out] * 2 + [narrow] * (2 if low else 5)
    args = (gains[:1], w_lin, w_out, bias, *places[0], *places[1], *inputs)
    return pl.pallas_call(
        functools.partial(attention_forward_kernel, low),
        out_shape=outs,
        in_specs=[VMEM] * len(args),
        out_specs=[VMEM] * len(outs),
        scratch_shapes=[pltpu.VMEM((rows, width), BF16)]
        + [pltpu.SemaphoreType.DMA((2, count))] * 2
        + [pltpu.VMEM((rows, width), BF16)] * low
        + chain_scratch((rows, width)) * 2,
        compiler_params=params(5 + low),
        cost_estimate=cost(),
    )(*args)


def attention_backward_stage(ins, sum_in, gain, w_lin, w_out, places, outs, gain_grad, result, scratch, tick):
    upstream, layer_in, attn_out, query, kv, lse, attended = ins
    cosine, sine, seg_rows, seg_keys = places
    attn_grad, lin = outs
    heads_grad, kv_grad, sent, got, kv_sems = scratch
    rows, q_cols = query.shape
    heads = q_cols // HEAD
    count = kv.shape[0] // rows
    me = lax.axis_index("ctx")
    block = min(256, rows)
    kv_grad[...] = jnp.zeros_like(kv_grad)
    norm_back_rows(
        upstream, sum_in, lambda r: layer_in[r].astype(F32) + attn_out[r].astype(F32), gain, gain_grad, attn_grad
    )
    heads_grad[...] = mm(attn_grad[...], w_out[...]).astype(BF16)
    tick(0)

    @pl.loop(0, rows // block)
    def _(i):
        at = pl.ds(pl.multiple_of(i * block, block), block)
        allowed = allowed_keys(seg_rows, seg_keys, i, block)
        for h in range(heads):
            columns = slice(h * HEAD, (h + 1) * HEAD)
            scores = mm_t(query[at, columns], kv[:, :HEAD]) * SCALE - lse[at, h : h + 1]
            probs = jnp.exp(jnp.where(allowed, scores, NEG))
            grad = heads_grad[at, columns]
            row_sum = jnp.sum(attended[at, columns].astype(F32) * grad.astype(F32), axis=-1, keepdims=True)
            score_grad = (probs * (mm_t(grad, kv[:, HEAD:]) - row_sum)).astype(BF16)
            q_grad = mm(score_grad, kv[:, :HEAD]) * SCALE
            lin[at, columns] = unroped(q_grad, cosine[at], sine[at]).astype(BF16)
            kv_grad[:, :HEAD] += mm_0(score_grad, query[at, columns])
            kv_grad[:, HEAD:] += mm_0(probs.astype(BF16), grad)
            tick(1 + heads * i + h)

    def passing(offset):
        return pltpu.make_async_remote_copy(
            src_ref=sent.at[offset - 1],
            dst_ref=got.at[offset - 1],
            send_sem=kv_sems.at[0, offset],
            recv_sem=kv_sems.at[1, offset],
            device_id={"ctx": lax.rem(me + offset, count)},
            device_id_type=MESH,
        )

    for offset in range(1, count):
        peer = pl.ds(pl.multiple_of(lax.rem(me + offset, count) * rows, rows), rows)
        sent[offset - 1, :, :HEAD] = (kv_grad[peer, :HEAD] * SCALE).astype(BF16)
        sent[offset - 1, :, HEAD:] = kv_grad[peer, HEAD:].astype(BF16)
        passing(offset).start()
    mine = pl.ds(pl.multiple_of(me * rows, rows), rows)
    k_grad, v_grad = kv_grad[mine, :HEAD] * SCALE, kv_grad[mine, HEAD:]
    for offset in range(1, count):
        passing(offset).wait_recv()
        k_grad = k_grad + got[offset - 1, :, :HEAD].astype(F32)
        v_grad = v_grad + got[offset - 1, :, HEAD:].astype(F32)
    lin[:, q_cols : q_cols + HEAD] = unroped(k_grad, cosine[...], sine[...]).astype(BF16)
    lin[:, q_cols + HEAD :] = v_grad.astype(BF16)
    base = 1 + heads * (rows // block)

    @pl.loop(0, result.shape[1] // TILE)
    def _(n):
        tile_at(result, n)[...] = mm_t(lin[...], rows_at(w_lin, n)[...]).astype(BF16)
        tick(base + n)

    for offset in range(1, count):
        passing(offset).wait_send()
    return base + result.shape[1] // TILE


def attention_backward_kernel(*refs):
    take = Taker(refs)
    gain, w_lin, w_out = take(3)
    places_a, places_b = take(4), take(4)
    ins_a, ins_b = take(7), take(7)
    sum_a, last_b = take(2)
    outs_a, outs_b = take(2), take(2)
    gain_grad, result_b, total_a, total_b = take(4)
    heads_grad, kv_grad, result_a = take(3)
    exchange_a, exchange_b = take(3), take(3)
    chain_a = Chain(result_a, total_a, *take(CHAIN_REFS))
    chain_b = Chain(last_b, total_b, *take(CHAIN_REFS))
    greet(exchange_a[2].shape[1])
    chain_b.start()
    gain_grad[...] = jnp.zeros_like(gain_grad)
    scratch = (heads_grad, kv_grad, *exchange_a)
    done = attention_backward_stage(
        ins_a, sum_a, gain, w_lin, w_out, places_a, outs_a, gain_grad, result_a, scratch, chain_b.step
    )
    chain_a.start()
    chain_b.finish(done)
    scratch = (heads_grad, kv_grad, *exchange_b)
    done = attention_backward_stage(
        ins_b, total_b, gain, w_lin, w_out, places_b, outs_b, gain_grad, result_b, scratch, chain_a.step
    )
    chain_a.finish(done)


def attention_backward(upstream, sum_a, last_b, kept, weights, places):
    w_lin, w_out, gains, bias = weights
    rows, width = sum_a.shape
    q_cols = w_out.shape[1]
    keys = places[0][3].shape[1]
    count = keys // rows
    narrow = jax.ShapeDtypeStruct((rows, width), BF16)
    lin_out = jax.ShapeDtypeStruct((rows, q_cols + 2 * HEAD), BF16)
    outs = [narrow, lin_out] * 2 + [jax.ShapeDtypeStruct((8, width), F32)] + [narrow] * 3
    names = ("layer_in", "attn_out", "query", "kv", "lse", "attended")
    args = (gains[1:], w_lin, w_out, *places[0], *places[1])
    for q in range(2):
        args += (upstream[q], *[kept[q][name] for name in names])
    args += (sum_a, last_b)
    exchange = [pltpu.VMEM((max(count - 1, 1), rows, 2 * HEAD), BF16)] * 2 + [pltpu.SemaphoreType.DMA((2, count))]
    return pl.pallas_call(
        attention_backward_kernel,
        out_shape=outs,
        in_specs=[VMEM] * len(args),
        out_specs=[VMEM] * len(outs),
        scratch_shapes=[
            pltpu.VMEM((rows, q_cols), BF16),
            pltpu.VMEM((keys, 2 * HEAD), F32),
            pltpu.VMEM((rows, width), BF16),
        ]
        + exchange * 2
        + chain_scratch((rows, width)) * 2,
        compiler_params=params(7),
        cost_estimate=cost(),
    )(*args)


def rope_tables(places):
    steps = jnp.arange(HEAD // 2, dtype=F32) * (2.0 / HEAD)
    inverse = ROPE_BASE ** (-steps)
    angles = places.astype(F32)[..., None] * inverse
    angles = jnp.concatenate([angles, angles], axis=-1)
    return (jnp.cos(angles), jnp.sin(angles))


def norm_back(grad_out, rows_in, factor, gain):
    unit = rows_in * factor
    gain_grad = jnp.sum(grad_out * unit, axis=0)
    weighted = grad_out * gain
    return (
        factor * (weighted - unit * jnp.mean(weighted * unit, axis=-1, keepdims=True)),
        gain_grad,
    )


def over_ctx(value):
    if lax.axis_size("ctx") == 2:
        other = lax.ppermute(value, "ctx", [(0, 1), (1, 0)])
        low = lax.axis_index("ctx") == 0
        return jnp.concatenate([jnp.where(low, value, other), jnp.where(low, other, value)], axis=-1)
    return lax.all_gather(value, "ctx", axis=value.ndim - 1, tiled=True)


def input_backward(normed_one_grad, middle_grad, kept, gains):
    layer_in = kept["layer_in"].astype(F32)
    factor = lax.rsqrt(jnp.mean(layer_in * layer_in, axis=-1, keepdims=True) + EPS)
    norm_grad, gain_one = norm_back(normed_one_grad.astype(F32), layer_in, factor, gains[0])
    return (middle_grad.astype(F32) + norm_grad).astype(BF16), gain_one


def local(
    section_in,
    segments,
    positions,
    query_weight,
    kv_weight,
    output_weight,
    gate_up,
    down_weight,
    norm_gains,
    query_bias,
    kv_bias,
    out_grad,
):
    sec = lax.axis_index("section")
    first = sec == 0
    group = HEADS // KV_HEADS
    heads_here = HEADS // lax.axis_size("tp")
    head_pick = lax.axis_index("tp") * heads_here // group
    shards = lax.axis_size("dp") * lax.axis_size("ctx")
    ranks = ("dp", "ctx")
    seqs, span, width = section_in.shape[1:]
    shard = query_weight.shape[1]
    q_cols = query_weight.shape[2]
    ff = gate_up.shape[3]

    def per_layer(mine, theirs):
        return jnp.where(first, mine, theirs), jnp.where(first, theirs, mine)

    half = shard // 2
    kv_width = KV_HEADS * HEAD

    def halves(rows):
        mine = lax.dynamic_slice_in_dim(rows, sec * half, half, 0)
        return per_layer(mine, swap(lax.dynamic_slice_in_dim(rows, (1 - sec) * half, half, 0)))

    def joined(own):
        return jnp.stack(per_layer(own, swap(own)), axis=1).reshape(width, own.shape[-1])

    def after(value, event):
        return lax.optimization_barrier((value, event))[0]

    piece = HEAD // shards
    biases = jnp.concatenate([query_bias[0].reshape(-1), kv_bias[0].reshape(-1)])
    n_biases = biases.shape[0]
    biases = jnp.pad(biases, (0, -n_biases % shard)).reshape(-1, shard).T
    extra = jnp.concatenate([norm_gains[0].T, biases], axis=1)
    n_extra = extra.shape[1]
    extra = jnp.pad(extra, ((0, 0), (0, HEAD - n_extra)))
    packed = jnp.concatenate([query_weight[0], kv_weight[0, 0], kv_weight[0, 1], output_weight[0].T, extra], axis=1)
    packed_shards = halves(packed)
    spare = -ff % TILE
    wide = jnp.pad(gate_up[0], ((0, 0), (0, 0), (0, spare)))
    mine = lax.dynamic_index_in_dim(wide, sec, 0, keepdims=False)
    theirs = swap(lax.dynamic_index_in_dim(wide, 1 - sec, 0, keepdims=False))
    gate_up_shards = per_layer(mine, theirs)
    down_shards = halves(jnp.pad(down_weight[0].T, ((0, 0), (0, spare))))

    micro = sec
    seg = lax.dynamic_index_in_dim(segments, micro, 0, keepdims=False)
    pos = lax.dynamic_index_in_dim(positions, micro, 0, keepdims=False)
    hidden = lax.dynamic_index_in_dim(section_in, micro, 0, keepdims=False)
    seg_keys = over_ctx(seg)
    segs, tables = [], []
    for q in range(seqs):
        segs.append((seg[q][:, None], seg_keys[q][None]))
        cosine, sine = rope_tables(pos[q])
        tables.append((cosine, jnp.where(jnp.arange(HEAD) < HEAD // 2, -sine, sine)))
    hidden = [hidden[0], hidden[1]]

    packed_low = lax.all_gather(packed_shards[0], ranks, axis=0)
    packed_low, gate_up_shards, down_shards, packed_shards, segs, tables, hidden = lax.optimization_barrier(
        (packed_low, gate_up_shards, down_shards, packed_shards, segs, tables, hidden)
    )
    own_low = lax.all_gather(gate_up_shards[0], ranks, axis=0, tiled=True)
    down_low = lax.all_gather(down_shards[0], ranks, axis=0)

    def attention_weights(own):
        p = joined(own)
        wq = p[:, :q_cols]
        wk = lax.dynamic_slice_in_dim(p[:, q_cols : q_cols + kv_width], head_pick * HEAD, HEAD, 1)
        wv = lax.dynamic_slice_in_dim(p[:, q_cols + kv_width : q_cols + 2 * kv_width], head_pick * HEAD, HEAD, 1)
        wo = p[:, q_cols + 2 * kv_width : 2 * q_cols + 2 * kv_width]
        s = p[:, 2 * q_cols + 2 * kv_width :]
        gains = s[:, :2].T
        s = s[:, 2:n_extra].T.reshape(-1, shards, shard).transpose(1, 0, 2).reshape(shards, -1)[:, :n_biases]
        q_b = s[:, : heads_here * piece].reshape(shards, heads_here, piece).transpose(1, 0, 2).reshape(heads_here, HEAD)
        kv_b = s[:, heads_here * piece :].reshape(shards, 2, KV_HEADS, piece)
        kv_b = kv_b.transpose(1, 2, 0, 3).reshape(2, KV_HEADS, HEAD)
        kv_b = lax.dynamic_slice_in_dim(kv_b, head_pick, 1, 1)
        bias = jnp.concatenate([q_b.reshape(1, -1), kv_b.reshape(1, -1)], axis=1).astype(F32)
        return jnp.concatenate([wq, wk, wv], axis=1), wo, gains.astype(F32), bias

    kept = [[dict(), dict()] for _ in range(2)]
    names = ("normed", "query", "kv", "lse", "attended")
    more_names = ("normed_two", "gate", "up", "inner")
    attn_weights, ffn_weights = [attention_weights(packed_low), None], [None, None]
    places = [(*tables[q], *segs[q]) for q in range(seqs)]

    def keep(layer, names, values):
        for q in range(2):
            kept[layer][q].update(zip(names, values[q * len(names) : (q + 1) * len(names)]))
        return values[2 * len(names) :]

    outs = []

    attn_a, attn_b = keep(0, names, attention_forward(attn_weights[0], places, hidden))
    attn_b, own_low, down_low = lax.optimization_barrier((attn_b, own_low, down_low))
    ffn_weights[0] = own_low, swap(own_low), joined(down_low)
    packed_high = lax.all_gather(after(packed_shards[1], attn_b), ranks, axis=0)
    own_high = lax.all_gather(after(gate_up_shards[1], attn_b), ranks, axis=0, tiled=True)
    down_high = lax.all_gather(after(down_shards[1], attn_b), ranks, axis=0)
    gain = attn_weights[0][2][1:]
    part_b, ffn_a = keep(
        0, more_names, ffn_forward(False, hidden[0], attn_a, hidden[1], attn_b, gain, ffn_weights[0])
    )
    kept[0][0].update(layer_in=hidden[0], attn_out=attn_a)
    kept[0][1].update(layer_in=hidden[1], attn_out=attn_b)

    packed_high, part_b = lax.optimization_barrier((packed_high, part_b))
    attn_weights[1] = attention_weights(packed_high)
    inputs = (hidden[0], attn_a, ffn_a, hidden[1], attn_b, part_b)
    part_b, attn_a, _, layer_a, layer_b = keep(1, names, attention_forward(attn_weights[1], places, inputs))
    outs.append(jnp.stack([layer_a, layer_b]))
    part_b, own_high, down_high = lax.optimization_barrier((part_b, own_high, down_high))
    ffn_weights[1] = own_high, swap(own_high), joined(down_high)
    gain = attn_weights[1][2][1:]
    part_b, ffn_a, attn_b = keep(1, more_names, ffn_forward(True, layer_a, attn_a, layer_b, part_b, gain, ffn_weights[1]))
    kept[1][0].update(layer_in=layer_a, attn_out=attn_a)
    kept[1][1].update(layer_in=layer_b, attn_out=attn_b)
    grad_top = lax.dynamic_index_in_dim(out_grad, micro, 0, keepdims=False)
    upstream = [grad_top[0], grad_top[1]]
    *wide_grads, grad_b, sum_a, ffn_b = ffn_backward(upstream, kept[1], ffn_weights[1], part_b)
    k = kept[1]
    outs.append(
        jnp.stack(
            [
                (k[q]["layer_in"].astype(F32) + k[q]["attn_out"].astype(F32) + out.astype(F32)).astype(BF16)
                for q, out in enumerate((ffn_a, ffn_b))
            ]
        )
    )

    def to_section(values):
        low = lax.ppermute(values[0], "section", [(1, 0)])
        high = lax.ppermute(values[1], "section", [(0, 1)])
        return jnp.stack([jnp.where(first, values[0], high), jnp.where(first, low, values[1])])

    section_out = to_section(outs)

    in_grads = [None, None]
    gate_up_grads, down_grads, packed_grads, gains_grads = [[None, None] for _ in range(4)]
    for layer in (1, 0):
        weights, k = attn_weights[layer], kept[layer]
        if layer == 0:
            below = (sum_a, kept[1][0]["layer_in"], kept[1][1]["layer_in"], attn_weights[1][2][:1])
            *wide_grads, grad_b, sum_a, _, made_a, made_b, gain_one = ffn_backward(
                attn_grads, k, ffn_weights[0], part_b, below
            )
            upstream = [made_a, made_b]
            in_grads[1] = jnp.stack(upstream)
            gains_grads[1] = jnp.stack([jnp.sum(gain_one, axis=0), gain_two])
            sum_a, gate_up_grads[1] = lax.optimization_barrier((sum_a, gate_up_grads[1]))
        own_a, other_a, own_b, other_b = wide_grads
        own_grads, other_grads = (own_a, own_b), (other_a, other_b)
        normed_two = jnp.concatenate([k[q]["normed_two"] for q in range(seqs)])
        own_w = dot("rd,rf->df", normed_two, jnp.concatenate(own_grads)).astype(BF16)
        other_w = dot("rd,rf->df", normed_two, jnp.concatenate(other_grads)).astype(BF16)
        own_w = (own_w.astype(F32) + swap(other_w).astype(F32)).astype(BF16)
        own_w, sum_a = lax.optimization_barrier((own_w, sum_a))
        gate_up_grads[layer] = lax.psum_scatter(own_w, ranks, scatter_dimension=0, tiled=True)
        down_w = dot("rd,rf->df", jnp.concatenate(upstream), jnp.concatenate([k[q]["inner"] for q in range(seqs)])).astype(BF16)
        down_w = down_w.reshape(shards, 2, half, ff + spare)
        down_own = lax.dynamic_index_in_dim(down_w, sec, 1, keepdims=False)
        down_other = lax.dynamic_index_in_dim(down_w, 1 - sec, 1, keepdims=False)
        down_own = (down_own.astype(F32) + swap(down_other).astype(F32)).astype(BF16)
        down_own, sum_a = lax.optimization_barrier((down_own, sum_a))
        down_grads[layer] = lax.psum_scatter(
            down_own.reshape(shards * half, ff + spare), ranks, scatter_dimension=0, tiled=True
        )

        attn_a, lin_a, attn_b, lin_b, gain_two, part_b, sum_a, _ = attention_backward(
            upstream, sum_a, grad_b, k, weights, places
        )
        attn_grads, lin_grads = (attn_a, attn_b), (lin_a, lin_b)
        gain_two = jnp.sum(gain_two, axis=0)
        if layer == 0:
            part_b, down_grads[1] = lax.optimization_barrier((part_b, down_grads[1]))
        lin_grad = jnp.concatenate(lin_grads)
        normed_one = jnp.concatenate([k[q]["normed"] for q in range(seqs)])
        lin_w = dot("rd,re->de", normed_one, lin_grad)
        attended = jnp.concatenate([k[q]["attended"] for q in range(seqs)])
        out_w = dot("rd,re->de", jnp.concatenate(attn_grads), attended)
        bias = jnp.sum(lin_grad.astype(F32), axis=0)
        bias = bias.reshape(heads_here + 2, shards, piece).transpose(1, 0, 2).reshape(shards, (heads_here + 2) * piece)
        bias = jnp.pad(bias, ((0, 0), (0, -bias.shape[1] % shard)))
        bias = bias.reshape(shards, -1, shard).transpose(0, 2, 1).reshape(width, -1)
        bias = jnp.pad(bias, ((0, 0), (0, HEAD - bias.shape[1])))
        packed_grads[layer] = jnp.concatenate([lin_w, out_w, bias], axis=1).astype(BF16)

    low = lax.ppermute(packed_grads[0], "section", [(1, 0)])
    high = lax.ppermute(packed_grads[1], "section", [(0, 1)])
    packed_total = jnp.where(
        first, packed_grads[0].astype(F32) + low.astype(F32), packed_grads[1].astype(F32) + high.astype(F32)
    ).astype(BF16)
    last_part, gate_up_grads[0], packed_total = lax.optimization_barrier((part_b, gate_up_grads[0], packed_total))
    packed_total = lax.psum_scatter(packed_total, ranks, scatter_dimension=0, tiled=True).astype(F32)
    sum_b, down_grads[0] = lax.optimization_barrier((tp_sum(last_part), down_grads[0]))
    made_a, gain_a = input_backward(sum_a, attn_grads[0], kept[0][0], attn_weights[0][2])
    made_b, gain_b = input_backward(sum_b, attn_grads[1], kept[0][1], attn_weights[0][2])
    in_grads[0] = jnp.stack([made_a, made_b])
    gains_grads[0] = jnp.stack([gain_a + gain_b, gain_two])
    input_grad = to_section(in_grads)
    low = lax.ppermute(gains_grads[0], "section", [(1, 0)])
    high = lax.ppermute(gains_grads[1], "section", [(0, 1)])
    gains_grad = jnp.where(first, gains_grads[0] + low, gains_grads[1] + high)
    for axis in ranks:
        if lax.axis_size(axis) == 2:
            gains_grad = gains_grad + lax.ppermute(gains_grad, axis, [(0, 1), (1, 0)])
        else:
            gains_grad = lax.psum(gains_grad, axis)
    at = (lax.axis_index("dp") * lax.axis_size("ctx") + lax.axis_index("ctx")) * shard
    gains_grad = lax.dynamic_slice_in_dim(gains_grad, at, shard, 1)
    q_grad = packed_total[:, :q_cols]
    kv_narrow = packed_total[:, q_cols : q_cols + 2 * HEAD].reshape(shard, 2, HEAD)
    o_grad = packed_total[:, q_cols + 2 * HEAD : 2 * q_cols + 2 * HEAD].T
    extra = packed_total[:, 2 * q_cols + 2 * HEAD :]
    bias_cols = -(-(heads_here + 2) * piece // shard)
    bias = extra[:, :bias_cols].T.reshape(-1)[: (heads_here + 2) * piece].reshape(heads_here + 2, piece)
    q_bias_grad = bias[:heads_here]
    kv_full = jnp.zeros((shard, 2, KV_HEADS, HEAD), F32)
    kv_full = lax.dynamic_update_slice_in_dim(kv_full, kv_narrow[:, :, None], head_pick, 2)
    bias_full = jnp.zeros((2, KV_HEADS, piece), F32)
    bias_full = lax.dynamic_update_slice_in_dim(bias_full, bias[heads_here:, None], head_pick, 1)
    flat = bias_full.reshape(-1)
    flat = jnp.pad(flat, (0, -flat.shape[0] % (2 * KV_HEADS * HEAD)))
    flat_rows = flat.shape[0] // (2 * KV_HEADS * HEAD)
    joined = jnp.concatenate([kv_full.reshape(shard, -1), flat.reshape(flat_rows, -1)]).astype(BF16)
    joined = chain_sum(joined).astype(F32)
    kv_grad = joined[:shard].reshape(shard, 2, KV_HEADS * HEAD).transpose(1, 0, 2)
    kv_bias_grad = joined[shard:].reshape(-1)[: 2 * KV_HEADS * piece].reshape(2, KV_HEADS, piece)

    def collect(values):
        kept_half = jnp.where(first, values[0], values[1])
        other = swap(jnp.where(first, values[1], values[0]))
        return jnp.where(first, kept_half, other), jnp.where(first, other, kept_half)

    gate_up_grad = jnp.stack(collect(gate_up_grads))[..., :ff].astype(F32)
    down_grad = jnp.concatenate(collect(down_grads), axis=0)[:, :ff].T.astype(F32)
    return (
        section_out[None],
        input_grad[None],
        q_grad[None],
        kv_grad[None],
        o_grad[None],
        gate_up_grad[None],
        down_grad[None],
        gains_grad[None],
        q_bias_grad[None],
        kv_bias_grad[None],
    )


def solution(mesh):
    in_specs = (
        P(None, "dp", "ctx", None),
        P(None, "dp", "ctx"),
        P(None, "dp", "ctx"),
        P("section", ("dp", "ctx"), "tp"),
        P("section", None, ("dp", "ctx"), None),
        P("section", "tp", ("dp", "ctx")),
        P("section", None, ("dp", "ctx"), "tp"),
        P("section", "tp", ("dp", "ctx")),
        P("section", None, ("dp", "ctx")),
        P("section", "tp", ("dp", "ctx")),
        P("section", None, None, ("dp", "ctx")),
        P(None, "dp", "ctx", None),
    )
    out_specs = (
        P("section", None, "dp", "ctx", None),
        P("section", None, "dp", "ctx", None),
        P("section", ("dp", "ctx"), "tp"),
        P("section", None, ("dp", "ctx"), None),
        P("section", "tp", ("dp", "ctx")),
        P("section", None, ("dp", "ctx"), "tp"),
        P("section", "tp", ("dp", "ctx")),
        P("section", None, ("dp", "ctx")),
        P("section", "tp", ("dp", "ctx")),
        P("section", None, None, ("dp", "ctx")),
    )
    return jax.shard_map(local, mesh=mesh, in_specs=in_specs, out_specs=out_specs, check_vma=False)
```

```python
import functools

import jax
import jax.numpy as jnp
from jax import lax
from jax.experimental import pallas as pl
from jax.experimental.pallas import tpu as pltpu
from jax.sharding import PartitionSpec as P

HEADS = 12
KV_HEADS = 2
HEAD = 128

EPS = 1e-06
ROPE_BASE = 1000000.0
NEG = -1e30
SCALE = HEAD ** (-0.5)
TILE = 768
VMEM_LIMIT = 60 << 20
MESH = pl.DeviceIdType.MESH

F32 = jnp.float32
BF16 = jnp.bfloat16


def dot(form, left, right):
    return jnp.einsum(form, left, right, preferred_element_type=F32)


def swap(value):
    return lax.ppermute(value, "section", [(0, 1), (1, 0)])


class Chain:
    def __init__(self, part, total, from_end, from_peer, sems):
        self.part, self.total = part, total
        self.from_end, self.from_peer = from_end, from_peer
        self.sems = sems
        self.chunks = sems.shape[1]
        self.rows = part.shape[0] // self.chunks
        self.is_middle, self.inner, self.outer = line_places()

    def at(self, ref, c):
        return ref.at[pl.ds(pl.multiple_of(c * self.rows, self.rows), self.rows)]

    def copy(self, source, target, c, step, place):
        return pltpu.make_async_remote_copy(
            src_ref=self.at(source, c),
            dst_ref=self.at(target, c),
            send_sem=self.sems.at[2 * step, c],
            recv_sem=self.sems.at[2 * step + 1, c],
            device_id={"tp": place},
            device_id_type=MESH,
        )

    def inward(self, c):
        return self.copy(self.part, self.from_end, c, 0, self.inner)

    def across(self, c):
        return self.copy(self.total, self.from_peer, c, 1, self.inner)

    def outward(self, c):
        return self.copy(self.total, self.total, c, 2, self.outer)

    def start(self):
        @pl.when(jnp.logical_not(self.is_middle))
        def _():
            @pl.loop(0, self.chunks)
            def _(c):
                self.inward(c).start()

    def join(self, c):
        self.inward(c).wait_recv()
        self.at(self.total, c)[...] = self.at(self.part, c)[...] + self.at(self.from_end, c)[...]
        self.across(c).start()

    def close(self, c):
        self.across(c).wait()
        self.at(self.total, c)[...] = self.at(self.total, c)[...] + self.at(self.from_peer, c)[...]
        self.outward(c).start()

    def step(self, c):
        @pl.when(self.is_middle & (c < self.chunks))
        def _():
            self.join(c)

            @pl.when(c > 0)
            def _():
                self.close(c - 1)

    def finish(self, done):
        @pl.when(self.is_middle)
        def _():
            if done < self.chunks:

                @pl.loop(done, self.chunks)
                def _(c):
                    self.step(c)

            self.close(self.chunks - 1)

            @pl.loop(0, self.chunks)
            def _(c):
                self.outward(c).wait_send()

        @pl.when(jnp.logical_not(self.is_middle))
        def _():
            @pl.loop(0, self.chunks)
            def _(c):
                self.inward(c).wait_send()
                self.outward(c).wait_recv()


def line_places():
    place = lax.axis_index("tp")
    is_middle = (place == 1) | (place == 2)
    return is_middle, jnp.where(place < 2, place + 1, place - 1), jnp.where(place < 2, place - 1, place + 1)


def greet(ctx_count=1, cores=0):
    is_middle, inner, outer = line_places()
    me = lax.axis_index("ctx")
    barrier = pltpu.get_barrier_semaphore()
    for step in range(1, ctx_count):
        pl.semaphore_signal(barrier, inc=1, device_id={"ctx": lax.rem(me + step, ctx_count)}, device_id_type=MESH)
    if cores:
        peer = 1 - lax.axis_index("section")
        pl.semaphore_signal(barrier, inc=1, device_id={"section": peer}, device_id_type=MESH)
    pl.semaphore_signal(barrier, inc=1, device_id={"tp": inner}, device_id_type=MESH)

    @pl.when(is_middle)
    def _():
        pl.semaphore_signal(barrier, inc=1, device_id={"tp": outer}, device_id_type=MESH)
        pl.semaphore_wait(barrier, 1 + ctx_count + cores)

    @pl.when(jnp.logical_not(is_middle))
    def _():
        pl.semaphore_wait(barrier, ctx_count + cores)


def ab(ref):
    rows = ref.shape[0] // 2
    return ref.at[pl.ds(0, rows)], ref.at[pl.ds(rows, rows)]


def chain_scratch(shape):
    return [pltpu.VMEM(shape, BF16)] * 2 + [pltpu.SemaphoreType.DMA((6, min(8, shape[0] // 16)))]


CHAIN_REFS = 3
VMEM = pl.BlockSpec(memory_space=pltpu.VMEM)
ANY = pl.BlockSpec(memory_space=pl.ANY)


def params(collective_id):
    return pltpu.CompilerParams(collective_id=collective_id, has_side_effects=True, vmem_limit_bytes=VMEM_LIMIT)


def cost():
    return pl.CostEstimate(flops=1 << 20, bytes_accessed=1 << 20, transcendentals=0)


class Taker:
    def __init__(self, refs):
        self.refs = list(refs)

    def __call__(self, count):
        taken, self.refs = self.refs[:count], self.refs[count:]
        return taken


def ticker(chain):
    return (lambda c: None) if chain is None else chain.step


def mm(left, right):
    return jnp.dot(left, right, preferred_element_type=F32)


def mm_t(left, right):
    return lax.dot_general(left, right, (((1,), (1,)), ((), ())), preferred_element_type=F32)


def mm_0(left, right):
    return lax.dot_general(left, right, (((0,), (0,)), ((), ())), preferred_element_type=F32)


def tile_at(ref, j, size=TILE):
    return ref.at[:, pl.ds(pl.multiple_of(j * size, size), size)]


def rows_at(ref, j, size=TILE):
    return ref.at[pl.ds(pl.multiple_of(j * size, size), size)]


def by_rows(rows, body, block=64):
    @pl.loop(0, rows // block)
    def _(i):
        body(pl.ds(pl.multiple_of(i * block, block), block))


def send_either(first, source, one, two, sem, start):
    @pl.when(first)
    def _():
        copy = pltpu.make_async_copy(source, one, sem)
        copy.start() if start else copy.wait()

    @pl.when(jnp.logical_not(first))
    def _():
        copy = pltpu.make_async_copy(source, two, sem)
        copy.start() if start else copy.wait()


def norm_factor(values):
    return lax.rsqrt(jnp.mean(values * values, axis=-1, keepdims=True) + EPS)


def normalize_rows(source, gain, target):
    def body(rows):
        values = source(rows)
        target[rows] = (values * norm_factor(values) * gain[...]).astype(BF16)

    by_rows(target.shape[0], body)


def norm_back_rows(upstream, grad_in, source, gain, gain_grad, target):
    def body(rows):
        values = source(rows)
        factor = norm_factor(values)
        unit = values * factor
        grad = grad_in[rows].astype(F32)
        per_row = grad * unit
        mean = jnp.mean(per_row * gain[...], axis=-1, keepdims=True)
        target[rows] = (upstream[rows].astype(F32) + factor * (grad * gain[...] - unit * mean)).astype(BF16)
        gain_grad[...] += jnp.sum(per_row.reshape(-1, 8, per_row.shape[1]), axis=0)

    by_rows(target.shape[0], body)


class FfnWeights:
    def __init__(self, sources, targets, sems, down_sems, by_columns):
        self.own, self.down_own = sources
        self.gate, self.up, self.down = targets
        self.sems, self.down_sems = sems, down_sems
        self.sec = lax.axis_index("section")
        self.first = self.sec == 0
        self.by_columns = by_columns
        self.wide = tile_at if by_columns else rows_at
        self.tiles, self.outs = self.gate.shape[1] // TILE, self.gate.shape[0] // TILE
        self.wide_count, self.deep_count = (self.tiles, self.outs) if by_columns else (self.outs, self.tiles)

    def here(self, j, target):
        return pltpu.make_async_copy(self.wide(self.own, j), self.wide(target, j), self.sems.at[0, j])

    def there(self, j, target):
        return pltpu.make_async_remote_copy(
            src_ref=self.wide(self.own, j),
            dst_ref=self.wide(target, j),
            send_sem=self.sems.at[1, j],
            recv_sem=self.sems.at[2, j],
            device_id={"section": 1 - self.sec},
            device_id_type=MESH,
        )

    def on_own(self, action):
        @pl.when(self.first)
        def _():
            action(self.gate, self.up)

        @pl.when(jnp.logical_not(self.first))
        def _():
            action(self.up, self.gate)

    def wait_gate(self, j):
        @pl.when(self.first)
        def _():
            self.here(j, self.gate).wait()

        @pl.when(jnp.logical_not(self.first))
        def _():
            self.there(j, self.gate).wait_recv()

    def wait_up(self, j):
        @pl.when(self.first)
        def _():
            self.there(j, self.up).wait_recv()

        @pl.when(jnp.logical_not(self.first))
        def _():
            self.here(j, self.up).wait()

    def down_parts(self, j):
        shards, half = self.down_own.shape[0], self.down_own.shape[1]
        per_tile = shards if not self.by_columns else shards // self.outs
        for i in range(per_tile):
            if self.by_columns:
                shard = j * per_tile + i
                source, columns = self.down_own.at[shard], slice(None)
            else:
                shard, columns = i, pl.ds(pl.multiple_of(j * TILE, TILE), TILE)
                source = self.down_own.at[shard, :, columns]

            def place(sec, shard=shard, columns=columns):
                return self.down.at[pl.ds(pl.multiple_of((2 * shard + sec) * half, 16), half), columns]

            yield source, place(self.sec), place(1 - self.sec), i

    def down_here(self, source, place, i, j):
        return pltpu.make_async_copy(source, place, self.down_sems.at[0, j, i])

    def down_there(self, source, place, i, j):
        return pltpu.make_async_remote_copy(
            src_ref=source,
            dst_ref=place,
            send_sem=self.down_sems.at[1, j, i],
            recv_sem=self.down_sems.at[2, j, i],
            device_id={"section": 1 - self.sec},
            device_id_type=MESH,
        )

    def start_wide(self, local):
        def action(own, other):
            @pl.loop(0, self.wide_count)
            def _(j):
                (self.here if local else self.there)(j, own).start()

        self.on_own(action)

    def start_deep(self, local):
        @pl.loop(0, self.deep_count)
        def _(j):
            for source, mine, theirs, i in self.down_parts(j):
                (self.down_here if local else self.down_there)(source, mine, i, j).start()

    def wait_down(self, j):
        for source, mine, theirs, i in self.down_parts(j):
            self.down_here(source, mine, i, j).wait()
            self.down_there(source, theirs, i, j).wait_recv()

    def finish(self):
        def action(own, other):
            @pl.loop(0, self.wide_count)
            def _(j):
                self.there(j, own).wait_send()

        self.on_own(action)

        @pl.loop(0, self.deep_count)
        def _(j):
            for source, mine, theirs, i in self.down_parts(j):
                self.down_there(source, mine, i, j).wait_send()


def ffn_forward_stage(weights, normed, outs, held, one, two, out_sems, result, tick, wait):
    gate, up, inner = held

    @pl.loop(0, weights.tiles)
    def _(j):
        if wait:
            weights.wait_gate(j)
        one[...] = mm(normed[...], tile_at(weights.gate, j)[...])
        tick(2 * j)
        if wait:
            weights.wait_up(j)
        two[...] = mm(normed[...], tile_at(weights.up, j)[...])
        columns = pl.ds(pl.multiple_of(j * TILE, TILE), TILE)

        def body(rows):
            g, u = one[rows], two[rows]
            gate[rows, columns] = g.astype(BF16)
            up[rows, columns] = u.astype(BF16)
            inner[rows, columns] = (g * jax.nn.sigmoid(g) * u).astype(BF16)

        by_rows(one.shape[0], body)
        tick(2 * j + 1)
        for k in range(3):
            pltpu.make_async_copy(tile_at(held[k], j), tile_at(outs[k], j), out_sems.at[k, j]).start()

    @pl.loop(0, weights.outs)
    def _(n):
        if wait:
            weights.wait_down(n)
        tile_at(result, n)[...] = mm_t(inner[...], rows_at(weights.down, n)[...]).astype(BF16)
        tick(2 * weights.tiles + n)

    return 2 * weights.tiles + weights.outs


def wait_out(held, outs, out_sems):
    @pl.loop(0, held[0].shape[1] // TILE)
    def _(j):
        for k in range(len(held)):
            pltpu.make_async_copy(tile_at(held[k], j), tile_at(outs[k], j), out_sems.at[k, j]).wait()


def ffn_forward_kernel(lead, *refs):
    take = Taker(refs)
    layer, attn_a, last_b, gain = take(4)
    layer_a, layer_b = ab(layer)
    sources = take(2)
    (normed_a, normed_b), *outs = [ab(ref) for ref in take(4)]
    outs_a, outs_b = zip(*outs)
    result_b, total_a = take(2)
    attn_b = take(1)[0] if lead else last_b
    targets, held = take(3), take(3)
    one, two, result_a, w_sems, down_sems, out_sems = take(6)
    chain_a = Chain(result_a, total_a, *take(CHAIN_REFS))
    chain_b = Chain(last_b, attn_b, *take(CHAIN_REFS)) if lead else None
    weights = FfnWeights(sources, targets, w_sems, down_sems, True)
    weights.start_wide(True)
    weights.start_deep(True)
    greet(cores=1)
    if lead:
        chain_b.start()
    weights.start_wide(False)
    weights.start_deep(False)
    normalize_rows(lambda r: layer_a[r].astype(F32) + attn_a[r].astype(F32), gain, normed_a)
    done = ffn_forward_stage(weights, normed_a, outs_a, held, one, two, out_sems, result_a, ticker(chain_b), True)
    chain_a.start()
    if lead:
        chain_b.finish(done)
    normalize_rows(lambda r: layer_b[r].astype(F32) + attn_b[r].astype(F32), gain, normed_b)
    wait_out(held, outs_a, out_sems)
    done = ffn_forward_stage(weights, normed_b, outs_b, held, one, two, out_sems, result_b, ticker(chain_a), False)
    chain_a.finish(done)
    weights.finish()
    wait_out(held, outs_b, out_sems)


def down_sem_shape(weights, tiles):
    return pltpu.SemaphoreType.DMA((3, tiles, weights[1].shape[0]))


def ffn_forward(lead, layer_in, attn_a, last_b, gain, weights):
    rows, width = attn_a.shape
    ff = weights[0].shape[1]
    tiles = max(ff, width) // TILE
    narrow = jax.ShapeDtypeStruct((rows, width), BF16)
    both, wide = jax.ShapeDtypeStruct((2 * rows, width), BF16), jax.ShapeDtypeStruct((2 * rows, ff), BF16)
    return pl.pallas_call(
        functools.partial(ffn_forward_kernel, lead),
        out_shape=[both, wide, wide, wide] + [narrow] * (2 + lead),
        in_specs=[VMEM] * 4 + [ANY] * 2,
        out_specs=[VMEM] + [ANY] * 3 + [VMEM] * (2 + lead),
        scratch_shapes=[pltpu.VMEM((width, ff), BF16)] * 3
        + [pltpu.VMEM((rows, ff), BF16)] * 3
        + [pltpu.VMEM((rows, TILE), F32)] * 2
        + [pltpu.VMEM((rows, width), BF16)]
        + [pltpu.SemaphoreType.DMA((3, tiles)), down_sem_shape(weights, tiles), pltpu.SemaphoreType.DMA((3, tiles))]
        + chain_scratch((rows, width)) * (1 + lead),
        compiler_params=params(1 + lead),
        cost_estimate=cost(),
    )(layer_in, attn_a, last_b, gain, *weights)


def ffn_backward_stage(weights, grad, ins, outs, held, one, in_sems, out_sems, result, tick, wait):
    gate, up = held
    own_out, other_out = outs

    @pl.loop(0, weights.tiles)
    def _(j):
        if wait:
            weights.wait_down(j)
        one[...] = mm(grad[...], tile_at(weights.down, j)[...])
        tick(j)
        for k in range(2):
            pltpu.make_async_copy(tile_at(ins[k], j), tile_at(held[k], j), in_sems.at[k, j]).wait()
        columns = pl.ds(pl.multiple_of(j * TILE, TILE), TILE)

        def body(rows):
            g, u, d = gate[rows, columns].astype(F32), up[rows, columns].astype(F32), one[rows]
            sig = jax.nn.sigmoid(g)
            d = d * sig
            gate[rows, columns] = (d * u * (1.0 + g * (1.0 - sig))).astype(BF16)
            up[rows, columns] = (d * g).astype(BF16)

        by_rows(one.shape[0], body)

    def sending(start):
        @pl.loop(0, weights.tiles)
        def _(j):
            own, other = tile_at(own_out, j), tile_at(other_out, j)
            send_either(weights.first, tile_at(gate, j), own, other, out_sems.at[0, j], start)
            send_either(weights.first, tile_at(up, j), other, own, out_sems.at[1, j], start)

    sending(True)

    @pl.loop(0, weights.outs)
    def _(n):
        if wait:
            weights.wait_gate(n)
            weights.wait_up(n)
        one[...] = mm_t(gate[...], rows_at(weights.gate, n)[...])
        tick(weights.tiles + 2 * n)
        tile_at(result, n)[...] = (one[...] + mm_t(up[...], rows_at(weights.up, n)[...])).astype(BF16)
        tick(weights.tiles + 2 * n + 1)

    return weights.tiles + 2 * weights.outs, lambda: sending(False)


def ffn_backward_kernel(low, *refs):
    take = Taker(refs)
    grad, last_b = take(2)
    grad_a, grad_b = ab(grad)
    ins_a, ins_b = zip(*[ab(ref) for ref in take(2)])
    sources = take(2)
    if low:
        sum_a, layer, gain = take(3)
        layer_a, layer_b = ab(layer)
    outs_a, outs_b = zip(*[ab(ref) for ref in take(2)])
    result_b, total_a, total_b = take(3)
    if low:
        made, gain_grad = take(2)
        made_a, made_b = ab(made)
    targets, held = take(3), take(2)
    one, result_a, w_sems, down_sems, in_sems, out_sems = take(6)
    chain_a = Chain(result_a, total_a, *take(CHAIN_REFS))
    chain_b = Chain(last_b, total_b, *take(CHAIN_REFS))
    weights = FfnWeights(sources, targets, w_sems, down_sems, False)

    def fetch(ins):
        @pl.loop(0, weights.tiles)
        def _(j):
            for k in range(2):
                pltpu.make_async_copy(tile_at(ins[k], j), tile_at(held[k], j), in_sems.at[k, j]).start()

    weights.start_deep(True)
    fetch(ins_a)
    weights.start_wide(True)
    greet(cores=1)
    chain_b.start()
    weights.start_deep(False)
    weights.start_wide(False)
    if low:
        gain_grad[...] = jnp.zeros_like(gain_grad)
        norm_back_rows(grad_a, sum_a, lambda r: layer_a[r].astype(F32), gain, gain_grad, made_a)
        grad_a = made_a
    done, sent_a = ffn_backward_stage(
        weights, grad_a, ins_a, outs_a, held, one, in_sems, out_sems, result_a, chain_b.step, True
    )
    chain_a.start()
    sent_a()
    fetch(ins_b)
    chain_b.finish(done)
    if low:
        norm_back_rows(grad_b, total_b, lambda r: layer_b[r].astype(F32), gain, gain_grad, made_b)
        grad_b = made_b
    done, sent_b = ffn_backward_stage(
        weights, grad_b, ins_b, outs_b, held, one, in_sems, out_sems, result_b, chain_a.step, False
    )
    chain_a.finish(done)
    weights.finish()
    sent_b()


def ffn_backward(grad, gate, up, weights, last_b, below=None):
    rows, width = last_b.shape
    ff = weights[0].shape[1]
    tiles = max(ff, width) // TILE
    low = below is not None
    narrow = jax.ShapeDtypeStruct((rows, width), BF16)
    both, wide = jax.ShapeDtypeStruct((2 * rows, width), BF16), jax.ShapeDtypeStruct((2 * rows, ff), BF16)
    more = [both, jax.ShapeDtypeStruct((8, width), F32)] if low else []
    return pl.pallas_call(
        functools.partial(ffn_backward_kernel, low),
        out_shape=[wide] * 2 + [narrow] * 3 + more,
        in_specs=[VMEM] * 2 + [ANY] * 4 + [VMEM] * (3 if low else 0),
        out_specs=[ANY] * 2 + [VMEM] * (3 + len(more)),
        scratch_shapes=[pltpu.VMEM((width, ff), BF16)] * 3
        + [pltpu.VMEM((rows, ff), BF16)] * 2
        + [pltpu.VMEM((rows, TILE), F32)]
        + [pltpu.VMEM((rows, width), BF16)]
        + [pltpu.SemaphoreType.DMA((3, tiles)), down_sem_shape(weights, tiles)]
        + [pltpu.SemaphoreType.DMA((2, tiles))] * 2
        + chain_scratch((rows, width)) * 2,
        compiler_params=params(3 + low),
        cost_estimate=cost(),
    )(grad, last_b, gate, up, *weights, *(below or ()))


def last_kernel(part, sum_a, grad, layer, gain, made, gain_grad, total, *scratch):
    chain = Chain(part, total, *scratch)
    greet()
    chain.start()
    gain_grad[...] = jnp.zeros_like(gain_grad)
    grads, layers, mades = ab(grad), ab(layer), ab(made)
    chain.step(0)
    norm_back_rows(grads[0], sum_a, lambda r: layers[0][r].astype(F32), gain, gain_grad, mades[0])
    chain.finish(1)
    norm_back_rows(grads[1], total, lambda r: layers[1][r].astype(F32), gain, gain_grad, mades[1])


def last_grads(part, sum_a, grad, layer, gain):
    shape = part.shape
    return pl.pallas_call(
        last_kernel,
        out_shape=[jax.ShapeDtypeStruct(grad.shape, BF16), jax.ShapeDtypeStruct((8, shape[1]), F32)],
        in_specs=[VMEM] * 5,
        out_specs=[VMEM] * 2,
        scratch_shapes=[pltpu.VMEM(shape, BF16)] + chain_scratch(shape),
        compiler_params=params(0),
        cost_estimate=cost(),
    )(part, sum_a, grad, layer, gain)


def roped(values, cosine, sine):
    return values * cosine + pltpu.roll(values, HEAD // 2, 1) * sine


def unroped(grads, cosine, sine):
    return grads * cosine + pltpu.roll(grads * sine, HEAD // 2, 1)


def allowed_keys(seg_rows, seg_keys, i, block):
    rows, keys = seg_rows.shape[0], seg_keys.shape[1]
    first_row = lax.axis_index("ctx") * rows + i * block
    row_at = first_row + lax.broadcasted_iota(jnp.int32, (block, keys), 0)
    key_at = lax.broadcasted_iota(jnp.int32, (block, keys), 1)
    own = seg_rows[pl.ds(pl.multiple_of(i * block, block), block)]
    return (key_at <= row_at) & (own == seg_keys[...])


def attention_forward_stage(layer_in, gain, w_lin, w_out, bias, places, outs, result, kv_sems, tick):
    cosine, sine, seg_rows, seg_keys = places
    normed, query, kv, lse, attended = outs
    rows, q_cols = query.shape
    heads = q_cols // HEAD
    count = kv.shape[0] // rows
    me = lax.axis_index("ctx")
    block = min(256, rows)
    normalize_rows(lambda r: layer_in[r].astype(F32), gain, normed)
    mine = kv.at[pl.ds(pl.multiple_of(me * rows, rows), rows)]
    lin = mm(normed[...], w_lin[:, q_cols:]) + bias[:, q_cols:]
    mine[:, :HEAD] = roped(lin[:, :HEAD], cosine[...], sine[...]).astype(BF16)
    mine[:, HEAD:] = lin[:, HEAD:].astype(BF16)

    def passing(offset):
        return pltpu.make_async_remote_copy(
            src_ref=mine,
            dst_ref=mine,
            send_sem=kv_sems.at[0, offset],
            recv_sem=kv_sems.at[1, offset],
            device_id={"ctx": lax.rem(me + offset, count)},
            device_id_type=MESH,
        )

    for offset in range(1, count):
        passing(offset).start()
    tick(0)
    lin = mm(normed[...], w_lin[:, :q_cols]) + bias[:, :q_cols]
    for h in range(heads):
        columns = slice(h * HEAD, (h + 1) * HEAD)
        query[:, columns] = roped(lin[:, columns], cosine[...], sine[...]).astype(BF16)
    for offset in range(1, count):
        passing(offset).wait_recv()

    @pl.loop(0, rows // block)
    def _(i):
        at = pl.ds(pl.multiple_of(i * block, block), block)
        allowed = allowed_keys(seg_rows, seg_keys, i, block)
        lane = lax.broadcasted_iota(jnp.int32, (block, HEAD), 1)
        logs = jnp.zeros((block, HEAD), F32)
        for h in range(heads):
            columns = slice(h * HEAD, (h + 1) * HEAD)
            scores = jnp.where(allowed, mm_t(query[at, columns], kv[:, :HEAD]) * SCALE, NEG)
            top = jnp.max(scores, axis=-1, keepdims=True)
            probs = jnp.exp(scores - top)
            sums = jnp.sum(probs, axis=-1, keepdims=True)
            probs = (probs * (1.0 / sums)).astype(BF16)
            attended[at, columns] = mm(probs, kv[:, HEAD:]).astype(BF16)
            logs = jnp.where(lane == h, top + jnp.log(sums), logs)
            tick(1 + heads * i + h)
        lse[at] = logs

    base = 1 + heads * (rows // block)

    @pl.loop(0, result.shape[1] // TILE)
    def _(n):
        tile_at(result, n)[...] = mm_t(attended[...], rows_at(w_out, n)[...]).astype(BF16)
        tick(base + n)

    for offset in range(1, count):
        passing(offset).wait_send()
    return base + result.shape[1] // TILE


def attention_forward_kernel(low, *refs):
    take = Taker(refs)
    gain, w_lin, w_out, bias = take(4)
    places_a, places_b = take(4), take(4)
    layer_a, layer_b = ab(take(1)[0])
    if not low:
        adds_a, adds_b, (last_b,) = (layer_a, *take(2)), (layer_b, *take(1)), take(1)
    outs_a, outs_b = zip(*[ab(ref) for ref in take(5)])
    if low:
        total_a, total_b = take(2)
    else:
        result_b, total_a, last_sum_b, layer = take(4)
        layer_a, layer_b = ab(layer)
    result_a, kv_sems_a, kv_sems_b = take(3)
    if low:
        (result_b,) = take(1)
    chain_a = Chain(result_a, total_a, *take(CHAIN_REFS))
    chain_b = Chain(result_b, total_b, *take(CHAIN_REFS)) if low else Chain(last_b, last_sum_b, *take(CHAIN_REFS))
    greet(kv_sems_a.shape[1])
    if not low:
        chain_b.start()

        def body(rows):
            layer_a[rows] = sum(ref[rows].astype(F32) for ref in adds_a).astype(BF16)

        by_rows(layer_a.shape[0], body)
    tick = ticker(None if low else chain_b)
    done = attention_forward_stage(layer_a, gain, w_lin, w_out, bias, places_a, outs_a, result_a, kv_sems_a, tick)
    chain_a.start()
    if not low:
        chain_b.finish(done)

        def body(rows):
            layer_b[rows] = sum(ref[rows].astype(F32) for ref in (*adds_b, last_sum_b)).astype(BF16)

        by_rows(layer_b.shape[0], body)
    done = attention_forward_stage(layer_b, gain, w_lin, w_out, bias, places_b, outs_b, result_b, kv_sems_b, chain_a.step)
    if low:
        chain_b.start()
    chain_a.finish(done)
    if low:
        chain_b.finish(0)


def attention_forward(weights, places, inputs):
    w_lin, w_out, gains, bias = weights
    rows, width = inputs[0].shape[0] // 2, inputs[0].shape[1]
    q_cols = w_out.shape[1]
    keys = places[0][3].shape[1]
    count = keys // rows
    low = len(inputs) == 1
    narrow, both = jax.ShapeDtypeStruct((rows, width), BF16), jax.ShapeDtypeStruct((2 * rows, width), BF16)
    heads_out = jax.ShapeDtypeStruct((2 * rows, q_cols), BF16)
    kv_out = jax.ShapeDtypeStruct((2 * keys, 2 * HEAD), BF16)
    lse_out = jax.ShapeDtypeStruct((2 * rows, HEAD), F32)
    outs = [both, heads_out, kv_out, lse_out, heads_out] + ([narrow] * 2 if low else [narrow] * 3 + [both])
    args = (gains[:1], w_lin, w_out, bias, *places[0], *places[1], *inputs)
    return pl.pallas_call(
        functools.partial(attention_forward_kernel, low),
        out_shape=outs,
        in_specs=[VMEM] * len(args),
        out_specs=[VMEM] * len(outs),
        scratch_shapes=[pltpu.VMEM((rows, width), BF16)]
        + [pltpu.SemaphoreType.DMA((2, count))] * 2
        + [pltpu.VMEM((rows, width), BF16)] * low
        + chain_scratch((rows, width)) * 2,
        compiler_params=params(5 + low),
        cost_estimate=cost(),
    )(*args)


def attention_backward_stage(ins, sum_in, gain, w_lin, w_out, places, outs, gain_grad, result, scratch, tick):
    upstream, layer_in, attn_out, query, kv, lse, attended = ins
    cosine, sine, seg_rows, seg_keys = places
    attn_grad, lin = outs
    heads_grad, kv_grad, q_part, sent, got, kv_sems = scratch
    rows, q_cols = query.shape
    heads = q_cols // HEAD
    count = kv.shape[0] // rows
    me = lax.axis_index("ctx")
    block = min(256, rows)
    kv_grad[...] = jnp.zeros_like(kv_grad)
    norm_back_rows(
        upstream, sum_in, lambda r: layer_in[r].astype(F32) + attn_out[r].astype(F32), gain, gain_grad, attn_grad
    )
    heads_grad[...] = mm(attn_grad[...], w_out[...]).astype(BF16)
    tick(0)

    @pl.loop(0, rows // block)
    def _(i):
        at = pl.ds(pl.multiple_of(i * block, block), block)
        allowed = allowed_keys(seg_rows, seg_keys, i, block)
        for h in range(heads):
            columns = slice(h * HEAD, (h + 1) * HEAD)
            scores = mm_t(query[at, columns], kv[:, :HEAD]) * SCALE - lse[at, h : h + 1]
            probs = jnp.exp(jnp.where(allowed, scores, NEG))
            grad = heads_grad[at, columns]
            row_sum = jnp.sum(attended[at, columns].astype(F32) * grad.astype(F32), axis=-1, keepdims=True)
            score_grad = (probs * (mm_t(grad, kv[:, HEAD:]) - row_sum)).astype(BF16)
            q_grad = mm(score_grad, kv[:, :HEAD]) * SCALE
            lin[at, columns] = unroped(q_grad, cosine[at], sine[at]).astype(BF16)
            kv_grad[:, :HEAD] += mm_0(score_grad, query[at, columns])
            kv_grad[:, HEAD:] += mm_0(probs.astype(BF16), grad)
            tick(1 + heads * i + h)

    def passing(offset):
        return pltpu.make_async_remote_copy(
            src_ref=sent.at[offset - 1],
            dst_ref=got.at[offset - 1],
            send_sem=kv_sems.at[0, offset],
            recv_sem=kv_sems.at[1, offset],
            device_id={"ctx": lax.rem(me + offset, count)},
            device_id_type=MESH,
        )

    for offset in range(1, count):
        peer = pl.ds(pl.multiple_of(lax.rem(me + offset, count) * rows, rows), rows)
        sent[offset - 1, :, :HEAD] = (kv_grad[peer, :HEAD] * SCALE).astype(BF16)
        sent[offset - 1, :, HEAD:] = kv_grad[peer, HEAD:].astype(BF16)
        passing(offset).start()
    base = 1 + heads * (rows // block)

    @pl.loop(0, result.shape[1] // TILE)
    def _(n):
        tile_at(q_part, n)[...] = mm_t(lin[:, :q_cols], rows_at(w_lin, n)[:, :q_cols])
        tick(base + n)

    mine = pl.ds(pl.multiple_of(me * rows, rows), rows)
    k_grad, v_grad = kv_grad[mine, :HEAD] * SCALE, kv_grad[mine, HEAD:]
    for offset in range(1, count):
        passing(offset).wait_recv()
        k_grad = k_grad + got[offset - 1, :, :HEAD].astype(F32)
        v_grad = v_grad + got[offset - 1, :, HEAD:].astype(F32)
    lin[:, q_cols : q_cols + HEAD] = unroped(k_grad, cosine[...], sine[...]).astype(BF16)
    lin[:, q_cols + HEAD :] = v_grad.astype(BF16)

    @pl.loop(0, result.shape[1] // TILE)
    def _(n):
        kv_part = mm_t(lin[:, q_cols:], rows_at(w_lin, n)[:, q_cols:])
        tile_at(result, n)[...] = (tile_at(q_part, n)[...] + kv_part).astype(BF16)


    for offset in range(1, count):
        passing(offset).wait_send()
    return base + result.shape[1] // TILE


def attention_backward_kernel(*refs):
    take = Taker(refs)
    gain, w_lin, w_out = take(3)
    places_a, places_b = take(4), take(4)
    ins_a, ins_b = zip(*[ab(ref) for ref in take(6)])
    attn_a, attn_b = take(2)
    ins_a, ins_b = (*ins_a[:2], attn_a, *ins_a[2:]), (*ins_b[:2], attn_b, *ins_b[2:])
    sum_a, last_b = take(2)
    outs_a, outs_b = zip(*[ab(ref) for ref in take(2)])
    gain_grad, result_b, total_a, total_b = take(4)
    heads_grad, kv_grad, q_part, result_a = take(4)
    exchange_a, exchange_b = take(3), take(3)
    chain_a = Chain(result_a, total_a, *take(CHAIN_REFS))
    chain_b = Chain(last_b, total_b, *take(CHAIN_REFS))
    greet(exchange_a[2].shape[1])
    chain_b.start()
    gain_grad[...] = jnp.zeros_like(gain_grad)
    scratch = (heads_grad, kv_grad, q_part, *exchange_a)
    done = attention_backward_stage(
        ins_a, sum_a, gain, w_lin, w_out, places_a, outs_a, gain_grad, result_a, scratch, chain_b.step
    )
    chain_a.start()
    chain_b.finish(done)
    scratch = (heads_grad, kv_grad, q_part, *exchange_b)
    done = attention_backward_stage(
        ins_b, total_b, gain, w_lin, w_out, places_b, outs_b, gain_grad, result_b, scratch, chain_a.step
    )
    chain_a.finish(done)


def attention_backward(upstream, sum_a, last_b, kept, weights, places):
    w_lin, w_out, gains, bias = weights
    rows, width = sum_a.shape
    q_cols = w_out.shape[1]
    keys = places[0][3].shape[1]
    count = keys // rows
    narrow = jax.ShapeDtypeStruct((rows, width), BF16)
    both = jax.ShapeDtypeStruct((2 * rows, width), BF16)
    lin_out = jax.ShapeDtypeStruct((2 * rows, q_cols + 2 * HEAD), BF16)
    outs = [both, lin_out] + [jax.ShapeDtypeStruct((8, width), F32)] + [narrow] * 3
    names = ("layer_in", "query", "kv", "lse", "attended", "attn_a", "attn_b")
    args = (gains[1:], w_lin, w_out, *places[0], *places[1], upstream)
    args += (*[kept[name] for name in names], sum_a, last_b)
    exchange = [pltpu.VMEM((max(count - 1, 1), rows, 2 * HEAD), BF16)] * 2 + [pltpu.SemaphoreType.DMA((2, count))]
    return pl.pallas_call(
        attention_backward_kernel,
        out_shape=outs,
        in_specs=[VMEM] * len(args),
        out_specs=[VMEM] * len(outs),
        scratch_shapes=[
            pltpu.VMEM((rows, q_cols), BF16),
            pltpu.VMEM((keys, 2 * HEAD), F32),
            pltpu.VMEM((rows, width), F32),
            pltpu.VMEM((rows, width), BF16),
        ]
        + exchange * 2
        + chain_scratch((rows, width)) * 2,
        compiler_params=params(7),
        cost_estimate=cost(),
    )(*args)


def rope_tables(places):
    steps = jnp.arange(HEAD // 2, dtype=F32) * (2.0 / HEAD)
    inverse = ROPE_BASE ** (-steps)
    angles = places.astype(F32)[..., None] * inverse
    angles = jnp.concatenate([angles, angles], axis=-1)
    return (jnp.cos(angles), jnp.sin(angles))


def over_ctx(value):
    if lax.axis_size("ctx") == 2:
        other = lax.ppermute(value, "ctx", [(0, 1), (1, 0)])
        low = lax.axis_index("ctx") == 0
        return jnp.concatenate([jnp.where(low, value, other), jnp.where(low, other, value)], axis=-1)
    return lax.all_gather(value, "ctx", axis=value.ndim - 1, tiled=True)


def local(
    section_in,
    segments,
    positions,
    query_weight,
    kv_weight,
    output_weight,
    gate_up,
    down_weight,
    norm_gains,
    query_bias,
    kv_bias,
    out_grad,
):
    sec = lax.axis_index("section")
    first = sec == 0
    group = HEADS // KV_HEADS
    heads_here = HEADS // lax.axis_size("tp")
    head_pick = lax.axis_index("tp") * heads_here // group
    shards = lax.axis_size("dp") * lax.axis_size("ctx")
    ranks = ("dp", "ctx")
    seqs, span, width = section_in.shape[1:]
    shard = query_weight.shape[1]
    q_cols = query_weight.shape[2]
    ff = gate_up.shape[3]

    def per_layer(mine, theirs):
        return jnp.where(first, mine, theirs), jnp.where(first, theirs, mine)

    half = shard // 2
    kv_width = KV_HEADS * HEAD

    def halves(rows):
        mine = lax.dynamic_slice_in_dim(rows, sec * half, half, 0)
        return per_layer(mine, swap(lax.dynamic_slice_in_dim(rows, (1 - sec) * half, half, 0)))

    def joined(own):
        return jnp.stack(per_layer(own, swap(own)), axis=1).reshape(width, own.shape[-1])

    def after(value, event):
        return lax.optimization_barrier((value, event))[0]

    piece = HEAD // shards
    biases = jnp.concatenate([query_bias[0].reshape(-1), kv_bias[0].reshape(-1)])
    n_biases = biases.shape[0]
    biases = jnp.pad(biases, (0, -n_biases % shard)).reshape(-1, shard).T
    extra = jnp.concatenate([norm_gains[0].T, biases], axis=1)
    n_extra = extra.shape[1]
    extra = jnp.pad(extra, ((0, 0), (0, HEAD - n_extra)))
    packed = jnp.concatenate([query_weight[0], kv_weight[0, 0], kv_weight[0, 1], output_weight[0].T, extra], axis=1)
    packed_shards = halves(packed)
    spare = -ff % TILE
    wide = jnp.pad(gate_up[0], ((0, 0), (0, 0), (0, spare)))
    mine = lax.dynamic_index_in_dim(wide, sec, 0, keepdims=False)
    theirs = swap(lax.dynamic_index_in_dim(wide, 1 - sec, 0, keepdims=False))
    gate_up_shards = per_layer(mine, theirs)
    down_shards = halves(jnp.pad(down_weight[0].T, ((0, 0), (0, spare))))

    micro = sec
    seg = lax.dynamic_index_in_dim(segments, micro, 0, keepdims=False)
    pos = lax.dynamic_index_in_dim(positions, micro, 0, keepdims=False)
    hidden = lax.dynamic_index_in_dim(section_in, micro, 0, keepdims=False)
    seg_keys = over_ctx(seg)
    segs, tables = [], []
    for q in range(seqs):
        segs.append((seg[q][:, None], seg_keys[q][None]))
        cosine, sine = rope_tables(pos[q])
        tables.append((cosine, jnp.where(jnp.arange(HEAD) < HEAD // 2, -sine, sine)))
    hidden = hidden.reshape(seqs * span, width)

    packed_low = lax.all_gather(packed_shards[0], ranks, axis=0)
    packed_low, gate_up_shards, down_shards, packed_shards, segs, tables, hidden = lax.optimization_barrier(
        (packed_low, gate_up_shards, down_shards, packed_shards, segs, tables, hidden)
    )
    own_low = lax.all_gather(gate_up_shards[0], ranks, axis=0, tiled=True)
    down_low = lax.all_gather(down_shards[0], ranks, axis=0)

    def attention_weights(own):
        p = joined(own)
        wq = p[:, :q_cols]
        wk = lax.dynamic_slice_in_dim(p[:, q_cols : q_cols + kv_width], head_pick * HEAD, HEAD, 1)
        wv = lax.dynamic_slice_in_dim(p[:, q_cols + kv_width : q_cols + 2 * kv_width], head_pick * HEAD, HEAD, 1)
        wo = p[:, q_cols + 2 * kv_width : 2 * q_cols + 2 * kv_width]
        s = p[:, 2 * q_cols + 2 * kv_width :]
        gains = s[:, :2].T
        s = s[:, 2:n_extra].T.reshape(-1, shards, shard).transpose(1, 0, 2).reshape(shards, -1)[:, :n_biases]
        q_b = s[:, : heads_here * piece].reshape(shards, heads_here, piece).transpose(1, 0, 2).reshape(heads_here, HEAD)
        kv_b = s[:, heads_here * piece :].reshape(shards, 2, KV_HEADS, piece)
        kv_b = kv_b.transpose(1, 2, 0, 3).reshape(2, KV_HEADS, HEAD)
        kv_b = lax.dynamic_slice_in_dim(kv_b, head_pick, 1, 1)
        bias = jnp.concatenate([q_b.reshape(1, -1), kv_b.reshape(1, -1)], axis=1).astype(F32)
        return jnp.concatenate([wq, wk, wv], axis=1), wo, gains.astype(F32), bias

    names = ("layer_in", "query", "kv", "lse", "attended", "attn_a", "attn_b")
    args = (gains[1:], w_lin, w_out, *places[0], *places[1], upstream)
    args += (*[kept[name] for name in names], sum_a, last_b)
    exchange = [pltpu.VMEM((max(count - 1, 1), rows, 2 * HEAD), BF16)] * 2 + [pltpu.SemaphoreType.DMA((2, count))]
    return pl.pallas_call(
        attention_backward_kernel,
        out_shape=outs,
        in_specs=[VMEM] * len(args),
        out_specs=[VMEM] * len(outs),
        scratch_shapes=[
            pltpu.VMEM((rows, q_cols), BF16),
            pltpu.VMEM((keys, 2 * HEAD), F32),
            pltpu.VMEM((rows, width), F32),
            pltpu.VMEM((rows, width), BF16),
        ]
        + exchange * 2
        + chain_scratch((rows, width)) * 2,
        compiler_params=params(7),
        cost_estimate=cost(),
    )(*args)


def rope_tables(places):
    steps = jnp.arange(HEAD // 2, dtype=F32) * (2.0 / HEAD)
    inverse = ROPE_BASE ** (-steps)
    angles = places.astype(F32)[..., None] * inverse
    angles = jnp.concatenate([angles, angles], axis=-1)
    return (jnp.cos(angles), jnp.sin(angles))


def norm_back(grad_out, rows_in, factor, gain):
    unit = rows_in * factor
    gain_grad = jnp.sum(grad_out * unit, axis=0)
    weighted = grad_out * gain
    return (
        factor * (weighted - unit * jnp.mean(weighted * unit, axis=-1, keepdims=True)),
        gain_grad,
    )


def over_ctx(value):
    if lax.axis_size("ctx") == 2:
        other = lax.ppermute(value, "ctx", [(0, 1), (1, 0)])
        low = lax.axis_index("ctx") == 0
        return jnp.concatenate([jnp.where(low, value, other), jnp.where(low, other, value)], axis=-1)
    return lax.all_gather(value, "ctx", axis=value.ndim - 1, tiled=True)


def input_backward(normed_one_grad, middle_grad, kept, gains):
    layer_in = kept["layer_in"].astype(F32)
    factor = lax.rsqrt(jnp.mean(layer_in * layer_in, axis=-1, keepdims=True) + EPS)
    norm_grad, gain_one = norm_back(normed_one_grad.astype(F32), layer_in, factor, gains[0])
    return (middle_grad.astype(F32) + norm_grad).astype(BF16), gain_one


def local(
    section_in,
    segments,
    positions,
    query_weight,
    kv_weight,
    output_weight,
    gate_up,
    down_weight,
    norm_gains,
    query_bias,
    kv_bias,
    out_grad,
):
    sec = lax.axis_index("section")
    first = sec == 0
    group = HEADS // KV_HEADS
    heads_here = HEADS // lax.axis_size("tp")
    head_pick = lax.axis_index("tp") * heads_here // group
    shards = lax.axis_size("dp") * lax.axis_size("ctx")
    ranks = ("dp", "ctx")
    seqs, span, width = section_in.shape[1:]
    shard = query_weight.shape[1]
    q_cols = query_weight.shape[2]
    ff = gate_up.shape[3]

    def per_layer(mine, theirs):
        return jnp.where(first, mine, theirs), jnp.where(first, theirs, mine)

    half = shard // 2
    kv_width = KV_HEADS * HEAD

    def halves(rows):
        mine = lax.dynamic_slice_in_dim(rows, sec * half, half, 0)
        return per_layer(mine, swap(lax.dynamic_slice_in_dim(rows, (1 - sec) * half, half, 0)))

    def joined(own):
        return jnp.stack(per_layer(own, swap(own)), axis=1).reshape(width, own.shape[-1])

    def after(value, event):
        return lax.optimization_barrier((value, event))[0]

    piece = HEAD // shards
    biases = jnp.concatenate([query_bias[0].reshape(-1), kv_bias[0].reshape(-1)])
    n_biases = biases.shape[0]
    biases = jnp.pad(biases, (0, -n_biases % shard)).reshape(-1, shard).T
    extra = jnp.concatenate([norm_gains[0].T, biases], axis=1)
    n_extra = extra.shape[1]
    extra = jnp.pad(extra, ((0, 0), (0, HEAD - n_extra)))
    packed = jnp.concatenate([query_weight[0], kv_weight[0, 0], kv_weight[0, 1], output_weight[0].T, extra], axis=1)
    packed_shards = halves(packed)
    spare = -ff % TILE
    wide = jnp.pad(gate_up[0], ((0, 0), (0, 0), (0, spare)))
    mine = lax.dynamic_index_in_dim(wide, sec, 0, keepdims=False)
    theirs = swap(lax.dynamic_index_in_dim(wide, 1 - sec, 0, keepdims=False))
    gate_up_shards = per_layer(mine, theirs)
    down_shards = halves(jnp.pad(down_weight[0].T, ((0, 0), (0, spare))))

    micro = sec
    seg = lax.dynamic_index_in_dim(segments, micro, 0, keepdims=False)
    pos = lax.dynamic_index_in_dim(positions, micro, 0, keepdims=False)
    hidden = lax.dynamic_index_in_dim(section_in, micro, 0, keepdims=False)
    seg_keys = over_ctx(seg)
    segs, tables = [], []
    for q in range(seqs):
        segs.append((seg[q][:, None], seg_keys[q][None]))
        cosine, sine = rope_tables(pos[q])
        tables.append((cosine, jnp.where(jnp.arange(HEAD) < HEAD // 2, -sine, sine)))
    hidden = hidden.reshape(seqs * span, width)

    packed_low = lax.all_gather(packed_shards[0], ranks, axis=0)
    packed_low, gate_up_shards, down_shards, packed_shards, segs, tables, hidden = lax.optimization_barrier(
        (packed_low, gate_up_shards, down_shards, packed_shards, segs, tables, hidden)
    )
    own_low = lax.all_gather(gate_up_shards[0], ranks, axis=0, tiled=True)
    down_low = lax.all_gather(down_shards[0], ranks, axis=0)

    def attention_weights(own):
        p = joined(own)
        wq = p[:, :q_cols]
        wk = lax.dynamic_slice_in_dim(p[:, q_cols : q_cols + kv_width], head_pick * HEAD, HEAD, 1)
        wv = lax.dynamic_slice_in_dim(p[:, q_cols + kv_width : q_cols + 2 * kv_width], head_pick * HEAD, HEAD, 1)
        wo = p[:, q_cols + 2 * kv_width : 2 * q_cols + 2 * kv_width]
        s = p[:, 2 * q_cols + 2 * kv_width :]
        gains = s[:, :2].T
        s = s[:, 2:n_extra].T.reshape(-1, shards, shard).transpose(1, 0, 2).reshape(shards, -1)[:, :n_biases]
        q_b = s[:, : heads_here * piece].reshape(shards, heads_here, piece).transpose(1, 0, 2).reshape(heads_here, HEAD)
        kv_b = s[:, heads_here * piece :].reshape(shards, 2, KV_HEADS, piece)
        kv_b = kv_b.transpose(1, 2, 0, 3).reshape(2, KV_HEADS, HEAD)
        kv_b = lax.dynamic_slice_in_dim(kv_b, head_pick, 1, 1)
        bias = jnp.concatenate([q_b.reshape(1, -1), kv_b.reshape(1, -1)], axis=1).astype(F32)
        return jnp.concatenate([wq, wk, wv], axis=1), wo, gains.astype(F32), bias

    kept = [[dict(), dict()] for _ in range(2)]
    names = ("normed", "query", "kv", "lse", "attended")
    more_names = ("normed_two", "gate", "up", "inner")
    attn_weights, ffn_weights = [attention_weights(packed_low), None], [None, None]
    places = [(*tables[q], *segs[q]) for q in range(seqs)]

    def keep(layer, names, values):
        kept[layer].update(zip(names, values))
        return values[len(names) :]

    kept = [dict(), dict()]
    attn_a, attn_b = keep(0, names, attention_forward(attn_weights[0], places, (hidden,)))
    kept[0].update(layer_in=hidden, attn_a=attn_a, attn_b=attn_b)
    attn_b, own_low, down_low = lax.optimization_barrier((attn_b, own_low, down_low))
    ffn_weights[0] = own_low, down_low
    packed_high = lax.all_gather(after(packed_shards[1], attn_b), ranks, axis=0)
    own_high = lax.all_gather(after(gate_up_shards[1], attn_b), ranks, axis=0, tiled=True)
    down_high = lax.all_gather(after(down_shards[1], attn_b), ranks, axis=0)
    gain = attn_weights[0][2][1:]
    part_b, ffn_a = keep(
        0, more_names, ffn_forward(False, hidden, attn_a, attn_b, gain, ffn_weights[0])
    )

    packed_high, part_b = lax.optimization_barrier((packed_high, part_b))
    attn_weights[1] = attention_weights(packed_high)
    inputs = (hidden, attn_a, ffn_a, attn_b, part_b)
    part_b, attn_a, _, layer_in = keep(1, names, attention_forward(attn_weights[1], places, inputs))
    part_b, own_high, down_high = lax.optimization_barrier((part_b, own_high, down_high))
    ffn_weights[1] = own_high, down_high
    gain = attn_weights[1][2][1:]
    part_b, ffn_a, attn_b = keep(
        1, more_names, ffn_forward(True, layer_in, attn_a, part_b, gain, ffn_weights[1])
    )
    kept[1].update(layer_in=layer_in, attn_a=attn_a, attn_b=attn_b)
    upstream = lax.dynamic_index_in_dim(out_grad, micro, 0, keepdims=False).reshape(seqs * span, width)
    k = kept[1]
    *wide_grads, grad_b, sum_a, ffn_b = ffn_backward(upstream, k["gate"], k["up"], ffn_weights[1], part_b)
    attn_sum, ffn_sum = jnp.concatenate([attn_a, attn_b]), jnp.concatenate([ffn_a, ffn_b])
    outs = [layer_in, (layer_in.astype(F32) + attn_sum.astype(F32) + ffn_sum.astype(F32)).astype(BF16)]

    def to_section(values):
        low = lax.ppermute(values[0], "section", [(1, 0)])
        high = lax.ppermute(values[1], "section", [(0, 1)])
        both = jnp.stack([jnp.where(first, values[0], high), jnp.where(first, low, values[1])])
        return both.reshape(2, seqs, span, width)

    section_out = to_section(outs)

    in_grads = [None, None]
    gate_up_grads, down_grads, packed_grads, gains_grads = [[None, None] for _ in range(4)]
    for layer in (1, 0):
        weights, k = attn_weights[layer], kept[layer]
        if layer == 0:
            below = (sum_a, kept[1]["layer_in"], attn_weights[1][2][:1])
            *wide_grads, grad_b, sum_a, _, upstream, gain_one = ffn_backward(
                attn_grad, k["gate"], k["up"], ffn_weights[0], part_b, below
            )
            in_grads[1] = upstream
            gains_grads[1] = jnp.stack([jnp.sum(gain_one, axis=0), gain_two])
            sum_a, gate_up_grads[1] = lax.optimization_barrier((sum_a, gate_up_grads[1]))
        own_w, other_w = [dot("rd,rf->df", k["normed_two"], g).astype(BF16) for g in wide_grads]
        own_w = (own_w.astype(F32) + swap(other_w).astype(F32)).astype(BF16)
        own_w, sum_a = lax.optimization_barrier((own_w, sum_a))
        gate_up_grads[layer] = lax.psum_scatter(own_w, ranks, scatter_dimension=0, tiled=True)
        down_w = dot("rd,rf->df", upstream, k["inner"]).astype(BF16)
        down_w = down_w.reshape(shards, 2, half, ff + spare)
        down_own = lax.dynamic_index_in_dim(down_w, sec, 1, keepdims=False)
        down_other = lax.dynamic_index_in_dim(down_w, 1 - sec, 1, keepdims=False)
        down_own = (down_own.astype(F32) + swap(down_other).astype(F32)).astype(BF16)
        down_own, sum_a = lax.optimization_barrier((down_own, sum_a))
        down_grads[layer] = lax.psum_scatter(
            down_own.reshape(shards * half, ff + spare), ranks, scatter_dimension=0, tiled=True
        )

        attn_grad, lin_grad, gain_two, part_b, sum_a, _ = attention_backward(upstream, sum_a, grad_b, k, weights, places)
        gain_two = jnp.sum(gain_two, axis=0)
        if layer == 0:
            part_b, down_grads[1] = lax.optimization_barrier((part_b, down_grads[1]))
        lin_w = dot("rd,re->de", k["normed"], lin_grad)
        out_w = dot("rd,re->de", attn_grad, k["attended"])
        bias = jnp.sum(lin_grad.astype(F32), axis=0)
        bias = bias.reshape(heads_here + 2, shards, piece).transpose(1, 0, 2).reshape(shards, (heads_here + 2) * piece)
        bias = jnp.pad(bias, ((0, 0), (0, -bias.shape[1] % shard)))
        bias = bias.reshape(shards, -1, shard).transpose(0, 2, 1).reshape(width, -1)
        bias = jnp.pad(bias, ((0, 0), (0, HEAD - bias.shape[1])))
        packed_grads[layer] = jnp.concatenate([lin_w, out_w, bias], axis=1).astype(BF16)

    low = lax.ppermute(packed_grads[0], "section", [(1, 0)])
    high = lax.ppermute(packed_grads[1], "section", [(0, 1)])
    packed_total = jnp.where(
        first, packed_grads[0].astype(F32) + low.astype(F32), packed_grads[1].astype(F32) + high.astype(F32)
    ).astype(BF16)
    last_part, gate_up_grads[0], down_grads[0], packed_total = lax.optimization_barrier(
        (part_b, gate_up_grads[0], down_grads[0], packed_total)
    )
    packed_total = lax.psum_scatter(packed_total, ranks, scatter_dimension=0, tiled=True).astype(F32)
    in_grads[0], gain_one = last_grads(last_part, sum_a, attn_grad, kept[0]["layer_in"], attn_weights[0][2][:1])
    gains_grads[0] = jnp.stack([jnp.sum(gain_one, axis=0), gain_two])
    input_grad = to_section(in_grads)
    low = lax.ppermute(gains_grads[0], "section", [(1, 0)])
    high = lax.ppermute(gains_grads[1], "section", [(0, 1)])
    gains_grad = jnp.where(first, gains_grads[0] + low, gains_grads[1] + high)
    for axis in ranks:
        if lax.axis_size(axis) == 2:
            gains_grad = gains_grad + lax.ppermute(gains_grad, axis, [(0, 1), (1, 0)])
        else:
            gains_grad = lax.psum(gains_grad, axis)
    at = (lax.axis_index("dp") * lax.axis_size("ctx") + lax.axis_index("ctx")) * shard
    gains_grad = lax.dynamic_slice_in_dim(gains_grad, at, shard, 1)
    q_grad = packed_total[:, :q_cols]
    kv_narrow = packed_total[:, q_cols : q_cols + 2 * HEAD].reshape(shard, 2, HEAD)
    o_grad = packed_total[:, q_cols + 2 * HEAD : 2 * q_cols + 2 * HEAD].T
    extra = packed_total[:, 2 * q_cols + 2 * HEAD :]
    bias_cols = -(-(heads_here + 2) * piece // shard)
    bias = extra[:, :bias_cols].T.reshape(-1)[: (heads_here + 2) * piece].reshape(heads_here + 2, piece)
    q_bias_grad = bias[:heads_here]
    kv_bias = bias[heads_here:].reshape(1, -1)
    kv_bias = jnp.pad(kv_bias, ((0, 15), (0, -kv_bias.shape[1] % (2 * HEAD))))
    mine = jnp.concatenate([kv_narrow.reshape(shard, 2 * HEAD), kv_bias[:, : 2 * HEAD]]).astype(BF16)
    mine = (mine.astype(F32) + lax.ppermute(mine, "tp", [(0, 1), (1, 0), (2, 3), (3, 2)]).astype(F32)).astype(BF16)
    theirs = lax.ppermute(mine, "tp", [(0, 2), (2, 0), (1, 3), (3, 1)])
    mine, theirs = mine.astype(F32), theirs.astype(F32)
    low = head_pick == 0
    heads = jnp.stack([jnp.where(low, mine, theirs), jnp.where(low, theirs, mine)])
    kv_grad = heads[:, :shard].reshape(KV_HEADS, shard, 2, HEAD).transpose(2, 1, 0, 3).reshape(2, shard, KV_HEADS * HEAD)
    kv_bias_grad = heads[:, shard, : 2 * piece].reshape(KV_HEADS, 2, piece).transpose(1, 0, 2)

    def collect(values):
        kept_half = jnp.where(first, values[0], values[1])
        other = swap(jnp.where(first, values[1], values[0]))
        return jnp.where(first, kept_half, other), jnp.where(first, other, kept_half)

    gate_up_grad = jnp.stack(collect(gate_up_grads))[..., :ff].astype(F32)
    down_grad = jnp.concatenate(collect(down_grads), axis=0)[:, :ff].T.astype(F32)
    return (
        section_out[None],
        input_grad[None],
        q_grad[None],
        kv_grad[None],
        o_grad[None],
        gate_up_grad[None],
        down_grad[None],
        gains_grad[None],
        q_bias_grad[None],
        kv_bias_grad[None],
    )


def solution(mesh):
    in_specs = (
        P(None, "dp", "ctx", None),
        P(None, "dp", "ctx"),
        P(None, "dp", "ctx"),
        P("section", ("dp", "ctx"), "tp"),
        P("section", None, ("dp", "ctx"), None),
        P("section", "tp", ("dp", "ctx")),
        P("section", None, ("dp", "ctx"), "tp"),
        P("section", "tp", ("dp", "ctx")),
        P("section", None, ("dp", "ctx")),
        P("section", "tp", ("dp", "ctx")),
        P("section", None, None, ("dp", "ctx")),
        P(None, "dp", "ctx", None),
    )
    out_specs = (
        P("section", None, "dp", "ctx", None),
        P("section", None, "dp", "ctx", None),
        P("section", ("dp", "ctx"), "tp"),
        P("section", None, ("dp", "ctx"), None),
        P("section", "tp", ("dp", "ctx")),
        P("section", None, ("dp", "ctx"), "tp"),
        P("section", "tp", ("dp", "ctx")),
        P("section", None, ("dp", "ctx")),
        P("section", "tp", ("dp", "ctx")),
        P("section", None, None, ("dp", "ctx")),
    )
    return jax.shard_map(local, mesh=mesh, in_specs=in_specs, out_specs=out_specs, check_vma=False)
```

```python
import functools

import jax
import jax.numpy as jnp
from jax import lax
from jax.experimental import pallas as pl
from jax.experimental.pallas import tpu as pltpu
from jax.sharding import PartitionSpec as P

HEADS = 12
KV_HEADS = 2
HEAD = 128

EPS = 1e-06
ROPE_BASE = 1000000.0
NEG = -1e30
SCALE = HEAD ** (-0.5)
TILE = 768
VMEM_LIMIT = 60 << 20
MESH = pl.DeviceIdType.MESH

F32 = jnp.float32
BF16 = jnp.bfloat16


def dot(form, left, right):
    return jnp.einsum(form, left, right, preferred_element_type=F32)


def swap(value):
    return lax.ppermute(value, "section", [(0, 1), (1, 0)])


class Chain:
    def __init__(self, part, total, from_end, from_peer, sems):
        self.part, self.total = part, total
        self.from_end, self.from_peer = from_end, from_peer
        self.sems = sems
        self.chunks = sems.shape[1]
        self.rows = part.shape[0] // self.chunks
        self.is_middle, self.inner, self.outer = line_places()

    def at(self, ref, c):
        return ref.at[pl.ds(pl.multiple_of(c * self.rows, self.rows), self.rows)]

    def copy(self, source, target, c, step, place):
        return pltpu.make_async_remote_copy(
            src_ref=self.at(source, c),
            dst_ref=self.at(target, c),
            send_sem=self.sems.at[2 * step, c],
            recv_sem=self.sems.at[2 * step + 1, c],
            device_id={"tp": place},
            device_id_type=MESH,
        )

    def inward(self, c):
        return self.copy(self.part, self.from_end, c, 0, self.inner)

    def across(self, c):
        return self.copy(self.total, self.from_peer, c, 1, self.inner)

    def outward(self, c):
        return self.copy(self.total, self.total, c, 2, self.outer)

    def start(self):
        @pl.when(jnp.logical_not(self.is_middle))
        def _():
            @pl.loop(0, self.chunks)
            def _(c):
                self.inward(c).start()

    def join(self, c):
        self.inward(c).wait_recv()
        self.at(self.total, c)[...] = self.at(self.part, c)[...] + self.at(self.from_end, c)[...]
        self.across(c).start()

    def close(self, c):
        self.across(c).wait()
        self.at(self.total, c)[...] = self.at(self.total, c)[...] + self.at(self.from_peer, c)[...]
        self.outward(c).start()

    def step(self, c):
        @pl.when(self.is_middle & (c < self.chunks))
        def _():
            self.join(c)

            @pl.when(c > 0)
            def _():
                self.close(c - 1)

    def drain(self, done):
        @pl.when(self.is_middle)
        def _():
            if done < self.chunks:

                @pl.loop(done, self.chunks)
                def _(c):
                    self.step(c)

            self.close(self.chunks - 1)

        @pl.when(jnp.logical_not(self.is_middle))
        def _():
            @pl.loop(0, self.chunks)
            def _(c):
                self.outward(c).wait_recv()

    def settle(self):
        @pl.when(self.is_middle)
        def _():
            @pl.loop(0, self.chunks)
            def _(c):
                self.outward(c).wait_send()

        @pl.when(jnp.logical_not(self.is_middle))
        def _():
            @pl.loop(0, self.chunks)
            def _(c):
                self.inward(c).wait_send()


def line_places():
    place = lax.axis_index("tp")
    is_middle = (place == 1) | (place == 2)
    return is_middle, jnp.where(place < 2, place + 1, place - 1), jnp.where(place < 2, place - 1, place + 1)


def greet(ctx_count=1, cores=0):
    is_middle, inner, outer = line_places()
    me = lax.axis_index("ctx")
    barrier = pltpu.get_barrier_semaphore()
    for step in range(1, ctx_count):
        pl.semaphore_signal(barrier, inc=1, device_id={"ctx": lax.rem(me + step, ctx_count)}, device_id_type=MESH)
    if cores:
        peer = 1 - lax.axis_index("section")
        pl.semaphore_signal(barrier, inc=1, device_id={"section": peer}, device_id_type=MESH)
    pl.semaphore_signal(barrier, inc=1, device_id={"tp": inner}, device_id_type=MESH)

    @pl.when(is_middle)
    def _():
        pl.semaphore_signal(barrier, inc=1, device_id={"tp": outer}, device_id_type=MESH)
        pl.semaphore_wait(barrier, 1 + ctx_count + cores)

    @pl.when(jnp.logical_not(is_middle))
    def _():
        pl.semaphore_wait(barrier, ctx_count + cores)


def ab(ref):
    rows = ref.shape[0] // 2
    return ref.at[pl.ds(0, rows)], ref.at[pl.ds(rows, rows)]


def chain_scratch(shape):
    return [pltpu.VMEM(shape, BF16)] * 2 + [pltpu.SemaphoreType.DMA((6, min(8, shape[0] // 16)))]


CHAIN_REFS = 3
VMEM = pl.BlockSpec(memory_space=pltpu.VMEM)
ANY = pl.BlockSpec(memory_space=pl.ANY)


def params(collective_id):
    return pltpu.CompilerParams(collective_id=collective_id, has_side_effects=True, vmem_limit_bytes=VMEM_LIMIT)


def cost():
    return pl.CostEstimate(flops=1 << 20, bytes_accessed=1 << 20, transcendentals=0)


class Taker:
    def __init__(self, refs):
        self.refs = list(refs)

    def __call__(self, count):
        taken, self.refs = self.refs[:count], self.refs[count:]
        return taken


def ticker(chain, taken):
    return (lambda c: None) if chain is None else (lambda c: chain.step(c + taken))


def mm(left, right):
    return jnp.dot(left, right, preferred_element_type=F32)


def mm_t(left, right):
    return lax.dot_general(left, right, (((1,), (1,)), ((), ())), preferred_element_type=F32)


def mm_0(left, right):
    return lax.dot_general(left, right, (((0,), (0,)), ((), ())), preferred_element_type=F32)


def tile_at(ref, j, size=TILE):
    return ref.at[:, pl.ds(pl.multiple_of(j * size, size), size)]


def rows_at(ref, j, size=TILE):
    return ref.at[pl.ds(pl.multiple_of(j * size, size), size)]


def by_rows(rows, body, block=64):
    @pl.loop(0, rows // block)
    def _(i):
        body(pl.ds(pl.multiple_of(i * block, block), block))


def send_either(first, source, one, two, sem, start):
    @pl.when(first)
    def _():
        copy = pltpu.make_async_copy(source, one, sem)
        copy.start() if start else copy.wait()

    @pl.when(jnp.logical_not(first))
    def _():
        copy = pltpu.make_async_copy(source, two, sem)
        copy.start() if start else copy.wait()


def norm_factor(values):
    return lax.rsqrt(jnp.mean(values * values, axis=-1, keepdims=True) + EPS)


def normalize_rows(source, gain, target):
    def body(rows):
        values = source(rows)
        target[rows] = (values * norm_factor(values) * gain[...]).astype(BF16)

    by_rows(target.shape[0], body)


def norm_back_rows(upstream, grad_in, source, gain, gain_grad, target):
    def body(rows):
        values = source(rows)
        factor = norm_factor(values)
        unit = values * factor
        grad = grad_in[rows].astype(F32)
        per_row = grad * unit
        mean = jnp.mean(per_row * gain[...], axis=-1, keepdims=True)
        target[rows] = (upstream[rows].astype(F32) + factor * (grad * gain[...] - unit * mean)).astype(BF16)
        gain_grad[...] += jnp.sum(per_row.reshape(-1, 8, per_row.shape[1]), axis=0)

    by_rows(target.shape[0], body)


class FfnWeights:
    def __init__(self, sources, targets, sems, down_sems, by_columns):
        self.own, self.down_own = sources
        self.gate, self.up, self.down = targets
        self.sems, self.down_sems = sems, down_sems
        self.sec = lax.axis_index("section")
        self.first = self.sec == 0
        self.by_columns = by_columns
        self.wide = tile_at if by_columns else rows_at
        self.tiles, self.outs = self.gate.shape[1] // TILE, self.gate.shape[0] // TILE
        self.wide_count, self.deep_count = (self.tiles, self.outs) if by_columns else (self.outs, self.tiles)

    def here(self, j, target):
        return pltpu.make_async_copy(self.wide(self.own, j), self.wide(target, j), self.sems.at[0, j])

    def there(self, j, target):
        return pltpu.make_async_remote_copy(
            src_ref=self.wide(self.own, j),
            dst_ref=self.wide(target, j),
            send_sem=self.sems.at[1, j],
            recv_sem=self.sems.at[2, j],
            device_id={"section": 1 - self.sec},
            device_id_type=MESH,
        )

    def on_own(self, action):
        @pl.when(self.first)
        def _():
            action(self.gate, self.up)

        @pl.when(jnp.logical_not(self.first))
        def _():
            action(self.up, self.gate)

    def wait_gate(self, j):
        @pl.when(self.first)
        def _():
            self.here(j, self.gate).wait()

        @pl.when(jnp.logical_not(self.first))
        def _():
            self.there(j, self.gate).wait_recv()

    def wait_up(self, j):
        @pl.when(self.first)
        def _():
            self.there(j, self.up).wait_recv()

        @pl.when(jnp.logical_not(self.first))
        def _():
            self.here(j, self.up).wait()

    def down_parts(self, j):
        shards, half = self.down_own.shape[0], self.down_own.shape[1]
        per_tile = shards if not self.by_columns else shards // self.outs
        for i in range(per_tile):
            if self.by_columns:
                shard = j * per_tile + i
                source, columns = self.down_own.at[shard], slice(None)
            else:
                shard, columns = i, pl.ds(pl.multiple_of(j * TILE, TILE), TILE)
                source = self.down_own.at[shard, :, columns]

            def place(sec, shard=shard, columns=columns):
                return self.down.at[pl.ds(pl.multiple_of((2 * shard + sec) * half, 16), half), columns]

            yield source, place(self.sec), place(1 - self.sec), i

    def down_here(self, source, place, i, j):
        return pltpu.make_async_copy(source, place, self.down_sems.at[0, j, i])

    def down_there(self, source, place, i, j):
        return pltpu.make_async_remote_copy(
            src_ref=source,
            dst_ref=place,
            send_sem=self.down_sems.at[1, j, i],
            recv_sem=self.down_sems.at[2, j, i],
            device_id={"section": 1 - self.sec},
            device_id_type=MESH,
        )

    def start_wide(self, local):
        def action(own, other):
            @pl.loop(0, self.wide_count)
            def _(j):
                (self.here if local else self.there)(j, own).start()

        self.on_own(action)

    def start_deep(self, local):
        @pl.loop(0, self.deep_count)
        def _(j):
            for source, mine, theirs, i in self.down_parts(j):
                (self.down_here if local else self.down_there)(source, mine, i, j).start()

    def wait_down(self, j):
        for source, mine, theirs, i in self.down_parts(j):
            self.down_here(source, mine, i, j).wait()
            self.down_there(source, theirs, i, j).wait_recv()

    def finish(self):
        def action(own, other):
            @pl.loop(0, self.wide_count)
            def _(j):
                self.there(j, own).wait_send()

        self.on_own(action)

        @pl.loop(0, self.deep_count)
        def _(j):
            for source, mine, theirs, i in self.down_parts(j):
                self.down_there(source, mine, i, j).wait_send()


def ffn_forward_stage(weights, normed, outs, held, one, two, out_sems, result, tick, wait):
    gate, up, inner = held

    @pl.loop(0, weights.tiles)
    def _(j):
        if wait:
            weights.wait_gate(j)
        one[...] = mm(normed[...], tile_at(weights.gate, j)[...])
        tick(2 * j)
        if wait:
            weights.wait_up(j)
        two[...] = mm(normed[...], tile_at(weights.up, j)[...])
        columns = pl.ds(pl.multiple_of(j * TILE, TILE), TILE)

        def body(rows):
            g, u = one[rows], two[rows]
            gate[rows, columns] = g.astype(BF16)
            up[rows, columns] = u.astype(BF16)
            inner[rows, columns] = (g * jax.nn.sigmoid(g) * u).astype(BF16)

        by_rows(one.shape[0], body)
        tick(2 * j + 1)
        for k in range(3):
            pltpu.make_async_copy(tile_at(held[k], j), tile_at(outs[k], j), out_sems.at[k, j]).start()

    @pl.loop(0, weights.outs)
    def _(n):
        if wait:
            weights.wait_down(n)
        tile_at(result, n)[...] = mm_t(inner[...], rows_at(weights.down, n)[...]).astype(BF16)
        tick(2 * weights.tiles + n)

    return 2 * weights.tiles + weights.outs


def wait_out(held, outs, out_sems):
    @pl.loop(0, held[0].shape[1] // TILE)
    def _(j):
        for k in range(len(held)):
            pltpu.make_async_copy(tile_at(held[k], j), tile_at(outs[k], j), out_sems.at[k, j]).wait()


def ffn_forward_kernel(lead, *refs):
    take = Taker(refs)
    layer, attn_a, last_b, gain = take(4)
    layer_a, layer_b = ab(layer)
    sources = take(2)
    (normed_a, normed_b), *outs = [ab(ref) for ref in take(4)]
    outs_a, outs_b = zip(*outs)
    result_b, total_a = take(2)
    attn_b = take(1)[0] if lead else last_b
    targets, held = take(3), take(3)
    one, two, result_a, w_sems, down_sems, out_sems = take(6)
    chain_a = Chain(result_a, total_a, *take(CHAIN_REFS))
    chain_b = Chain(last_b, attn_b, *take(CHAIN_REFS)) if lead else None
    weights = FfnWeights(sources, targets, w_sems, down_sems, True)
    weights.start_wide(True)
    weights.start_deep(True)
    greet(cores=1)
    if lead:
        chain_b.start()
    weights.start_wide(False)
    weights.start_deep(False)
    normalize_rows(lambda r: layer_a[r].astype(F32) + attn_a[r].astype(F32), gain, normed_a)
    if lead:
        chain_b.step(0)
    tick = ticker(chain_b, 1)
    done = ffn_forward_stage(weights, normed_a, outs_a, held, one, two, out_sems, result_a, tick, True)
    chain_a.start()
    if lead:
        chain_b.drain(1 + done)
        chain_a.step(0)
    normalize_rows(lambda r: layer_b[r].astype(F32) + attn_b[r].astype(F32), gain, normed_b)
    wait_out(held, outs_a, out_sems)
    if not lead:
        chain_a.step(0)
    tick = ticker(chain_a, 1)
    done = ffn_forward_stage(weights, normed_b, outs_b, held, one, two, out_sems, result_b, tick, False)
    chain_a.drain(1 + done)
    chain_a.settle()
    if lead:
        chain_b.settle()
    weights.finish()
    wait_out(held, outs_b, out_sems)


def down_sem_shape(weights, tiles):
    return pltpu.SemaphoreType.DMA((3, tiles, weights[1].shape[0]))


def ffn_forward(lead, layer_in, attn_a, last_b, gain, weights):
    rows, width = attn_a.shape
    ff = weights[0].shape[1]
    tiles = max(ff, width) // TILE
    narrow = jax.ShapeDtypeStruct((rows, width), BF16)
    both, wide = jax.ShapeDtypeStruct((2 * rows, width), BF16), jax.ShapeDtypeStruct((2 * rows, ff), BF16)
    return pl.pallas_call(
        functools.partial(ffn_forward_kernel, lead),
        out_shape=[both, wide, wide, wide] + [narrow] * (2 + lead),
        in_specs=[VMEM] * 4 + [ANY] * 2,
        out_specs=[VMEM] + [ANY] * 3 + [VMEM] * (2 + lead),
        scratch_shapes=[pltpu.VMEM((width, ff), BF16)] * 3
        + [pltpu.VMEM((rows, ff), BF16)] * 3
        + [pltpu.VMEM((rows, TILE), F32)] * 2
        + [pltpu.VMEM((rows, width), BF16)]
        + [pltpu.SemaphoreType.DMA((3, tiles)), down_sem_shape(weights, tiles), pltpu.SemaphoreType.DMA((3, tiles))]
        + chain_scratch((rows, width)) * (1 + lead),
        compiler_params=params(1 + lead),
        cost_estimate=cost(),
    )(layer_in, attn_a, last_b, gain, *weights)


def ffn_backward_stage(weights, grad, ins, outs, held, one, in_sems, out_sems, result, tick, wait):
    gate, up = held
    own_out, other_out = outs

    @pl.loop(0, weights.tiles)
    def _(j):
        if wait:
            weights.wait_down(j)
        one[...] = mm(grad[...], tile_at(weights.down, j)[...])
        tick(j)
        for k in range(2):
            pltpu.make_async_copy(tile_at(ins[k], j), tile_at(held[k], j), in_sems.at[k, j]).wait()
        columns = pl.ds(pl.multiple_of(j * TILE, TILE), TILE)

        def body(rows):
            g, u, d = gate[rows, columns].astype(F32), up[rows, columns].astype(F32), one[rows]
            sig = jax.nn.sigmoid(g)
            d = d * sig
            gate[rows, columns] = (d * u * (1.0 + g * (1.0 - sig))).astype(BF16)
            up[rows, columns] = (d * g).astype(BF16)

        by_rows(one.shape[0], body)

    def sending(start):
        @pl.loop(0, weights.tiles)
        def _(j):
            own, other = tile_at(own_out, j), tile_at(other_out, j)
            send_either(weights.first, tile_at(gate, j), own, other, out_sems.at[0, j], start)
            send_either(weights.first, tile_at(up, j), other, own, out_sems.at[1, j], start)

    sending(True)

    @pl.loop(0, weights.outs)
    def _(n):
        if wait:
            weights.wait_gate(n)
            weights.wait_up(n)
        one[...] = mm_t(gate[...], rows_at(weights.gate, n)[...])
        tick(weights.tiles + 2 * n)
        tile_at(result, n)[...] = (one[...] + mm_t(up[...], rows_at(weights.up, n)[...])).astype(BF16)
        tick(weights.tiles + 2 * n + 1)

    return weights.tiles + 2 * weights.outs, lambda: sending(False)


def ffn_backward_kernel(low, *refs):
    take = Taker(refs)
    grad, last_b = take(2)
    grad_a, grad_b = ab(grad)
    ins_a, ins_b = zip(*[ab(ref) for ref in take(2)])
    sources = take(2)
    if low:
        sum_a, layer, gain = take(3)
        layer_a, layer_b = ab(layer)
    outs_a, outs_b = zip(*[ab(ref) for ref in take(2)])
    result_b, total_a, total_b = take(3)
    if low:
        made, gain_grad = take(2)
        made_a, made_b = ab(made)
    targets, held = take(3), take(2)
    one, result_a, w_sems, down_sems, in_sems, out_sems = take(6)
    chain_a = Chain(result_a, total_a, *take(CHAIN_REFS))
    chain_b = Chain(last_b, total_b, *take(CHAIN_REFS))
    weights = FfnWeights(sources, targets, w_sems, down_sems, False)

    def fetch(ins):
        @pl.loop(0, weights.tiles)
        def _(j):
            for k in range(2):
                pltpu.make_async_copy(tile_at(ins[k], j), tile_at(held[k], j), in_sems.at[k, j]).start()

    weights.start_deep(True)
    fetch(ins_a)
    weights.start_wide(True)
    greet(cores=1)
    chain_b.start()
    weights.start_deep(False)
    weights.start_wide(False)
    if low:
        gain_grad[...] = jnp.zeros_like(gain_grad)
        norm_back_rows(grad_a, sum_a, lambda r: layer_a[r].astype(F32), gain, gain_grad, made_a)
        grad_a = made_a
    chain_b.step(0)
    done, sent_a = ffn_backward_stage(
        weights, grad_a, ins_a, outs_a, held, one, in_sems, out_sems, result_a, ticker(chain_b, 1), True
    )
    chain_a.start()
    sent_a()
    fetch(ins_b)
    chain_b.drain(1 + done)
    chain_a.step(0)
    if low:
        norm_back_rows(grad_b, total_b, lambda r: layer_b[r].astype(F32), gain, gain_grad, made_b)
        grad_b = made_b
    done, sent_b = ffn_backward_stage(
        weights, grad_b, ins_b, outs_b, held, one, in_sems, out_sems, result_b, ticker(chain_a, 1), False
    )
    chain_a.drain(1 + done)
    chain_a.settle()
    chain_b.settle()
    weights.finish()
    sent_b()


def ffn_backward(grad, gate, up, weights, last_b, below=None):
    rows, width = last_b.shape
    ff = weights[0].shape[1]
    tiles = max(ff, width) // TILE
    low = below is not None
    narrow = jax.ShapeDtypeStruct((rows, width), BF16)
    both, wide = jax.ShapeDtypeStruct((2 * rows, width), BF16), jax.ShapeDtypeStruct((2 * rows, ff), BF16)
    more = [both, jax.ShapeDtypeStruct((8, width), F32)] if low else []
    return pl.pallas_call(
        functools.partial(ffn_backward_kernel, low),
        out_shape=[wide] * 2 + [narrow] * 3 + more,
        in_specs=[VMEM] * 2 + [ANY] * 4 + [VMEM] * (3 if low else 0),
        out_specs=[ANY] * 2 + [VMEM] * (3 + len(more)),
        scratch_shapes=[pltpu.VMEM((width, ff), BF16)] * 3
        + [pltpu.VMEM((rows, ff), BF16)] * 2
        + [pltpu.VMEM((rows, TILE), F32)]
        + [pltpu.VMEM((rows, width), BF16)]
        + [pltpu.SemaphoreType.DMA((3, tiles)), down_sem_shape(weights, tiles)]
        + [pltpu.SemaphoreType.DMA((2, tiles))] * 2
        + chain_scratch((rows, width)) * 2,
        compiler_params=params(3 + low),
        cost_estimate=cost(),
    )(grad, last_b, gate, up, *weights, *(below or ()))


def last_kernel(part, sum_a, grad, layer, gain, made, gain_grad, total, *scratch):
    chain = Chain(part, total, *scratch)
    greet()
    chain.start()
    gain_grad[...] = jnp.zeros_like(gain_grad)
    grads, layers, mades = ab(grad), ab(layer), ab(made)
    chain.step(0)
    norm_back_rows(grads[0], sum_a, lambda r: layers[0][r].astype(F32), gain, gain_grad, mades[0])
    chain.drain(1)
    norm_back_rows(grads[1], total, lambda r: layers[1][r].astype(F32), gain, gain_grad, mades[1])
    chain.settle()


def last_grads(part, sum_a, grad, layer, gain):
    shape = part.shape
    return pl.pallas_call(
        last_kernel,
        out_shape=[jax.ShapeDtypeStruct(grad.shape, BF16), jax.ShapeDtypeStruct((8, shape[1]), F32)],
        in_specs=[VMEM] * 5,
        out_specs=[VMEM] * 2,
        scratch_shapes=[pltpu.VMEM(shape, BF16)] + chain_scratch(shape),
        compiler_params=params(0),
        cost_estimate=cost(),
    )(part, sum_a, grad, layer, gain)


def roped(values, cosine, sine):
    return values * cosine + pltpu.roll(values, HEAD // 2, 1) * sine


def unroped(grads, cosine, sine):
    return grads * cosine + pltpu.roll(grads * sine, HEAD // 2, 1)


def allowed_keys(seg_rows, seg_keys, i, block):
    rows, keys = seg_rows.shape[0], seg_keys.shape[1]
    first_row = lax.axis_index("ctx") * rows + i * block
    row_at = first_row + lax.broadcasted_iota(jnp.int32, (block, keys), 0)
    key_at = lax.broadcasted_iota(jnp.int32, (block, keys), 1)
    own = seg_rows[pl.ds(pl.multiple_of(i * block, block), block)]
    return (key_at <= row_at) & (own == seg_keys[...])


def attention_forward_stage(layer_in, gain, w_lin, w_out, bias, places, outs, result, kv_sems, tick):
    cosine, sine, seg_rows, seg_keys = places
    normed, query, kv, lse, attended = outs
    rows, q_cols = query.shape
    heads = q_cols // HEAD
    count = kv.shape[0] // rows
    me = lax.axis_index("ctx")
    block = min(256, rows)
    normalize_rows(lambda r: layer_in[r].astype(F32), gain, normed)
    tick(0)
    mine = kv.at[pl.ds(pl.multiple_of(me * rows, rows), rows)]
    lin = mm(normed[...], w_lin[:, q_cols:]) + bias[:, q_cols:]
    mine[:, :HEAD] = roped(lin[:, :HEAD], cosine[...], sine[...]).astype(BF16)
    mine[:, HEAD:] = lin[:, HEAD:].astype(BF16)

    def passing(offset):
        return pltpu.make_async_remote_copy(
            src_ref=mine,
            dst_ref=mine,
            send_sem=kv_sems.at[0, offset],
            recv_sem=kv_sems.at[1, offset],
            device_id={"ctx": lax.rem(me + offset, count)},
            device_id_type=MESH,
        )

    for offset in range(1, count):
        passing(offset).start()
    tick(1)
    lin = mm(normed[...], w_lin[:, :q_cols]) + bias[:, :q_cols]
    for h in range(heads):
        columns = slice(h * HEAD, (h + 1) * HEAD)
        query[:, columns] = roped(lin[:, columns], cosine[...], sine[...]).astype(BF16)
    for offset in range(1, count):
        passing(offset).wait_recv()

    @pl.loop(0, rows // block)
    def _(i):
        at = pl.ds(pl.multiple_of(i * block, block), block)
        allowed = allowed_keys(seg_rows, seg_keys, i, block)
        lane = lax.broadcasted_iota(jnp.int32, (block, HEAD), 1)
        logs = jnp.zeros((block, HEAD), F32)
        for h in range(heads):
            columns = slice(h * HEAD, (h + 1) * HEAD)
            scores = jnp.where(allowed, mm_t(query[at, columns], kv[:, :HEAD]) * SCALE, NEG)
            top = jnp.max(scores, axis=-1, keepdims=True)
            probs = jnp.exp(scores - top)
            sums = jnp.sum(probs, axis=-1, keepdims=True)
            probs = (probs * (1.0 / sums)).astype(BF16)
            attended[at, columns] = mm(probs, kv[:, HEAD:]).astype(BF16)
            logs = jnp.where(lane == h, top + jnp.log(sums), logs)
            tick(2 + heads * i + h)
        lse[at] = logs

    base = 2 + heads * (rows // block)

    @pl.loop(0, result.shape[1] // TILE)
    def _(n):
        tile_at(result, n)[...] = mm_t(attended[...], rows_at(w_out, n)[...]).astype(BF16)
        tick(base + n)

    for offset in range(1, count):
        passing(offset).wait_send()
    return base + result.shape[1] // TILE


def attention_forward_kernel(low, *refs):
    take = Taker(refs)
    gain, w_lin, w_out, bias = take(4)
    places_a, places_b = take(4), take(4)
    layer_a, layer_b = ab(take(1)[0])
    if not low:
        adds_a, adds_b, (last_b,) = (layer_a, *take(2)), (layer_b, *take(1)), take(1)
    outs_a, outs_b = zip(*[ab(ref) for ref in take(5)])
    if low:
        total_a, total_b = take(2)
    else:
        result_b, total_a, last_sum_b, layer = take(4)
        layer_a, layer_b = ab(layer)
    result_a, kv_sems_a, kv_sems_b = take(3)
    if low:
        (result_b,) = take(1)
    chain_a = Chain(result_a, total_a, *take(CHAIN_REFS))
    chain_b = Chain(result_b, total_b, *take(CHAIN_REFS)) if low else Chain(last_b, last_sum_b, *take(CHAIN_REFS))
    greet(kv_sems_a.shape[1])
    if not low:
        chain_b.start()

        def body(rows):
            layer_a[rows] = sum(ref[rows].astype(F32) for ref in adds_a).astype(BF16)

        by_rows(layer_a.shape[0], body)
    tick = ticker(None if low else chain_b, 0)
    done = attention_forward_stage(layer_a, gain, w_lin, w_out, bias, places_a, outs_a, result_a, kv_sems_a, tick)
    chain_a.start()
    if not low:
        chain_b.drain(done)
        chain_a.step(0)

        def body(rows):
            layer_b[rows] = sum(ref[rows].astype(F32) for ref in (*adds_b, last_sum_b)).astype(BF16)

        by_rows(layer_b.shape[0], body)
    taken = 0 if low else 1
    tick = ticker(chain_a, taken)
    done = attention_forward_stage(layer_b, gain, w_lin, w_out, bias, places_b, outs_b, result_b, kv_sems_b, tick)
    if low:
        chain_b.start()
    chain_a.drain(taken + done)
    if low:
        chain_b.drain(0)
    chain_a.settle()
    chain_b.settle()


def attention_forward(weights, places, inputs):
    w_lin, w_out, gains, bias = weights
    rows, width = inputs[0].shape[0] // 2, inputs[0].shape[1]
    q_cols = w_out.shape[1]
    keys = places[0][3].shape[1]
    count = keys // rows
    low = len(inputs) == 1
    narrow, both = jax.ShapeDtypeStruct((rows, width), BF16), jax.ShapeDtypeStruct((2 * rows, width), BF16)
    heads_out = jax.ShapeDtypeStruct((2 * rows, q_cols), BF16)
    kv_out = jax.ShapeDtypeStruct((2 * keys, 2 * HEAD), BF16)
    lse_out = jax.ShapeDtypeStruct((2 * rows, HEAD), F32)
    outs = [both, heads_out, kv_out, lse_out, heads_out] + ([narrow] * 2 if low else [narrow] * 3 + [both])
    args = (gains[:1], w_lin, w_out, bias, *places[0], *places[1], *inputs)
    return pl.pallas_call(
        functools.partial(attention_forward_kernel, low),
        out_shape=outs,
        in_specs=[VMEM] * len(args),
        out_specs=[VMEM] * len(outs),
        scratch_shapes=[pltpu.VMEM((rows, width), BF16)]
        + [pltpu.SemaphoreType.DMA((2, count))] * 2
        + [pltpu.VMEM((rows, width), BF16)] * low
        + chain_scratch((rows, width)) * 2,
        compiler_params=params(5 + low),
        cost_estimate=cost(),
    )(*args)


def attention_backward_stage(ins, sum_in, gain, w_lin, w_out, places, outs, gain_grad, result, scratch, tick):
    upstream, layer_in, attn_out, query, kv, lse, attended = ins
    cosine, sine, seg_rows, seg_keys = places
    attn_grad, lin = outs
    heads_grad, kv_grad, q_part, sent, got, kv_sems = scratch
    rows, q_cols = query.shape
    heads = q_cols // HEAD
    count = kv.shape[0] // rows
    me = lax.axis_index("ctx")
    block = min(256, rows)
    kv_grad[...] = jnp.zeros_like(kv_grad)
    norm_back_rows(
        upstream, sum_in, lambda r: layer_in[r].astype(F32) + attn_out[r].astype(F32), gain, gain_grad, attn_grad
    )
    tick(0)
    heads_grad[...] = mm(attn_grad[...], w_out[...]).astype(BF16)
    tick(1)

    @pl.loop(0, rows // block)
    def _(i):
        at = pl.ds(pl.multiple_of(i * block, block), block)
        allowed = allowed_keys(seg_rows, seg_keys, i, block)
        for h in range(heads):
            columns = slice(h * HEAD, (h + 1) * HEAD)
            scores = mm_t(query[at, columns], kv[:, :HEAD]) * SCALE - lse[at, h : h + 1]
            probs = jnp.exp(jnp.where(allowed, scores, NEG))
            grad = heads_grad[at, columns]
            row_sum = jnp.sum(attended[at, columns].astype(F32) * grad.astype(F32), axis=-1, keepdims=True)
            score_grad = (probs * (mm_t(grad, kv[:, HEAD:]) - row_sum)).astype(BF16)
            q_grad = mm(score_grad, kv[:, :HEAD]) * SCALE
            lin[at, columns] = unroped(q_grad, cosine[at], sine[at]).astype(BF16)
            kv_grad[:, :HEAD] += mm_0(score_grad, query[at, columns])
            kv_grad[:, HEAD:] += mm_0(probs.astype(BF16), grad)
            tick(2 + heads * i + h)

    def passing(offset):
        return pltpu.make_async_remote_copy(
            src_ref=sent.at[offset - 1],
            dst_ref=got.at[offset - 1],
            send_sem=kv_sems.at[0, offset],
            recv_sem=kv_sems.at[1, offset],
            device_id={"ctx": lax.rem(me + offset, count)},
            device_id_type=MESH,
        )

    for offset in range(1, count):
        peer = pl.ds(pl.multiple_of(lax.rem(me + offset, count) * rows, rows), rows)
        sent[offset - 1, :, :HEAD] = (kv_grad[peer, :HEAD] * SCALE).astype(BF16)
        sent[offset - 1, :, HEAD:] = kv_grad[peer, HEAD:].astype(BF16)
        passing(offset).start()
    base = 2 + heads * (rows // block)

    @pl.loop(0, result.shape[1] // TILE)
    def _(n):
        tile_at(q_part, n)[...] = mm_t(lin[:, :q_cols], rows_at(w_lin, n)[:, :q_cols])
        tick(base + n)

    mine = pl.ds(pl.multiple_of(me * rows, rows), rows)
    k_grad, v_grad = kv_grad[mine, :HEAD] * SCALE, kv_grad[mine, HEAD:]
    for offset in range(1, count):
        passing(offset).wait_recv()
        k_grad = k_grad + got[offset - 1, :, :HEAD].astype(F32)
        v_grad = v_grad + got[offset - 1, :, HEAD:].astype(F32)
    lin[:, q_cols : q_cols + HEAD] = unroped(k_grad, cosine[...], sine[...]).astype(BF16)
    lin[:, q_cols + HEAD :] = v_grad.astype(BF16)

    @pl.loop(0, result.shape[1] // TILE)
    def _(n):
        kv_part = mm_t(lin[:, q_cols:], rows_at(w_lin, n)[:, q_cols:])
        tile_at(result, n)[...] = (tile_at(q_part, n)[...] + kv_part).astype(BF16)


    for offset in range(1, count):
        passing(offset).wait_send()
    return base + result.shape[1] // TILE


def attention_backward_kernel(*refs):
    take = Taker(refs)
    gain, w_lin, w_out = take(3)
    places_a, places_b = take(4), take(4)
    ins_a, ins_b = zip(*[ab(ref) for ref in take(6)])
    attn_a, attn_b = take(2)
    ins_a, ins_b = (*ins_a[:2], attn_a, *ins_a[2:]), (*ins_b[:2], attn_b, *ins_b[2:])
    sum_a, last_b = take(2)
    outs_a, outs_b = zip(*[ab(ref) for ref in take(2)])
    gain_grad, result_b, total_a, total_b = take(4)
    heads_grad, kv_grad, q_part, result_a = take(4)
    exchange_a, exchange_b = take(3), take(3)
    chain_a = Chain(result_a, total_a, *take(CHAIN_REFS))
    chain_b = Chain(last_b, total_b, *take(CHAIN_REFS))
    greet(exchange_a[2].shape[1])
    chain_b.start()
    gain_grad[...] = jnp.zeros_like(gain_grad)
    scratch = (heads_grad, kv_grad, q_part, *exchange_a)
    done = attention_backward_stage(
        ins_a, sum_a, gain, w_lin, w_out, places_a, outs_a, gain_grad, result_a, scratch, ticker(chain_b, 0)
    )
    chain_a.start()
    chain_b.drain(done)
    chain_a.step(0)
    scratch = (heads_grad, kv_grad, q_part, *exchange_b)
    done = attention_backward_stage(
        ins_b, total_b, gain, w_lin, w_out, places_b, outs_b, gain_grad, result_b, scratch, ticker(chain_a, 1)
    )
    chain_a.drain(1 + done)
    chain_a.settle()
    chain_b.settle()


def attention_backward(upstream, sum_a, last_b, kept, weights, places):
    w_lin, w_out, gains, bias = weights
    rows, width = sum_a.shape
    q_cols = w_out.shape[1]
    keys = places[0][3].shape[1]
    count = keys // rows
    narrow = jax.ShapeDtypeStruct((rows, width), BF16)
    both = jax.ShapeDtypeStruct((2 * rows, width), BF16)
    lin_out = jax.ShapeDtypeStruct((2 * rows, q_cols + 2 * HEAD), BF16)
    outs = [both, lin_out] + [jax.ShapeDtypeStruct((8, width), F32)] + [narrow] * 3
    names = ("layer_in", "query", "kv", "lse", "attended", "attn_a", "attn_b")
    args = (gains[1:], w_lin, w_out, *places[0], *places[1], upstream)
    args += (*[kept[name] for name in names], sum_a, last_b)
    exchange = [pltpu.VMEM((max(count - 1, 1), rows, 2 * HEAD), BF16)] * 2 + [pltpu.SemaphoreType.DMA((2, count))]
    return pl.pallas_call(
        attention_backward_kernel,
        out_shape=outs,
        in_specs=[VMEM] * len(args),
        out_specs=[VMEM] * len(outs),
        scratch_shapes=[
            pltpu.VMEM((rows, q_cols), BF16),
            pltpu.VMEM((keys, 2 * HEAD), F32),
            pltpu.VMEM((rows, width), F32),
            pltpu.VMEM((rows, width), BF16),
        ]
        + exchange * 2
        + chain_scratch((rows, width)) * 2,
        compiler_params=params(7),
        cost_estimate=cost(),
    )(*args)


def rope_tables(places):
    steps = jnp.arange(HEAD // 2, dtype=F32) * (2.0 / HEAD)
    inverse = ROPE_BASE ** (-steps)
    angles = places.astype(F32)[..., None] * inverse
    angles = jnp.concatenate([angles, angles], axis=-1)
    return (jnp.cos(angles), jnp.sin(angles))


def over_ctx(value):
    if lax.axis_size("ctx") == 2:
        other = lax.ppermute(value, "ctx", [(0, 1), (1, 0)])
        low = lax.axis_index("ctx") == 0
        return jnp.concatenate([jnp.where(low, value, other), jnp.where(low, other, value)], axis=-1)
    return lax.all_gather(value, "ctx", axis=value.ndim - 1, tiled=True)


def local(
    section_in,
    segments,
    positions,
    query_weight,
    kv_weight,
    output_weight,
    gate_up,
    down_weight,
    norm_gains,
    query_bias,
    kv_bias,
    out_grad,
):
    sec = lax.axis_index("section")
    first = sec == 0
    group = HEADS // KV_HEADS
    heads_here = HEADS // lax.axis_size("tp")
    head_pick = lax.axis_index("tp") * heads_here // group
    shards = lax.axis_size("dp") * lax.axis_size("ctx")
    ranks = ("dp", "ctx")
    seqs, span, width = section_in.shape[1:]
    shard = query_weight.shape[1]
    q_cols = query_weight.shape[2]
    ff = gate_up.shape[3]

    def per_layer(mine, theirs):
        return jnp.where(first, mine, theirs), jnp.where(first, theirs, mine)

    half = shard // 2
    kv_width = KV_HEADS * HEAD

    def halves(rows):
        mine = lax.dynamic_slice_in_dim(rows, sec * half, half, 0)
        return per_layer(mine, swap(lax.dynamic_slice_in_dim(rows, (1 - sec) * half, half, 0)))

    def joined(own):
        return jnp.stack(per_layer(own, swap(own)), axis=1).reshape(width, own.shape[-1])

    def after(value, event):
        return lax.optimization_barrier((value, event))[0]

    piece = HEAD // shards
    biases = jnp.concatenate([query_bias[0].reshape(-1), kv_bias[0].reshape(-1)])
    n_biases = biases.shape[0]
    biases = jnp.pad(biases, (0, -n_biases % shard)).reshape(-1, shard).T
    extra = jnp.concatenate([norm_gains[0].T, biases], axis=1)
    n_extra = extra.shape[1]
    extra = jnp.pad(extra, ((0, 0), (0, HEAD - n_extra)))
    packed = jnp.concatenate([query_weight[0], kv_weight[0, 0], kv_weight[0, 1], output_weight[0].T, extra], axis=1)
    packed_shards = halves(packed)
    first_shard, gate_up, down_weight, positions, segments, section_in = lax.optimization_barrier(
        (packed_shards[0], gate_up, down_weight, positions, segments, section_in)
    )
    packed_low = lax.all_gather(first_shard, ranks, axis=0)
    spare = -ff % TILE
    wide = jnp.pad(gate_up[0], ((0, 0), (0, 0), (0, spare)))
    mine = lax.dynamic_index_in_dim(wide, sec, 0, keepdims=False)
    theirs = swap(lax.dynamic_index_in_dim(wide, 1 - sec, 0, keepdims=False))
    gate_up_shards = per_layer(mine, theirs)
    down_shards = halves(jnp.pad(down_weight[0].T, ((0, 0), (0, spare))))

    micro = sec
    seg = lax.dynamic_index_in_dim(segments, micro, 0, keepdims=False)
    pos = lax.dynamic_index_in_dim(positions, micro, 0, keepdims=False)
    hidden = lax.dynamic_index_in_dim(section_in, micro, 0, keepdims=False)
    seg_keys = over_ctx(seg)
    segs, tables = [], []
    for q in range(seqs):
        segs.append((seg[q][:, None], seg_keys[q][None]))
        cosine, sine = rope_tables(pos[q])
        tables.append((cosine, jnp.where(jnp.arange(HEAD) < HEAD // 2, -sine, sine)))
    hidden = hidden.reshape(seqs * span, width)

    packed_low, gate_up_shards, down_shards, packed_shards, segs, tables, hidden = lax.optimization_barrier(
        (packed_low, gate_up_shards, down_shards, packed_shards, segs, tables, hidden)
    )
    own_low = lax.all_gather(gate_up_shards[0], ranks, axis=0, tiled=True)
    down_low = lax.all_gather(down_shards[0], ranks, axis=0)

    def attention_weights(own):
        p = joined(own)
        wq = p[:, :q_cols]
        wk = lax.dynamic_slice_in_dim(p[:, q_cols : q_cols + kv_width], head_pick * HEAD, HEAD, 1)
        wv = lax.dynamic_slice_in_dim(p[:, q_cols + kv_width : q_cols + 2 * kv_width], head_pick * HEAD, HEAD, 1)
        wo = p[:, q_cols + 2 * kv_width : 2 * q_cols + 2 * kv_width]
        s = p[:, 2 * q_cols + 2 * kv_width :]
        gains = s[:, :2].T
        s = s[:, 2:n_extra].T.reshape(-1, shards, shard).transpose(1, 0, 2).reshape(shards, -1)[:, :n_biases]
        q_b = s[:, : heads_here * piece].reshape(shards, heads_here, piece).transpose(1, 0, 2).reshape(heads_here, HEAD)
        kv_b = s[:, heads_here * piece :].reshape(shards, 2, KV_HEADS, piece)
        kv_b = kv_b.transpose(1, 2, 0, 3).reshape(2, KV_HEADS, HEAD)
        kv_b = lax.dynamic_slice_in_dim(kv_b, head_pick, 1, 1)
        bias = jnp.concatenate([q_b.reshape(1, -1), kv_b.reshape(1, -1)], axis=1).astype(F32)
        return jnp.concatenate([wq, wk, wv], axis=1), wo, gains.astype(F32), bias

    names = ("layer_in", "query", "kv", "lse", "attended", "attn_a", "attn_b")
    args = (gains[1:], w_lin, w_out, *places[0], *places[1], upstream)
    args += (*[kept[name] for name in names], sum_a, last_b)
    exchange = [pltpu.VMEM((max(count - 1, 1), rows, 2 * HEAD), BF16)] * 2 + [pltpu.SemaphoreType.DMA((2, count))]
    return pl.pallas_call(
        attention_backward_kernel,
        out_shape=outs,
        in_specs=[VMEM] * len(args),
        out_specs=[VMEM] * len(outs),
        scratch_shapes=[
            pltpu.VMEM((rows, q_cols), BF16),
            pltpu.VMEM((keys, 2 * HEAD), F32),
            pltpu.VMEM((rows, width), F32),
            pltpu.VMEM((rows, width), BF16),
        ]
        + exchange * 2
        + chain_scratch((rows, width)) * 2,
        compiler_params=params(7),
        cost_estimate=cost(),
    )(*args)


def rope_tables(places):
    steps = jnp.arange(HEAD // 2, dtype=F32) * (2.0 / HEAD)
    inverse = ROPE_BASE ** (-steps)
    angles = places.astype(F32)[..., None] * inverse
    angles = jnp.concatenate([angles, angles], axis=-1)
    return (jnp.cos(angles), jnp.sin(angles))


def norm_back(grad_out, rows_in, factor, gain):
    unit = rows_in * factor
    gain_grad = jnp.sum(grad_out * unit, axis=0)
    weighted = grad_out * gain
    return (
        factor * (weighted - unit * jnp.mean(weighted * unit, axis=-1, keepdims=True)),
        gain_grad,
    )


def over_ctx(value):
    if lax.axis_size("ctx") == 2:
        other = lax.ppermute(value, "ctx", [(0, 1), (1, 0)])
        low = lax.axis_index("ctx") == 0
        return jnp.concatenate([jnp.where(low, value, other), jnp.where(low, other, value)], axis=-1)
    return lax.all_gather(value, "ctx", axis=value.ndim - 1, tiled=True)


def input_backward(normed_one_grad, middle_grad, kept, gains):
    layer_in = kept["layer_in"].astype(F32)
    factor = lax.rsqrt(jnp.mean(layer_in * layer_in, axis=-1, keepdims=True) + EPS)
    norm_grad, gain_one = norm_back(normed_one_grad.astype(F32), layer_in, factor, gains[0])
    return (middle_grad.astype(F32) + norm_grad).astype(BF16), gain_one


def local(
    section_in,
    segments,
    positions,
    query_weight,
    kv_weight,
    output_weight,
    gate_up,
    down_weight,
    norm_gains,
    query_bias,
    kv_bias,
    out_grad,
):
    sec = lax.axis_index("section")
    first = sec == 0
    group = HEADS // KV_HEADS
    heads_here = HEADS // lax.axis_size("tp")
    head_pick = lax.axis_index("tp") * heads_here // group
    shards = lax.axis_size("dp") * lax.axis_size("ctx")
    ranks = ("dp", "ctx")
    seqs, span, width = section_in.shape[1:]
    shard = query_weight.shape[1]
    q_cols = query_weight.shape[2]
    ff = gate_up.shape[3]

    def per_layer(mine, theirs):
        return jnp.where(first, mine, theirs), jnp.where(first, theirs, mine)

    half = shard // 2
    kv_width = KV_HEADS * HEAD

    def halves(rows):
        mine = lax.dynamic_slice_in_dim(rows, sec * half, half, 0)
        return per_layer(mine, swap(lax.dynamic_slice_in_dim(rows, (1 - sec) * half, half, 0)))

    def joined(own):
        return jnp.stack(per_layer(own, swap(own)), axis=1).reshape(width, own.shape[-1])

    def after(value, event):
        return lax.optimization_barrier((value, event))[0]

    piece = HEAD // shards
    biases = jnp.concatenate([query_bias[0].reshape(-1), kv_bias[0].reshape(-1)])
    n_biases = biases.shape[0]
    biases = jnp.pad(biases, (0, -n_biases % shard)).reshape(-1, shard).T
    extra = jnp.concatenate([norm_gains[0].T, biases], axis=1)
    n_extra = extra.shape[1]
    extra = jnp.pad(extra, ((0, 0), (0, HEAD - n_extra)))
    packed = jnp.concatenate([query_weight[0], kv_weight[0, 0], kv_weight[0, 1], output_weight[0].T, extra], axis=1)
    packed_shards = halves(packed)
    first_shard, gate_up, down_weight, positions, segments, section_in = lax.optimization_barrier(
        (packed_shards[0], gate_up, down_weight, positions, segments, section_in)
    )
    packed_low = lax.all_gather(first_shard, ranks, axis=0)
    spare = -ff % TILE
    wide = jnp.pad(gate_up[0], ((0, 0), (0, 0), (0, spare)))
    mine = lax.dynamic_index_in_dim(wide, sec, 0, keepdims=False)
    theirs = swap(lax.dynamic_index_in_dim(wide, 1 - sec, 0, keepdims=False))
    gate_up_shards = per_layer(mine, theirs)
    down_shards = halves(jnp.pad(down_weight[0].T, ((0, 0), (0, spare))))

    micro = sec
    seg = lax.dynamic_index_in_dim(segments, micro, 0, keepdims=False)
    pos = lax.dynamic_index_in_dim(positions, micro, 0, keepdims=False)
    hidden = lax.dynamic_index_in_dim(section_in, micro, 0, keepdims=False)
    seg_keys = over_ctx(seg)
    segs, tables = [], []
    for q in range(seqs):
        segs.append((seg[q][:, None], seg_keys[q][None]))
        cosine, sine = rope_tables(pos[q])
        tables.append((cosine, jnp.where(jnp.arange(HEAD) < HEAD // 2, -sine, sine)))
    hidden = hidden.reshape(seqs * span, width)

    packed_low, gate_up_shards, down_shards, packed_shards, segs, tables, hidden = lax.optimization_barrier(
        (packed_low, gate_up_shards, down_shards, packed_shards, segs, tables, hidden)
    )
    own_low = lax.all_gather(gate_up_shards[0], ranks, axis=0, tiled=True)
    down_low = lax.all_gather(down_shards[0], ranks, axis=0)

    def attention_weights(own):
        p = joined(own)
        wq = p[:, :q_cols]
        wk = lax.dynamic_slice_in_dim(p[:, q_cols : q_cols + kv_width], head_pick * HEAD, HEAD, 1)
        wv = lax.dynamic_slice_in_dim(p[:, q_cols + kv_width : q_cols + 2 * kv_width], head_pick * HEAD, HEAD, 1)
        wo = p[:, q_cols + 2 * kv_width : 2 * q_cols + 2 * kv_width]
        s = p[:, 2 * q_cols + 2 * kv_width :]
        gains = s[:, :2].T
        s = s[:, 2:n_extra].T.reshape(-1, shards, shard).transpose(1, 0, 2).reshape(shards, -1)[:, :n_biases]
        q_b = s[:, : heads_here * piece].reshape(shards, heads_here, piece).transpose(1, 0, 2).reshape(heads_here, HEAD)
        kv_b = s[:, heads_here * piece :].reshape(shards, 2, KV_HEADS, piece)
        kv_b = kv_b.transpose(1, 2, 0, 3).reshape(2, KV_HEADS, HEAD)
        kv_b = lax.dynamic_slice_in_dim(kv_b, head_pick, 1, 1)
        bias = jnp.concatenate([q_b.reshape(1, -1), kv_b.reshape(1, -1)], axis=1).astype(F32)
        return jnp.concatenate([wq, wk, wv], axis=1), wo, gains.astype(F32), bias

    kept = [[dict(), dict()] for _ in range(2)]
    names = ("normed", "query", "kv", "lse", "attended")
    more_names = ("normed_two", "gate", "up", "inner")
    attn_weights, ffn_weights = [attention_weights(packed_low), None], [None, None]
    places = [(*tables[q], *segs[q]) for q in range(seqs)]

    def keep(layer, names, values):
        kept[layer].update(zip(names, values))
        return values[len(names) :]

    kept = [dict(), dict()]
    attn_a, attn_b = keep(0, names, attention_forward(attn_weights[0], places, (hidden,)))
    kept[0].update(layer_in=hidden, attn_a=attn_a, attn_b=attn_b)
    attn_b, own_low, down_low = lax.optimization_barrier((attn_b, own_low, down_low))
    ffn_weights[0] = own_low, down_low
    packed_high = lax.all_gather(after(packed_shards[1], attn_b), ranks, axis=0)
    own_high = lax.all_gather(after(gate_up_shards[1], attn_b), ranks, axis=0, tiled=True)
    down_high = lax.all_gather(after(down_shards[1], attn_b), ranks, axis=0)
    gain = attn_weights[0][2][1:]
    part_b, ffn_a = keep(
        0, more_names, ffn_forward(False, hidden, attn_a, attn_b, gain, ffn_weights[0])
    )

    packed_high, part_b = lax.optimization_barrier((packed_high, part_b))
    attn_weights[1] = attention_weights(packed_high)
    inputs = (hidden, attn_a, ffn_a, attn_b, part_b)
    part_b, attn_a, _, layer_in = keep(1, names, attention_forward(attn_weights[1], places, inputs))
    part_b, own_high, down_high = lax.optimization_barrier((part_b, own_high, down_high))
    ffn_weights[1] = own_high, down_high
    gain = attn_weights[1][2][1:]
    part_b, ffn_a, attn_b = keep(
        1, more_names, ffn_forward(True, layer_in, attn_a, part_b, gain, ffn_weights[1])
    )
    kept[1].update(layer_in=layer_in, attn_a=attn_a, attn_b=attn_b)
    upstream = lax.dynamic_index_in_dim(out_grad, micro, 0, keepdims=False).reshape(seqs * span, width)
    k = kept[1]
    *wide_grads, grad_b, sum_a, ffn_b = ffn_backward(upstream, k["gate"], k["up"], ffn_weights[1], part_b)
    attn_sum, ffn_sum = jnp.concatenate([attn_a, attn_b]), jnp.concatenate([ffn_a, ffn_b])
    outs = [layer_in, (layer_in.astype(F32) + attn_sum.astype(F32) + ffn_sum.astype(F32)).astype(BF16)]

    def to_section(values):
        low = lax.ppermute(values[0], "section", [(1, 0)])
        high = lax.ppermute(values[1], "section", [(0, 1)])
        both = jnp.stack([jnp.where(first, values[0], high), jnp.where(first, low, values[1])])
        return both.reshape(2, seqs, span, width)

    section_out = to_section(outs)

    in_grads = [None, None]
    gate_up_grads, down_grads, packed_grads, gains_grads = [[None, None] for _ in range(4)]
    for layer in (1, 0):
        weights, k = attn_weights[layer], kept[layer]
        if layer == 0:
            below = (sum_a, kept[1]["layer_in"], attn_weights[1][2][:1])
            *wide_grads, grad_b, sum_a, _, upstream, gain_one = ffn_backward(
                attn_grad, k["gate"], k["up"], ffn_weights[0], part_b, below
            )
            in_grads[1] = upstream
            gains_grads[1] = jnp.stack([jnp.sum(gain_one, axis=0), gain_two])
            sum_a, gate_up_grads[1] = lax.optimization_barrier((sum_a, gate_up_grads[1]))
        own_w, other_w = [dot("rd,rf->df", k["normed_two"], g).astype(BF16) for g in wide_grads]
        own_w = (own_w.astype(F32) + swap(other_w).astype(F32)).astype(BF16)
        down_w = dot("rd,rf->df", upstream, k["inner"]).astype(BF16)
        down_w = down_w.reshape(shards, 2, half, ff + spare)
        down_own = lax.dynamic_index_in_dim(down_w, sec, 1, keepdims=False)
        down_other = lax.dynamic_index_in_dim(down_w, 1 - sec, 1, keepdims=False)
        down_own = (down_own.astype(F32) + swap(down_other).astype(F32)).astype(BF16)
        own_w, down_own, sum_a = lax.optimization_barrier((own_w, down_own, sum_a))
        gate_up_grads[layer] = lax.psum_scatter(own_w, ranks, scatter_dimension=0, tiled=True)
        down_grads[layer] = lax.psum_scatter(
            down_own.reshape(shards * half, ff + spare), ranks, scatter_dimension=0, tiled=True
        )

        attn_grad, lin_grad, gain_two, part_b, sum_a, _ = attention_backward(upstream, sum_a, grad_b, k, weights, places)
        gain_two = jnp.sum(gain_two, axis=0)
        if layer == 0:
            part_b, down_grads[1] = lax.optimization_barrier((part_b, down_grads[1]))
        lin_w = dot("rd,re->de", k["normed"], lin_grad)
        out_w = dot("rd,re->de", attn_grad, k["attended"])
        bias = jnp.sum(lin_grad.astype(F32), axis=0)
        bias = bias.reshape(heads_here + 2, shards, piece).transpose(1, 0, 2).reshape(shards, (heads_here + 2) * piece)
        bias = jnp.pad(bias, ((0, 0), (0, -bias.shape[1] % shard)))
        bias = bias.reshape(shards, -1, shard).transpose(0, 2, 1).reshape(width, -1)
        bias = jnp.pad(bias, ((0, 0), (0, HEAD - bias.shape[1])))
        packed_grads[layer] = jnp.concatenate([lin_w, out_w, bias], axis=1).astype(BF16)

    low = lax.ppermute(packed_grads[0], "section", [(1, 0)])
    high = lax.ppermute(packed_grads[1], "section", [(0, 1)])
    packed_total = jnp.where(
        first, packed_grads[0].astype(F32) + low.astype(F32), packed_grads[1].astype(F32) + high.astype(F32)
    ).astype(BF16)
    last_part, gate_up_grads[0], down_grads[0], packed_total = lax.optimization_barrier(
        (part_b, gate_up_grads[0], down_grads[0], packed_total)
    )
    packed_total = lax.psum_scatter(packed_total, ranks, scatter_dimension=0, tiled=True).astype(F32)
    in_grads[0], gain_one = last_grads(last_part, sum_a, attn_grad, kept[0]["layer_in"], attn_weights[0][2][:1])
    gains_grads[0] = jnp.stack([jnp.sum(gain_one, axis=0), gain_two])
    input_grad = to_section(in_grads)
    low = lax.ppermute(gains_grads[0], "section", [(1, 0)])
    high = lax.ppermute(gains_grads[1], "section", [(0, 1)])
    gains_grad = jnp.where(first, gains_grads[0] + low, gains_grads[1] + high)
    for axis in ranks:
        if lax.axis_size(axis) == 2:
            gains_grad = gains_grad + lax.ppermute(gains_grad, axis, [(0, 1), (1, 0)])
        else:
            gains_grad = lax.psum(gains_grad, axis)
    at = (lax.axis_index("dp") * lax.axis_size("ctx") + lax.axis_index("ctx")) * shard
    gains_grad = lax.dynamic_slice_in_dim(gains_grad, at, shard, 1)
    q_grad = packed_total[:, :q_cols]
    kv_narrow = packed_total[:, q_cols : q_cols + 2 * HEAD].reshape(shard, 2, HEAD)
    o_grad = packed_total[:, q_cols + 2 * HEAD : 2 * q_cols + 2 * HEAD].T
    extra = packed_total[:, 2 * q_cols + 2 * HEAD :]
    bias_cols = -(-(heads_here + 2) * piece // shard)
    bias = extra[:, :bias_cols].T.reshape(-1)[: (heads_here + 2) * piece].reshape(heads_here + 2, piece)
    q_bias_grad = bias[:heads_here]
    kv_bias = bias[heads_here:].reshape(1, -1)
    kv_bias = jnp.pad(kv_bias, ((0, 15), (0, -kv_bias.shape[1] % (2 * HEAD))))
    mine = jnp.concatenate([kv_narrow.reshape(shard, 2 * HEAD), kv_bias[:, : 2 * HEAD]]).astype(BF16)
    mine = (mine.astype(F32) + lax.ppermute(mine, "tp", [(0, 1), (1, 0), (2, 3), (3, 2)]).astype(F32)).astype(BF16)
    theirs = lax.ppermute(mine, "tp", [(0, 2), (2, 0), (1, 3), (3, 1)])
    mine, theirs = mine.astype(F32), theirs.astype(F32)
    low = head_pick == 0
    heads = jnp.stack([jnp.where(low, mine, theirs), jnp.where(low, theirs, mine)])
    kv_grad = heads[:, :shard].reshape(KV_HEADS, shard, 2, HEAD).transpose(2, 1, 0, 3).reshape(2, shard, KV_HEADS * HEAD)
    kv_bias_grad = heads[:, shard, : 2 * piece].reshape(KV_HEADS, 2, piece).transpose(1, 0, 2)

    def collect(values):
        kept_half = jnp.where(first, values[0], values[1])
        other = swap(jnp.where(first, values[1], values[0]))
        return jnp.where(first, kept_half, other), jnp.where(first, other, kept_half)

    gate_up_grad = jnp.stack(collect(gate_up_grads))[..., :ff].astype(F32)
    down_grad = jnp.concatenate(collect(down_grads), axis=0)[:, :ff].T.astype(F32)
    return (
        section_out[None],
        input_grad[None],
        q_grad[None],
        kv_grad[None],
        o_grad[None],
        gate_up_grad[None],
        down_grad[None],
        gains_grad[None],
        q_bias_grad[None],
        kv_bias_grad[None],
    )


def solution(mesh):
    in_specs = (
        P(None, "dp", "ctx", None),
        P(None, "dp", "ctx"),
        P(None, "dp", "ctx"),
        P("section", ("dp", "ctx"), "tp"),
        P("section", None, ("dp", "ctx"), None),
        P("section", "tp", ("dp", "ctx")),
        P("section", None, ("dp", "ctx"), "tp"),
        P("section", "tp", ("dp", "ctx")),
        P("section", None, ("dp", "ctx")),
        P("section", "tp", ("dp", "ctx")),
        P("section", None, None, ("dp", "ctx")),
        P(None, "dp", "ctx", None),
    )
    out_specs = (
        P("section", None, "dp", "ctx", None),
        P("section", None, "dp", "ctx", None),
        P("section", ("dp", "ctx"), "tp"),
        P("section", None, ("dp", "ctx"), None),
        P("section", "tp", ("dp", "ctx")),
        P("section", None, ("dp", "ctx"), "tp"),
        P("section", "tp", ("dp", "ctx")),
        P("section", None, ("dp", "ctx")),
        P("section", "tp", ("dp", "ctx")),
        P("section", None, None, ("dp", "ctx")),
    )
    return jax.shard_map(local, mesh=mesh, in_specs=in_specs, out_specs=out_specs, check_vma=False)
```

```python
import functools

import jax
import jax.numpy as jnp
from jax import lax
from jax.experimental import pallas as pl
from jax.experimental.pallas import tpu as pltpu
from jax.sharding import PartitionSpec as P

HEADS = 12
KV_HEADS = 2
HEAD = 128

EPS = 1e-06
ROPE_BASE = 1000000.0
NEG = -1e30
SCALE = HEAD ** (-0.5)
TILE = 768
VMEM_LIMIT = 60 << 20
MESH = pl.DeviceIdType.MESH

F32 = jnp.float32
BF16 = jnp.bfloat16


def dot(form, left, right):
    return jnp.einsum(form, left, right, preferred_element_type=F32)


def swap(value):
    return lax.ppermute(value, "section", [(0, 1), (1, 0)])


class Chain:
    def __init__(self, part, total, from_end, from_peer, sems):
        self.part, self.total = part, total
        self.from_end, self.from_peer = from_end, from_peer
        self.sems = sems
        self.chunks = sems.shape[1]
        self.rows = part.shape[0] // self.chunks
        self.is_middle, self.inner, self.outer = line_places()

    def at(self, ref, c):
        return ref.at[pl.ds(pl.multiple_of(c * self.rows, self.rows), self.rows)]

    def copy(self, source, target, c, step, place):
        return pltpu.make_async_remote_copy(
            src_ref=self.at(source, c),
            dst_ref=self.at(target, c),
            send_sem=self.sems.at[2 * step, c],
            recv_sem=self.sems.at[2 * step + 1, c],
            device_id={"tp": place},
            device_id_type=MESH,
        )

    def inward(self, c):
        return self.copy(self.part, self.from_end, c, 0, self.inner)

    def across(self, c):
        return self.copy(self.total, self.from_peer, c, 1, self.inner)

    def outward(self, c):
        return self.copy(self.total, self.total, c, 2, self.outer)

    def start(self):
        @pl.when(jnp.logical_not(self.is_middle))
        def _():
            @pl.loop(0, self.chunks)
            def _(c):
                self.inward(c).start()

    def join(self, c):
        self.inward(c).wait_recv()
        self.at(self.total, c)[...] = self.at(self.part, c)[...] + self.at(self.from_end, c)[...]
        self.across(c).start()

    def close(self, c):
        self.across(c).wait()
        self.at(self.total, c)[...] = self.at(self.total, c)[...] + self.at(self.from_peer, c)[...]
        self.outward(c).start()

    def step(self, c):
        @pl.when(self.is_middle & (c < self.chunks))
        def _():
            self.join(c)

            @pl.when(c > 0)
            def _():
                self.close(c - 1)

    def drain(self, done):
        @pl.when(self.is_middle)
        def _():
            if done < self.chunks:

                @pl.loop(done, self.chunks)
                def _(c):
                    self.step(c)

            self.close(self.chunks - 1)

        @pl.when(jnp.logical_not(self.is_middle))
        def _():
            @pl.loop(0, self.chunks)
            def _(c):
                self.outward(c).wait_recv()

    def settle(self):
        @pl.when(self.is_middle)
        def _():
            @pl.loop(0, self.chunks)
            def _(c):
                self.outward(c).wait_send()

        @pl.when(jnp.logical_not(self.is_middle))
        def _():
            @pl.loop(0, self.chunks)
            def _(c):
                self.inward(c).wait_send()


def line_places():
    place = lax.axis_index("tp")
    is_middle = (place == 1) | (place == 2)
    return is_middle, jnp.where(place < 2, place + 1, place - 1), jnp.where(place < 2, place - 1, place + 1)


def greet(ctx_count=1, cores=0):
    is_middle, inner, outer = line_places()
    me = lax.axis_index("ctx")
    barrier = pltpu.get_barrier_semaphore()
    for step in range(1, ctx_count):
        pl.semaphore_signal(barrier, inc=1, device_id={"ctx": lax.rem(me + step, ctx_count)}, device_id_type=MESH)
    if cores:
        peer = 1 - lax.axis_index("section")
        pl.semaphore_signal(barrier, inc=1, device_id={"section": peer}, device_id_type=MESH)
    pl.semaphore_signal(barrier, inc=1, device_id={"tp": inner}, device_id_type=MESH)

    @pl.when(is_middle)
    def _():
        pl.semaphore_signal(barrier, inc=1, device_id={"tp": outer}, device_id_type=MESH)
        pl.semaphore_wait(barrier, 1 + ctx_count + cores)

    @pl.when(jnp.logical_not(is_middle))
    def _():
        pl.semaphore_wait(barrier, ctx_count + cores)


def ab(ref):
    rows = ref.shape[0] // 2
    return ref.at[pl.ds(0, rows)], ref.at[pl.ds(rows, rows)]


def chain_scratch(shape):
    return [pltpu.VMEM(shape, BF16)] * 2 + [pltpu.SemaphoreType.DMA((6, min(8, shape[0] // 16)))]


CHAIN_REFS = 3
VMEM = pl.BlockSpec(memory_space=pltpu.VMEM)
ANY = pl.BlockSpec(memory_space=pl.ANY)


def params(collective_id):
    return pltpu.CompilerParams(collective_id=collective_id, has_side_effects=True, vmem_limit_bytes=VMEM_LIMIT)


def cost():
    return pl.CostEstimate(flops=1 << 20, bytes_accessed=1 << 20, transcendentals=0)


class Taker:
    def __init__(self, refs):
        self.refs = list(refs)

    def __call__(self, count):
        taken, self.refs = self.refs[:count], self.refs[count:]
        return taken


def ticker(chain, taken):
    return (lambda c: None) if chain is None else (lambda c: chain.step(c + taken))


def mm(left, right):
    return jnp.dot(left, right, preferred_element_type=F32)


def mm_t(left, right):
    return lax.dot_general(left, right, (((1,), (1,)), ((), ())), preferred_element_type=F32)


def mm_0(left, right):
    return lax.dot_general(left, right, (((0,), (0,)), ((), ())), preferred_element_type=F32)


def tile_at(ref, j, size=TILE):
    return ref.at[:, pl.ds(pl.multiple_of(j * size, size), size)]


def rows_at(ref, j, size=TILE):
    return ref.at[pl.ds(pl.multiple_of(j * size, size), size)]


def by_rows(rows, body, block=64):
    @pl.loop(0, rows // block)
    def _(i):
        body(pl.ds(pl.multiple_of(i * block, block), block))


def send_either(first, source, one, two, sem, start):
    @pl.when(first)
    def _():
        copy = pltpu.make_async_copy(source, one, sem)
        copy.start() if start else copy.wait()

    @pl.when(jnp.logical_not(first))
    def _():
        copy = pltpu.make_async_copy(source, two, sem)
        copy.start() if start else copy.wait()


def norm_factor(values):
    return lax.rsqrt(jnp.mean(values * values, axis=-1, keepdims=True) + EPS)


def normalize_rows(source, gain, target):
    def body(rows):
        values = source(rows)
        target[rows] = (values * norm_factor(values) * gain[...]).astype(BF16)

    by_rows(target.shape[0], body)


def norm_back_rows(upstream, grad_in, source, gain, gain_grad, target):
    def body(rows):
        values = source(rows)
        factor = norm_factor(values)
        unit = values * factor
        grad = grad_in[rows].astype(F32)
        per_row = grad * unit
        mean = jnp.mean(per_row * gain[...], axis=-1, keepdims=True)
        target[rows] = (upstream[rows].astype(F32) + factor * (grad * gain[...] - unit * mean)).astype(BF16)
        gain_grad[...] += jnp.sum(per_row.reshape(-1, 8, per_row.shape[1]), axis=0)

    by_rows(target.shape[0], body)


class FfnWeights:
    def __init__(self, sources, targets, sems, down_sems, by_columns):
        self.own, self.down_own = sources
        self.gate, self.up, self.down = targets
        self.sems, self.down_sems = sems, down_sems
        self.sec = lax.axis_index("section")
        self.first = self.sec == 0
        self.by_columns = by_columns
        self.wide = tile_at if by_columns else rows_at
        self.tiles, self.outs = self.gate.shape[1] // TILE, self.gate.shape[0] // TILE
        self.wide_count, self.deep_count = (self.tiles, self.outs) if by_columns else (self.outs, self.tiles)

    def here(self, j, target):
        return pltpu.make_async_copy(self.wide(self.own, j), self.wide(target, j), self.sems.at[0, j])

    def there(self, j, target):
        return pltpu.make_async_remote_copy(
            src_ref=self.wide(self.own, j),
            dst_ref=self.wide(target, j),
            send_sem=self.sems.at[1, j],
            recv_sem=self.sems.at[2, j],
            device_id={"section": 1 - self.sec},
            device_id_type=MESH,
        )

    def on_own(self, action):
        @pl.when(self.first)
        def _():
            action(self.gate, self.up)

        @pl.when(jnp.logical_not(self.first))
        def _():
            action(self.up, self.gate)

    def wait_gate(self, j):
        @pl.when(self.first)
        def _():
            self.here(j, self.gate).wait()

        @pl.when(jnp.logical_not(self.first))
        def _():
            self.there(j, self.gate).wait_recv()

    def wait_up(self, j):
        @pl.when(self.first)
        def _():
            self.there(j, self.up).wait_recv()

        @pl.when(jnp.logical_not(self.first))
        def _():
            self.here(j, self.up).wait()

    def down_parts(self, j):
        shards, half = self.down_own.shape[0], self.down_own.shape[1]
        per_tile = shards if not self.by_columns else shards // self.outs
        for i in range(per_tile):
            if self.by_columns:
                shard = j * per_tile + i
                source, columns = self.down_own.at[shard], slice(None)
            else:
                shard, columns = i, pl.ds(pl.multiple_of(j * TILE, TILE), TILE)
                source = self.down_own.at[shard, :, columns]

            def place(sec, shard=shard, columns=columns):
                return self.down.at[pl.ds(pl.multiple_of((2 * shard + sec) * half, 16), half), columns]

            yield source, place(self.sec), place(1 - self.sec), i

    def down_here(self, source, place, i, j):
        return pltpu.make_async_copy(source, place, self.down_sems.at[0, j, i])

    def down_there(self, source, place, i, j):
        return pltpu.make_async_remote_copy(
            src_ref=source,
            dst_ref=place,
            send_sem=self.down_sems.at[1, j, i],
            recv_sem=self.down_sems.at[2, j, i],
            device_id={"section": 1 - self.sec},
            device_id_type=MESH,
        )

    def start_wide(self, local):
        def action(own, other):
            @pl.loop(0, self.wide_count)
            def _(j):
                (self.here if local else self.there)(j, own).start()

        self.on_own(action)

    def start_deep(self, local):
        @pl.loop(0, self.deep_count)
        def _(j):
            for source, mine, theirs, i in self.down_parts(j):
                (self.down_here if local else self.down_there)(source, mine, i, j).start()

    def wait_down(self, j):
        for source, mine, theirs, i in self.down_parts(j):
            self.down_here(source, mine, i, j).wait()
            self.down_there(source, theirs, i, j).wait_recv()

    def finish(self):
        def action(own, other):
            @pl.loop(0, self.wide_count)
            def _(j):
                self.there(j, own).wait_send()

        self.on_own(action)

        @pl.loop(0, self.deep_count)
        def _(j):
            for source, mine, theirs, i in self.down_parts(j):
                self.down_there(source, mine, i, j).wait_send()


def ffn_forward_stage(weights, normed, outs, held, one, two, out_sems, result, tick, wait):
    gate, up, inner = held

    @pl.loop(0, weights.tiles)
    def _(j):
        if wait:
            weights.wait_gate(j)
        one[...] = mm(normed[...], tile_at(weights.gate, j)[...])
        tick(2 * j)
        if wait:
            weights.wait_up(j)
        two[...] = mm(normed[...], tile_at(weights.up, j)[...])
        columns = pl.ds(pl.multiple_of(j * TILE, TILE), TILE)

        def body(rows):
            g, u = one[rows], two[rows]
            gate[rows, columns] = g.astype(BF16)
            up[rows, columns] = u.astype(BF16)
            inner[rows, columns] = (g * jax.nn.sigmoid(g) * u).astype(BF16)

        by_rows(one.shape[0], body)
        tick(2 * j + 1)
        for k in range(3):
            pltpu.make_async_copy(tile_at(held[k], j), tile_at(outs[k], j), out_sems.at[k, j]).start()

    @pl.loop(0, weights.outs)
    def _(n):
        if wait:
            weights.wait_down(n)
        tile_at(result, n)[...] = mm_t(inner[...], rows_at(weights.down, n)[...]).astype(BF16)
        tick(2 * weights.tiles + n)

    return 2 * weights.tiles + weights.outs


def wait_out(held, outs, out_sems):
    @pl.loop(0, held[0].shape[1] // TILE)
    def _(j):
        for k in range(len(held)):
            pltpu.make_async_copy(tile_at(held[k], j), tile_at(outs[k], j), out_sems.at[k, j]).wait()


def ffn_forward_kernel(lead, *refs):
    take = Taker(refs)
    layer, attn_a, last_b, gain = take(4)
    layer_a, layer_b = ab(layer)
    sources = take(2)
    (normed_a, normed_b), *outs = [ab(ref) for ref in take(4)]
    outs_a, outs_b = zip(*outs)
    result_b, total_a = take(2)
    attn_b = take(1)[0] if lead else last_b
    targets, held = take(3), take(3)
    one, two, result_a, w_sems, down_sems, out_sems = take(6)
    chain_a = Chain(result_a, total_a, *take(CHAIN_REFS))
    chain_b = Chain(last_b, attn_b, *take(CHAIN_REFS)) if lead else None
    weights = FfnWeights(sources, targets, w_sems, down_sems, True)
    weights.start_wide(True)
    weights.start_deep(True)
    greet(cores=1)
    if lead:
        chain_b.start()
    weights.start_wide(False)
    weights.start_deep(False)
    normalize_rows(lambda r: layer_a[r].astype(F32) + attn_a[r].astype(F32), gain, normed_a)
    if lead:
        chain_b.step(0)
    tick = ticker(chain_b, 1)
    done = ffn_forward_stage(weights, normed_a, outs_a, held, one, two, out_sems, result_a, tick, True)
    chain_a.start()
    if lead:
        chain_b.drain(1 + done)
        chain_a.step(0)
    normalize_rows(lambda r: layer_b[r].astype(F32) + attn_b[r].astype(F32), gain, normed_b)
    wait_out(held, outs_a, out_sems)
    if not lead:
        chain_a.step(0)
    tick = ticker(chain_a, 1)
    done = ffn_forward_stage(weights, normed_b, outs_b, held, one, two, out_sems, result_b, tick, False)
    chain_a.drain(1 + done)
    chain_a.settle()
    if lead:
        chain_b.settle()
    weights.finish()
    wait_out(held, outs_b, out_sems)


def down_sem_shape(weights, tiles):
    return pltpu.SemaphoreType.DMA((3, tiles, weights[1].shape[0]))


def ffn_forward(lead, layer_in, attn_a, last_b, gain, weights):
    rows, width = attn_a.shape
    ff = weights[0].shape[1]
    tiles = max(ff, width) // TILE
    narrow = jax.ShapeDtypeStruct((rows, width), BF16)
    both, wide = jax.ShapeDtypeStruct((2 * rows, width), BF16), jax.ShapeDtypeStruct((2 * rows, ff), BF16)
    return pl.pallas_call(
        functools.partial(ffn_forward_kernel, lead),
        out_shape=[both, wide, wide, wide] + [narrow] * (2 + lead),
        in_specs=[VMEM] * 4 + [ANY] * 2,
        out_specs=[VMEM] + [ANY] * 3 + [VMEM] * (2 + lead),
        scratch_shapes=[pltpu.VMEM((width, ff), BF16)] * 3
        + [pltpu.VMEM((rows, ff), BF16)] * 3
        + [pltpu.VMEM((rows, TILE), F32)] * 2
        + [pltpu.VMEM((rows, width), BF16)]
        + [pltpu.SemaphoreType.DMA((3, tiles)), down_sem_shape(weights, tiles), pltpu.SemaphoreType.DMA((3, tiles))]
        + chain_scratch((rows, width)) * (1 + lead),
        compiler_params=params(1 + lead),
        cost_estimate=cost(),
    )(layer_in, attn_a, last_b, gain, *weights)


def ffn_backward_stage(weights, grad, ins, outs, held, one, in_sems, out_sems, result, tick, wait):
    gate, up = held
    own_out, other_out = outs

    @pl.loop(0, weights.tiles)
    def _(j):
        if wait:
            weights.wait_down(j)
        one[...] = mm(grad[...], tile_at(weights.down, j)[...])
        tick(j)
        for k in range(2):
            pltpu.make_async_copy(tile_at(ins[k], j), tile_at(held[k], j), in_sems.at[k, j]).wait()
        columns = pl.ds(pl.multiple_of(j * TILE, TILE), TILE)

        def body(rows):
            g, u, d = gate[rows, columns].astype(F32), up[rows, columns].astype(F32), one[rows]
            sig = jax.nn.sigmoid(g)
            d = d * sig
            gate[rows, columns] = (d * u * (1.0 + g * (1.0 - sig))).astype(BF16)
            up[rows, columns] = (d * g).astype(BF16)

        by_rows(one.shape[0], body)

    def sending(start):
        @pl.loop(0, weights.tiles)
        def _(j):
            own, other = tile_at(own_out, j), tile_at(other_out, j)
            send_either(weights.first, tile_at(gate, j), own, other, out_sems.at[0, j], start)
            send_either(weights.first, tile_at(up, j), other, own, out_sems.at[1, j], start)

    sending(True)

    @pl.loop(0, weights.outs)
    def _(n):
        if wait:
            weights.wait_gate(n)
            weights.wait_up(n)
        one[...] = mm_t(gate[...], rows_at(weights.gate, n)[...])
        tick(weights.tiles + 2 * n)
        tile_at(result, n)[...] = (one[...] + mm_t(up[...], rows_at(weights.up, n)[...])).astype(BF16)
        tick(weights.tiles + 2 * n + 1)

    return weights.tiles + 2 * weights.outs, lambda: sending(False)


def ffn_backward_kernel(low, *refs):
    take = Taker(refs)
    grad, last_b = take(2)
    grad_a, grad_b = ab(grad)
    ins_a, ins_b = zip(*[ab(ref) for ref in take(2)])
    sources = take(2)
    if low:
        sum_a, layer, gain = take(3)
        layer_a, layer_b = ab(layer)
    outs_a, outs_b = zip(*[ab(ref) for ref in take(2)])
    result_b, total_a, total_b = take(3)
    if low:
        made, gain_grad = take(2)
        made_a, made_b = ab(made)
    targets, held = take(3), take(2)
    one, result_a, w_sems, down_sems, in_sems, out_sems = take(6)
    chain_a = Chain(result_a, total_a, *take(CHAIN_REFS))
    chain_b = Chain(last_b, total_b, *take(CHAIN_REFS))
    weights = FfnWeights(sources, targets, w_sems, down_sems, False)

    def fetch(ins):
        @pl.loop(0, weights.tiles)
        def _(j):
            for k in range(2):
                pltpu.make_async_copy(tile_at(ins[k], j), tile_at(held[k], j), in_sems.at[k, j]).start()

    weights.start_deep(True)
    fetch(ins_a)
    weights.start_wide(True)
    greet(cores=1)
    chain_b.start()
    weights.start_deep(False)
    weights.start_wide(False)
    if low:
        gain_grad[...] = jnp.zeros_like(gain_grad)
        norm_back_rows(grad_a, sum_a, lambda r: layer_a[r].astype(F32), gain, gain_grad, made_a)
        grad_a = made_a
    chain_b.step(0)
    done, sent_a = ffn_backward_stage(
        weights, grad_a, ins_a, outs_a, held, one, in_sems, out_sems, result_a, ticker(chain_b, 1), True
    )
    chain_a.start()
    sent_a()
    fetch(ins_b)
    chain_b.drain(1 + done)
    chain_a.step(0)
    if low:
        norm_back_rows(grad_b, total_b, lambda r: layer_b[r].astype(F32), gain, gain_grad, made_b)
        grad_b = made_b
    done, sent_b = ffn_backward_stage(
        weights, grad_b, ins_b, outs_b, held, one, in_sems, out_sems, result_b, ticker(chain_a, 1), False
    )
    chain_a.drain(1 + done)
    chain_a.settle()
    chain_b.settle()
    weights.finish()
    sent_b()


def ffn_backward(grad, gate, up, weights, last_b, below=None):
    rows, width = last_b.shape
    ff = weights[0].shape[1]
    tiles = max(ff, width) // TILE
    low = below is not None
    narrow = jax.ShapeDtypeStruct((rows, width), BF16)
    both, wide = jax.ShapeDtypeStruct((2 * rows, width), BF16), jax.ShapeDtypeStruct((2 * rows, ff), BF16)
    more = [both, jax.ShapeDtypeStruct((8, width), F32)] if low else []
    return pl.pallas_call(
        functools.partial(ffn_backward_kernel, low),
        out_shape=[wide] * 2 + [narrow] * 3 + more,
        in_specs=[VMEM] * 2 + [ANY] * 4 + [VMEM] * (3 if low else 0),
        out_specs=[ANY] * 2 + [VMEM] * (3 + len(more)),
        scratch_shapes=[pltpu.VMEM((width, ff), BF16)] * 3
        + [pltpu.VMEM((rows, ff), BF16)] * 2
        + [pltpu.VMEM((rows, TILE), F32)]
        + [pltpu.VMEM((rows, width), BF16)]
        + [pltpu.SemaphoreType.DMA((3, tiles)), down_sem_shape(weights, tiles)]
        + [pltpu.SemaphoreType.DMA((2, tiles))] * 2
        + chain_scratch((rows, width)) * 2,
        compiler_params=params(3 + low),
        cost_estimate=cost(),
    )(grad, last_b, gate, up, *weights, *(below or ()))


def last_kernel(part, sum_a, grad, layer, gain, made, gain_grad, total, *scratch):
    chain = Chain(part, total, *scratch)
    greet()
    chain.start()
    gain_grad[...] = jnp.zeros_like(gain_grad)
    grads, layers, mades = ab(grad), ab(layer), ab(made)
    chain.step(0)
    norm_back_rows(grads[0], sum_a, lambda r: layers[0][r].astype(F32), gain, gain_grad, mades[0])
    chain.drain(1)
    norm_back_rows(grads[1], total, lambda r: layers[1][r].astype(F32), gain, gain_grad, mades[1])
    chain.settle()


def last_grads(part, sum_a, grad, layer, gain):
    shape = part.shape
    return pl.pallas_call(
        last_kernel,
        out_shape=[jax.ShapeDtypeStruct(grad.shape, BF16), jax.ShapeDtypeStruct((8, shape[1]), F32)],
        in_specs=[VMEM] * 5,
        out_specs=[VMEM] * 2,
        scratch_shapes=[pltpu.VMEM(shape, BF16)] + chain_scratch(shape),
        compiler_params=params(0),
        cost_estimate=cost(),
    )(part, sum_a, grad, layer, gain)


def roped(values, cosine, sine):
    return values * cosine + pltpu.roll(values, HEAD // 2, 1) * sine


def unroped(grads, cosine, sine):
    return grads * cosine + pltpu.roll(grads * sine, HEAD // 2, 1)


def allowed_keys(seg_rows, seg_keys, i, block):
    rows, keys = seg_rows.shape[0], seg_keys.shape[1]
    first_row = lax.axis_index("ctx") * rows + i * block
    row_at = first_row + lax.broadcasted_iota(jnp.int32, (block, keys), 0)
    key_at = lax.broadcasted_iota(jnp.int32, (block, keys), 1)
    own = seg_rows[pl.ds(pl.multiple_of(i * block, block), block)]
    return (key_at <= row_at) & (own == seg_keys[...])


class AttentionWeights:
    def __init__(self, sources, targets, sems):
        self.own, self.other = sources
        self.w_lin, self.w_out = targets
        self.sems = sems

    def copies(self):
        sec = lax.axis_index("section")
        q_cols = self.w_out.shape[1]
        heads_here = q_cols // HEAD
        head = lax.axis_index("tp") * heads_here // (HEADS // KV_HEADS)
        shards, half = self.own.shape[:2]
        for k, (source, side) in enumerate(((self.own, sec), (self.other, 1 - sec))):
            for i in range(shards):
                rows = pl.ds(pl.multiple_of((2 * i + side) * half, 16), half)
                key_at = pl.multiple_of(q_cols + head * HEAD, HEAD)
                value_at = pl.multiple_of(q_cols + (KV_HEADS + head) * HEAD, HEAD)
                pieces = (
                    (pl.ds(0, q_cols), self.w_lin.at[rows, pl.ds(0, q_cols)]),
                    (pl.ds(key_at, HEAD), self.w_lin.at[rows, pl.ds(q_cols, HEAD)]),
                    (pl.ds(value_at, HEAD), self.w_lin.at[rows, pl.ds(q_cols + HEAD, HEAD)]),
                    (pl.ds(q_cols + 2 * KV_HEADS * HEAD, q_cols), self.w_out.at[rows]),
                )
                for p, (columns, target) in enumerate(pieces):
                    yield pltpu.make_async_copy(source.at[i, :, columns], target, self.sems.at[k, i, p])

    def start(self):
        for copy in self.copies():
            copy.start()

    def wait(self):
        for copy in self.copies():
            copy.wait()


def attention_scratch(halves, q_cols):
    shards, half = halves[0].shape[:2]
    width = 2 * shards * half
    return [
        pltpu.VMEM((width, q_cols + 2 * HEAD), BF16),
        pltpu.VMEM((width, q_cols), BF16),
        pltpu.SemaphoreType.DMA((2, shards, 4)),
    ]


def attention_forward_stage(layer_in, gain, w_lin, w_out, bias, places, outs, result, kv_sems, tick):
    cosine, sine, seg_rows, seg_keys = places
    normed, query, kv, lse, attended = outs
    rows, q_cols = query.shape
    heads = q_cols // HEAD
    count = kv.shape[0] // rows
    me = lax.axis_index("ctx")
    block = min(256, rows)
    normalize_rows(lambda r: layer_in[r].astype(F32), gain, normed)
    tick(0)
    mine = kv.at[pl.ds(pl.multiple_of(me * rows, rows), rows)]
    lin = mm(normed[...], w_lin[:, q_cols:]) + bias[:, q_cols:]
    mine[:, :HEAD] = roped(lin[:, :HEAD], cosine[...], sine[...]).astype(BF16)
    mine[:, HEAD:] = lin[:, HEAD:].astype(BF16)

    def passing(offset):
        return pltpu.make_async_remote_copy(
            src_ref=mine,
            dst_ref=mine,
            send_sem=kv_sems.at[0, offset],
            recv_sem=kv_sems.at[1, offset],
            device_id={"ctx": lax.rem(me + offset, count)},
            device_id_type=MESH,
        )

    for offset in range(1, count):
        passing(offset).start()
    tick(1)
    lin = mm(normed[...], w_lin[:, :q_cols]) + bias[:, :q_cols]
    for h in range(heads):
        columns = slice(h * HEAD, (h + 1) * HEAD)
        query[:, columns] = roped(lin[:, columns], cosine[...], sine[...]).astype(BF16)
    for offset in range(1, count):
        passing(offset).wait_recv()

    @pl.loop(0, rows // block)
    def _(i):
        at = pl.ds(pl.multiple_of(i * block, block), block)
        allowed = allowed_keys(seg_rows, seg_keys, i, block)
        lane = lax.broadcasted_iota(jnp.int32, (block, HEAD), 1)
        logs = jnp.zeros((block, HEAD), F32)
        for h in range(heads):
            columns = slice(h * HEAD, (h + 1) * HEAD)
            scores = jnp.where(allowed, mm_t(query[at, columns], kv[:, :HEAD]) * SCALE, NEG)
            top = jnp.max(scores, axis=-1, keepdims=True)
            probs = jnp.exp(scores - top)
            sums = jnp.sum(probs, axis=-1, keepdims=True)
            probs = (probs * (1.0 / sums)).astype(BF16)
            attended[at, columns] = mm(probs, kv[:, HEAD:]).astype(BF16)
            logs = jnp.where(lane == h, top + jnp.log(sums), logs)
            tick(2 + heads * i + h)
        lse[at] = logs

    base = 2 + heads * (rows // block)

    @pl.loop(0, result.shape[1] // TILE)
    def _(n):
        tile_at(result, n)[...] = mm_t(attended[...], rows_at(w_out, n)[...]).astype(BF16)
        tick(base + n)

    for offset in range(1, count):
        passing(offset).wait_send()
    return base + result.shape[1] // TILE


def attention_forward_kernel(low, *refs):
    take = Taker(refs)
    gain, bias = take(2)
    halves = take(2)
    places_a, places_b = take(4), take(4)
    layer_a, layer_b = ab(take(1)[0])
    if not low:
        adds_a, adds_b, (last_b,) = (layer_a, *take(2)), (layer_b, *take(1)), take(1)
    outs_a, outs_b = zip(*[ab(ref) for ref in take(5)])
    if low:
        total_a, total_b = take(2)
    else:
        result_b, total_a, last_sum_b, layer = take(4)
        layer_a, layer_b = ab(layer)
    result_a, kv_sems_a, kv_sems_b = take(3)
    w_lin, w_out, w_sems = take(3)
    weights = AttentionWeights(halves, (w_lin, w_out), w_sems)
    weights.start()
    if low:
        (result_b,) = take(1)
    chain_a = Chain(result_a, total_a, *take(CHAIN_REFS))
    chain_b = Chain(result_b, total_b, *take(CHAIN_REFS)) if low else Chain(last_b, last_sum_b, *take(CHAIN_REFS))
    greet(kv_sems_a.shape[1])
    if not low:
        chain_b.start()

        def body(rows):
            layer_a[rows] = sum(ref[rows].astype(F32) for ref in adds_a).astype(BF16)

        by_rows(layer_a.shape[0], body)
    weights.wait()
    tick = ticker(None if low else chain_b, 0)
    done = attention_forward_stage(layer_a, gain, w_lin, w_out, bias, places_a, outs_a, result_a, kv_sems_a, tick)
    chain_a.start()
    if not low:
        chain_b.drain(done)
        chain_a.step(0)

        def body(rows):
            layer_b[rows] = sum(ref[rows].astype(F32) for ref in (*adds_b, last_sum_b)).astype(BF16)

        by_rows(layer_b.shape[0], body)
    taken = 0 if low else 1
    tick = ticker(chain_a, taken)
    done = attention_forward_stage(layer_b, gain, w_lin, w_out, bias, places_b, outs_b, result_b, kv_sems_b, tick)
    if low:
        chain_b.start()
    chain_a.drain(taken + done)
    if low:
        chain_b.drain(0)
    chain_a.settle()
    chain_b.settle()


def attention_forward(weights, places, inputs):
    halves, q_cols, gains, bias = weights
    rows, width = inputs[0].shape[0] // 2, inputs[0].shape[1]
    keys = places[0][3].shape[1]
    count = keys // rows
    low = len(inputs) == 1
    narrow, both = jax.ShapeDtypeStruct((rows, width), BF16), jax.ShapeDtypeStruct((2 * rows, width), BF16)
    heads_out = jax.ShapeDtypeStruct((2 * rows, q_cols), BF16)
    kv_out = jax.ShapeDtypeStruct((2 * keys, 2 * HEAD), BF16)
    lse_out = jax.ShapeDtypeStruct((2 * rows, HEAD), F32)
    outs = [both, heads_out, kv_out, lse_out, heads_out] + ([narrow] * 2 if low else [narrow] * 3 + [both])
    args = (gains[:1], bias, *halves, *places[0], *places[1], *inputs)
    return pl.pallas_call(
        functools.partial(attention_forward_kernel, low),
        out_shape=outs,
        in_specs=[VMEM] * 2 + [ANY] * 2 + [VMEM] * (len(args) - 4),
        out_specs=[VMEM] * len(outs),
        scratch_shapes=[pltpu.VMEM((rows, width), BF16)]
        + [pltpu.SemaphoreType.DMA((2, count))] * 2
        + attention_scratch(halves, q_cols)
        + [pltpu.VMEM((rows, width), BF16)] * low
        + chain_scratch((rows, width)) * 2,
        compiler_params=params(5 + low),
        cost_estimate=cost(),
    )(*args)


def attention_backward_stage(ins, sum_in, gain, w_lin, w_out, places, outs, gain_grad, result, scratch, tick):
    upstream, layer_in, attn_out, query, kv, lse, attended = ins
    cosine, sine, seg_rows, seg_keys = places
    attn_grad, lin = outs
    heads_grad, kv_grad, q_part, sent, got, kv_sems = scratch
    rows, q_cols = query.shape
    heads = q_cols // HEAD
    count = kv.shape[0] // rows
    me = lax.axis_index("ctx")
    block = min(256, rows)
    kv_grad[...] = jnp.zeros_like(kv_grad)
    norm_back_rows(
        upstream, sum_in, lambda r: layer_in[r].astype(F32) + attn_out[r].astype(F32), gain, gain_grad, attn_grad
    )
    tick(0)
    heads_grad[...] = mm(attn_grad[...], w_out[...]).astype(BF16)
    tick(1)

    @pl.loop(0, rows // block)
    def _(i):
        at = pl.ds(pl.multiple_of(i * block, block), block)
        allowed = allowed_keys(seg_rows, seg_keys, i, block)
        for h in range(heads):
            columns = slice(h * HEAD, (h + 1) * HEAD)
            scores = mm_t(query[at, columns], kv[:, :HEAD]) * SCALE - lse[at, h : h + 1]
            probs = jnp.exp(jnp.where(allowed, scores, NEG))
            grad = heads_grad[at, columns]
            row_sum = jnp.sum(attended[at, columns].astype(F32) * grad.astype(F32), axis=-1, keepdims=True)
            score_grad = (probs * (mm_t(grad, kv[:, HEAD:]) - row_sum)).astype(BF16)
            q_grad = mm(score_grad, kv[:, :HEAD]) * SCALE
            lin[at, columns] = unroped(q_grad, cosine[at], sine[at]).astype(BF16)
            kv_grad[:, :HEAD] += mm_0(score_grad, query[at, columns])
            kv_grad[:, HEAD:] += mm_0(probs.astype(BF16), grad)
            tick(2 + heads * i + h)

    def passing(offset):
        return pltpu.make_async_remote_copy(
            src_ref=sent.at[offset - 1],
            dst_ref=got.at[offset - 1],
            send_sem=kv_sems.at[0, offset],
            recv_sem=kv_sems.at[1, offset],
            device_id={"ctx": lax.rem(me + offset, count)},
            device_id_type=MESH,
        )

    for offset in range(1, count):
        peer = pl.ds(pl.multiple_of(lax.rem(me + offset, count) * rows, rows), rows)
        sent[offset - 1, :, :HEAD] = (kv_grad[peer, :HEAD] * SCALE).astype(BF16)
        sent[offset - 1, :, HEAD:] = kv_grad[peer, HEAD:].astype(BF16)
        passing(offset).start()
    base = 2 + heads * (rows // block)

    @pl.loop(0, result.shape[1] // TILE)
    def _(n):
        tile_at(q_part, n)[...] = mm_t(lin[:, :q_cols], rows_at(w_lin, n)[:, :q_cols])
        tick(base + n)

    mine = pl.ds(pl.multiple_of(me * rows, rows), rows)
    k_grad, v_grad = kv_grad[mine, :HEAD] * SCALE, kv_grad[mine, HEAD:]
    for offset in range(1, count):
        passing(offset).wait_recv()
        k_grad = k_grad + got[offset - 1, :, :HEAD].astype(F32)
        v_grad = v_grad + got[offset - 1, :, HEAD:].astype(F32)
    lin[:, q_cols : q_cols + HEAD] = unroped(k_grad, cosine[...], sine[...]).astype(BF16)
    lin[:, q_cols + HEAD :] = v_grad.astype(BF16)

    @pl.loop(0, result.shape[1] // TILE)
    def _(n):
        kv_part = mm_t(lin[:, q_cols:], rows_at(w_lin, n)[:, q_cols:])
        tile_at(result, n)[...] = (tile_at(q_part, n)[...] + kv_part).astype(BF16)


    for offset in range(1, count):
        passing(offset).wait_send()
    return base + result.shape[1] // TILE


def attention_backward_kernel(*refs):
    take = Taker(refs)
    (gain,) = take(1)
    halves = take(2)
    places_a, places_b = take(4), take(4)
    ins_a, ins_b = zip(*[ab(ref) for ref in take(6)])
    attn_a, attn_b = take(2)
    ins_a, ins_b = (*ins_a[:2], attn_a, *ins_a[2:]), (*ins_b[:2], attn_b, *ins_b[2:])
    sum_a, last_b = take(2)
    outs_a, outs_b = zip(*[ab(ref) for ref in take(2)])
    gain_grad, result_b, total_a, total_b = take(4)
    heads_grad, kv_grad, q_part, result_a = take(4)
    w_lin, w_out, w_sems = take(3)
    weights = AttentionWeights(halves, (w_lin, w_out), w_sems)
    weights.start()
    exchange_a, exchange_b = take(3), take(3)
    chain_a = Chain(result_a, total_a, *take(CHAIN_REFS))
    chain_b = Chain(last_b, total_b, *take(CHAIN_REFS))
    greet(exchange_a[2].shape[1])
    chain_b.start()
    gain_grad[...] = jnp.zeros_like(gain_grad)
    weights.wait()
    scratch = (heads_grad, kv_grad, q_part, *exchange_a)
    done = attention_backward_stage(
        ins_a, sum_a, gain, w_lin, w_out, places_a, outs_a, gain_grad, result_a, scratch, ticker(chain_b, 0)
    )
    chain_a.start()
    chain_b.drain(done)
    chain_a.step(0)
    scratch = (heads_grad, kv_grad, q_part, *exchange_b)
    done = attention_backward_stage(
        ins_b, total_b, gain, w_lin, w_out, places_b, outs_b, gain_grad, result_b, scratch, ticker(chain_a, 1)
    )
    chain_a.drain(1 + done)
    chain_a.settle()
    chain_b.settle()


def attention_backward(upstream, sum_a, last_b, kept, weights, places):
    halves, q_cols, gains, bias = weights
    rows, width = sum_a.shape
    keys = places[0][3].shape[1]
    count = keys // rows
    narrow = jax.ShapeDtypeStruct((rows, width), BF16)
    both = jax.ShapeDtypeStruct((2 * rows, width), BF16)
    lin_out = jax.ShapeDtypeStruct((2 * rows, q_cols + 2 * HEAD), BF16)
    outs = [both, lin_out] + [jax.ShapeDtypeStruct((8, width), F32)] + [narrow] * 3
    names = ("layer_in", "query", "kv", "lse", "attended", "attn_a", "attn_b")
    args = (gains[1:], *halves, *places[0], *places[1], upstream)
    args += (*[kept[name] for name in names], sum_a, last_b)
    exchange = [pltpu.VMEM((max(count - 1, 1), rows, 2 * HEAD), BF16)] * 2 + [pltpu.SemaphoreType.DMA((2, count))]
    return pl.pallas_call(
        attention_backward_kernel,
        out_shape=outs,
        in_specs=[VMEM] + [ANY] * 2 + [VMEM] * (len(args) - 3),
        out_specs=[VMEM] * len(outs),
        scratch_shapes=[
            pltpu.VMEM((rows, q_cols), BF16),
            pltpu.VMEM((keys, 2 * HEAD), F32),
            pltpu.VMEM((rows, width), F32),
            pltpu.VMEM((rows, width), BF16),
        ]
        + attention_scratch(halves, q_cols)
        + exchange * 2
        + chain_scratch((rows, width)) * 2,
        compiler_params=params(7),
        cost_estimate=cost(),
    )(*args)


def rope_tables(places):
    steps = jnp.arange(HEAD // 2, dtype=F32) * (2.0 / HEAD)
    inverse = ROPE_BASE ** (-steps)
    angles = places.astype(F32)[..., None] * inverse
    angles = jnp.concatenate([angles, angles], axis=-1)
    return (jnp.cos(angles), jnp.sin(angles))


def norm_back(grad_out, rows_in, factor, gain):
    unit = rows_in * factor
    gain_grad = jnp.sum(grad_out * unit, axis=0)
    weighted = grad_out * gain
    return (
        factor * (weighted - unit * jnp.mean(weighted * unit, axis=-1, keepdims=True)),
        gain_grad,
    )


def over_ctx(value):
    if lax.axis_size("ctx") == 2:
        other = lax.ppermute(value, "ctx", [(0, 1), (1, 0)])
        low = lax.axis_index("ctx") == 0
        return jnp.concatenate([jnp.where(low, value, other), jnp.where(low, other, value)], axis=-1)
    return lax.all_gather(value, "ctx", axis=value.ndim - 1, tiled=True)


def input_backward(normed_one_grad, middle_grad, kept, gains):
    layer_in = kept["layer_in"].astype(F32)
    factor = lax.rsqrt(jnp.mean(layer_in * layer_in, axis=-1, keepdims=True) + EPS)
    norm_grad, gain_one = norm_back(normed_one_grad.astype(F32), layer_in, factor, gains[0])
    return (middle_grad.astype(F32) + norm_grad).astype(BF16), gain_one


def local(
    section_in,
    segments,
    positions,
    query_weight,
    kv_weight,
    output_weight,
    gate_up,
    down_weight,
    norm_gains,
    query_bias,
    kv_bias,
    out_grad,
):
    sec = lax.axis_index("section")
    first = sec == 0
    group = HEADS // KV_HEADS
    heads_here = HEADS // lax.axis_size("tp")
    head_pick = lax.axis_index("tp") * heads_here // group
    shards = lax.axis_size("dp") * lax.axis_size("ctx")
    ranks = ("dp", "ctx")
    seqs, span, width = section_in.shape[1:]
    shard = query_weight.shape[1]
    q_cols = query_weight.shape[2]
    ff = gate_up.shape[3]

    def per_layer(mine, theirs):
        return jnp.where(first, mine, theirs), jnp.where(first, theirs, mine)

    half = shard // 2
    kv_width = KV_HEADS * HEAD

    def halves(rows):
        mine = lax.dynamic_slice_in_dim(rows, sec * half, half, 0)
        return per_layer(mine, swap(lax.dynamic_slice_in_dim(rows, (1 - sec) * half, half, 0)))

    def after(value, event):
        return lax.optimization_barrier((value, event))[0]

    piece = HEAD // shards
    biases = jnp.concatenate([query_bias[0].reshape(-1), kv_bias[0].reshape(-1)])
    n_biases = biases.shape[0]
    biases = jnp.pad(biases, (0, -n_biases % shard)).reshape(-1, shard).T
    extra = jnp.concatenate([norm_gains[0].T, biases], axis=1)
    n_extra = extra.shape[1]
    extra = jnp.pad(extra, ((0, 0), (0, HEAD - n_extra)))
    packed = jnp.concatenate([query_weight[0], kv_weight[0, 0], kv_weight[0, 1], output_weight[0].T, extra], axis=1)
    packed_shards = halves(packed)
    first_shard, gate_up, down_weight, positions, segments, section_in = lax.optimization_barrier(
        (packed_shards[0], gate_up, down_weight, positions, segments, section_in)
    )
    packed_low = lax.all_gather(first_shard, ranks, axis=0)
    spare = -ff % TILE
    wide = jnp.pad(gate_up[0], ((0, 0), (0, 0), (0, spare)))
    mine = lax.dynamic_index_in_dim(wide, sec, 0, keepdims=False)
    theirs = swap(lax.dynamic_index_in_dim(wide, 1 - sec, 0, keepdims=False))
    gate_up_shards = per_layer(mine, theirs)
    down_shards = halves(jnp.pad(down_weight[0].T, ((0, 0), (0, spare))))

    micro = sec
    seg = lax.dynamic_index_in_dim(segments, micro, 0, keepdims=False)
    pos = lax.dynamic_index_in_dim(positions, micro, 0, keepdims=False)
    hidden = lax.dynamic_index_in_dim(section_in, micro, 0, keepdims=False)
    seg_keys = over_ctx(seg)
    segs, tables = [], []
    for q in range(seqs):
        segs.append((seg[q][:, None], seg_keys[q][None]))
        cosine, sine = rope_tables(pos[q])
        tables.append((cosine, jnp.where(jnp.arange(HEAD) < HEAD // 2, -sine, sine)))
    hidden = hidden.reshape(seqs * span, width)

    packed_low, gate_up_shards, down_shards, packed_shards, segs, tables, hidden = lax.optimization_barrier(
        (packed_low, gate_up_shards, down_shards, packed_shards, segs, tables, hidden)
    )
    own_low = lax.all_gather(gate_up_shards[0], ranks, axis=0, tiled=True)
    down_low = lax.all_gather(down_shards[0], ranks, axis=0)

    def attention_weights(own):
        parts = own, swap(own)
        small = [part[..., 2 * q_cols + 2 * kv_width :] for part in parts]
        s = jnp.stack(per_layer(*small), axis=1).reshape(width, -1)
        gains = s[:, :2].T
        s = s[:, 2:n_extra].T.reshape(-1, shards, shard).transpose(1, 0, 2).reshape(shards, -1)[:, :n_biases]
        q_b = s[:, : heads_here * piece].reshape(shards, heads_here, piece).transpose(1, 0, 2).reshape(heads_here, HEAD)
        kv_b = s[:, heads_here * piece :].reshape(shards, 2, KV_HEADS, piece)
        kv_b = kv_b.transpose(1, 2, 0, 3).reshape(2, KV_HEADS, HEAD)
        kv_b = lax.dynamic_slice_in_dim(kv_b, head_pick, 1, 1)
        bias = jnp.concatenate([q_b.reshape(1, -1), kv_b.reshape(1, -1)], axis=1).astype(F32)
        return parts, q_cols, gains.astype(F32), bias

    names = ("normed", "query", "kv", "lse", "attended")
    more_names = ("normed_two", "gate", "up", "inner")
    attn_weights, ffn_weights = [attention_weights(packed_low), None], [None, None]
    places = [(*tables[q], *segs[q]) for q in range(seqs)]

    def keep(layer, names, values):
        kept[layer].update(zip(names, values))
        return values[len(names) :]

    kept = [dict(), dict()]
    attn_a, attn_b = keep(0, names, attention_forward(attn_weights[0], places, (hidden,)))
    kept[0].update(layer_in=hidden, attn_a=attn_a, attn_b=attn_b)
    attn_b, own_low, down_low = lax.optimization_barrier((attn_b, own_low, down_low))
    ffn_weights[0] = own_low, down_low
    packed_high = lax.all_gather(after(packed_shards[1], attn_b), ranks, axis=0)
    own_high = lax.all_gather(after(gate_up_shards[1], attn_b), ranks, axis=0, tiled=True)
    down_high = lax.all_gather(after(down_shards[1], attn_b), ranks, axis=0)
    gain = attn_weights[0][2][1:]
    part_b, ffn_a = keep(
        0, more_names, ffn_forward(False, hidden, attn_a, attn_b, gain, ffn_weights[0])
    )

    packed_high, part_b = lax.optimization_barrier((packed_high, part_b))
    attn_weights[1] = attention_weights(packed_high)
    inputs = (hidden, attn_a, ffn_a, attn_b, part_b)
    part_b, attn_a, _, layer_in = keep(1, names, attention_forward(attn_weights[1], places, inputs))
    part_b, own_high, down_high = lax.optimization_barrier((part_b, own_high, down_high))
    ffn_weights[1] = own_high, down_high
    gain = attn_weights[1][2][1:]
    part_b, ffn_a, attn_b = keep(
        1, more_names, ffn_forward(True, layer_in, attn_a, part_b, gain, ffn_weights[1])
    )
    kept[1].update(layer_in=layer_in, attn_a=attn_a, attn_b=attn_b)
    upstream = lax.dynamic_index_in_dim(out_grad, micro, 0, keepdims=False).reshape(seqs * span, width)
    k = kept[1]
    *wide_grads, grad_b, sum_a, ffn_b = ffn_backward(upstream, k["gate"], k["up"], ffn_weights[1], part_b)
    attn_sum, ffn_sum = jnp.concatenate([attn_a, attn_b]), jnp.concatenate([ffn_a, ffn_b])
    outs = [layer_in, (layer_in.astype(F32) + attn_sum.astype(F32) + ffn_sum.astype(F32)).astype(BF16)]

    def to_section(values, low, high):
        both = jnp.stack([jnp.where(first, values[0], high), jnp.where(first, low, values[1])])
        return both.reshape(2, seqs, span, width)

    def to_low(value):
        return lax.ppermute(value, "section", [(1, 0)])

    def to_high(value):
        return lax.ppermute(value, "section", [(0, 1)])

    out_low, out_high = to_low(outs[0]), to_high(outs[1])

    in_grads = [None, None]
    gate_up_grads, down_grads, packed_grads, gains_grads = [[None, None] for _ in range(4)]
    for layer in (1, 0):
        weights, k = attn_weights[layer], kept[layer]
        if layer == 0:
            below = (sum_a, kept[1]["layer_in"], attn_weights[1][2][:1])
            *wide_grads, grad_b, sum_a, _, upstream, gain_one = ffn_backward(
                attn_grad, k["gate"], k["up"], ffn_weights[0], part_b, below
            )
            in_grads[1] = upstream
            in_high = to_high(upstream)
            gains_grads[1] = jnp.stack([jnp.sum(gain_one, axis=0), gain_two])
            sum_a, gate_up_grads[1] = lax.optimization_barrier((sum_a, gate_up_grads[1]))
        own_w, other_w = [dot("rd,rf->df", k["normed_two"], g).astype(BF16) for g in wide_grads]
        other_w = swap(other_w)
        down_w = dot("rd,rf->df", upstream, k["inner"]).astype(BF16)
        down_w = down_w.reshape(shards, 2, half, ff + spare)
        down_own = lax.dynamic_index_in_dim(down_w, sec, 1, keepdims=False)
        down_other = swap(lax.dynamic_index_in_dim(down_w, 1 - sec, 1, keepdims=False))
        own_w = (own_w.astype(F32) + other_w.astype(F32)).astype(BF16)
        own_w, down_other = lax.optimization_barrier((own_w, down_other))
        down_own = (down_own.astype(F32) + down_other.astype(F32)).astype(BF16)
        own_w, down_own, sum_a = lax.optimization_barrier((own_w, down_own, sum_a))
        gate_up_grads[layer] = lax.psum_scatter(own_w, ranks, scatter_dimension=0, tiled=True)
        down_grads[layer] = lax.psum_scatter(
            down_own.reshape(shards * half, ff + spare), ranks, scatter_dimension=0, tiled=True
        )

        attn_grad, lin_grad, gain_two, part_b, sum_a, _ = attention_backward(upstream, sum_a, grad_b, k, weights, places)
        gain_two = jnp.sum(gain_two, axis=0)
        if layer == 0:
            part_b, down_grads[1], out_low, out_high, in_high = lax.optimization_barrier(
                (part_b, down_grads[1], out_low, out_high, in_high)
            )
        lin_w = dot("rd,re->de", k["normed"], lin_grad)
        out_w = dot("rd,re->de", attn_grad, k["attended"])
        bias = jnp.sum(lin_grad.astype(F32), axis=0)
        bias = bias.reshape(heads_here + 2, shards, piece).transpose(1, 0, 2).reshape(shards, (heads_here + 2) * piece)
        bias = jnp.pad(bias, ((0, 0), (0, -bias.shape[1] % shard)))
        bias = bias.reshape(shards, -1, shard).transpose(0, 2, 1).reshape(width, -1)
        bias = jnp.pad(bias, ((0, 0), (0, HEAD - bias.shape[1])))
        packed_grads[layer] = jnp.concatenate([lin_w, out_w, bias], axis=1).astype(BF16)

    low = lax.ppermute(packed_grads[0], "section", [(1, 0)])
    high = lax.ppermute(packed_grads[1], "section", [(0, 1)])
    packed_total = jnp.where(
        first, packed_grads[0].astype(F32) + low.astype(F32), packed_grads[1].astype(F32) + high.astype(F32)
    ).astype(BF16)
    last_part, gate_up_grads[0], down_grads[0], packed_total = lax.optimization_barrier(
        (part_b, gate_up_grads[0], down_grads[0], packed_total)
    )
    packed_total = lax.psum_scatter(packed_total, ranks, scatter_dimension=0, tiled=True).astype(F32)
    in_grads[0], gain_one = last_grads(last_part, sum_a, attn_grad, kept[0]["layer_in"], attn_weights[0][2][:1])
    gains_grads[0] = jnp.stack([jnp.sum(gain_one, axis=0), gain_two])
    in_low = to_low(in_grads[0])
    low = lax.ppermute(gains_grads[0], "section", [(1, 0)])
    high = lax.ppermute(gains_grads[1], "section", [(0, 1)])
    gains_grad = jnp.where(first, gains_grads[0] + low, gains_grads[1] + high)
    for axis in ranks:
        if lax.axis_size(axis) == 2:
            gains_grad = gains_grad + lax.ppermute(gains_grad, axis, [(0, 1), (1, 0)])
        else:
            gains_grad = lax.psum(gains_grad, axis)
    at = (lax.axis_index("dp") * lax.axis_size("ctx") + lax.axis_index("ctx")) * shard
    gains_grad = lax.dynamic_slice_in_dim(gains_grad, at, shard, 1)
    q_grad = packed_total[:, :q_cols]
    kv_narrow = packed_total[:, q_cols : q_cols + 2 * HEAD].reshape(shard, 2, HEAD)
    o_grad = packed_total[:, q_cols + 2 * HEAD : 2 * q_cols + 2 * HEAD].T
    extra = packed_total[:, 2 * q_cols + 2 * HEAD :]
    bias_cols = -(-(heads_here + 2) * piece // shard)
    bias = extra[:, :bias_cols].T.reshape(-1)[: (heads_here + 2) * piece].reshape(heads_here + 2, piece)
    q_bias_grad = bias[:heads_here]
    kv_bias = bias[heads_here:].reshape(1, -1)
    kv_bias = jnp.pad(kv_bias, ((0, 15), (0, -kv_bias.shape[1] % (2 * HEAD))))
    mine = jnp.concatenate([kv_narrow.reshape(shard, 2 * HEAD), kv_bias[:, : 2 * HEAD]]).astype(BF16)
    mine, gate_up_grads, down_grads = lax.optimization_barrier((mine, gate_up_grads, down_grads))
    mine = (mine.astype(F32) + lax.ppermute(mine, "tp", [(0, 1), (1, 0), (2, 3), (3, 2)]).astype(F32)).astype(BF16)
    theirs = lax.ppermute(mine, "tp", [(0, 2), (2, 0), (1, 3), (3, 1)])
    mine, theirs = mine.astype(F32), theirs.astype(F32)
    low = head_pick == 0
    heads = jnp.stack([jnp.where(low, mine, theirs), jnp.where(low, theirs, mine)])
    kv_grad = heads[:, :shard].reshape(KV_HEADS, shard, 2, HEAD).transpose(2, 1, 0, 3).reshape(2, shard, KV_HEADS * HEAD)
    kv_bias_grad = heads[:, shard, : 2 * piece].reshape(KV_HEADS, 2, piece).transpose(1, 0, 2)

    def collect(values):
        kept_half = jnp.where(first, values[0], values[1])
        other = swap(jnp.where(first, values[1], values[0]))
        return jnp.where(first, kept_half, other), jnp.where(first, other, kept_half)

    section_out = to_section(outs, out_low, out_high)
    input_grad = to_section(in_grads, in_low, in_high)
    gate_up_grad = jnp.stack(collect(gate_up_grads))[..., :ff].astype(F32)
    down_grad = jnp.concatenate(collect(down_grads), axis=0)[:, :ff].T.astype(F32)
    return (
        section_out[None],
        input_grad[None],
        q_grad[None],
        kv_grad[None],
        o_grad[None],
        gate_up_grad[None],
        down_grad[None],
        gains_grad[None],
        q_bias_grad[None],
        kv_bias_grad[None],
    )


def solution(mesh):
    in_specs = (
        P(None, "dp", "ctx", None),
        P(None, "dp", "ctx"),
        P(None, "dp", "ctx"),
        P("section", ("dp", "ctx"), "tp"),
        P("section", None, ("dp", "ctx"), None),
        P("section", "tp", ("dp", "ctx")),
        P("section", None, ("dp", "ctx"), "tp"),
        P("section", "tp", ("dp", "ctx")),
        P("section", None, ("dp", "ctx")),
        P("section", "tp", ("dp", "ctx")),
        P("section", None, None, ("dp", "ctx")),
        P(None, "dp", "ctx", None),
    )
    out_specs = (
        P("section", None, "dp", "ctx", None),
        P("section", None, "dp", "ctx", None),
        P("section", ("dp", "ctx"), "tp"),
        P("section", None, ("dp", "ctx"), None),
        P("section", "tp", ("dp", "ctx")),
        P("section", None, ("dp", "ctx"), "tp"),
        P("section", "tp", ("dp", "ctx")),
        P("section", None, ("dp", "ctx")),
        P("section", "tp", ("dp", "ctx")),
        P("section", None, None, ("dp", "ctx")),
    )
    return jax.shard_map(local, mesh=mesh, in_specs=in_specs, out_specs=out_specs, check_vma=False)
```

```python
import functools

import jax
import jax.numpy as jnp
from jax import lax
from jax.experimental import pallas as pl
from jax.experimental.pallas import tpu as pltpu
from jax.sharding import PartitionSpec as P

HEADS = 12
KV_HEADS = 2
HEAD = 128

EPS = 1e-06
ROPE_BASE = 1000000.0
NEG = -1e30
SCALE = HEAD ** (-0.5)
TILE = 768
VMEM_LIMIT = 60 << 20
MESH = pl.DeviceIdType.MESH

F32 = jnp.float32
BF16 = jnp.bfloat16


def dot(form, left, right):
    return jnp.einsum(form, left, right, preferred_element_type=F32)


def swap(value):
    return lax.ppermute(value, "section", [(0, 1), (1, 0)])


class Chain:
    def __init__(self, part, total, from_end, from_peer, sems):
        self.part, self.total = part, total
        self.from_end, self.from_peer = from_end, from_peer
        self.sems = sems
        self.chunks = sems.shape[1]
        self.rows = part.shape[0] // self.chunks
        self.is_middle, self.inner, self.outer = line_places()

    def at(self, ref, c):
        return ref.at[pl.ds(pl.multiple_of(c * self.rows, self.rows), self.rows)]

    def copy(self, source, target, c, step, place):
        return pltpu.make_async_remote_copy(
            src_ref=self.at(source, c),
            dst_ref=self.at(target, c),
            send_sem=self.sems.at[2 * step, c],
            recv_sem=self.sems.at[2 * step + 1, c],
            device_id={"tp": place},
            device_id_type=MESH,
        )

    def inward(self, c):
        return self.copy(self.part, self.from_end, c, 0, self.inner)

    def across(self, c):
        return self.copy(self.total, self.from_peer, c, 1, self.inner)

    def outward(self, c):
        return self.copy(self.total, self.total, c, 2, self.outer)

    def start(self):
        @pl.when(jnp.logical_not(self.is_middle))
        def _():
            @pl.loop(0, self.chunks)
            def _(c):
                self.inward(c).start()

    def join(self, c):
        self.inward(c).wait_recv()
        self.at(self.total, c)[...] = self.at(self.part, c)[...] + self.at(self.from_end, c)[...]
        self.across(c).start()

    def close(self, c):
        self.across(c).wait()
        self.at(self.total, c)[...] = self.at(self.total, c)[...] + self.at(self.from_peer, c)[...]
        self.outward(c).start()

    def step(self, c):
        @pl.when(self.is_middle & (c < self.chunks))
        def _():
            self.join(c)

            @pl.when(c > 0)
            def _():
                self.close(c - 1)

    def drain(self, done):
        @pl.when(self.is_middle)
        def _():
            if done < self.chunks:

                @pl.loop(done, self.chunks)
                def _(c):
                    self.step(c)

            self.close(self.chunks - 1)

        @pl.when(jnp.logical_not(self.is_middle))
        def _():
            @pl.loop(0, self.chunks)
            def _(c):
                self.outward(c).wait_recv()

    def settle(self):
        @pl.when(self.is_middle)
        def _():
            @pl.loop(0, self.chunks)
            def _(c):
                self.outward(c).wait_send()

        @pl.when(jnp.logical_not(self.is_middle))
        def _():
            @pl.loop(0, self.chunks)
            def _(c):
                self.inward(c).wait_send()


def line_places():
    place = lax.axis_index("tp")
    is_middle = (place == 1) | (place == 2)
    return is_middle, jnp.where(place < 2, place + 1, place - 1), jnp.where(place < 2, place - 1, place + 1)


def greet(ctx_count=1, cores=0):
    is_middle, inner, outer = line_places()
    me = lax.axis_index("ctx")
    barrier = pltpu.get_barrier_semaphore()
    for step in range(1, ctx_count):
        pl.semaphore_signal(barrier, inc=1, device_id={"ctx": lax.rem(me + step, ctx_count)}, device_id_type=MESH)
    if cores:
        peer = 1 - lax.axis_index("section")
        pl.semaphore_signal(barrier, inc=1, device_id={"section": peer}, device_id_type=MESH)
    pl.semaphore_signal(barrier, inc=1, device_id={"tp": inner}, device_id_type=MESH)

    @pl.when(is_middle)
    def _():
        pl.semaphore_signal(barrier, inc=1, device_id={"tp": outer}, device_id_type=MESH)
        pl.semaphore_wait(barrier, 1 + ctx_count + cores)

    @pl.when(jnp.logical_not(is_middle))
    def _():
        pl.semaphore_wait(barrier, ctx_count + cores)


def ab(ref):
    rows = ref.shape[0] // 2
    return ref.at[pl.ds(0, rows)], ref.at[pl.ds(rows, rows)]


def chain_scratch(shape):
    return [pltpu.VMEM(shape, BF16)] * 2 + [pltpu.SemaphoreType.DMA((6, min(8, shape[0] // 16)))]


CHAIN_REFS = 3
VMEM = pl.BlockSpec(memory_space=pltpu.VMEM)
ANY = pl.BlockSpec(memory_space=pl.ANY)


def params(collective_id):
    return pltpu.CompilerParams(collective_id=collective_id, has_side_effects=True, vmem_limit_bytes=VMEM_LIMIT)


def cost():
    return pl.CostEstimate(flops=1 << 20, bytes_accessed=1 << 20, transcendentals=0)


class Taker:
    def __init__(self, refs):
        self.refs = list(refs)

    def __call__(self, count):
        taken, self.refs = self.refs[:count], self.refs[count:]
        return taken


def ticker(chain, taken):
    return (lambda c: None) if chain is None else (lambda c: chain.step(c + taken))


def mm(left, right):
    return jnp.dot(left, right, preferred_element_type=F32)


def mm_t(left, right):
    return lax.dot_general(left, right, (((1,), (1,)), ((), ())), preferred_element_type=F32)


def mm_0(left, right):
    return lax.dot_general(left, right, (((0,), (0,)), ((), ())), preferred_element_type=F32)


def tile_at(ref, j, size=TILE):
    return ref.at[:, pl.ds(pl.multiple_of(j * size, size), size)]


def rows_at(ref, j, size=TILE):
    return ref.at[pl.ds(pl.multiple_of(j * size, size), size)]


def by_rows(rows, body, block=64):
    @pl.loop(0, rows // block)
    def _(i):
        body(pl.ds(pl.multiple_of(i * block, block), block))


def send_either(first, source, one, two, sem, start):
    @pl.when(first)
    def _():
        copy = pltpu.make_async_copy(source, one, sem)
        copy.start() if start else copy.wait()

    @pl.when(jnp.logical_not(first))
    def _():
        copy = pltpu.make_async_copy(source, two, sem)
        copy.start() if start else copy.wait()


def norm_factor(values):
    return lax.rsqrt(jnp.mean(values * values, axis=-1, keepdims=True) + EPS)


def normalize_rows(source, gain, target):
    def body(rows):
        values = source(rows)
        target[rows] = (values * norm_factor(values) * gain[...]).astype(BF16)

    by_rows(target.shape[0], body)


def norm_back_rows(upstream, grad_in, source, gain, gain_grad, target):
    def body(rows):
        values = source(rows)
        factor = norm_factor(values)
        unit = values * factor
        grad = grad_in[rows].astype(F32)
        per_row = grad * unit
        mean = jnp.mean(per_row * gain[...], axis=-1, keepdims=True)
        target[rows] = (upstream[rows].astype(F32) + factor * (grad * gain[...] - unit * mean)).astype(BF16)
        gain_grad[...] += jnp.sum(per_row.reshape(-1, 8, per_row.shape[1]), axis=0)

    by_rows(target.shape[0], body)


class FfnWeights:
    def __init__(self, sources, targets, sems, down_sems, by_columns):
        self.own, self.down_own = sources
        self.gate, self.up, self.down = targets
        self.sems, self.down_sems = sems, down_sems
        self.sec = lax.axis_index("section")
        self.first = self.sec == 0
        self.by_columns = by_columns
        self.wide = tile_at if by_columns else rows_at
        self.tiles, self.outs = self.gate.shape[1] // TILE, self.gate.shape[0] // TILE
        self.wide_count, self.deep_count = (self.tiles, self.outs) if by_columns else (self.outs, self.tiles)

    def here(self, j, target):
        return pltpu.make_async_copy(self.wide(self.own, j), self.wide(target, j), self.sems.at[0, j])

    def there(self, j, target):
        return pltpu.make_async_remote_copy(
            src_ref=self.wide(self.own, j),
            dst_ref=self.wide(target, j),
            send_sem=self.sems.at[1, j],
            recv_sem=self.sems.at[2, j],
            device_id={"section": 1 - self.sec},
            device_id_type=MESH,
        )

    def on_own(self, action):
        @pl.when(self.first)
        def _():
            action(self.gate, self.up)

        @pl.when(jnp.logical_not(self.first))
        def _():
            action(self.up, self.gate)

    def wait_gate(self, j):
        @pl.when(self.first)
        def _():
            self.here(j, self.gate).wait()

        @pl.when(jnp.logical_not(self.first))
        def _():
            self.there(j, self.gate).wait_recv()

    def wait_up(self, j):
        @pl.when(self.first)
        def _():
            self.there(j, self.up).wait_recv()

        @pl.when(jnp.logical_not(self.first))
        def _():
            self.here(j, self.up).wait()

    def down_parts(self, j):
        shards, half = self.down_own.shape[0], self.down_own.shape[1]
        per_tile = shards if not self.by_columns else shards // self.outs
        for i in range(per_tile):
            if self.by_columns:
                shard = j * per_tile + i
                source, columns = self.down_own.at[shard], slice(None)
            else:
                shard, columns = i, pl.ds(pl.multiple_of(j * TILE, TILE), TILE)
                source = self.down_own.at[shard, :, columns]

            def place(sec, shard=shard, columns=columns):
                return self.down.at[pl.ds(pl.multiple_of((2 * shard + sec) * half, 16), half), columns]

            yield source, place(self.sec), place(1 - self.sec), i

    def down_here(self, source, place, i, j):
        return pltpu.make_async_copy(source, place, self.down_sems.at[0, j, i])

    def down_there(self, source, place, i, j):
        return pltpu.make_async_remote_copy(
            src_ref=source,
            dst_ref=place,
            send_sem=self.down_sems.at[1, j, i],
            recv_sem=self.down_sems.at[2, j, i],
            device_id={"section": 1 - self.sec},
            device_id_type=MESH,
        )

    def start_wide(self, local):
        def action(own, other):
            @pl.loop(0, self.wide_count)
            def _(j):
                (self.here if local else self.there)(j, own).start()

        self.on_own(action)

    def start_deep(self, local):
        @pl.loop(0, self.deep_count)
        def _(j):
            for source, mine, theirs, i in self.down_parts(j):
                (self.down_here if local else self.down_there)(source, mine, i, j).start()

    def wait_down(self, j):
        for source, mine, theirs, i in self.down_parts(j):
            self.down_here(source, mine, i, j).wait()
            self.down_there(source, theirs, i, j).wait_recv()

    def finish(self):
        def action(own, other):
            @pl.loop(0, self.wide_count)
            def _(j):
                self.there(j, own).wait_send()

        self.on_own(action)

        @pl.loop(0, self.deep_count)
        def _(j):
            for source, mine, theirs, i in self.down_parts(j):
                self.down_there(source, mine, i, j).wait_send()


def ffn_forward_stage(weights, normed, outs, held, one, two, out_sems, result, tick, wait):
    gate, up, inner = held

    @pl.loop(0, weights.tiles)
    def _(j):
        if wait:
            weights.wait_gate(j)
        one[...] = mm(normed[...], tile_at(weights.gate, j)[...])
        tick(2 * j)
        if wait:
            weights.wait_up(j)
        two[...] = mm(normed[...], tile_at(weights.up, j)[...])
        columns = pl.ds(pl.multiple_of(j * TILE, TILE), TILE)

        def body(rows):
            g, u = one[rows], two[rows]
            gate[rows, columns] = g.astype(BF16)
            up[rows, columns] = u.astype(BF16)
            inner[rows, columns] = (g * jax.nn.sigmoid(g) * u).astype(BF16)

        by_rows(one.shape[0], body)
        tick(2 * j + 1)
        for k in range(3):
            pltpu.make_async_copy(tile_at(held[k], j), tile_at(outs[k], j), out_sems.at[k, j]).start()

    @pl.loop(0, weights.outs)
    def _(n):
        if wait:
            weights.wait_down(n)
        tile_at(result, n)[...] = mm_t(inner[...], rows_at(weights.down, n)[...]).astype(BF16)
        tick(2 * weights.tiles + n)

    return 2 * weights.tiles + weights.outs


def wait_out(held, outs, out_sems):
    @pl.loop(0, held[0].shape[1] // TILE)
    def _(j):
        for k in range(len(held)):
            pltpu.make_async_copy(tile_at(held[k], j), tile_at(outs[k], j), out_sems.at[k, j]).wait()


def ffn_forward_kernel(lead, *refs):
    take = Taker(refs)
    layer, attn_a, last_b, gain = take(4)
    layer_a, layer_b = ab(layer)
    sources = take(2)
    (normed_a, normed_b), *outs = [ab(ref) for ref in take(4)]
    outs_a, outs_b = zip(*outs)
    result_b, total_a = take(2)
    attn_b = take(1)[0] if lead else last_b
    targets, held = take(3), take(3)
    one, two, result_a, w_sems, down_sems, out_sems = take(6)
    chain_a = Chain(result_a, total_a, *take(CHAIN_REFS))
    chain_b = Chain(last_b, attn_b, *take(CHAIN_REFS)) if lead else None
    weights = FfnWeights(sources, targets, w_sems, down_sems, True)
    weights.start_wide(True)
    weights.start_deep(True)
    greet(cores=1)
    if lead:
        chain_b.start()
    weights.start_wide(False)
    weights.start_deep(False)
    normalize_rows(lambda r: layer_a[r].astype(F32) + attn_a[r].astype(F32), gain, normed_a)
    if lead:
        chain_b.step(0)
    tick = ticker(chain_b, 1)
    done = ffn_forward_stage(weights, normed_a, outs_a, held, one, two, out_sems, result_a, tick, True)
    chain_a.start()
    if lead:
        chain_b.drain(1 + done)
        chain_a.step(0)
    normalize_rows(lambda r: layer_b[r].astype(F32) + attn_b[r].astype(F32), gain, normed_b)
    wait_out(held, outs_a, out_sems)
    if not lead:
        chain_a.step(0)
    tick = ticker(chain_a, 1)
    done = ffn_forward_stage(weights, normed_b, outs_b, held, one, two, out_sems, result_b, tick, False)
    chain_a.drain(1 + done)
    chain_a.settle()
    if lead:
        chain_b.settle()
    weights.finish()
    wait_out(held, outs_b, out_sems)


def down_sem_shape(weights, tiles):
    return pltpu.SemaphoreType.DMA((3, tiles, weights[1].shape[0]))


def ffn_forward(lead, layer_in, attn_a, last_b, gain, weights):
    rows, width = attn_a.shape
    ff = weights[0].shape[1]
    tiles = max(ff, width) // TILE
    narrow = jax.ShapeDtypeStruct((rows, width), BF16)
    both, wide = jax.ShapeDtypeStruct((2 * rows, width), BF16), jax.ShapeDtypeStruct((2 * rows, ff), BF16)
    return pl.pallas_call(
        functools.partial(ffn_forward_kernel, lead),
        out_shape=[both, wide, wide, wide] + [narrow] * (2 + lead),
        in_specs=[VMEM] * 4 + [ANY] * 2,
        out_specs=[VMEM] + [ANY] * 3 + [VMEM] * (2 + lead),
        scratch_shapes=[pltpu.VMEM((width, ff), BF16)] * 3
        + [pltpu.VMEM((rows, ff), BF16)] * 3
        + [pltpu.VMEM((rows, TILE), F32)] * 2
        + [pltpu.VMEM((rows, width), BF16)]
        + [pltpu.SemaphoreType.DMA((3, tiles)), down_sem_shape(weights, tiles), pltpu.SemaphoreType.DMA((3, tiles))]
        + chain_scratch((rows, width)) * (1 + lead),
        compiler_params=params(1 + lead),
        cost_estimate=cost(),
    )(layer_in, attn_a, last_b, gain, *weights)


def ffn_backward_stage(weights, grad, ins, outs, held, one, in_sems, out_sems, result, tick, wait):
    gate, up = held
    own_out, other_out = outs

    @pl.loop(0, weights.tiles)
    def _(j):
        if wait:
            weights.wait_down(j)
        one[...] = mm(grad[...], tile_at(weights.down, j)[...])
        tick(j)
        for k in range(2):
            pltpu.make_async_copy(tile_at(ins[k], j), tile_at(held[k], j), in_sems.at[k, j]).wait()
        columns = pl.ds(pl.multiple_of(j * TILE, TILE), TILE)

        def body(rows):
            g, u, d = gate[rows, columns].astype(F32), up[rows, columns].astype(F32), one[rows]
            sig = jax.nn.sigmoid(g)
            d = d * sig
            gate[rows, columns] = (d * u * (1.0 + g * (1.0 - sig))).astype(BF16)
            up[rows, columns] = (d * g).astype(BF16)

        by_rows(one.shape[0], body)

    def sending(start):
        @pl.loop(0, weights.tiles)
        def _(j):
            own, other = tile_at(own_out, j), tile_at(other_out, j)
            send_either(weights.first, tile_at(gate, j), own, other, out_sems.at[0, j], start)
            send_either(weights.first, tile_at(up, j), other, own, out_sems.at[1, j], start)

    sending(True)

    @pl.loop(0, weights.outs)
    def _(n):
        if wait:
            weights.wait_gate(n)
            weights.wait_up(n)
        one[...] = mm_t(gate[...], rows_at(weights.gate, n)[...])
        tick(weights.tiles + 2 * n)
        tile_at(result, n)[...] = (one[...] + mm_t(up[...], rows_at(weights.up, n)[...])).astype(BF16)
        tick(weights.tiles + 2 * n + 1)

    return weights.tiles + 2 * weights.outs, lambda: sending(False)


def ffn_backward_kernel(low, *refs):
    take = Taker(refs)
    grad, last_b = take(2)
    grad_a, grad_b = ab(grad)
    ins_a, ins_b = zip(*[ab(ref) for ref in take(2)])
    sources = take(2)
    if low:
        sum_a, layer, gain = take(3)
        layer_a, layer_b = ab(layer)
    outs_a, outs_b = zip(*[ab(ref) for ref in take(2)])
    result_b, total_a, total_b = take(3)
    if low:
        made, gain_grad = take(2)
        made_a, made_b = ab(made)
    targets, held = take(3), take(2)
    one, result_a, w_sems, down_sems, in_sems, out_sems = take(6)
    chain_a = Chain(result_a, total_a, *take(CHAIN_REFS))
    chain_b = Chain(last_b, total_b, *take(CHAIN_REFS))
    weights = FfnWeights(sources, targets, w_sems, down_sems, False)

    def fetch(ins):
        @pl.loop(0, weights.tiles)
        def _(j):
            for k in range(2):
                pltpu.make_async_copy(tile_at(ins[k], j), tile_at(held[k], j), in_sems.at[k, j]).start()

    weights.start_deep(True)
    fetch(ins_a)
    weights.start_wide(True)
    greet(cores=1)
    chain_b.start()
    weights.start_deep(False)
    weights.start_wide(False)
    if low:
        gain_grad[...] = jnp.zeros_like(gain_grad)
        norm_back_rows(grad_a, sum_a, lambda r: layer_a[r].astype(F32), gain, gain_grad, made_a)
        grad_a = made_a
    chain_b.step(0)
    done, sent_a = ffn_backward_stage(
        weights, grad_a, ins_a, outs_a, held, one, in_sems, out_sems, result_a, ticker(chain_b, 1), True
    )
    chain_a.start()
    sent_a()
    fetch(ins_b)
    chain_b.drain(1 + done)
    chain_a.step(0)
    if low:
        norm_back_rows(grad_b, total_b, lambda r: layer_b[r].astype(F32), gain, gain_grad, made_b)
        grad_b = made_b
    done, sent_b = ffn_backward_stage(
        weights, grad_b, ins_b, outs_b, held, one, in_sems, out_sems, result_b, ticker(chain_a, 1), False
    )
    chain_a.drain(1 + done)
    chain_a.settle()
    chain_b.settle()
    weights.finish()
    sent_b()


def ffn_backward(grad, gate, up, weights, last_b, below=None):
    rows, width = last_b.shape
    ff = weights[0].shape[1]
    tiles = max(ff, width) // TILE
    low = below is not None
    narrow = jax.ShapeDtypeStruct((rows, width), BF16)
    both, wide = jax.ShapeDtypeStruct((2 * rows, width), BF16), jax.ShapeDtypeStruct((2 * rows, ff), BF16)
    more = [both, jax.ShapeDtypeStruct((8, width), F32)] if low else []
    return pl.pallas_call(
        functools.partial(ffn_backward_kernel, low),
        out_shape=[wide] * 2 + [narrow] * 3 + more,
        in_specs=[VMEM] * 2 + [ANY] * 4 + [VMEM] * (3 if low else 0),
        out_specs=[ANY] * 2 + [VMEM] * (3 + len(more)),
        scratch_shapes=[pltpu.VMEM((width, ff), BF16)] * 3
        + [pltpu.VMEM((rows, ff), BF16)] * 2
        + [pltpu.VMEM((rows, TILE), F32)]
        + [pltpu.VMEM((rows, width), BF16)]
        + [pltpu.SemaphoreType.DMA((3, tiles)), down_sem_shape(weights, tiles)]
        + [pltpu.SemaphoreType.DMA((2, tiles))] * 2
        + chain_scratch((rows, width)) * 2,
        compiler_params=params(3 + low),
        cost_estimate=cost(),
    )(grad, last_b, gate, up, *weights, *(below or ()))


def last_kernel(part, sum_a, grad, layer, gain, made, gain_grad, total, *scratch):
    chain = Chain(part, total, *scratch)
    greet()
    chain.start()
    gain_grad[...] = jnp.zeros_like(gain_grad)
    grads, layers, mades = ab(grad), ab(layer), ab(made)
    chain.step(0)
    norm_back_rows(grads[0], sum_a, lambda r: layers[0][r].astype(F32), gain, gain_grad, mades[0])
    chain.drain(1)
    norm_back_rows(grads[1], total, lambda r: layers[1][r].astype(F32), gain, gain_grad, mades[1])
    chain.settle()


def last_grads(part, sum_a, grad, layer, gain):
    shape = part.shape
    return pl.pallas_call(
        last_kernel,
        out_shape=[jax.ShapeDtypeStruct(grad.shape, BF16), jax.ShapeDtypeStruct((8, shape[1]), F32)],
        in_specs=[VMEM] * 5,
        out_specs=[VMEM] * 2,
        scratch_shapes=[pltpu.VMEM(shape, BF16)] + chain_scratch(shape),
        compiler_params=params(0),
        cost_estimate=cost(),
    )(part, sum_a, grad, layer, gain)


def roped(values, cosine, sine):
    return values * cosine + pltpu.roll(values, HEAD // 2, 1) * sine


def unroped(grads, cosine, sine):
    return grads * cosine + pltpu.roll(grads * sine, HEAD // 2, 1)


def allowed_keys(seg_rows, seg_keys, i, block):
    rows, keys = seg_rows.shape[0], seg_keys.shape[1]
    first_row = lax.axis_index("ctx") * rows + i * block
    row_at = first_row + lax.broadcasted_iota(jnp.int32, (block, keys), 0)
    key_at = lax.broadcasted_iota(jnp.int32, (block, keys), 1)
    own = seg_rows[pl.ds(pl.multiple_of(i * block, block), block)]
    return (key_at <= row_at) & (own == seg_keys[...])


class AttentionWeights:
    def __init__(self, sources, targets, sems):
        self.own, self.other = sources
        self.w_lin, self.w_out = targets
        self.sems = sems

    def copies(self):
        sec = lax.axis_index("section")
        q_cols = self.w_out.shape[1]
        heads_here = q_cols // HEAD
        head = lax.axis_index("tp") * heads_here // (HEADS // KV_HEADS)
        shards, half = self.own.shape[:2]
        for k, (source, side) in enumerate(((self.own, sec), (self.other, 1 - sec))):
            for i in range(shards):
                rows = pl.ds(pl.multiple_of((2 * i + side) * half, 16), half)
                key_at = pl.multiple_of(q_cols + head * HEAD, HEAD)
                value_at = pl.multiple_of(q_cols + (KV_HEADS + head) * HEAD, HEAD)
                pieces = (
                    (pl.ds(0, q_cols), self.w_lin.at[rows, pl.ds(0, q_cols)]),
                    (pl.ds(key_at, HEAD), self.w_lin.at[rows, pl.ds(q_cols, HEAD)]),
                    (pl.ds(value_at, HEAD), self.w_lin.at[rows, pl.ds(q_cols + HEAD, HEAD)]),
                    (pl.ds(q_cols + 2 * KV_HEADS * HEAD, q_cols), self.w_out.at[rows]),
                )
                for p, (columns, target) in enumerate(pieces):
                    yield pltpu.make_async_copy(source.at[i, :, columns], target, self.sems.at[k, i, p])

    def start(self):
        for copy in self.copies():
            copy.start()

    def wait(self):
        for copy in self.copies():
            copy.wait()


def attention_scratch(halves, q_cols):
    shards, half = halves[0].shape[:2]
    width = 2 * shards * half
    return [
        pltpu.VMEM((width, q_cols + 2 * HEAD), BF16),
        pltpu.VMEM((width, q_cols), BF16),
        pltpu.SemaphoreType.DMA((2, shards, 4)),
    ]


def attention_forward_stage(layer_in, gain, w_lin, w_out, bias, places, outs, result, kv_sems, tick):
    cosine, sine, seg_rows, seg_keys = places
    normed, query, kv, lse, attended = outs
    rows, q_cols = query.shape
    heads = q_cols // HEAD
    count = kv.shape[0] // rows
    me = lax.axis_index("ctx")
    block = min(256, rows)
    normalize_rows(lambda r: layer_in[r].astype(F32), gain, normed)
    tick(0)
    mine = kv.at[pl.ds(pl.multiple_of(me * rows, rows), rows)]
    lin = mm(normed[...], w_lin[:, q_cols:]) + bias[:, q_cols:]
    mine[:, :HEAD] = roped(lin[:, :HEAD], cosine[...], sine[...]).astype(BF16)
    mine[:, HEAD:] = lin[:, HEAD:].astype(BF16)

    def passing(offset):
        return pltpu.make_async_remote_copy(
            src_ref=mine,
            dst_ref=mine,
            send_sem=kv_sems.at[0, offset],
            recv_sem=kv_sems.at[1, offset],
            device_id={"ctx": lax.rem(me + offset, count)},
            device_id_type=MESH,
        )

    for offset in range(1, count):
        passing(offset).start()
    tick(1)
    lin = mm(normed[...], w_lin[:, :q_cols]) + bias[:, :q_cols]
    for h in range(heads):
        columns = slice(h * HEAD, (h + 1) * HEAD)
        query[:, columns] = roped(lin[:, columns], cosine[...], sine[...]).astype(BF16)
    for offset in range(1, count):
        passing(offset).wait_recv()

    @pl.loop(0, rows // block)
    def _(i):
        at = pl.ds(pl.multiple_of(i * block, block), block)
        allowed = allowed_keys(seg_rows, seg_keys, i, block)
        lane = lax.broadcasted_iota(jnp.int32, (block, HEAD), 1)
        logs = jnp.zeros((block, HEAD), F32)
        for h in range(heads):
            columns = slice(h * HEAD, (h + 1) * HEAD)
            scores = jnp.where(allowed, mm_t(query[at, columns], kv[:, :HEAD]) * SCALE, NEG)
            top = jnp.max(scores, axis=-1, keepdims=True)
            probs = jnp.exp(scores - top)
            sums = jnp.sum(probs, axis=-1, keepdims=True)
            probs = (probs * (1.0 / sums)).astype(BF16)
            attended[at, columns] = mm(probs, kv[:, HEAD:]).astype(BF16)
            logs = jnp.where(lane == h, top + jnp.log(sums), logs)
            tick(2 + heads * i + h)
        lse[at] = logs

    base = 2 + heads * (rows // block)

    @pl.loop(0, result.shape[1] // TILE)
    def _(n):
        tile_at(result, n)[...] = mm_t(attended[...], rows_at(w_out, n)[...]).astype(BF16)
        tick(base + n)

    for offset in range(1, count):
        passing(offset).wait_send()
    return base + result.shape[1] // TILE


def attention_forward_kernel(low, *refs):
    take = Taker(refs)
    gain, bias = take(2)
    halves = take(2)
    places_a, places_b = take(4), take(4)
    layer_a, layer_b = ab(take(1)[0])
    if not low:
        adds_a, adds_b, (last_b,) = (layer_a, *take(2)), (layer_b, *take(1)), take(1)
    outs_a, outs_b = zip(*[ab(ref) for ref in take(5)])
    if low:
        total_a, total_b = take(2)
    else:
        result_b, total_a, last_sum_b, layer = take(4)
        layer_a, layer_b = ab(layer)
    result_a, kv_sems_a, kv_sems_b = take(3)
    w_lin, w_out, w_sems = take(3)
    weights = AttentionWeights(halves, (w_lin, w_out), w_sems)
    weights.start()
    if low:
        (result_b,) = take(1)
    chain_a = Chain(result_a, total_a, *take(CHAIN_REFS))
    chain_b = Chain(result_b, total_b, *take(CHAIN_REFS)) if low else Chain(last_b, last_sum_b, *take(CHAIN_REFS))
    greet(kv_sems_a.shape[1])
    if not low:
        chain_b.start()

        def body(rows):
            layer_a[rows] = sum(ref[rows].astype(F32) for ref in adds_a).astype(BF16)

        by_rows(layer_a.shape[0], body)
    weights.wait()
    tick = ticker(None if low else chain_b, 0)
    done = attention_forward_stage(layer_a, gain, w_lin, w_out, bias, places_a, outs_a, result_a, kv_sems_a, tick)
    chain_a.start()
    if not low:
        chain_b.drain(done)
        chain_a.step(0)

        def body(rows):
            layer_b[rows] = sum(ref[rows].astype(F32) for ref in (*adds_b, last_sum_b)).astype(BF16)

        by_rows(layer_b.shape[0], body)
    taken = 0 if low else 1
    tick = ticker(chain_a, taken)
    done = attention_forward_stage(layer_b, gain, w_lin, w_out, bias, places_b, outs_b, result_b, kv_sems_b, tick)
    if low:
        chain_b.start()
    chain_a.drain(taken + done)
    if low:
        chain_b.drain(0)
    chain_a.settle()
    chain_b.settle()


def attention_forward(weights, places, inputs):
    halves, q_cols, gains, bias = weights
    rows, width = inputs[0].shape[0] // 2, inputs[0].shape[1]
    keys = places[0][3].shape[1]
    count = keys // rows
    low = len(inputs) == 1
    narrow, both = jax.ShapeDtypeStruct((rows, width), BF16), jax.ShapeDtypeStruct((2 * rows, width), BF16)
    heads_out = jax.ShapeDtypeStruct((2 * rows, q_cols), BF16)
    kv_out = jax.ShapeDtypeStruct((2 * keys, 2 * HEAD), BF16)
    lse_out = jax.ShapeDtypeStruct((2 * rows, HEAD), F32)
    outs = [both, heads_out, kv_out, lse_out, heads_out] + ([narrow] * 2 if low else [narrow] * 3 + [both])
    args = (gains[:1], bias, *halves, *places[0], *places[1], *inputs)
    return pl.pallas_call(
        functools.partial(attention_forward_kernel, low),
        out_shape=outs,
        in_specs=[VMEM] * 2 + [ANY] * 2 + [VMEM] * (len(args) - 4),
        out_specs=[VMEM] * len(outs),
        scratch_shapes=[pltpu.VMEM((rows, width), BF16)]
        + [pltpu.SemaphoreType.DMA((2, count))] * 2
        + attention_scratch(halves, q_cols)
        + [pltpu.VMEM((rows, width), BF16)] * low
        + chain_scratch((rows, width)) * 2,
        compiler_params=params(5 + low),
        cost_estimate=cost(),
    )(*args)


def attention_backward_stage(ins, sum_in, gain, w_lin, w_out, places, outs, gain_grad, result, scratch, tick):
    upstream, layer_in, attn_out, query, kv, lse, attended = ins
    cosine, sine, seg_rows, seg_keys = places
    attn_grad, lin = outs
    heads_grad, kv_grad, q_part, sent, got, kv_sems = scratch
    rows, q_cols = query.shape
    heads = q_cols // HEAD
    count = kv.shape[0] // rows
    me = lax.axis_index("ctx")
    block = min(256, rows)
    kv_grad[...] = jnp.zeros_like(kv_grad)
    norm_back_rows(
        upstream, sum_in, lambda r: layer_in[r].astype(F32) + attn_out[r].astype(F32), gain, gain_grad, attn_grad
    )
    tick(0)
    heads_grad[...] = mm(attn_grad[...], w_out[...]).astype(BF16)
    tick(1)

    @pl.loop(0, rows // block)
    def _(i):
        at = pl.ds(pl.multiple_of(i * block, block), block)
        allowed = allowed_keys(seg_rows, seg_keys, i, block)
        for h in range(heads):
            columns = slice(h * HEAD, (h + 1) * HEAD)
            scores = mm_t(query[at, columns], kv[:, :HEAD]) * SCALE - lse[at, h : h + 1]
            probs = jnp.exp(jnp.where(allowed, scores, NEG))
            grad = heads_grad[at, columns]
            row_sum = jnp.sum(attended[at, columns].astype(F32) * grad.astype(F32), axis=-1, keepdims=True)
            score_grad = (probs * (mm_t(grad, kv[:, HEAD:]) - row_sum)).astype(BF16)
            q_grad = mm(score_grad, kv[:, :HEAD]) * SCALE
            lin[at, columns] = unroped(q_grad, cosine[at], sine[at]).astype(BF16)
            kv_grad[:, :HEAD] += mm_0(score_grad, query[at, columns])
            kv_grad[:, HEAD:] += mm_0(probs.astype(BF16), grad)
            tick(2 + heads * i + h)

    def passing(offset):
        return pltpu.make_async_remote_copy(
            src_ref=sent.at[offset - 1],
            dst_ref=got.at[offset - 1],
            send_sem=kv_sems.at[0, offset],
            recv_sem=kv_sems.at[1, offset],
            device_id={"ctx": lax.rem(me + offset, count)},
            device_id_type=MESH,
        )

    for offset in range(1, count):
        peer = pl.ds(pl.multiple_of(lax.rem(me + offset, count) * rows, rows), rows)
        sent[offset - 1, :, :HEAD] = (kv_grad[peer, :HEAD] * SCALE).astype(BF16)
        sent[offset - 1, :, HEAD:] = kv_grad[peer, HEAD:].astype(BF16)
        passing(offset).start()
    base = 2 + heads * (rows // block)

    @pl.loop(0, result.shape[1] // TILE)
    def _(n):
        tile_at(q_part, n)[...] = mm_t(lin[:, :q_cols], rows_at(w_lin, n)[:, :q_cols])
        tick(base + n)

    mine = pl.ds(pl.multiple_of(me * rows, rows), rows)
    k_grad, v_grad = kv_grad[mine, :HEAD] * SCALE, kv_grad[mine, HEAD:]
    for offset in range(1, count):
        passing(offset).wait_recv()
        k_grad = k_grad + got[offset - 1, :, :HEAD].astype(F32)
        v_grad = v_grad + got[offset - 1, :, HEAD:].astype(F32)
    lin[:, q_cols : q_cols + HEAD] = unroped(k_grad, cosine[...], sine[...]).astype(BF16)
    lin[:, q_cols + HEAD :] = v_grad.astype(BF16)

    @pl.loop(0, result.shape[1] // TILE)
    def _(n):
        kv_part = mm_t(lin[:, q_cols:], rows_at(w_lin, n)[:, q_cols:])
        tile_at(result, n)[...] = (tile_at(q_part, n)[...] + kv_part).astype(BF16)


    for offset in range(1, count):
        passing(offset).wait_send()
    return base + result.shape[1] // TILE


def attention_backward_kernel(*refs):
    take = Taker(refs)
    (gain,) = take(1)
    halves = take(2)
    places_a, places_b = take(4), take(4)
    ins_a, ins_b = zip(*[ab(ref) for ref in take(6)])
    attn_a, attn_b = take(2)
    ins_a, ins_b = (*ins_a[:2], attn_a, *ins_a[2:]), (*ins_b[:2], attn_b, *ins_b[2:])
    sum_a, last_b = take(2)
    outs_a, outs_b = zip(*[ab(ref) for ref in take(2)])
    gain_grad, result_b, total_a, total_b = take(4)
    heads_grad, kv_grad, q_part, result_a = take(4)
    w_lin, w_out, w_sems = take(3)
    weights = AttentionWeights(halves, (w_lin, w_out), w_sems)
    weights.start()
    exchange_a, exchange_b = take(3), take(3)
    chain_a = Chain(result_a, total_a, *take(CHAIN_REFS))
    chain_b = Chain(last_b, total_b, *take(CHAIN_REFS))
    greet(exchange_a[2].shape[1])
    chain_b.start()
    gain_grad[...] = jnp.zeros_like(gain_grad)
    weights.wait()
    scratch = (heads_grad, kv_grad, q_part, *exchange_a)
    done = attention_backward_stage(
        ins_a, sum_a, gain, w_lin, w_out, places_a, outs_a, gain_grad, result_a, scratch, ticker(chain_b, 0)
    )
    chain_a.start()
    chain_b.drain(done)
    chain_a.step(0)
    scratch = (heads_grad, kv_grad, q_part, *exchange_b)
    done = attention_backward_stage(
        ins_b, total_b, gain, w_lin, w_out, places_b, outs_b, gain_grad, result_b, scratch, ticker(chain_a, 1)
    )
    chain_a.drain(1 + done)
    chain_a.settle()
    chain_b.settle()


def attention_backward(upstream, sum_a, last_b, kept, weights, places):
    halves, q_cols, gains, bias = weights
    rows, width = sum_a.shape
    keys = places[0][3].shape[1]
    count = keys // rows
    narrow = jax.ShapeDtypeStruct((rows, width), BF16)
    both = jax.ShapeDtypeStruct((2 * rows, width), BF16)
    lin_out = jax.ShapeDtypeStruct((2 * rows, q_cols + 2 * HEAD), BF16)
    outs = [both, lin_out] + [jax.ShapeDtypeStruct((8, width), F32)] + [narrow] * 3
    names = ("layer_in", "query", "kv", "lse", "attended", "attn_a", "attn_b")
    args = (gains[1:], *halves, *places[0], *places[1], upstream)
    args += (*[kept[name] for name in names], sum_a, last_b)
    exchange = [pltpu.VMEM((max(count - 1, 1), rows, 2 * HEAD), BF16)] * 2 + [pltpu.SemaphoreType.DMA((2, count))]
    return pl.pallas_call(
        attention_backward_kernel,
        out_shape=outs,
        in_specs=[VMEM] + [ANY] * 2 + [VMEM] * (len(args) - 3),
        out_specs=[VMEM] * len(outs),
        scratch_shapes=[
            pltpu.VMEM((rows, q_cols), BF16),
            pltpu.VMEM((keys, 2 * HEAD), F32),
            pltpu.VMEM((rows, width), F32),
            pltpu.VMEM((rows, width), BF16),
        ]
        + attention_scratch(halves, q_cols)
        + exchange * 2
        + chain_scratch((rows, width)) * 2,
        compiler_params=params(7),
        cost_estimate=cost(),
    )(*args)


def rope_tables(places):
    steps = jnp.arange(HEAD // 2, dtype=F32) * (2.0 / HEAD)
    inverse = ROPE_BASE ** (-steps)
    angles = places.astype(F32)[..., None] * inverse
    angles = jnp.concatenate([angles, angles], axis=-1)
    return (jnp.cos(angles), jnp.sin(angles))


def norm_back(grad_out, rows_in, factor, gain):
    unit = rows_in * factor
    gain_grad = jnp.sum(grad_out * unit, axis=0)
    weighted = grad_out * gain
    return (
        factor * (weighted - unit * jnp.mean(weighted * unit, axis=-1, keepdims=True)),
        gain_grad,
    )


def over_ctx(value):
    if lax.axis_size("ctx") == 2:
        other = lax.ppermute(value, "ctx", [(0, 1), (1, 0)])
        low = lax.axis_index("ctx") == 0
        return jnp.concatenate([jnp.where(low, value, other), jnp.where(low, other, value)], axis=-1)
    return lax.all_gather(value, "ctx", axis=value.ndim - 1, tiled=True)


def input_backward(normed_one_grad, middle_grad, kept, gains):
    layer_in = kept["layer_in"].astype(F32)
    factor = lax.rsqrt(jnp.mean(layer_in * layer_in, axis=-1, keepdims=True) + EPS)
    norm_grad, gain_one = norm_back(normed_one_grad.astype(F32), layer_in, factor, gains[0])
    return (middle_grad.astype(F32) + norm_grad).astype(BF16), gain_one


def local(
    section_in,
    segments,
    positions,
    query_weight,
    kv_weight,
    output_weight,
    gate_up,
    down_weight,
    norm_gains,
    query_bias,
    kv_bias,
    out_grad,
):
    sec = lax.axis_index("section")
    first = sec == 0
    group = HEADS // KV_HEADS
    heads_here = HEADS // lax.axis_size("tp")
    head_pick = lax.axis_index("tp") * heads_here // group
    shards = lax.axis_size("dp") * lax.axis_size("ctx")
    ranks = ("dp", "ctx")
    seqs, span, width = section_in.shape[1:]
    shard = query_weight.shape[1]
    q_cols = query_weight.shape[2]
    ff = gate_up.shape[3]

    def per_layer(mine, theirs):
        return jnp.where(first, mine, theirs), jnp.where(first, theirs, mine)

    half = shard // 2
    kv_width = KV_HEADS * HEAD

    def halves(rows):
        mine = lax.dynamic_slice_in_dim(rows, sec * half, half, 0)
        return per_layer(mine, swap(lax.dynamic_slice_in_dim(rows, (1 - sec) * half, half, 0)))

    def after(value, event):
        return lax.optimization_barrier((value, event))[0]

    piece = HEAD // shards
    biases = jnp.concatenate([query_bias[0].reshape(-1), kv_bias[0].reshape(-1)])
    n_biases = biases.shape[0]
    biases = jnp.pad(biases, (0, -n_biases % shard)).reshape(-1, shard).T
    extra = jnp.concatenate([norm_gains[0].T, biases], axis=1)
    n_extra = extra.shape[1]
    extra = jnp.pad(extra, ((0, 0), (0, HEAD - n_extra)))
    packed = jnp.concatenate([query_weight[0], kv_weight[0, 0], kv_weight[0, 1], output_weight[0].T, extra], axis=1)
    packed_shards = halves(packed)
    first_shard, gate_up, down_weight, positions, segments, section_in = lax.optimization_barrier(
        (packed_shards[0], gate_up, down_weight, positions, segments, section_in)
    )
    packed_low = lax.all_gather(first_shard, ranks, axis=0)
    spare = -ff % TILE
    wide = jnp.pad(gate_up[0], ((0, 0), (0, 0), (0, spare)))
    mine = lax.dynamic_index_in_dim(wide, sec, 0, keepdims=False)
    theirs = swap(lax.dynamic_index_in_dim(wide, 1 - sec, 0, keepdims=False))
    gate_up_shards = per_layer(mine, theirs)
    down_shards = halves(jnp.pad(down_weight[0].T, ((0, 0), (0, spare))))

    micro = sec
    seg = lax.dynamic_index_in_dim(segments, micro, 0, keepdims=False)
    pos = lax.dynamic_index_in_dim(positions, micro, 0, keepdims=False)
    hidden = lax.dynamic_index_in_dim(section_in, micro, 0, keepdims=False)
    seg_keys = over_ctx(seg)
    segs, tables = [], []
    for q in range(seqs):
        segs.append((seg[q][:, None], seg_keys[q][None]))
        cosine, sine = rope_tables(pos[q])
        tables.append((cosine, jnp.where(jnp.arange(HEAD) < HEAD // 2, -sine, sine)))
    hidden = hidden.reshape(seqs * span, width)

    packed_low, gate_up_shards, down_shards, packed_shards, segs, tables, hidden = lax.optimization_barrier(
        (packed_low, gate_up_shards, down_shards, packed_shards, segs, tables, hidden)
    )
    own_low = lax.all_gather(gate_up_shards[0], ranks, axis=0, tiled=True)
    down_low = lax.all_gather(down_shards[0], ranks, axis=0)

    def attention_weights(own):
        parts = own, swap(own)
        small = [part[..., 2 * q_cols + 2 * kv_width :] for part in parts]
        s = jnp.stack(per_layer(*small), axis=1).reshape(width, -1)
        gains = s[:, :2].T
        s = s[:, 2:n_extra].T.reshape(-1, shards, shard).transpose(1, 0, 2).reshape(shards, -1)[:, :n_biases]
        q_b = s[:, : heads_here * piece].reshape(shards, heads_here, piece).transpose(1, 0, 2).reshape(heads_here, HEAD)
        kv_b = s[:, heads_here * piece :].reshape(shards, 2, KV_HEADS, piece)
        kv_b = kv_b.transpose(1, 2, 0, 3).reshape(2, KV_HEADS, HEAD)
        kv_b = lax.dynamic_slice_in_dim(kv_b, head_pick, 1, 1)
        bias = jnp.concatenate([q_b.reshape(1, -1), kv_b.reshape(1, -1)], axis=1).astype(F32)
        return parts, q_cols, gains.astype(F32), bias

    names = ("normed", "query", "kv", "lse", "attended")
    more_names = ("normed_two", "gate", "up", "inner")
    attn_weights, ffn_weights = [attention_weights(packed_low), None], [None, None]
    places = [(*tables[q], *segs[q]) for q in range(seqs)]

    def keep(layer, names, values):
        kept[layer].update(zip(names, values))
        return values[len(names) :]

    kept = [dict(), dict()]
    attn_a, attn_b = keep(0, names, attention_forward(attn_weights[0], places, (hidden,)))
    kept[0].update(layer_in=hidden, attn_a=attn_a, attn_b=attn_b)
    attn_b, own_low, down_low = lax.optimization_barrier((attn_b, own_low, down_low))
    ffn_weights[0] = own_low, down_low
    packed_high = lax.all_gather(after(packed_shards[1], attn_b), ranks, axis=0)
    own_high = lax.all_gather(after(gate_up_shards[1], attn_b), ranks, axis=0, tiled=True)
    down_high = lax.all_gather(after(down_shards[1], attn_b), ranks, axis=0)
    gain = attn_weights[0][2][1:]
    part_b, ffn_a = keep(
        0, more_names, ffn_forward(False, hidden, attn_a, attn_b, gain, ffn_weights[0])
    )

    packed_high, part_b = lax.optimization_barrier((packed_high, part_b))
    attn_weights[1] = attention_weights(packed_high)
    inputs = (hidden, attn_a, ffn_a, attn_b, part_b)
    part_b, attn_a, _, layer_in = keep(1, names, attention_forward(attn_weights[1], places, inputs))
    part_b, own_high, down_high = lax.optimization_barrier((part_b, own_high, down_high))
    ffn_weights[1] = own_high, down_high
    gain = attn_weights[1][2][1:]
    part_b, ffn_a, attn_b = keep(
        1, more_names, ffn_forward(True, layer_in, attn_a, part_b, gain, ffn_weights[1])
    )
    kept[1].update(layer_in=layer_in, attn_a=attn_a, attn_b=attn_b)
    upstream = lax.dynamic_index_in_dim(out_grad, micro, 0, keepdims=False).reshape(seqs * span, width)
    k = kept[1]
    *wide_grads, grad_b, sum_a, ffn_b = ffn_backward(upstream, k["gate"], k["up"], ffn_weights[1], part_b)
    attn_sum, ffn_sum = jnp.concatenate([attn_a, attn_b]), jnp.concatenate([ffn_a, ffn_b])
    outs = [layer_in, (layer_in.astype(F32) + attn_sum.astype(F32) + ffn_sum.astype(F32)).astype(BF16)]

    def to_section(values, low, high):
        both = jnp.stack([jnp.where(first, values[0], high), jnp.where(first, low, values[1])])
        return both.reshape(2, seqs, span, width)

    def to_low(value):
        return lax.ppermute(value, "section", [(1, 0)])

    def to_high(value):
        return lax.ppermute(value, "section", [(0, 1)])

    out_low, out_high = to_low(outs[0]), to_high(outs[1])

    in_grads = [None, None]
    gate_up_grads, down_grads, packed_grads, gains_grads = [[None, None] for _ in range(4)]
    for layer in (1, 0):
        weights, k = attn_weights[layer], kept[layer]
        if layer == 0:
            below = (sum_a, kept[1]["layer_in"], attn_weights[1][2][:1])
            *wide_grads, grad_b, sum_a, _, upstream, gain_one = ffn_backward(
                attn_grad, k["gate"], k["up"], ffn_weights[0], part_b, below
            )
            in_grads[1] = upstream
            in_high = to_high(upstream)
            gains_grads[1] = jnp.stack([jnp.sum(gain_one, axis=0), gain_two])
            sum_a, gate_up_grads[1] = lax.optimization_barrier((sum_a, gate_up_grads[1]))
        own_w, other_w = [dot("rd,rf->df", k["normed_two"], g).astype(BF16) for g in wide_grads]
        other_w = swap(other_w)
        down_w = dot("rd,rf->df", upstream, k["inner"]).astype(BF16)
        down_w = down_w.reshape(shards, 2, half, ff + spare)
        down_own = lax.dynamic_index_in_dim(down_w, sec, 1, keepdims=False)
        down_other = swap(lax.dynamic_index_in_dim(down_w, 1 - sec, 1, keepdims=False))
        own_w = (own_w.astype(F32) + other_w.astype(F32)).astype(BF16)
        own_w, down_other = lax.optimization_barrier((own_w, down_other))
        down_own = (down_own.astype(F32) + down_other.astype(F32)).astype(BF16)
        own_w, down_own, sum_a = lax.optimization_barrier((own_w, down_own, sum_a))
        gate_up_grads[layer] = lax.psum_scatter(own_w, ranks, scatter_dimension=0, tiled=True)
        down_grads[layer] = lax.psum_scatter(
            down_own.reshape(shards * half, ff + spare), ranks, scatter_dimension=0, tiled=True
        )

        attn_grad, lin_grad, gain_two, part_b, sum_a, _ = attention_backward(upstream, sum_a, grad_b, k, weights, places)
        gain_two = jnp.sum(gain_two, axis=0)
        if layer == 0:
            part_b, down_grads[1] = lax.optimization_barrier((part_b, down_grads[1]))
        lin_w = dot("rd,re->de", k["normed"], lin_grad)
        out_w = dot("rd,re->de", attn_grad, k["attended"])
        bias = jnp.sum(lin_grad.astype(F32), axis=0)
        bias = bias.reshape(heads_here + 2, shards, piece).transpose(1, 0, 2).reshape(shards, (heads_here + 2) * piece)
        bias = jnp.pad(bias, ((0, 0), (0, -bias.shape[1] % shard)))
        bias = bias.reshape(shards, -1, shard).transpose(0, 2, 1).reshape(width, -1)
        bias = jnp.pad(bias, ((0, 0), (0, HEAD - bias.shape[1])))
        packed_grads[layer] = jnp.concatenate([lin_w, out_w, bias], axis=1).astype(BF16)

    low = lax.ppermute(packed_grads[0], "section", [(1, 0)])
    high = lax.ppermute(packed_grads[1], "section", [(0, 1)])
    packed_total = jnp.where(
        first, packed_grads[0].astype(F32) + low.astype(F32), packed_grads[1].astype(F32) + high.astype(F32)
    ).astype(BF16)
    last_part, gate_up_grads[0], down_grads[0], packed_total = lax.optimization_barrier(
        (part_b, gate_up_grads[0], down_grads[0], packed_total)
    )
    packed_total = lax.psum_scatter(packed_total, ranks, scatter_dimension=0, tiled=True).astype(F32)
    in_grads[0], gain_one = last_grads(last_part, sum_a, attn_grad, kept[0]["layer_in"], attn_weights[0][2][:1])
    gains_grads[0] = jnp.stack([jnp.sum(gain_one, axis=0), gain_two])
    in_grads[0], out_low, out_high, in_high = lax.optimization_barrier((in_grads[0], out_low, out_high, in_high))
    in_low = to_low(in_grads[0])
    low = lax.ppermute(gains_grads[0], "section", [(1, 0)])
    high = lax.ppermute(gains_grads[1], "section", [(0, 1)])
    gains_grad = jnp.where(first, gains_grads[0] + low, gains_grads[1] + high)
    for axis in ranks:
        if lax.axis_size(axis) == 2:
            gains_grad = gains_grad + lax.ppermute(gains_grad, axis, [(0, 1), (1, 0)])
        else:
            gains_grad = lax.psum(gains_grad, axis)
    at = (lax.axis_index("dp") * lax.axis_size("ctx") + lax.axis_index("ctx")) * shard
    gains_grad = lax.dynamic_slice_in_dim(gains_grad, at, shard, 1)
    q_grad = packed_total[:, :q_cols]
    kv_narrow = packed_total[:, q_cols : q_cols + 2 * HEAD].reshape(shard, 2, HEAD)
    o_grad = packed_total[:, q_cols + 2 * HEAD : 2 * q_cols + 2 * HEAD].T
    extra = packed_total[:, 2 * q_cols + 2 * HEAD :]
    bias_cols = -(-(heads_here + 2) * piece // shard)
    bias = extra[:, :bias_cols].T.reshape(-1)[: (heads_here + 2) * piece].reshape(heads_here + 2, piece)
    q_bias_grad = bias[:heads_here]
    kv_bias = bias[heads_here:].reshape(1, -1)
    kv_bias = jnp.pad(kv_bias, ((0, 15), (0, -kv_bias.shape[1] % (2 * HEAD))))
    mine = jnp.concatenate([kv_narrow.reshape(shard, 2 * HEAD), kv_bias[:, : 2 * HEAD]]).astype(BF16)
    mine = (mine.astype(F32) + lax.ppermute(mine, "tp", [(0, 1), (1, 0), (2, 3), (3, 2)]).astype(F32)).astype(BF16)
    theirs = lax.ppermute(mine, "tp", [(0, 2), (2, 0), (1, 3), (3, 1)])
    mine, theirs = mine.astype(F32), theirs.astype(F32)
    low = head_pick == 0
    heads = jnp.stack([jnp.where(low, mine, theirs), jnp.where(low, theirs, mine)])
    kv_grad = heads[:, :shard].reshape(KV_HEADS, shard, 2, HEAD).transpose(2, 1, 0, 3).reshape(2, shard, KV_HEADS * HEAD)
    kv_bias_grad = heads[:, shard, : 2 * piece].reshape(KV_HEADS, 2, piece).transpose(1, 0, 2)

    def collect(values):
        kept_half = jnp.where(first, values[0], values[1])
        other = swap(jnp.where(first, values[1], values[0]))
        return jnp.where(first, kept_half, other), jnp.where(first, other, kept_half)

    section_out = to_section(outs, out_low, out_high)
    input_grad = to_section(in_grads, in_low, in_high)
    gate_up_grad = jnp.stack(collect(gate_up_grads))[..., :ff].astype(F32)
    down_grad = jnp.concatenate(collect(down_grads), axis=0)[:, :ff].T.astype(F32)
    return (
        section_out[None],
        input_grad[None],
        q_grad[None],
        kv_grad[None],
        o_grad[None],
        gate_up_grad[None],
        down_grad[None],
        gains_grad[None],
        q_bias_grad[None],
        kv_bias_grad[None],
    )


def solution(mesh):
    in_specs = (
        P(None, "dp", "ctx", None),
        P(None, "dp", "ctx"),
        P(None, "dp", "ctx"),
        P("section", ("dp", "ctx"), "tp"),
        P("section", None, ("dp", "ctx"), None),
        P("section", "tp", ("dp", "ctx")),
        P("section", None, ("dp", "ctx"), "tp"),
        P("section", "tp", ("dp", "ctx")),
        P("section", None, ("dp", "ctx")),
        P("section", "tp", ("dp", "ctx")),
        P("section", None, None, ("dp", "ctx")),
        P(None, "dp", "ctx", None),
    )
    out_specs = (
        P("section", None, "dp", "ctx", None),
        P("section", None, "dp", "ctx", None),
        P("section", ("dp", "ctx"), "tp"),
        P("section", None, ("dp", "ctx"), None),
        P("section", "tp", ("dp", "ctx")),
        P("section", None, ("dp", "ctx"), "tp"),
        P("section", "tp", ("dp", "ctx")),
        P("section", None, ("dp", "ctx")),
        P("section", "tp", ("dp", "ctx")),
        P("section", None, None, ("dp", "ctx")),
    )
    return jax.shard_map(local, mesh=mesh, in_specs=in_specs, out_specs=out_specs, check_vma=False)
```

```python
import functools

import jax
import jax.numpy as jnp
from jax import lax
from jax.experimental import pallas as pl
from jax.experimental.pallas import tpu as pltpu
from jax.sharding import PartitionSpec as P

HEADS = 12
KV_HEADS = 2
HEAD = 128

EPS = 1e-06
ROPE_BASE = 1000000.0
NEG = -1e30
SCALE = HEAD ** (-0.5)
TILE = 768
VMEM_LIMIT = 60 << 20
MESH = pl.DeviceIdType.MESH

F32 = jnp.float32
BF16 = jnp.bfloat16


def dot(form, left, right):
    return jnp.einsum(form, left, right, preferred_element_type=F32)


def swap(value):
    return lax.ppermute(value, "section", [(0, 1), (1, 0)])


class Chain:
    def __init__(self, part, total, from_end, from_peer, sems):
        self.part, self.total = part, total
        self.from_end, self.from_peer = from_end, from_peer
        self.sems = sems
        self.chunks = sems.shape[1]
        self.rows = part.shape[0] // self.chunks
        self.is_middle, self.inner, self.outer = line_places()

    def at(self, ref, c):
        return ref.at[pl.ds(pl.multiple_of(c * self.rows, self.rows), self.rows)]

    def copy(self, source, target, c, step, place):
        return pltpu.make_async_remote_copy(
            src_ref=self.at(source, c),
            dst_ref=self.at(target, c),
            send_sem=self.sems.at[2 * step, c],
            recv_sem=self.sems.at[2 * step + 1, c],
            device_id={"tp": place},
            device_id_type=MESH,
        )

    def inward(self, c):
        return self.copy(self.part, self.from_end, c, 0, self.inner)

    def across(self, c):
        return self.copy(self.total, self.from_peer, c, 1, self.inner)

    def outward(self, c):
        return self.copy(self.total, self.total, c, 2, self.outer)

    def start(self):
        @pl.when(jnp.logical_not(self.is_middle))
        def _():
            @pl.loop(0, self.chunks)
            def _(c):
                self.inward(c).start()

    def join(self, c):
        self.inward(c).wait_recv()
        self.at(self.total, c)[...] = self.at(self.part, c)[...] + self.at(self.from_end, c)[...]
        self.across(c).start()

    def close(self, c):
        self.across(c).wait()
        self.at(self.total, c)[...] = self.at(self.total, c)[...] + self.at(self.from_peer, c)[...]
        self.outward(c).start()

    def step(self, c):
        @pl.when(self.is_middle & (c < self.chunks))
        def _():
            self.join(c)

            @pl.when(c > 0)
            def _():
                self.close(c - 1)

    def drain(self, done):
        @pl.when(self.is_middle)
        def _():
            if done < self.chunks:

                @pl.loop(done, self.chunks)
                def _(c):
                    self.step(c)

            self.close(self.chunks - 1)

        @pl.when(jnp.logical_not(self.is_middle))
        def _():
            @pl.loop(0, self.chunks)
            def _(c):
                self.outward(c).wait_recv()

    def settle(self):
        @pl.when(self.is_middle)
        def _():
            @pl.loop(0, self.chunks)
            def _(c):
                self.outward(c).wait_send()

        @pl.when(jnp.logical_not(self.is_middle))
        def _():
            @pl.loop(0, self.chunks)
            def _(c):
                self.inward(c).wait_send()


def line_places():
    place = lax.axis_index("tp")
    is_middle = (place == 1) | (place == 2)
    return is_middle, jnp.where(place < 2, place + 1, place - 1), jnp.where(place < 2, place - 1, place + 1)


def greet(ctx_count=1, cores=0):
    is_middle, inner, outer = line_places()
    me = lax.axis_index("ctx")
    barrier = pltpu.get_barrier_semaphore()
    for step in range(1, ctx_count):
        pl.semaphore_signal(barrier, inc=1, device_id={"ctx": lax.rem(me + step, ctx_count)}, device_id_type=MESH)
    if cores:
        peer = 1 - lax.axis_index("section")
        pl.semaphore_signal(barrier, inc=1, device_id={"section": peer}, device_id_type=MESH)
    pl.semaphore_signal(barrier, inc=1, device_id={"tp": inner}, device_id_type=MESH)

    @pl.when(is_middle)
    def _():
        pl.semaphore_signal(barrier, inc=1, device_id={"tp": outer}, device_id_type=MESH)
        pl.semaphore_wait(barrier, 1 + ctx_count + cores)

    @pl.when(jnp.logical_not(is_middle))
    def _():
        pl.semaphore_wait(barrier, ctx_count + cores)


def ab(ref):
    rows = ref.shape[0] // 2
    return ref.at[pl.ds(0, rows)], ref.at[pl.ds(rows, rows)]


def chain_scratch(shape):
    return [pltpu.VMEM(shape, BF16)] * 2 + [pltpu.SemaphoreType.DMA((6, min(8, shape[0] // 16)))]


CHAIN_REFS = 3
VMEM = pl.BlockSpec(memory_space=pltpu.VMEM)
ANY = pl.BlockSpec(memory_space=pl.ANY)


def params(collective_id):
    return pltpu.CompilerParams(collective_id=collective_id, has_side_effects=True, vmem_limit_bytes=VMEM_LIMIT)


def cost():
    return pl.CostEstimate(flops=1 << 20, bytes_accessed=1 << 20, transcendentals=0)


class Taker:
    def __init__(self, refs):
        self.refs = list(refs)

    def __call__(self, count):
        taken, self.refs = self.refs[:count], self.refs[count:]
        return taken


def ticker(chain, taken):
    return (lambda c: None) if chain is None else (lambda c: chain.step(c + taken))


def mm(left, right):
    return jnp.dot(left, right, preferred_element_type=F32)


def mm_t(left, right):
    return lax.dot_general(left, right, (((1,), (1,)), ((), ())), preferred_element_type=F32)


def mm_0(left, right):
    return lax.dot_general(left, right, (((0,), (0,)), ((), ())), preferred_element_type=F32)


def tile_at(ref, j, size=TILE):
    return ref.at[:, pl.ds(pl.multiple_of(j * size, size), size)]


def rows_at(ref, j, size=TILE):
    return ref.at[pl.ds(pl.multiple_of(j * size, size), size)]


def by_rows(rows, body, block=64):
    @pl.loop(0, rows // block)
    def _(i):
        body(pl.ds(pl.multiple_of(i * block, block), block))


def send_either(first, source, one, two, sem, start):
    @pl.when(first)
    def _():
        copy = pltpu.make_async_copy(source, one, sem)
        copy.start() if start else copy.wait()

    @pl.when(jnp.logical_not(first))
    def _():
        copy = pltpu.make_async_copy(source, two, sem)
        copy.start() if start else copy.wait()


def norm_factor(values):
    return lax.rsqrt(jnp.mean(values * values, axis=-1, keepdims=True) + EPS)


def normalize_rows(source, gain, target):
    def body(rows):
        values = source(rows)
        target[rows] = (values * norm_factor(values) * gain[...]).astype(BF16)

    by_rows(target.shape[0], body)


def norm_back_rows(upstream, grad_in, source, gain, gain_grad, target):
    def body(rows):
        values = source(rows)
        factor = norm_factor(values)
        unit = values * factor
        grad = grad_in[rows].astype(F32)
        per_row = grad * unit
        mean = jnp.mean(per_row * gain[...], axis=-1, keepdims=True)
        target[rows] = (upstream[rows].astype(F32) + factor * (grad * gain[...] - unit * mean)).astype(BF16)
        gain_grad[...] += jnp.sum(per_row.reshape(-1, 8, per_row.shape[1]), axis=0)

    by_rows(target.shape[0], body)


class FfnWeights:
    def __init__(self, sources, targets, sems, down_sems, by_columns):
        self.own, self.down_own = sources
        self.gate, self.up, self.down = targets
        self.sems, self.down_sems = sems, down_sems
        self.sec = lax.axis_index("section")
        self.first = self.sec == 0
        self.by_columns = by_columns
        self.wide = tile_at if by_columns else rows_at
        self.tiles, self.outs = self.gate.shape[1] // TILE, self.gate.shape[0] // TILE
        self.wide_count, self.deep_count = (self.tiles, self.outs) if by_columns else (self.outs, self.tiles)

    def here(self, j, target):
        return pltpu.make_async_copy(self.wide(self.own, j), self.wide(target, j), self.sems.at[0, j])

    def there(self, j, target):
        return pltpu.make_async_remote_copy(
            src_ref=self.wide(self.own, j),
            dst_ref=self.wide(target, j),
            send_sem=self.sems.at[1, j],
            recv_sem=self.sems.at[2, j],
            device_id={"section": 1 - self.sec},
            device_id_type=MESH,
        )

    def on_own(self, action):
        @pl.when(self.first)
        def _():
            action(self.gate, self.up)

        @pl.when(jnp.logical_not(self.first))
        def _():
            action(self.up, self.gate)

    def wait_gate(self, j):
        @pl.when(self.first)
        def _():
            self.here(j, self.gate).wait()

        @pl.when(jnp.logical_not(self.first))
        def _():
            self.there(j, self.gate).wait_recv()

    def wait_up(self, j):
        @pl.when(self.first)
        def _():
            self.there(j, self.up).wait_recv()

        @pl.when(jnp.logical_not(self.first))
        def _():
            self.here(j, self.up).wait()

    def down_parts(self, j):
        shards, half = self.down_own.shape[0], self.down_own.shape[1]
        per_tile = shards if not self.by_columns else shards // self.outs
        for i in range(per_tile):
            if self.by_columns:
                shard = j * per_tile + i
                source, columns = self.down_own.at[shard], slice(None)
            else:
                shard, columns = i, pl.ds(pl.multiple_of(j * TILE, TILE), TILE)
                source = self.down_own.at[shard, :, columns]

            def place(sec, shard=shard, columns=columns):
                return self.down.at[pl.ds(pl.multiple_of((2 * shard + sec) * half, 16), half), columns]

            yield source, place(self.sec), place(1 - self.sec), i

    def down_here(self, source, place, i, j):
        return pltpu.make_async_copy(source, place, self.down_sems.at[0, j, i])

    def down_there(self, source, place, i, j):
        return pltpu.make_async_remote_copy(
            src_ref=source,
            dst_ref=place,
            send_sem=self.down_sems.at[1, j, i],
            recv_sem=self.down_sems.at[2, j, i],
            device_id={"section": 1 - self.sec},
            device_id_type=MESH,
        )

    def start_wide(self, local):
        def action(own, other):
            @pl.loop(0, self.wide_count)
            def _(j):
                (self.here if local else self.there)(j, own).start()

        self.on_own(action)

    def start_deep(self, local):
        @pl.loop(0, self.deep_count)
        def _(j):
            for source, mine, theirs, i in self.down_parts(j):
                (self.down_here if local else self.down_there)(source, mine, i, j).start()

    def wait_down(self, j):
        for source, mine, theirs, i in self.down_parts(j):
            self.down_here(source, mine, i, j).wait()
            self.down_there(source, theirs, i, j).wait_recv()

    def finish(self):
        def action(own, other):
            @pl.loop(0, self.wide_count)
            def _(j):
                self.there(j, own).wait_send()

        self.on_own(action)

        @pl.loop(0, self.deep_count)
        def _(j):
            for source, mine, theirs, i in self.down_parts(j):
                self.down_there(source, mine, i, j).wait_send()


def ffn_forward_stage(weights, normed, outs, held, one, two, out_sems, result, tick, wait):
    gate, up, inner = held

    @pl.loop(0, weights.tiles)
    def _(j):
        if wait:
            weights.wait_gate(j)
        one[...] = mm(normed[...], tile_at(weights.gate, j)[...])
        tick(2 * j)
        if wait:
            weights.wait_up(j)
        two[...] = mm(normed[...], tile_at(weights.up, j)[...])
        columns = pl.ds(pl.multiple_of(j * TILE, TILE), TILE)

        def body(rows):
            g, u = one[rows], two[rows]
            gate[rows, columns] = g.astype(BF16)
            up[rows, columns] = u.astype(BF16)
            inner[rows, columns] = (g * jax.nn.sigmoid(g) * u).astype(BF16)

        by_rows(one.shape[0], body)
        tick(2 * j + 1)
        for k in range(3):
            pltpu.make_async_copy(tile_at(held[k], j), tile_at(outs[k], j), out_sems.at[k, j]).start()

    @pl.loop(0, weights.outs)
    def _(n):
        if wait:
            weights.wait_down(n)
        tile_at(result, n)[...] = mm_t(inner[...], rows_at(weights.down, n)[...]).astype(BF16)
        tick(2 * weights.tiles + n)

    return 2 * weights.tiles + weights.outs


def wait_out(held, outs, out_sems):
    @pl.loop(0, held[0].shape[1] // TILE)
    def _(j):
        for k in range(len(held)):
            pltpu.make_async_copy(tile_at(held[k], j), tile_at(outs[k], j), out_sems.at[k, j]).wait()


def ffn_forward_kernel(lead, *refs):
    take = Taker(refs)
    layer, attn_a, last_b, gain = take(4)
    layer_a, layer_b = ab(layer)
    sources = take(2)
    (normed_a, normed_b), *outs = [ab(ref) for ref in take(4)]
    outs_a, outs_b = zip(*outs)
    result_b, total_a = take(2)
    attn_b = take(1)[0] if lead else last_b
    targets, held = take(3), take(3)
    one, two, result_a, w_sems, down_sems, out_sems = take(6)
    chain_a = Chain(result_a, total_a, *take(CHAIN_REFS))
    chain_b = Chain(last_b, attn_b, *take(CHAIN_REFS)) if lead else None
    weights = FfnWeights(sources, targets, w_sems, down_sems, True)
    weights.start_wide(True)
    weights.start_deep(True)
    greet(cores=1)
    if lead:
        chain_b.start()
    weights.start_wide(False)
    weights.start_deep(False)
    normalize_rows(lambda r: layer_a[r].astype(F32) + attn_a[r].astype(F32), gain, normed_a)
    if lead:
        chain_b.step(0)
    tick = ticker(chain_b, 1)
    done = ffn_forward_stage(weights, normed_a, outs_a, held, one, two, out_sems, result_a, tick, True)
    chain_a.start()
    if lead:
        chain_b.drain(1 + done)
        chain_a.step(0)
    normalize_rows(lambda r: layer_b[r].astype(F32) + attn_b[r].astype(F32), gain, normed_b)
    wait_out(held, outs_a, out_sems)
    if not lead:
        chain_a.step(0)
    tick = ticker(chain_a, 1)
    done = ffn_forward_stage(weights, normed_b, outs_b, held, one, two, out_sems, result_b, tick, False)
    chain_a.drain(1 + done)
    chain_a.settle()
    if lead:
        chain_b.settle()
    weights.finish()
    wait_out(held, outs_b, out_sems)


def down_sem_shape(weights, tiles):
    return pltpu.SemaphoreType.DMA((3, tiles, weights[1].shape[0]))


def ffn_forward(lead, layer_in, attn_a, last_b, gain, weights):
    rows, width = attn_a.shape
    ff = weights[0].shape[1]
    tiles = max(ff, width) // TILE
    narrow = jax.ShapeDtypeStruct((rows, width), BF16)
    both, wide = jax.ShapeDtypeStruct((2 * rows, width), BF16), jax.ShapeDtypeStruct((2 * rows, ff), BF16)
    return pl.pallas_call(
        functools.partial(ffn_forward_kernel, lead),
        out_shape=[both, wide, wide, wide] + [narrow] * (2 + lead),
        in_specs=[VMEM] * 4 + [ANY] * 2,
        out_specs=[VMEM] + [ANY] * 3 + [VMEM] * (2 + lead),
        scratch_shapes=[pltpu.VMEM((width, ff), BF16)] * 3
        + [pltpu.VMEM((rows, ff), BF16)] * 3
        + [pltpu.VMEM((rows, TILE), F32)] * 2
        + [pltpu.VMEM((rows, width), BF16)]
        + [pltpu.SemaphoreType.DMA((3, tiles)), down_sem_shape(weights, tiles), pltpu.SemaphoreType.DMA((3, tiles))]
        + chain_scratch((rows, width)) * (1 + lead),
        compiler_params=params(1 + lead),
        cost_estimate=cost(),
    )(layer_in, attn_a, last_b, gain, *weights)


def ffn_backward_stage(weights, grad, ins, outs, held, one, in_sems, out_sems, result, tick, wait):
    gate, up = held
    own_out, other_out = outs

    @pl.loop(0, weights.tiles)
    def _(j):
        if wait:
            weights.wait_down(j)
        one[...] = mm(grad[...], tile_at(weights.down, j)[...])
        tick(j)
        for k in range(2):
            pltpu.make_async_copy(tile_at(ins[k], j), tile_at(held[k], j), in_sems.at[k, j]).wait()
        columns = pl.ds(pl.multiple_of(j * TILE, TILE), TILE)

        def body(rows):
            g, u, d = gate[rows, columns].astype(F32), up[rows, columns].astype(F32), one[rows]
            sig = jax.nn.sigmoid(g)
            d = d * sig
            gate[rows, columns] = (d * u * (1.0 + g * (1.0 - sig))).astype(BF16)
            up[rows, columns] = (d * g).astype(BF16)

        by_rows(one.shape[0], body)

    def sending(start):
        @pl.loop(0, weights.tiles)
        def _(j):
            own, other = tile_at(own_out, j), tile_at(other_out, j)
            send_either(weights.first, tile_at(gate, j), own, other, out_sems.at[0, j], start)
            send_either(weights.first, tile_at(up, j), other, own, out_sems.at[1, j], start)

    sending(True)

    @pl.loop(0, weights.outs)
    def _(n):
        if wait:
            weights.wait_gate(n)
            weights.wait_up(n)
        one[...] = mm_t(gate[...], rows_at(weights.gate, n)[...])
        tick(weights.tiles + 2 * n)
        tile_at(result, n)[...] = (one[...] + mm_t(up[...], rows_at(weights.up, n)[...])).astype(BF16)
        tick(weights.tiles + 2 * n + 1)

    return weights.tiles + 2 * weights.outs, lambda: sending(False)


def ffn_backward_kernel(low, *refs):
    take = Taker(refs)
    grad, last_b = take(2)
    grad_a, grad_b = ab(grad)
    ins_a, ins_b = zip(*[ab(ref) for ref in take(2)])
    sources = take(2)
    if low:
        sum_a, layer, gain = take(3)
        layer_a, layer_b = ab(layer)
    outs_a, outs_b = zip(*[ab(ref) for ref in take(2)])
    result_b, total_a, total_b = take(3)
    if low:
        made, gain_grad = take(2)
        made_a, made_b = ab(made)
    targets, held = take(3), take(2)
    one, result_a, w_sems, down_sems, in_sems, out_sems = take(6)
    chain_a = Chain(result_a, total_a, *take(CHAIN_REFS))
    chain_b = Chain(last_b, total_b, *take(CHAIN_REFS))
    weights = FfnWeights(sources, targets, w_sems, down_sems, False)

    def fetch(ins):
        @pl.loop(0, weights.tiles)
        def _(j):
            for k in range(2):
                pltpu.make_async_copy(tile_at(ins[k], j), tile_at(held[k], j), in_sems.at[k, j]).start()

    weights.start_deep(True)
    fetch(ins_a)
    weights.start_wide(True)
    greet(cores=1)
    chain_b.start()
    weights.start_deep(False)
    weights.start_wide(False)
    if low:
        gain_grad[...] = jnp.zeros_like(gain_grad)
        norm_back_rows(grad_a, sum_a, lambda r: layer_a[r].astype(F32), gain, gain_grad, made_a)
        grad_a = made_a
    chain_b.step(0)
    done, sent_a = ffn_backward_stage(
        weights, grad_a, ins_a, outs_a, held, one, in_sems, out_sems, result_a, ticker(chain_b, 1), True
    )
    chain_a.start()
    sent_a()
    fetch(ins_b)
    chain_b.drain(1 + done)
    chain_a.step(0)
    if low:
        norm_back_rows(grad_b, total_b, lambda r: layer_b[r].astype(F32), gain, gain_grad, made_b)
        grad_b = made_b
    done, sent_b = ffn_backward_stage(
        weights, grad_b, ins_b, outs_b, held, one, in_sems, out_sems, result_b, ticker(chain_a, 1), False
    )
    chain_a.drain(1 + done)
    chain_a.settle()
    chain_b.settle()
    weights.finish()
    sent_b()


def ffn_backward(grad, gate, up, weights, last_b, below=None):
    rows, width = last_b.shape
    ff = weights[0].shape[1]
    tiles = max(ff, width) // TILE
    low = below is not None
    narrow = jax.ShapeDtypeStruct((rows, width), BF16)
    both, wide = jax.ShapeDtypeStruct((2 * rows, width), BF16), jax.ShapeDtypeStruct((2 * rows, ff), BF16)
    more = [both, jax.ShapeDtypeStruct((8, width), F32)] if low else []
    return pl.pallas_call(
        functools.partial(ffn_backward_kernel, low),
        out_shape=[wide] * 2 + [narrow] * 3 + more,
        in_specs=[VMEM] * 2 + [ANY] * 4 + [VMEM] * (3 if low else 0),
        out_specs=[ANY] * 2 + [VMEM] * (3 + len(more)),
        scratch_shapes=[pltpu.VMEM((width, ff), BF16)] * 3
        + [pltpu.VMEM((rows, ff), BF16)] * 2
        + [pltpu.VMEM((rows, TILE), F32)]
        + [pltpu.VMEM((rows, width), BF16)]
        + [pltpu.SemaphoreType.DMA((3, tiles)), down_sem_shape(weights, tiles)]
        + [pltpu.SemaphoreType.DMA((2, tiles))] * 2
        + chain_scratch((rows, width)) * 2,
        compiler_params=params(3 + low),
        cost_estimate=cost(),
    )(grad, last_b, gate, up, *weights, *(below or ()))


def last_kernel(part, sum_a, grad, layer, gain, made, gain_grad, total, *scratch):
    chain = Chain(part, total, *scratch)
    greet()
    chain.start()
    gain_grad[...] = jnp.zeros_like(gain_grad)
    grads, layers, mades = ab(grad), ab(layer), ab(made)
    chain.step(0)
    norm_back_rows(grads[0], sum_a, lambda r: layers[0][r].astype(F32), gain, gain_grad, mades[0])
    chain.drain(1)
    norm_back_rows(grads[1], total, lambda r: layers[1][r].astype(F32), gain, gain_grad, mades[1])
    chain.settle()


def last_grads(part, sum_a, grad, layer, gain):
    shape = part.shape
    return pl.pallas_call(
        last_kernel,
        out_shape=[jax.ShapeDtypeStruct(grad.shape, BF16), jax.ShapeDtypeStruct((8, shape[1]), F32)],
        in_specs=[VMEM] * 5,
        out_specs=[VMEM] * 2,
        scratch_shapes=[pltpu.VMEM(shape, BF16)] + chain_scratch(shape),
        compiler_params=params(0),
        cost_estimate=cost(),
    )(part, sum_a, grad, layer, gain)


def roped(values, cosine, sine):
    return values * cosine + pltpu.roll(values, HEAD // 2, 1) * sine


def unroped(grads, cosine, sine):
    return grads * cosine + pltpu.roll(grads * sine, HEAD // 2, 1)


def allowed_keys(seg_rows, seg_keys, i, block):
    rows, keys = seg_rows.shape[0], seg_keys.shape[1]
    first_row = lax.axis_index("ctx") * rows + i * block
    row_at = first_row + lax.broadcasted_iota(jnp.int32, (block, keys), 0)
    key_at = lax.broadcasted_iota(jnp.int32, (block, keys), 1)
    own = seg_rows[pl.ds(pl.multiple_of(i * block, block), block)]
    return (key_at <= row_at) & (own == seg_keys[...])


class AttentionWeights:
    def __init__(self, sources, targets, sems):
        self.own, self.other = sources
        self.w_lin, self.w_out = targets
        self.sems = sems

    def copies(self):
        sec = lax.axis_index("section")
        q_cols = self.w_out.shape[1]
        heads_here = q_cols // HEAD
        head = lax.axis_index("tp") * heads_here // (HEADS // KV_HEADS)
        shards, half = self.own.shape[:2]
        for k, (source, side) in enumerate(((self.own, sec), (self.other, 1 - sec))):
            for i in range(shards):
                rows = pl.ds(pl.multiple_of((2 * i + side) * half, 16), half)
                key_at = pl.multiple_of(q_cols + head * HEAD, HEAD)
                value_at = pl.multiple_of(q_cols + (KV_HEADS + head) * HEAD, HEAD)
                pieces = (
                    (pl.ds(0, q_cols), self.w_lin.at[rows, pl.ds(0, q_cols)]),
                    (pl.ds(key_at, HEAD), self.w_lin.at[rows, pl.ds(q_cols, HEAD)]),
                    (pl.ds(value_at, HEAD), self.w_lin.at[rows, pl.ds(q_cols + HEAD, HEAD)]),
                    (pl.ds(q_cols + 2 * KV_HEADS * HEAD, q_cols), self.w_out.at[rows]),
                )
                for p, (columns, target) in enumerate(pieces):
                    yield pltpu.make_async_copy(source.at[i, :, columns], target, self.sems.at[k, i, p])

    def start(self):
        for copy in self.copies():
            copy.start()

    def wait(self):
        for copy in self.copies():
            copy.wait()


def attention_scratch(halves, q_cols):
    shards, half = halves[0].shape[:2]
    width = 2 * shards * half
    return [
        pltpu.VMEM((width, q_cols + 2 * HEAD), BF16),
        pltpu.VMEM((width, q_cols), BF16),
        pltpu.SemaphoreType.DMA((2, shards, 4)),
    ]


def attention_forward_stage(layer_in, gain, w_lin, w_out, bias, places, outs, result, kv_sems, tick):
    cosine, sine, seg_rows, seg_keys = places
    normed, query, kv, lse, attended = outs
    rows, q_cols = query.shape
    heads = q_cols // HEAD
    count = kv.shape[0] // rows
    me = lax.axis_index("ctx")
    block = min(256, rows)
    normalize_rows(lambda r: layer_in[r].astype(F32), gain, normed)
    tick(0)
    mine = kv.at[pl.ds(pl.multiple_of(me * rows, rows), rows)]
    lin = mm(normed[...], w_lin[:, q_cols:]) + bias[:, q_cols:]
    mine[:, :HEAD] = roped(lin[:, :HEAD], cosine[...], sine[...]).astype(BF16)
    mine[:, HEAD:] = lin[:, HEAD:].astype(BF16)

    def passing(offset):
        return pltpu.make_async_remote_copy(
            src_ref=mine,
            dst_ref=mine,
            send_sem=kv_sems.at[0, offset],
            recv_sem=kv_sems.at[1, offset],
            device_id={"ctx": lax.rem(me + offset, count)},
            device_id_type=MESH,
        )

    for offset in range(1, count):
        passing(offset).start()
    tick(1)
    lin = mm(normed[...], w_lin[:, :q_cols]) + bias[:, :q_cols]
    for h in range(heads):
        columns = slice(h * HEAD, (h + 1) * HEAD)
        query[:, columns] = roped(lin[:, columns], cosine[...], sine[...]).astype(BF16)
    for offset in range(1, count):
        passing(offset).wait_recv()

    @pl.loop(0, rows // block)
    def _(i):
        at = pl.ds(pl.multiple_of(i * block, block), block)
        allowed = allowed_keys(seg_rows, seg_keys, i, block)
        lane = lax.broadcasted_iota(jnp.int32, (block, HEAD), 1)
        logs = jnp.zeros((block, HEAD), F32)
        for h in range(heads):
            columns = slice(h * HEAD, (h + 1) * HEAD)
            scores = jnp.where(allowed, mm_t(query[at, columns], kv[:, :HEAD]) * SCALE, NEG)
            top = jnp.max(scores, axis=-1, keepdims=True)
            probs = jnp.exp(scores - top)
            sums = jnp.sum(probs, axis=-1, keepdims=True)
            probs = (probs * (1.0 / sums)).astype(BF16)
            attended[at, columns] = mm(probs, kv[:, HEAD:]).astype(BF16)
            logs = jnp.where(lane == h, top + jnp.log(sums), logs)
            tick(2 + heads * i + h)
        lse[at] = logs

    base = 2 + heads * (rows // block)

    @pl.loop(0, result.shape[1] // TILE)
    def _(n):
        tile_at(result, n)[...] = mm_t(attended[...], rows_at(w_out, n)[...]).astype(BF16)
        tick(base + n)

    for offset in range(1, count):
        passing(offset).wait_send()
    return base + result.shape[1] // TILE


def attention_forward_kernel(low, *refs):
    take = Taker(refs)
    gain, bias = take(2)
    halves = take(2)
    places_a, places_b = take(4), take(4)
    layer_a, layer_b = ab(take(1)[0])
    if not low:
        adds_a, adds_b, (last_b,) = (layer_a, *take(2)), (layer_b, *take(1)), take(1)
    outs_a, outs_b = zip(*[ab(ref) for ref in take(5)])
    if low:
        total_a, total_b = take(2)
    else:
        result_b, total_a, last_sum_b, layer = take(4)
        layer_a, layer_b = ab(layer)
    result_a, kv_sems_a, kv_sems_b = take(3)
    w_lin, w_out, w_sems = take(3)
    weights = AttentionWeights(halves, (w_lin, w_out), w_sems)
    weights.start()
    if low:
        (result_b,) = take(1)
    chain_a = Chain(result_a, total_a, *take(CHAIN_REFS))
    chain_b = Chain(result_b, total_b, *take(CHAIN_REFS)) if low else Chain(last_b, last_sum_b, *take(CHAIN_REFS))
    greet(kv_sems_a.shape[1])
    if not low:
        chain_b.start()

        def body(rows):
            layer_a[rows] = sum(ref[rows].astype(F32) for ref in adds_a).astype(BF16)

        by_rows(layer_a.shape[0], body)
    weights.wait()
    tick = ticker(None if low else chain_b, 0)
    done = attention_forward_stage(layer_a, gain, w_lin, w_out, bias, places_a, outs_a, result_a, kv_sems_a, tick)
    chain_a.start()
    if not low:
        chain_b.drain(done)
        chain_a.step(0)

        def body(rows):
            layer_b[rows] = sum(ref[rows].astype(F32) for ref in (*adds_b, last_sum_b)).astype(BF16)

        by_rows(layer_b.shape[0], body)
    taken = 0 if low else 1
    tick = ticker(chain_a, taken)
    done = attention_forward_stage(layer_b, gain, w_lin, w_out, bias, places_b, outs_b, result_b, kv_sems_b, tick)
    if low:
        chain_b.start()
    chain_a.drain(taken + done)
    if low:
        chain_b.drain(0)
    chain_a.settle()
    chain_b.settle()


def attention_forward(weights, places, inputs):
    halves, q_cols, gains, bias = weights
    rows, width = inputs[0].shape[0] // 2, inputs[0].shape[1]
    keys = places[0][3].shape[1]
    count = keys // rows
    low = len(inputs) == 1
    narrow, both = jax.ShapeDtypeStruct((rows, width), BF16), jax.ShapeDtypeStruct((2 * rows, width), BF16)
    heads_out = jax.ShapeDtypeStruct((2 * rows, q_cols), BF16)
    kv_out = jax.ShapeDtypeStruct((2 * keys, 2 * HEAD), BF16)
    lse_out = jax.ShapeDtypeStruct((2 * rows, HEAD), F32)
    outs = [both, heads_out, kv_out, lse_out, heads_out] + ([narrow] * 2 if low else [narrow] * 3 + [both])
    args = (gains[:1], bias, *halves, *places[0], *places[1], *inputs)
    return pl.pallas_call(
        functools.partial(attention_forward_kernel, low),
        out_shape=outs,
        in_specs=[VMEM] * 2 + [ANY] * 2 + [VMEM] * (len(args) - 4),
        out_specs=[VMEM] * len(outs),
        scratch_shapes=[pltpu.VMEM((rows, width), BF16)]
        + [pltpu.SemaphoreType.DMA((2, count))] * 2
        + attention_scratch(halves, q_cols)
        + [pltpu.VMEM((rows, width), BF16)] * low
        + chain_scratch((rows, width)) * 2,
        compiler_params=params(5 + low),
        cost_estimate=cost(),
    )(*args)


def attention_backward_stage(ins, sum_in, gain, w_lin, w_out, places, outs, gain_grad, result, scratch, tick):
    upstream, layer_in, attn_out, query, kv, lse, attended = ins
    cosine, sine, seg_rows, seg_keys = places
    attn_grad, lin = outs
    heads_grad, kv_grad, q_part, sent, got, kv_sems = scratch
    rows, q_cols = query.shape
    heads = q_cols // HEAD
    count = kv.shape[0] // rows
    me = lax.axis_index("ctx")
    block = min(256, rows)
    kv_grad[...] = jnp.zeros_like(kv_grad)
    norm_back_rows(
        upstream, sum_in, lambda r: layer_in[r].astype(F32) + attn_out[r].astype(F32), gain, gain_grad, attn_grad
    )
    tick(0)
    heads_grad[...] = mm(attn_grad[...], w_out[...]).astype(BF16)
    tick(1)

    @pl.loop(0, rows // block)
    def _(i):
        at = pl.ds(pl.multiple_of(i * block, block), block)
        allowed = allowed_keys(seg_rows, seg_keys, i, block)
        for h in range(heads):
            columns = slice(h * HEAD, (h + 1) * HEAD)
            scores = mm_t(query[at, columns], kv[:, :HEAD]) * SCALE - lse[at, h : h + 1]
            probs = jnp.exp(jnp.where(allowed, scores, NEG))
            grad = heads_grad[at, columns]
            row_sum = jnp.sum(attended[at, columns].astype(F32) * grad.astype(F32), axis=-1, keepdims=True)
            score_grad = (probs * (mm_t(grad, kv[:, HEAD:]) - row_sum)).astype(BF16)
            q_grad = mm(score_grad, kv[:, :HEAD]) * SCALE
            lin[at, columns] = unroped(q_grad, cosine[at], sine[at]).astype(BF16)
            kv_grad[:, :HEAD] += mm_0(score_grad, query[at, columns])
            kv_grad[:, HEAD:] += mm_0(probs.astype(BF16), grad)
            tick(2 + heads * i + h)

    def passing(offset):
        return pltpu.make_async_remote_copy(
            src_ref=sent.at[offset - 1],
            dst_ref=got.at[offset - 1],
            send_sem=kv_sems.at[0, offset],
            recv_sem=kv_sems.at[1, offset],
            device_id={"ctx": lax.rem(me + offset, count)},
            device_id_type=MESH,
        )

    for offset in range(1, count):
        peer = pl.ds(pl.multiple_of(lax.rem(me + offset, count) * rows, rows), rows)
        sent[offset - 1, :, :HEAD] = (kv_grad[peer, :HEAD] * SCALE).astype(BF16)
        sent[offset - 1, :, HEAD:] = kv_grad[peer, HEAD:].astype(BF16)
        passing(offset).start()
    base = 2 + heads * (rows // block)

    @pl.loop(0, result.shape[1] // TILE)
    def _(n):
        tile_at(q_part, n)[...] = mm_t(lin[:, :q_cols], rows_at(w_lin, n)[:, :q_cols])
        tick(base + n)

    mine = pl.ds(pl.multiple_of(me * rows, rows), rows)
    k_grad, v_grad = kv_grad[mine, :HEAD] * SCALE, kv_grad[mine, HEAD:]
    for offset in range(1, count):
        passing(offset).wait_recv()
        k_grad = k_grad + got[offset - 1, :, :HEAD].astype(F32)
        v_grad = v_grad + got[offset - 1, :, HEAD:].astype(F32)
    lin[:, q_cols : q_cols + HEAD] = unroped(k_grad, cosine[...], sine[...]).astype(BF16)
    lin[:, q_cols + HEAD :] = v_grad.astype(BF16)

    @pl.loop(0, result.shape[1] // TILE)
    def _(n):
        kv_part = mm_t(lin[:, q_cols:], rows_at(w_lin, n)[:, q_cols:])
        tile_at(result, n)[...] = (tile_at(q_part, n)[...] + kv_part).astype(BF16)


    for offset in range(1, count):
        passing(offset).wait_send()
    return base + result.shape[1] // TILE


def attention_backward_kernel(*refs):
    take = Taker(refs)
    (gain,) = take(1)
    halves = take(2)
    places_a, places_b = take(4), take(4)
    ins_a, ins_b = zip(*[ab(ref) for ref in take(6)])
    attn_a, attn_b = take(2)
    ins_a, ins_b = (*ins_a[:2], attn_a, *ins_a[2:]), (*ins_b[:2], attn_b, *ins_b[2:])
    sum_a, last_b = take(2)
    outs_a, outs_b = zip(*[ab(ref) for ref in take(2)])
    gain_grad, result_b, total_a, total_b = take(4)
    heads_grad, kv_grad, q_part, result_a = take(4)
    w_lin, w_out, w_sems = take(3)
    weights = AttentionWeights(halves, (w_lin, w_out), w_sems)
    weights.start()
    exchange_a, exchange_b = take(3), take(3)
    chain_a = Chain(result_a, total_a, *take(CHAIN_REFS))
    chain_b = Chain(last_b, total_b, *take(CHAIN_REFS))
    greet(exchange_a[2].shape[1])
    chain_b.start()
    gain_grad[...] = jnp.zeros_like(gain_grad)
    weights.wait()
    scratch = (heads_grad, kv_grad, q_part, *exchange_a)
    done = attention_backward_stage(
        ins_a, sum_a, gain, w_lin, w_out, places_a, outs_a, gain_grad, result_a, scratch, ticker(chain_b, 0)
    )
    chain_a.start()
    chain_b.drain(done)
    chain_a.step(0)
    scratch = (heads_grad, kv_grad, q_part, *exchange_b)
    done = attention_backward_stage(
        ins_b, total_b, gain, w_lin, w_out, places_b, outs_b, gain_grad, result_b, scratch, ticker(chain_a, 1)
    )
    chain_a.drain(1 + done)
    chain_a.settle()
    chain_b.settle()


def attention_backward(upstream, sum_a, last_b, kept, weights, places):
    halves, q_cols, gains, bias = weights
    rows, width = sum_a.shape
    keys = places[0][3].shape[1]
    count = keys // rows
    narrow = jax.ShapeDtypeStruct((rows, width), BF16)
    both = jax.ShapeDtypeStruct((2 * rows, width), BF16)
    lin_out = jax.ShapeDtypeStruct((2 * rows, q_cols + 2 * HEAD), BF16)
    outs = [both, lin_out] + [jax.ShapeDtypeStruct((8, width), F32)] + [narrow] * 3
    names = ("layer_in", "query", "kv", "lse", "attended", "attn_a", "attn_b")
    args = (gains[1:], *halves, *places[0], *places[1], upstream)
    args += (*[kept[name] for name in names], sum_a, last_b)
    exchange = [pltpu.VMEM((max(count - 1, 1), rows, 2 * HEAD), BF16)] * 2 + [pltpu.SemaphoreType.DMA((2, count))]
    return pl.pallas_call(
        attention_backward_kernel,
        out_shape=outs,
        in_specs=[VMEM] + [ANY] * 2 + [VMEM] * (len(args) - 3),
        out_specs=[VMEM] * len(outs),
        scratch_shapes=[
            pltpu.VMEM((rows, q_cols), BF16),
            pltpu.VMEM((keys, 2 * HEAD), F32),
            pltpu.VMEM((rows, width), F32),
            pltpu.VMEM((rows, width), BF16),
        ]
        + attention_scratch(halves, q_cols)
        + exchange * 2
        + chain_scratch((rows, width)) * 2,
        compiler_params=params(7),
        cost_estimate=cost(),
    )(*args)


def rope_tables(places):
    steps = jnp.arange(HEAD // 2, dtype=F32) * (2.0 / HEAD)
    inverse = ROPE_BASE ** (-steps)
    angles = places.astype(F32)[..., None] * inverse
    angles = jnp.concatenate([angles, angles], axis=-1)
    return (jnp.cos(angles), jnp.sin(angles))


def norm_back(grad_out, rows_in, factor, gain):
    unit = rows_in * factor
    gain_grad = jnp.sum(grad_out * unit, axis=0)
    weighted = grad_out * gain
    return (
        factor * (weighted - unit * jnp.mean(weighted * unit, axis=-1, keepdims=True)),
        gain_grad,
    )


def over_ctx(value):
    if lax.axis_size("ctx") == 2:
        other = lax.ppermute(value, "ctx", [(0, 1), (1, 0)])
        low = lax.axis_index("ctx") == 0
        return jnp.concatenate([jnp.where(low, value, other), jnp.where(low, other, value)], axis=-1)
    return lax.all_gather(value, "ctx", axis=value.ndim - 1, tiled=True)


def input_backward(normed_one_grad, middle_grad, kept, gains):
    layer_in = kept["layer_in"].astype(F32)
    factor = lax.rsqrt(jnp.mean(layer_in * layer_in, axis=-1, keepdims=True) + EPS)
    norm_grad, gain_one = norm_back(normed_one_grad.astype(F32), layer_in, factor, gains[0])
    return (middle_grad.astype(F32) + norm_grad).astype(BF16), gain_one


def local(
    section_in,
    segments,
    positions,
    query_weight,
    kv_weight,
    output_weight,
    gate_up,
    down_weight,
    norm_gains,
    query_bias,
    kv_bias,
    out_grad,
):
    sec = lax.axis_index("section")
    first = sec == 0
    group = HEADS // KV_HEADS
    heads_here = HEADS // lax.axis_size("tp")
    head_pick = lax.axis_index("tp") * heads_here // group
    shards = lax.axis_size("dp") * lax.axis_size("ctx")
    ranks = ("dp", "ctx")
    seqs, span, width = section_in.shape[1:]
    shard = query_weight.shape[1]
    q_cols = query_weight.shape[2]
    ff = gate_up.shape[3]

    def per_layer(mine, theirs):
        return jnp.where(first, mine, theirs), jnp.where(first, theirs, mine)

    half = shard // 2
    kv_width = KV_HEADS * HEAD

    def halves(rows):
        mine = lax.dynamic_slice_in_dim(rows, sec * half, half, 0)
        return per_layer(mine, swap(lax.dynamic_slice_in_dim(rows, (1 - sec) * half, half, 0)))

    def after(value, event):
        return lax.optimization_barrier((value, event))[0]

    piece = HEAD // shards
    biases = jnp.concatenate([query_bias[0].reshape(-1), kv_bias[0].reshape(-1)])
    n_biases = biases.shape[0]
    biases = jnp.pad(biases, (0, -n_biases % shard)).reshape(-1, shard).T
    extra = jnp.concatenate([norm_gains[0].T, biases], axis=1)
    n_extra = extra.shape[1]
    extra = jnp.pad(extra, ((0, 0), (0, HEAD - n_extra)))
    packed = jnp.concatenate([query_weight[0], kv_weight[0, 0], kv_weight[0, 1], output_weight[0].T, extra], axis=1)
    packed_shards = halves(packed)
    first_shard, gate_up, down_weight, positions, segments, section_in = lax.optimization_barrier(
        (packed_shards[0], gate_up, down_weight, positions, segments, section_in)
    )
    packed_low = lax.all_gather(first_shard, ranks, axis=0)
    spare = -ff % TILE
    wide = jnp.pad(gate_up[0], ((0, 0), (0, 0), (0, spare)))
    mine = lax.dynamic_index_in_dim(wide, sec, 0, keepdims=False)
    theirs = swap(lax.dynamic_index_in_dim(wide, 1 - sec, 0, keepdims=False))
    gate_up_shards = per_layer(mine, theirs)
    down_shards = halves(jnp.pad(down_weight[0].T, ((0, 0), (0, spare))))

    micro = sec
    seg = lax.dynamic_index_in_dim(segments, micro, 0, keepdims=False)
    pos = lax.dynamic_index_in_dim(positions, micro, 0, keepdims=False)
    hidden = lax.dynamic_index_in_dim(section_in, micro, 0, keepdims=False)
    seg_keys = over_ctx(seg)
    segs, tables = [], []
    for q in range(seqs):
        segs.append((seg[q][:, None], seg_keys[q][None]))
        cosine, sine = rope_tables(pos[q])
        tables.append((cosine, jnp.where(jnp.arange(HEAD) < HEAD // 2, -sine, sine)))
    hidden = hidden.reshape(seqs * span, width)

    packed_low, gate_up_shards, down_shards, packed_shards, segs, tables, hidden = lax.optimization_barrier(
        (packed_low, gate_up_shards, down_shards, packed_shards, segs, tables, hidden)
    )
    own_low = lax.all_gather(gate_up_shards[0], ranks, axis=0, tiled=True)
    down_low = lax.all_gather(down_shards[0], ranks, axis=0)

    def attention_weights(own):
        parts = own, swap(own)
        small = [part[..., 2 * q_cols + 2 * kv_width :] for part in parts]
        s = jnp.stack(per_layer(*small), axis=1).reshape(width, -1)
        gains = s[:, :2].T
        s = s[:, 2:n_extra].T.reshape(-1, shards, shard).transpose(1, 0, 2).reshape(shards, -1)[:, :n_biases]
        q_b = s[:, : heads_here * piece].reshape(shards, heads_here, piece).transpose(1, 0, 2).reshape(heads_here, HEAD)
        kv_b = s[:, heads_here * piece :].reshape(shards, 2, KV_HEADS, piece)
        kv_b = kv_b.transpose(1, 2, 0, 3).reshape(2, KV_HEADS, HEAD)
        kv_b = lax.dynamic_slice_in_dim(kv_b, head_pick, 1, 1)
        bias = jnp.concatenate([q_b.reshape(1, -1), kv_b.reshape(1, -1)], axis=1).astype(F32)
        return parts, q_cols, gains.astype(F32), bias

    names = ("normed", "query", "kv", "lse", "attended")
    more_names = ("normed_two", "gate", "up", "inner")
    attn_weights, ffn_weights = [attention_weights(packed_low), None], [None, None]
    places = [(*tables[q], *segs[q]) for q in range(seqs)]

    def keep(layer, names, values):
        kept[layer].update(zip(names, values))
        return values[len(names) :]

    kept = [dict(), dict()]
    attn_a, attn_b = keep(0, names, attention_forward(attn_weights[0], places, (hidden,)))
    kept[0].update(layer_in=hidden, attn_a=attn_a, attn_b=attn_b)
    attn_b, own_low, down_low = lax.optimization_barrier((attn_b, own_low, down_low))
    ffn_weights[0] = own_low, down_low
    packed_high = lax.all_gather(after(packed_shards[1], attn_b), ranks, axis=0)
    own_high = lax.all_gather(after(gate_up_shards[1], attn_b), ranks, axis=0, tiled=True)
    down_high = lax.all_gather(after(down_shards[1], attn_b), ranks, axis=0)
    gain = attn_weights[0][2][1:]
    part_b, ffn_a = keep(
        0, more_names, ffn_forward(False, hidden, attn_a, attn_b, gain, ffn_weights[0])
    )

    packed_high, part_b = lax.optimization_barrier((packed_high, part_b))
    attn_weights[1] = attention_weights(packed_high)
    inputs = (hidden, attn_a, ffn_a, attn_b, part_b)
    part_b, attn_a, _, layer_in = keep(1, names, attention_forward(attn_weights[1], places, inputs))
    part_b, own_high, down_high = lax.optimization_barrier((part_b, own_high, down_high))
    ffn_weights[1] = own_high, down_high
    gain = attn_weights[1][2][1:]
    part_b, ffn_a, attn_b = keep(
        1, more_names, ffn_forward(True, layer_in, attn_a, part_b, gain, ffn_weights[1])
    )
    kept[1].update(layer_in=layer_in, attn_a=attn_a, attn_b=attn_b)
    upstream = lax.dynamic_index_in_dim(out_grad, micro, 0, keepdims=False).reshape(seqs * span, width)
    k = kept[1]
    *wide_grads, grad_b, sum_a, ffn_b = ffn_backward(upstream, k["gate"], k["up"], ffn_weights[1], part_b)
    attn_sum, ffn_sum = jnp.concatenate([attn_a, attn_b]), jnp.concatenate([ffn_a, ffn_b])
    outs = [layer_in, (layer_in.astype(F32) + attn_sum.astype(F32) + ffn_sum.astype(F32)).astype(BF16)]

    def to_section(values, low, high):
        both = jnp.stack([jnp.where(first, values[0], high), jnp.where(first, low, values[1])])
        return both.reshape(2, seqs, span, width)

    def to_low(value):
        return lax.ppermute(value, "section", [(1, 0)])

    def to_high(value):
        return lax.ppermute(value, "section", [(0, 1)])

    def exchanged(values):
        return swap(jnp.where(first, values[1], values[0]))

    out_other = exchanged(outs)

    in_grads = [None, None]
    gate_up_grads, down_grads, packed_grads, gains_grads = [[None, None] for _ in range(4)]
    for layer in (1, 0):
        weights, k = attn_weights[layer], kept[layer]
        if layer == 0:
            below = (sum_a, kept[1]["layer_in"], attn_weights[1][2][:1])
            *wide_grads, grad_b, sum_a, _, upstream, gain_one = ffn_backward(
                attn_grad, k["gate"], k["up"], ffn_weights[0], part_b, below
            )
            in_grads[1] = upstream
            in_high = to_high(upstream)
            gains_grads[1] = jnp.stack([jnp.sum(gain_one, axis=0), gain_two])
            sum_a, gate_up_grads[1] = lax.optimization_barrier((sum_a, gate_up_grads[1]))
        own_w, other_w = [dot("rd,rf->df", k["normed_two"], g).astype(BF16) for g in wide_grads]
        other_w = swap(other_w)
        down_w = dot("rd,rf->df", upstream, k["inner"]).astype(BF16)
        down_w = down_w.reshape(shards, 2, half, ff + spare)
        down_own = lax.dynamic_index_in_dim(down_w, sec, 1, keepdims=False)
        down_other = swap(lax.dynamic_index_in_dim(down_w, 1 - sec, 1, keepdims=False))
        own_w = (own_w.astype(F32) + other_w.astype(F32)).astype(BF16)
        own_w, down_other = lax.optimization_barrier((own_w, down_other))
        down_own = (down_own.astype(F32) + down_other.astype(F32)).astype(BF16)
        own_w, down_own, sum_a = lax.optimization_barrier((own_w, down_own, sum_a))
        gate_up_grads[layer] = lax.psum_scatter(own_w, ranks, scatter_dimension=0, tiled=True)
        down_grads[layer] = lax.psum_scatter(
            down_own.reshape(shards * half, ff + spare), ranks, scatter_dimension=0, tiled=True
        )

        attn_grad, lin_grad, gain_two, part_b, sum_a, _ = attention_backward(upstream, sum_a, grad_b, k, weights, places)
        gain_two = jnp.sum(gain_two, axis=0)
        if layer == 0:
            part_b, down_grads[1] = lax.optimization_barrier((part_b, down_grads[1]))
        lin_w = dot("rd,re->de", k["normed"], lin_grad)
        out_w = dot("rd,re->de", attn_grad, k["attended"])
        bias = jnp.sum(lin_grad.astype(F32), axis=0)
        bias = bias.reshape(heads_here + 2, shards, piece).transpose(1, 0, 2).reshape(shards, (heads_here + 2) * piece)
        bias = jnp.pad(bias, ((0, 0), (0, -bias.shape[1] % shard)))
        bias = bias.reshape(shards, -1, shard).transpose(0, 2, 1).reshape(width, -1)
        bias = jnp.pad(bias, ((0, 0), (0, HEAD - bias.shape[1])))
        packed_grads[layer] = jnp.concatenate([lin_w, out_w, bias], axis=1).astype(BF16)

    packed_total = jnp.where(first, packed_grads[0], packed_grads[1]).astype(F32)
    packed_total = (packed_total + exchanged(packed_grads).astype(F32)).astype(BF16)
    last_part, gate_up_grads[0], down_grads[0], packed_total = lax.optimization_barrier(
        (part_b, gate_up_grads[0], down_grads[0], packed_total)
    )
    packed_total = lax.psum_scatter(packed_total, ranks, scatter_dimension=0, tiled=True).astype(F32)
    in_grads[0], gain_one = last_grads(last_part, sum_a, attn_grad, kept[0]["layer_in"], attn_weights[0][2][:1])
    gains_grads[0] = jnp.stack([jnp.sum(gain_one, axis=0), gain_two])
    in_grads[0], out_other, in_high = lax.optimization_barrier((in_grads[0], out_other, in_high))
    in_low = to_low(in_grads[0])
    gains_grad = jnp.where(first, gains_grads[0], gains_grads[1]) + exchanged(gains_grads)
    for axis in ranks:
        if lax.axis_size(axis) == 2:
            gains_grad = gains_grad + lax.ppermute(gains_grad, axis, [(0, 1), (1, 0)])
        else:
            gains_grad = lax.psum(gains_grad, axis)
    at = (lax.axis_index("dp") * lax.axis_size("ctx") + lax.axis_index("ctx")) * shard
    gains_grad = lax.dynamic_slice_in_dim(gains_grad, at, shard, 1)
    q_grad = packed_total[:, :q_cols]
    kv_narrow = packed_total[:, q_cols : q_cols + 2 * HEAD].reshape(shard, 2, HEAD)
    o_grad = packed_total[:, q_cols + 2 * HEAD : 2 * q_cols + 2 * HEAD].T
    extra = packed_total[:, 2 * q_cols + 2 * HEAD :]
    bias_cols = -(-(heads_here + 2) * piece // shard)
    bias = extra[:, :bias_cols].T.reshape(-1)[: (heads_here + 2) * piece].reshape(heads_here + 2, piece)
    q_bias_grad = bias[:heads_here]
    kv_bias = bias[heads_here:].reshape(1, -1)
    kv_bias = jnp.pad(kv_bias, ((0, 15), (0, -kv_bias.shape[1] % (2 * HEAD))))
    mine = jnp.concatenate([kv_narrow.reshape(shard, 2 * HEAD), kv_bias[:, : 2 * HEAD]]).astype(BF16)
    mine = (mine.astype(F32) + lax.ppermute(mine, "tp", [(0, 1), (1, 0), (2, 3), (3, 2)]).astype(F32)).astype(BF16)
    theirs = lax.ppermute(mine, "tp", [(0, 2), (2, 0), (1, 3), (3, 1)])
    mine, theirs = mine.astype(F32), theirs.astype(F32)
    low = head_pick == 0
    heads = jnp.stack([jnp.where(low, mine, theirs), jnp.where(low, theirs, mine)])
    kv_grad = heads[:, :shard].reshape(KV_HEADS, shard, 2, HEAD).transpose(2, 1, 0, 3).reshape(2, shard, KV_HEADS * HEAD)
    kv_bias_grad = heads[:, shard, : 2 * piece].reshape(KV_HEADS, 2, piece).transpose(1, 0, 2)

    def collect(values):
        kept_half = jnp.where(first, values[0], values[1])
        other = swap(jnp.where(first, values[1], values[0]))
        return jnp.where(first, kept_half, other), jnp.where(first, other, kept_half)

    section_out = to_section(outs, out_other, out_other)
    input_grad = to_section(in_grads, in_low, in_high)
    gate_up_grad = jnp.stack(collect(gate_up_grads))[..., :ff].astype(F32)
    down_grad = jnp.concatenate(collect(down_grads), axis=0)[:, :ff].T.astype(F32)
    return (
        section_out[None],
        input_grad[None],
        q_grad[None],
        kv_grad[None],
        o_grad[None],
        gate_up_grad[None],
        down_grad[None],
        gains_grad[None],
        q_bias_grad[None],
        kv_bias_grad[None],
    )


def solution(mesh):
    in_specs = (
        P(None, "dp", "ctx", None),
        P(None, "dp", "ctx"),
        P(None, "dp", "ctx"),
        P("section", ("dp", "ctx"), "tp"),
        P("section", None, ("dp", "ctx"), None),
        P("section", "tp", ("dp", "ctx")),
        P("section", None, ("dp", "ctx"), "tp"),
        P("section", "tp", ("dp", "ctx")),
        P("section", None, ("dp", "ctx")),
        P("section", "tp", ("dp", "ctx")),
        P("section", None, None, ("dp", "ctx")),
        P(None, "dp", "ctx", None),
    )
    out_specs = (
        P("section", None, "dp", "ctx", None),
        P("section", None, "dp", "ctx", None),
        P("section", ("dp", "ctx"), "tp"),
        P("section", None, ("dp", "ctx"), None),
        P("section", "tp", ("dp", "ctx")),
        P("section", None, ("dp", "ctx"), "tp"),
        P("section", "tp", ("dp", "ctx")),
        P("section", None, ("dp", "ctx")),
        P("section", "tp", ("dp", "ctx")),
        P("section", None, None, ("dp", "ctx")),
    )
    return jax.shard_map(local, mesh=mesh, in_specs=in_specs, out_specs=out_specs, check_vma=False)
```
